32 devices in a mesh: gx: 8 (over z, x), gy: 4 (over y, core).
Axes of the slice: x: 2, y: 2, z: 4, core: 2. Of those that a mesh axis runs over, the one named last changes fastest.
Arguments:
- conc: float32 [64, 128, 256], P('gx', 'gy'), may hold values from 0 to 1
- labels: int32 [64, 128, 256], P('gx', 'gy'), may hold values from 0 to 2
- kappa: float32 [3], replicated, may hold values from 0.1 to 1
- adjoint_source: float32 [64, 128, 256], P('gx', 'gy'), may hold values from -40 to 40
Outputs:
- adjoint: float32 [64, 128, 256], P('gx', 'gy')
- residual: float32 [64, 128, 256], P('gx', 'gy')
The draws below stay inside these ranges and needn't reach their ends.
All inputs are finite; a program needn't handle non-finite values.
Results may differ from the reference program's by a relative error of at most 0.008.
Values sent between devices are 32-bit elements; how exact they have to be, the bound alone decides.
No kernel may reach another device: no remote copies, remote signals or barrier semaphores. Data moves between devices by JAX's collectives and lax.ppermute only.
A program may use at most 64 MiB of HBM per device.

```python
import math
import jax
import jax.numpy as jnp

CZ = 256
PHASES = 3
ITERS = 2
NX = 64
NY = 128


def draw_adjoint_source(key, part):
    key_x, key_y, key_v = jax.random.split(key, 3)
    along_x = 10.0 ** jax.random.uniform(key_x, (NX, 1, 1), jnp.float32, -0.5, 0.5)
    along_y = 10.0 ** jax.random.uniform(key_y, (1, NY, 1), jnp.float32, -0.5, 0.5)
    values = jax.random.truncated_normal(key_v, -4.0, 4.0, (NX, NY, CZ), jnp.float32)
    return (values * along_x * along_y).astype(jnp.float32)


def set_ends(drawn, stream_key, low, high):
    index_at = [jax.random.randint(jax.random.fold_in(stream_key, axis), (), 0, length) for axis, length in enumerate(drawn.shape)]
    widest = drawn.shape.index(max(drawn.shape))
    beside = index_at[:widest] + [(index_at[widest] + 1) % drawn.shape[widest]] + index_at[widest + 1:]
    return drawn.at[tuple(index_at)].set(low).at[tuple(beside)].set(high)


def levels(rng, shape, shards, low, largest):
    def one(axis_at, blocks):
        heights = jax.random.uniform(jax.random.fold_in(jax.random.fold_in(rng, 6), axis_at), (blocks,), jnp.float32, low / len(shards), largest / len(shards))
        return jnp.repeat(jnp.exp(heights), shape[axis_at] // blocks).reshape((-1,) + (1,) * (len(shape) - axis_at - 1))

    factor_of = one(*shards[0])
    for cut in shards[1:]:
        factor_of = factor_of * one(*cut)
    return factor_of


def setup_inputs(seed: int = 0) -> dict:
    key_of = jax.random.split(jax.random.key(seed), 5)
    return {
        "conc": jnp.clip(1.0 * jax.random.uniform(key_of[0], (NX, NY, CZ), jnp.float32) ** levels(key_of[0], (NX, NY, CZ), ((0, 8), (1, 4)), -0.2, 0.2), 0.0, 1.0),
        "labels": set_ends(jax.random.randint(key_of[1], (NX, NY, CZ), 0, 3), jax.random.fold_in(key_of[1], 1), 0, 2).astype(jnp.int32),
        "kappa": jnp.clip(jnp.exp(jax.random.uniform(key_of[2], (PHASES,), jnp.float32, math.log(0.1), math.log(1.0))), 0.1, 1.0),
        "adjoint_source": draw_adjoint_source(jax.random.fold_in(key_of[4], 71), 0),
    }


DT = 0.5


def zup(c):
    return jnp.concatenate([c[..., 1:], jnp.zeros_like(c[..., :1])], -1)


def zdown(c):
    return jnp.concatenate([jnp.zeros_like(c[..., :1]), c[..., :-1]], -1)


def beside_all(padded):
    center = padded[1:-1, 1:-1]
    return center, [padded[2:, 1:-1], padded[:-2, 1:-1], padded[1:-1, 2:], padded[1:-1, :-2], zup(center), zdown(center)]


def apply_op(field, conc_pad, diff_pad, transpose):
    w_mid, w_side = beside_all(field)
    u_mid, u_side = beside_all(conc_pad)
    d_mid, d_side = beside_all(diff_pad)
    total = w_mid
    for w_nb, u_nb, d_nb in zip(w_side, u_side, d_side):
        total = total + DT * 0.5 * (d_mid + d_nb) * (w_mid - w_nb)
        if transpose:
            total = total + 0.5 * DT * d_mid * (u_nb - u_mid) * (w_nb - w_mid)
        else:
            total = total - 0.5 * DT * (d_mid * w_mid + d_nb * w_nb) * (u_nb - u_mid)
    return total


def sectioned_total(values):
    return jnp.sum(jnp.sum(jnp.sum(values, axis=2), axis=1), axis=0)


def pad_xy(a):
    return jnp.pad(a, ((1, 1), (1, 1), (0, 0)))


def reference(conc, labels, kappa, adjoint_source):
    base = jnp.zeros_like(conc)
    for phase in range(3):
        base = base + jnp.where(labels == phase, kappa[phase], 0.0)
    diffuse = base * jnp.exp(conc)
    conc_pad = pad_xy(conc)
    diff_pad = pad_xy(diffuse)
    adjoint = jnp.zeros_like(adjoint_source)
    residual = adjoint_source
    direction = adjoint_source
    norm_now = sectioned_total(residual * residual)
    for step in range(ITERS):
        image = apply_op(pad_xy(direction), conc_pad, diff_pad, True)
        alpha = norm_now / sectioned_total(image * image)
        adjoint = adjoint + alpha * image
        residual = residual - alpha * apply_op(pad_xy(image), conc_pad, diff_pad, False)
        norm_next = sectioned_total(residual * residual)
        direction = residual + (norm_next / norm_now) * direction
        norm_now = norm_next
    return adjoint, residual
```

```python
import functools

import jax
import jax.numpy as jnp
from jax import lax
from jax.experimental import pallas as pl
from jax.experimental.pallas import tpu as pltpu
from jax.sharding import PartitionSpec as P

ITERS = 2
DT = 0.5
W = 2 * ITERS
F32 = jnp.float32


def pack_kernel(kappa, conc, labels, source, diff, xhead, xtail, yhead, ytail):
    nx, ny, _ = conc.shape

    def body(x, carry):
        u = conc[x]
        lab = labels[x]
        base = jnp.where(lab == 0, kappa[0], jnp.where(lab == 1, kappa[1], kappa[2]))
        diff[x] = (0.5 * DT) * base * jnp.exp(u)
        return carry

    lax.fori_loop(0, nx, body, 0)
    for k, ref in enumerate((conc, diff, source)):
        xhead[k] = ref[0:W]
        xtail[k] = ref[nx - W : nx]
        yhead[k] = ref[:, 0:W, :]
        ytail[k] = ref[:, ny - W : ny, :]


def pack(conc, labels, kappa, source):
    nx, ny, nz = conc.shape
    whole = pl.BlockSpec(memory_space=pltpu.VMEM)
    return pl.pallas_call(
        pack_kernel,
        out_shape=(
            jax.ShapeDtypeStruct((nx, ny, nz), F32),
            jax.ShapeDtypeStruct((3, W, ny, nz), F32),
            jax.ShapeDtypeStruct((3, W, ny, nz), F32),
            jax.ShapeDtypeStruct((3, nx, W, nz), F32),
            jax.ShapeDtypeStruct((3, nx, W, nz), F32),
        ),
        in_specs=[pl.BlockSpec(memory_space=pltpu.SMEM), whole, whole, whole],
        out_specs=(whole,) * 5,
        compiler_params=pltpu.CompilerParams(vmem_limit_bytes=16 << 20),
        name="pack",
    )(kappa, conc, labels, source)


def krylov_kernel(
    conc, diff, source, xlo, xhi, ylo, yhi, clo, chi,
    p1, p2, p3, p4, moments,
    u_s, d_s, s_s, fx, gx, fy, gy, fz, gz, dg, a_s, b_s,
):
    nx, ny, nz = conc.shape
    nq = nx + 2 * W
    rows = ny + 2 * W
    for k, (own, ref) in enumerate(((conc, u_s), (diff, d_s), (source, s_s))):
        ref[W : W + nx, 0:ny, :] = own[...]
        ref[0:W, 0:ny, :] = xlo[k]
        ref[W + nx :, 0:ny, :] = xhi[k]
        ref[W : W + nx, ny : ny + W, :] = yhi[k]
        ref[W : W + nx, ny + W :, :] = ylo[k]
        ref[1:W, ny:, :] = clo[k]
        ref[W + nx : nq - 1, ny:, :] = chi[k]
        ref[0, ny:, :] = jnp.zeros((2 * W, nz), F32)
        ref[nq - 1, ny:, :] = jnp.zeros((2 * W, nz), F32)

    lane = lax.broadcasted_iota(jnp.int32, (rows, nz), 1)
    first = lane == 0
    last = lane == nz - 1

    def up(v, axis):
        return pltpu.roll(v, v.shape[axis] - 1, axis)

    def down(v, axis):
        return pltpu.roll(v, 1, axis)

    def coefficients(q, carry):
        u, d = u_s[q], d_s[q]
        e = d + d * u

        def toward(un, dn):
            return e - d * un + dn

        fxq = toward(u_s[q + 1], d_s[q + 1])
        gxq = toward(u_s[q - 1], d_s[q - 1])
        fyq = toward(up(u, 0), up(d, 0))
        gyq = toward(down(u, 0), down(d, 0))
        fzq = toward(jnp.where(last, 0.0, up(u, 1)), jnp.where(last, 0.0, up(d, 1)))
        gzq = toward(jnp.where(first, 0.0, down(u, 1)), jnp.where(first, 0.0, down(d, 1)))
        dg[q] = 1.0 + ((fxq + gxq) + (fyq + gyq)) + (fzq + gzq)
        fx[q] = fxq
        gx[q] = gxq
        fy[q] = fyq
        gy[q] = gyq
        fz[q] = jnp.where(last, 0.0, fzq)
        gz[q] = jnp.where(first, 0.0, gzq)
        return carry

    lax.fori_loop(1, nq - 1, coefficients, 0)
    def adjoint_at(w, q):
        v = w[q]
        total = dg[q] * v - fx[q] * w[q + 1] - gx[q] * w[q - 1]
        total = total - fy[q] * up(v, 0) - gy[q] * down(v, 0)
        total = total - fz[q] * up(v, 1) - gz[q] * down(v, 1)
        return jnp.where(d_s[q] > 0.0, total, 0.0)

    def forward_at(w, q):
        v = w[q]
        total = dg[q] * v - gx[q + 1] * w[q + 1] - fx[q - 1] * w[q - 1]
        total = total - up(gy[q] * v, 0) - down(fy[q] * v, 0)
        total = total - up(gz[q] * v, 1) - down(fz[q] * v, 1)
        return jnp.where(d_s[q] > 0.0, total, 0.0)

    def sweep(apply, w, margin, out_s, out):
        def edge(q, carry):
            out_s[q] = apply(w, q)
            return carry

        def middle(q, carry):
            value = apply(w, q)
            if out_s is not None:
                out_s[q] = value
            mine = value[0:ny]
            out[q - W] = mine
            return carry + jnp.sum((mine * mine).reshape(ny // 8, 8, nz), axis=0)

        if margin < W:
            lax.fori_loop(margin, W, edge, 0)
            lax.fori_loop(W + nx, nq - margin, edge, 0)
        return lax.fori_loop(W, W + nx, middle, jnp.zeros((8, nz), F32))

    def source_norm(q, carry):
        mine = source[q]
        return carry + jnp.sum((mine * mine).reshape(ny // 8, 8, nz), axis=0)

    m0 = lax.fori_loop(0, nx, source_norm, jnp.zeros((8, nz), F32))
    m1 = sweep(adjoint_at, s_s, 1, a_s, p1)
    m2 = sweep(forward_at, a_s, 2, b_s, p2)
    m3 = sweep(adjoint_at, b_s, 3, a_s, p3)
    sweep(forward_at, a_s, 4, None, p4)

    def row(m):
        return jnp.sum(m, axis=0, keepdims=True)

    folded = [row(m) for m in (m0, m1, m2, m3)]
    folded = [m[:, : nz // 2] + m[:, nz // 2 :] for m in folded]
    moments[...] = jnp.concatenate(folded + [jnp.zeros((4, nz // 2), F32)], axis=0)


def krylov(conc, diff, source, *halos):
    nx, ny, nz = conc.shape
    whole = pl.BlockSpec(memory_space=pltpu.VMEM)
    block = jax.ShapeDtypeStruct((nx, ny, nz), F32)
    scratch = pltpu.VMEM((nx + 2 * W, ny + 2 * W, nz), F32)
    return pl.pallas_call(
        krylov_kernel,
        out_shape=(block,) * 4 + (jax.ShapeDtypeStruct((8, nz // 2), F32),),
        in_specs=[whole] * 9,
        out_specs=(whole,) * 5,
        scratch_shapes=[scratch] * 12,
        compiler_params=pltpu.CompilerParams(vmem_limit_bytes=32 << 20),
        name="krylov",
    )(conc, diff, source, *halos)


def combine_kernel(moments, source, p1, p2, p3, p4, adjoint, residual):
    m = jnp.sum(moments[...], axis=1, keepdims=True)
    m0, m1, m2, m3 = (m[k : k + 1] for k in range(4))
    alpha = m0 / m1
    beta = alpha * (m2 / m1) - 1.0
    grow = 1.0 + beta
    image = grow * grow * m1 - 2.0 * grow * alpha * m2 + alpha * alpha * m3
    step = (beta * m0) / image
    near = alpha + step * grow
    far = step * alpha
    adjoint[...] = near[None] * p1[...] - far[None] * p3[...]
    residual[...] = source[...] - near[None] * p2[...] + far[None] * p4[...]


def combine(moments, source, p1, p2, p3, p4):
    whole = pl.BlockSpec(memory_space=pltpu.VMEM)
    block = jax.ShapeDtypeStruct(source.shape, F32)
    return pl.pallas_call(
        combine_kernel,
        out_shape=(block, block),
        in_specs=[whole] * 6,
        out_specs=(whole, whole),
        compiler_params=pltpu.CompilerParams(vmem_limit_bytes=16 << 20),
        name="combine",
    )(moments, source, p1, p2, p3, p4)


def forth(cells, axis):
    count = lax.axis_size(axis)
    return lax.ppermute(cells, axis, [(i, i + 1) for i in range(count - 1)])


def back(cells, axis):
    count = lax.axis_size(axis)
    return lax.ppermute(cells, axis, [(i + 1, i) for i in range(count - 1)])


def local(conc, labels, kappa, source):
    nx = conc.shape[0]
    diff, xhead, xtail, yhead, ytail = pack(conc, labels, kappa, source)
    xlo = forth(xtail, "gx")
    xhi = back(xhead, "gx")
    ylo = forth(ytail, "gy")
    yhi = back(yhead, "gy")
    ctail = jnp.concatenate([yhi[:, nx - W + 1 :], ylo[:, nx - W + 1 :]], axis=2)
    chead = jnp.concatenate([yhi[:, : W - 1], ylo[:, : W - 1]], axis=2)
    clo = forth(ctail, "gx")
    chi = back(chead, "gx")
    p1, p2, p3, p4, moments = krylov(
        conc, diff, source, xlo, xhi, ylo, yhi, clo, chi
    )
    moments = lax.psum(moments, ("gx", "gy"))
    return combine(moments, source, p1, p2, p3, p4)


def solution(mesh):
    return jax.shard_map(
        local,
        mesh=mesh,
        in_specs=(P("gx", "gy", None), P("gx", "gy", None), P(), P("gx", "gy", None)),
        out_specs=(P("gx", "gy", None), P("gx", "gy", None)),
        check_vma=False,
    )
```

```python
import functools

import jax
import jax.numpy as jnp
from jax import lax
from jax.experimental import pallas as pl
from jax.experimental.pallas import tpu as pltpu
from jax.sharding import PartitionSpec as P

ITERS = 2
DT = 0.5
W = 2 * ITERS
F32 = jnp.float32
LANES = 128


def pack_kernel(
    kappa, conc_in, labels_in, source_in,
    conc, source, diff, xhead, xtail, yhead, ytail,
    labels, sems,
):
    nx, ny, _ = conc.shape
    copies = [
        pltpu.make_async_copy(src, dst, sems.at[k])
        for k, (src, dst) in enumerate(
            ((conc_in, conc), (labels_in, labels), (source_in, source))
        )
    ]
    for copy in copies:
        copy.start()
    for copy in copies:
        copy.wait()

    def body(x, carry):
        u = conc[x]
        lab = labels[x]
        base = jnp.where(lab == 0, kappa[0], jnp.where(lab == 1, kappa[1], kappa[2]))
        diff[x] = (0.5 * DT) * base * jnp.exp(u)
        return carry

    lax.fori_loop(0, nx, body, 0)
    for k, ref in enumerate((conc, diff, source)):
        xhead[k] = ref[0:W]
        xtail[k] = ref[nx - W : nx]
        yhead[k] = ref[:, 0:W, :]
        ytail[k] = ref[:, ny - W : ny, :]


def pack(conc, labels, kappa, source):
    nx, ny, nz = conc.shape
    whole = pl.BlockSpec(memory_space=pltpu.VMEM)
    return pl.pallas_call(
        pack_kernel,
        out_shape=(
            jax.ShapeDtypeStruct((nx, ny, nz), F32),
            jax.ShapeDtypeStruct((nx, ny, nz), F32),
            jax.ShapeDtypeStruct((nx, ny, nz), F32),
            jax.ShapeDtypeStruct((3, W, ny, nz), F32),
            jax.ShapeDtypeStruct((3, W, ny, nz), F32),
            jax.ShapeDtypeStruct((3, nx, W, nz), F32),
            jax.ShapeDtypeStruct((3, nx, W, nz), F32),
        ),
        in_specs=[pl.BlockSpec(memory_space=pltpu.SMEM)]
        + [pl.BlockSpec(memory_space=pl.ANY)] * 3,
        out_specs=(whole,) * 7,
        scratch_shapes=[
            pltpu.VMEM((nx, ny, nz), jnp.int32),
            pltpu.SemaphoreType.DMA((3,)),
        ],
        compiler_params=pltpu.CompilerParams(vmem_limit_bytes=48 << 20),
        name="pack",
    )(kappa, conc, labels, source)


def krylov_kernel(
    conc, diff, source, xlo, xhi, ylo, yhi, clo, chi,
    p1, p2, p3, p4, moments,
    u_s, d_s, s_s, fx, gx, fy, gy, fz, gz, dg, a_s, b_s,
):
    nx, ny, nz = conc.shape
    nq = nx + 2 * W
    rows = ny + 2 * W
    for k, (own, ref) in enumerate(((conc, u_s), (diff, d_s), (source, s_s))):
        ref[W : W + nx, 0:ny, :] = own[...]
        ref[0:W, 0:ny, :] = xlo[k]
        ref[W + nx :, 0:ny, :] = xhi[k]
        ref[W : W + nx, ny : ny + W, :] = yhi[k]
        ref[W : W + nx, ny + W :, :] = ylo[k]
        ref[1:W, ny:, :] = clo[k]
        ref[W + nx : nq - 1, ny:, :] = chi[k]
        ref[0, ny:, :] = jnp.zeros((2 * W, nz), F32)
        ref[nq - 1, ny:, :] = jnp.zeros((2 * W, nz), F32)

    lane = lax.broadcasted_iota(jnp.int32, (rows, nz), 1)
    first = lane == 0
    last = lane == nz - 1

    def up(v, axis):
        return pltpu.roll(v, v.shape[axis] - 1, axis)

    def down(v, axis):
        return pltpu.roll(v, 1, axis)

    def coefficients(q, carry):
        u, d = u_s[q], d_s[q]
        e = d + d * u

        def toward(un, dn):
            return e - d * un + dn

        fxq = toward(u_s[q + 1], d_s[q + 1])
        gxq = toward(u_s[q - 1], d_s[q - 1])
        fyq = toward(up(u, 0), up(d, 0))
        gyq = toward(down(u, 0), down(d, 0))
        fzq = toward(jnp.where(last, 0.0, up(u, 1)), jnp.where(last, 0.0, up(d, 1)))
        gzq = toward(jnp.where(first, 0.0, down(u, 1)), jnp.where(first, 0.0, down(d, 1)))
        dg[q] = 1.0 + ((fxq + gxq) + (fyq + gyq)) + (fzq + gzq)
        fx[q] = fxq
        gx[q] = gxq
        fy[q] = fyq
        gy[q] = gyq
        fz[q] = jnp.where(last, 0.0, fzq)
        gz[q] = jnp.where(first, 0.0, gzq)
        return carry

    lax.fori_loop(1, nq - 1, coefficients, 0)
    def adjoint_at(w, q):
        v = w[q]
        total = dg[q] * v - fx[q] * w[q + 1] - gx[q] * w[q - 1]
        total = total - fy[q] * up(v, 0) - gy[q] * down(v, 0)
        total = total - fz[q] * up(v, 1) - gz[q] * down(v, 1)
        return jnp.where(d_s[q] > 0.0, total, 0.0)

    def forward_at(w, q):
        v = w[q]
        total = dg[q] * v - gx[q + 1] * w[q + 1] - fx[q - 1] * w[q - 1]
        total = total - up(gy[q] * v, 0) - down(fy[q] * v, 0)
        total = total - up(gz[q] * v, 1) - down(fz[q] * v, 1)
        return jnp.where(d_s[q] > 0.0, total, 0.0)

    def sweep(apply, w, margin, out_s, out):
        def edge(q, carry):
            out_s[q] = apply(w, q)
            return carry

        def middle(q, carry):
            value = apply(w, q)
            if out_s is not None:
                out_s[q] = value
            mine = value[0:ny]
            out[q - W] = mine
            return carry + jnp.sum((mine * mine).reshape(ny // 8, 8, nz), axis=0)

        if margin < W:
            lax.fori_loop(margin, W, edge, 0)
            lax.fori_loop(W + nx, nq - margin, edge, 0)
        return lax.fori_loop(W, W + nx, middle, jnp.zeros((8, nz), F32))

    def source_norm(q, carry):
        mine = source[q]
        return carry + jnp.sum((mine * mine).reshape(ny // 8, 8, nz), axis=0)

    m0 = lax.fori_loop(0, nx, source_norm, jnp.zeros((8, nz), F32))
    m1 = sweep(adjoint_at, s_s, 1, a_s, p1)
    m2 = sweep(forward_at, a_s, 2, b_s, p2)
    m3 = sweep(adjoint_at, b_s, 3, a_s, p3)
    sweep(forward_at, a_s, 4, None, p4)

    slot = lax.broadcasted_iota(jnp.int32, (1, LANES), 1)
    row = jnp.zeros((1, LANES), F32)
    for k, m in enumerate((m0, m1, m2, m3)):
        row = jnp.where(slot == k, jnp.sum(m), row)
    moments[...] = jnp.broadcast_to(row, moments.shape)


def krylov(copies, conc, diff, source, *halos):
    nx, ny, nz = conc.shape
    whole = pl.BlockSpec(memory_space=pltpu.VMEM)
    block = jax.ShapeDtypeStruct((nx, ny, nz), F32)
    scratch = pltpu.VMEM((nx + 2 * W, ny + 2 * W, nz), F32)
    return pl.pallas_call(
        krylov_kernel,
        out_shape=(block,) * 4 + (jax.ShapeDtypeStruct((copies, 1, LANES), F32),),
        in_specs=[whole] * 9,
        out_specs=(whole,) * 5,
        scratch_shapes=[scratch] * 12,
        compiler_params=pltpu.CompilerParams(vmem_limit_bytes=32 << 20),
        name="krylov",
    )(conc, diff, source, *halos)


def combine_kernel(moments, source, p1, p2, p3, p4, adjoint, residual):
    m = jnp.sum(moments[...], axis=0)
    m0, m1, m2, m3 = (m[:, k : k + 1] for k in range(4))
    alpha = m0 / m1
    beta = alpha * (m2 / m1) - 1.0
    grow = 1.0 + beta
    image = grow * grow * m1 - 2.0 * grow * alpha * m2 + alpha * alpha * m3
    step = (beta * m0) / image
    near = alpha + step * grow
    far = step * alpha
    adjoint[...] = near[None] * p1[...] - far[None] * p3[...]
    residual[...] = source[...] - near[None] * p2[...] + far[None] * p4[...]


def combine(moments, source, p1, p2, p3, p4):
    whole = pl.BlockSpec(memory_space=pltpu.VMEM)
    block = jax.ShapeDtypeStruct(source.shape, F32)
    return pl.pallas_call(
        combine_kernel,
        out_shape=(block, block),
        in_specs=[whole] * 6,
        out_specs=(whole, whole),
        compiler_params=pltpu.CompilerParams(vmem_limit_bytes=16 << 20),
        name="combine",
    )(moments, source, p1, p2, p3, p4)


def forth(cells, axis):
    count = lax.axis_size(axis)
    return lax.ppermute(cells, axis, [(i, i + 1) for i in range(count - 1)])


def back(cells, axis):
    count = lax.axis_size(axis)
    return lax.ppermute(cells, axis, [(i + 1, i) for i in range(count - 1)])


def local(conc, labels, kappa, source):
    nx = conc.shape[0]
    conc, source, diff, xhead, xtail, yhead, ytail = pack(conc, labels, kappa, source)
    xlo = forth(xtail, "gx")
    xhi = back(xhead, "gx")
    ylo = forth(ytail, "gy")
    yhi = back(yhead, "gy")
    ctail = jnp.concatenate([yhi[:, nx - W + 1 :], ylo[:, nx - W + 1 :]], axis=2)
    chead = jnp.concatenate([yhi[:, : W - 1], ylo[:, : W - 1]], axis=2)
    clo = forth(ctail, "gx")
    chi = back(chead, "gx")
    count = lax.axis_size(("gx", "gy"))
    p1, p2, p3, p4, moments = krylov(
        count, conc, diff, source, xlo, xhi, ylo, yhi, clo, chi
    )
    moments = lax.all_to_all(moments, ("gx", "gy"), 0, 0, tiled=True)
    return combine(moments, source, p1, p2, p3, p4)


def solution(mesh):
    return jax.shard_map(
        local,
        mesh=mesh,
        in_specs=(P("gx", "gy", None), P("gx", "gy", None), P(), P("gx", "gy", None)),
        out_specs=(P("gx", "gy", None), P("gx", "gy", None)),
        check_vma=False,
    )
```

```python
import functools

import jax
import jax.numpy as jnp
from jax import lax
from jax.experimental import pallas as pl
from jax.experimental.pallas import tpu as pltpu
from jax.sharding import PartitionSpec as P

ITERS = 2
DT = 0.5
W = 2 * ITERS
H = W - 1
F32 = jnp.float32
LANES = 128


def up(v, axis):
    return pltpu.roll(v, v.shape[axis] - 1, axis)


def down(v, axis):
    return pltpu.roll(v, 1, axis)


def positions(shape, axis):
    index = lax.broadcasted_iota(jnp.int32, shape, axis)
    return index == 0, index == shape[axis] - 1


def pack_kernel(
    kappa_in, conc_in, labels_in, source_in,
    conc, source, diff, xhead, xtail,
    labels, kappa, sems,
):
    nx, ny, nz = conc.shape
    copies = [
        pltpu.make_async_copy(src, dst, sems.at[k])
        for k, (src, dst) in enumerate(
            (
                (kappa_in, kappa),
                (labels_in, labels),
                (conc_in, conc),
                (source_in, source),
            )
        )
    ]
    for copy in copies:
        copy.start()
    for copy in copies:
        copy.wait()
    k0, k1, k2 = ((0.5 * DT) * kappa[k] for k in range(3))

    def body(x, carry):
        lab = labels[x]
        base = jnp.where(lab == 0, k0, jnp.where(lab == 1, k1, k2))
        diff[x] = base * jnp.exp(conc[x])
        return carry

    lax.fori_loop(0, nx, body, 0)
    bottom, top = positions((ny, nz), 0)
    first, last = positions((ny, nz), 1)

    def partial_image(x):
        u, d, w = conc[x], diff[x], source[x]
        e = d + d * u

        def term(un, dn, wn):
            return (e - d * un + dn) * (w - wn)

        def shifted(move, edge, axis):
            return [jnp.where(edge, 0.0, move(v, axis)) for v in (u, d, w)]

        total = w + term(conc[x + 1], diff[x + 1], source[x + 1])
        total = total + term(conc[x - 1], diff[x - 1], source[x - 1])
        total = total + jnp.where(top, 0.0, term(*shifted(up, top, 0)))
        total = total + jnp.where(bottom, 0.0, term(*shifted(down, bottom, 0)))
        total = total + term(*shifted(up, last, 1))
        return total + term(*shifted(down, first, 1))

    for k, ref in enumerate((conc, diff, source)):
        xhead[k * H : (k + 1) * H] = ref[0:H]
        xtail[k * H : (k + 1) * H] = ref[nx - H : nx]
    xhead[3 * H] = partial_image(H - 1)
    xtail[3 * H] = partial_image(nx - H)


def pack(conc, labels, kappa, source):
    nx, ny, nz = conc.shape
    whole = pl.BlockSpec(memory_space=pltpu.VMEM)
    block = jax.ShapeDtypeStruct((nx, ny, nz), F32)
    slab = jax.ShapeDtypeStruct((3 * H + 1, ny, nz), F32)
    outside = [
        pltpu.with_memory_space_constraint(v, pltpu.HBM)
        for v in (kappa, conc, labels, source)
    ]
    return pl.pallas_call(
        pack_kernel,
        out_shape=(block, block, block, slab, slab),
        in_specs=[pl.BlockSpec(memory_space=pltpu.HBM)] * 4,
        out_specs=(whole,) * 5,
        scratch_shapes=[
            pltpu.VMEM((nx, ny, nz), jnp.int32),
            pltpu.SMEM((3,), F32),
            pltpu.SemaphoreType.DMA((4,)),
        ],
        compiler_params=pltpu.CompilerParams(vmem_limit_bytes=16 << 20),
        name="pack",
    )(*outside)


def pack_rows_kernel(conc, diff, source, yhead, ytail):
    ny = conc.shape[1]
    for k, ref in enumerate((conc, diff, source)):
        yhead[k] = ref[:, 0:W, :]
        ytail[k] = ref[:, ny - W : ny, :]


def pack_rows(conc, diff, source):
    nx, ny, nz = conc.shape
    whole = pl.BlockSpec(memory_space=pltpu.VMEM)
    rows = jax.ShapeDtypeStruct((3, nx, W, nz), F32)
    return pl.pallas_call(
        pack_rows_kernel,
        out_shape=(rows, rows),
        in_specs=[whole] * 3,
        out_specs=(whole, whole),
        compiler_params=pltpu.CompilerParams(vmem_limit_bytes=16 << 20),
        cost_estimate=pl.CostEstimate(
            flops=1 << 22, bytes_accessed=1 << 24, transcendentals=0
        ),
        name="pack_rows",
    )(conc, diff, source)


def corner_slots():
    at = 0
    for k in range(3):
        for dx in range(1, H + 1):
            for side in range(2):
                yield k, dx, side, at
                at += W - dx


CORNER_ROWS = 3 * sum(2 * (W - dx) for dx in range(1, H + 1))


def pack_corners_kernel(ylo, yhi, chead, ctail):
    nx = ylo.shape[1]
    for k, dx, side, at in corner_slots():
        n = W - dx
        ref = yhi if side == 0 else ylo
        begin = 0 if side == 0 else W - n
        chead[at : at + n] = ref[k, dx - 1, begin : begin + n]
        ctail[at : at + n] = ref[k, nx - dx, begin : begin + n]


def pack_corners(ylo, yhi):
    nz = ylo.shape[3]
    whole = pl.BlockSpec(memory_space=pltpu.VMEM)
    rows = jax.ShapeDtypeStruct((CORNER_ROWS, nz), F32)
    return pl.pallas_call(
        pack_corners_kernel,
        out_shape=(rows, rows),
        in_specs=[whole] * 2,
        out_specs=(whole, whole),
        compiler_params=pltpu.CompilerParams(vmem_limit_bytes=16 << 20),
        name="pack_corners",
    )(ylo, yhi)


def krylov_kernel(
    conc, diff, source, xlo, xhi, ylo, yhi, clo, chi,
    p1, p2, p3, p4, moments,
    u_s, d_s, s_s, fx, gx, fy, gy, fz, gz, dg, a_s, b_s,
):
    nx, ny, nz = conc.shape
    nq = nx + 2 * H
    rows = ny + 2 * W
    fields = (u_s, d_s, s_s)
    for k, (own, ref) in enumerate(zip((conc, diff, source), fields)):
        ref[H : H + nx, 0:ny, :] = own[...]
        ref[H : H + nx, ny : ny + W, :] = yhi[k]
        ref[H : H + nx, ny + W :, :] = ylo[k]
        ref[0:H, 0:ny, :] = xlo[k * H : (k + 1) * H]
        ref[H + nx :, 0:ny, :] = xhi[k * H : (k + 1) * H]
        ref[0:H, ny:, :] = jnp.zeros((H, 2 * W, nz), F32)
        ref[H + nx :, ny:, :] = jnp.zeros((H, 2 * W, nz), F32)
    for k, dx, side, at in corner_slots():
        n = W - dx
        begin = ny if side == 0 else rows - n
        fields[k][H - dx, begin : begin + n, :] = clo[at : at + n]
        fields[k][H + nx - 1 + dx, begin : begin + n, :] = chi[at : at + n]

    first, last = positions((rows, nz), 1)

    def coefficients(q, carry):
        u, d = u_s[q], d_s[q]
        e = d + d * u

        def toward(un, dn):
            return e - d * un + dn

        fxq = toward(u_s[q + 1], d_s[q + 1])
        gxq = toward(u_s[q - 1], d_s[q - 1])
        fyq = toward(up(u, 0), up(d, 0))
        gyq = toward(down(u, 0), down(d, 0))
        fzq = toward(jnp.where(last, 0.0, up(u, 1)), jnp.where(last, 0.0, up(d, 1)))
        gzq = toward(jnp.where(first, 0.0, down(u, 1)), jnp.where(first, 0.0, down(d, 1)))
        dg[q] = 1.0 + ((fxq + gxq) + (fyq + gyq)) + (fzq + gzq)
        fx[q] = fxq
        gx[q] = gxq
        fy[q] = fyq
        gy[q] = gyq
        fz[q] = jnp.where(last, 0.0, fzq)
        gz[q] = jnp.where(first, 0.0, gzq)
        return carry

    lax.fori_loop(1, nq - 1, coefficients, 0)

    def across(q, inner):
        u, d = u_s[q], d_s[q]
        return d + d * u - d * u_s[inner] + d_s[inner]

    fx[0] = across(0, 1)
    gx[nq - 1] = across(nq - 1, nq - 2)

    def finish(q, part):
        def edge(here, there):
            u, d, w = (ref[q, here : here + 1] for ref in fields)
            un, dn, wn = (ref[q, there : there + 1] for ref in fields)
            return (d + d * u - d * un + dn) * (w - wn)

        a_s[q, 0:ny] = part
        a_s[q, ny:] = jnp.zeros((2 * W, nz), F32)
        a_s[q, 0:1] += edge(0, rows - 1)
        a_s[q, ny - 1 : ny] += edge(ny - 1, ny)

    finish(0, xlo[3 * H])
    finish(nq - 1, xhi[3 * H])

    def adjoint_at(w, q):
        v = w[q]
        total = dg[q] * v - fx[q] * w[q + 1] - gx[q] * w[q - 1]
        total = total - fy[q] * up(v, 0) - gy[q] * down(v, 0)
        total = total - fz[q] * up(v, 1) - gz[q] * down(v, 1)
        return jnp.where(d_s[q] > 0.0, total, 0.0)

    def forward_at(w, q):
        v = w[q]
        total = dg[q] * v - gx[q + 1] * w[q + 1] - fx[q - 1] * w[q - 1]
        total = total - up(gy[q] * v, 0) - down(fy[q] * v, 0)
        total = total - up(gz[q] * v, 1) - down(fz[q] * v, 1)
        return jnp.where(d_s[q] > 0.0, total, 0.0)

    def sweep(apply, w, margin, out_s, out):
        def edge(q, carry):
            out_s[q] = apply(w, q)
            return carry

        def middle(q, carry):
            value = apply(w, q)
            if out_s is not None:
                out_s[q] = value
            mine = value[0:ny]
            out[q - H] = mine
            return carry + jnp.sum((mine * mine).reshape(ny // 8, 8, nz), axis=0)

        if margin < H:
            lax.fori_loop(margin, H, edge, 0)
            lax.fori_loop(H + nx, nq - margin, edge, 0)
        return lax.fori_loop(H, H + nx, middle, jnp.zeros((8, nz), F32))

    def source_norm(q, carry):
        mine = source[q]
        return carry + jnp.sum((mine * mine).reshape(ny // 8, 8, nz), axis=0)

    m0 = lax.fori_loop(0, nx, source_norm, jnp.zeros((8, nz), F32))
    m1 = sweep(adjoint_at, s_s, 1, a_s, p1)
    m2 = sweep(forward_at, a_s, 1, b_s, p2)
    m3 = sweep(adjoint_at, b_s, 2, a_s, p3)
    sweep(forward_at, a_s, 3, None, p4)

    slot = lax.broadcasted_iota(jnp.int32, (1, LANES), 1)
    row = jnp.zeros((1, LANES), F32)
    for k, m in enumerate((m0, m1, m2, m3)):
        row = jnp.where(slot == k, jnp.sum(m), row)
    moments[...] = jnp.broadcast_to(row, moments.shape)


def krylov(copies, conc, diff, source, *halos):
    nx, ny, nz = conc.shape
    whole = pl.BlockSpec(memory_space=pltpu.VMEM)
    block = jax.ShapeDtypeStruct((nx, ny, nz), F32)
    scratch = pltpu.VMEM((nx + 2 * H, ny + 2 * W, nz), F32)
    return pl.pallas_call(
        krylov_kernel,
        out_shape=(block,) * 4 + (jax.ShapeDtypeStruct((copies, 1, LANES), F32),),
        in_specs=[whole] * 9,
        out_specs=(whole,) * 5,
        scratch_shapes=[scratch] * 12,
        compiler_params=pltpu.CompilerParams(vmem_limit_bytes=32 << 20),
        name="krylov",
    )(conc, diff, source, *halos)


def combine_kernel(moments, source, p1, p2, p3, p4, adjoint, residual):
    m = jnp.sum(moments[...], axis=0)
    m0, m1, m2, m3 = (m[:, k : k + 1] for k in range(4))
    alpha = m0 / m1
    beta = alpha * (m2 / m1) - 1.0
    grow = 1.0 + beta
    image = grow * grow * m1 - 2.0 * grow * alpha * m2 + alpha * alpha * m3
    step = (beta * m0) / image
    near = alpha + step * grow
    far = step * alpha
    adjoint[...] = near[None] * p1[...] - far[None] * p3[...]
    residual[...] = source[...] - near[None] * p2[...] + far[None] * p4[...]


def combine(moments, source, p1, p2, p3, p4):
    whole = pl.BlockSpec(memory_space=pltpu.VMEM)
    block = jax.ShapeDtypeStruct(source.shape, F32)
    return pl.pallas_call(
        combine_kernel,
        out_shape=(block, block),
        in_specs=[whole] * 6,
        out_specs=(whole, whole),
        compiler_params=pltpu.CompilerParams(vmem_limit_bytes=16 << 20),
        name="combine",
    )(moments, source, p1, p2, p3, p4)


def forth(cells, axis):
    count = lax.axis_size(axis)
    return lax.ppermute(cells, axis, [(i, i + 1) for i in range(count - 1)])


def back(cells, axis):
    count = lax.axis_size(axis)
    return lax.ppermute(cells, axis, [(i + 1, i) for i in range(count - 1)])


def local(conc, labels, kappa, source):
    conc, source, diff, xhead, xtail = pack(conc, labels, kappa, source)
    xlo = forth(xtail, "gx")
    xhi = back(xhead, "gx")
    yhead, ytail = pack_rows(conc, diff, source)
    ylo = forth(ytail, "gy")
    yhi = back(yhead, "gy")
    chead, ctail = pack_corners(ylo, yhi)
    clo = forth(ctail, "gx")
    chi = back(chead, "gx")
    count = lax.axis_size(("gx", "gy"))
    p1, p2, p3, p4, moments = krylov(
        count, conc, diff, source, xlo, xhi, ylo, yhi, clo, chi
    )
    moments = lax.all_to_all(moments, ("gx", "gy"), 0, 0, tiled=True)
    return combine(moments, source, p1, p2, p3, p4)


def solution(mesh):
    return jax.shard_map(
        local,
        mesh=mesh,
        in_specs=(P("gx", "gy", None), P("gx", "gy", None), P(), P("gx", "gy", None)),
        out_specs=(P("gx", "gy", None), P("gx", "gy", None)),
        check_vma=False,
    )
```

```python
import functools

import jax
import jax.numpy as jnp
from jax import lax
from jax.experimental import pallas as pl
from jax.experimental.pallas import tpu as pltpu
from jax.sharding import PartitionSpec as P

ITERS = 2
DT = 0.5
W = 2 * ITERS
H = W - 1
F32 = jnp.float32
LANES = 128


def up(v, axis):
    return pltpu.roll(v, v.shape[axis] - 1, axis)


def down(v, axis):
    return pltpu.roll(v, 1, axis)


def positions(shape, axis):
    index = lax.broadcasted_iota(jnp.int32, shape, axis)
    return index == 0, index == shape[axis] - 1


def pack_kernel(
    kappa_in, conc_in, labels_in, source_in,
    conc, source, diff, xtail,
    labels, kappa, sems,
):
    nx, ny, nz = conc.shape
    copies = [
        pltpu.make_async_copy(src, dst, sems.at[k])
        for k, (src, dst) in enumerate(
            (
                (kappa_in, kappa),
                (labels_in, labels),
                (conc_in, conc),
                (source_in, source),
            )
        )
    ]
    for copy in copies:
        copy.start()
    for copy in copies:
        copy.wait()
    k0, k1, k2 = ((0.5 * DT) * kappa[k] for k in range(3))

    def body(x, carry):
        lab = labels[x]
        base = jnp.where(lab == 0, k0, jnp.where(lab == 1, k1, k2))
        diff[x] = base * jnp.exp(conc[x])
        return carry

    lax.fori_loop(0, nx, body, 0, unroll=True)
    pack_face((conc, diff, source), nx - H, nx - H, xtail)


def pack_face(fields, begin, inner, slab):
    for k, ref in enumerate(fields):
        slab[k * H : (k + 1) * H] = ref[begin : begin + H]
    slab[3 * H] = partial_image(fields, inner)


def partial_image(fields, x):
    conc, diff, source = fields
    u, d, w = conc[x], diff[x], source[x]
    bottom, top = positions(u.shape, 0)
    first, last = positions(u.shape, 1)
    e = d + d * u

    def term(un, dn, wn):
        return (e - d * un + dn) * (w - wn)

    def shifted(move, edge, axis):
        return [jnp.where(edge, 0.0, move(v, axis)) for v in (u, d, w)]

    total = w + term(conc[x + 1], diff[x + 1], source[x + 1])
    total = total + term(conc[x - 1], diff[x - 1], source[x - 1])
    total = total + jnp.where(top, 0.0, term(*shifted(up, top, 0)))
    total = total + jnp.where(bottom, 0.0, term(*shifted(down, bottom, 0)))
    total = total + term(*shifted(up, last, 1))
    return total + term(*shifted(down, first, 1))


def pack(conc, labels, kappa, source):
    nx, ny, nz = conc.shape
    whole = pl.BlockSpec(memory_space=pltpu.VMEM)
    block = jax.ShapeDtypeStruct((nx, ny, nz), F32)
    slab = jax.ShapeDtypeStruct((3 * H + 1, ny, nz), F32)
    outside = [
        pltpu.with_memory_space_constraint(v, pltpu.HBM)
        for v in (kappa, conc, labels, source)
    ]
    return pl.pallas_call(
        pack_kernel,
        out_shape=(block, block, block, slab),
        in_specs=[pl.BlockSpec(memory_space=pltpu.HBM)] * 4,
        out_specs=(whole,) * 4,
        scratch_shapes=[
            pltpu.VMEM((nx, ny, nz), jnp.int32),
            pltpu.SMEM((3,), F32),
            pltpu.SemaphoreType.DMA((4,)),
        ],
        compiler_params=pltpu.CompilerParams(vmem_limit_bytes=16 << 20),
        name="pack",
    )(*outside)


def pack_rows_kernel(conc, diff, source, yhead, ytail):
    ny = conc.shape[1]
    for k, ref in enumerate((conc, diff, source)):
        yhead[k] = ref[:, 0:W, :]
        ytail[k] = ref[:, ny - W : ny, :]


def pack_rows(conc, diff, source):
    nx, ny, nz = conc.shape
    whole = pl.BlockSpec(memory_space=pltpu.VMEM)
    rows = jax.ShapeDtypeStruct((3, nx, W, nz), F32)
    return pl.pallas_call(
        pack_rows_kernel,
        out_shape=(rows, rows),
        in_specs=[whole] * 3,
        out_specs=(whole, whole),
        compiler_params=pltpu.CompilerParams(vmem_limit_bytes=16 << 20),
        cost_estimate=pl.CostEstimate(
            flops=1 << 22, bytes_accessed=1 << 24, transcendentals=0
        ),
        name="pack_rows",
    )(conc, diff, source)


def pack_head_kernel(conc, diff, source, after, xhead):
    pack_face((conc, diff, source), 0, H - 1, xhead)


def pack_head(conc, diff, source, after):
    nx, ny, nz = conc.shape
    whole = pl.BlockSpec(memory_space=pltpu.VMEM)
    return pl.pallas_call(
        pack_head_kernel,
        out_shape=jax.ShapeDtypeStruct((3 * H + 1, ny, nz), F32),
        in_specs=[whole] * 4,
        out_specs=whole,
        compiler_params=pltpu.CompilerParams(vmem_limit_bytes=16 << 20),
        name="pack_head",
    )(conc, diff, source, after)


def corner_slots():
    at = 0
    for k in range(3):
        for dx in range(1, H + 1):
            for side in range(2):
                yield k, dx, side, at
                at += W - dx


CORNER_ROWS = 3 * sum(2 * (W - dx) for dx in range(1, H + 1))


def pack_corners_kernel(ylo, yhi, chead, ctail):
    nx = ylo.shape[1]
    for k, dx, side, at in corner_slots():
        n = W - dx
        ref = yhi if side == 0 else ylo
        begin = 0 if side == 0 else W - n
        chead[at : at + n] = ref[k, dx - 1, begin : begin + n]
        ctail[at : at + n] = ref[k, nx - dx, begin : begin + n]


def pack_corners(ylo, yhi):
    nz = ylo.shape[3]
    whole = pl.BlockSpec(memory_space=pltpu.VMEM)
    rows = jax.ShapeDtypeStruct((CORNER_ROWS, nz), F32)
    return pl.pallas_call(
        pack_corners_kernel,
        out_shape=(rows, rows),
        in_specs=[whole] * 2,
        out_specs=(whole, whole),
        compiler_params=pltpu.CompilerParams(vmem_limit_bytes=16 << 20),
        name="pack_corners",
    )(ylo, yhi)


def krylov_kernel(
    conc, diff, source, xlo, xhi, ylo, yhi, clo, chi,
    p1, p2, p3, p4, moments,
    u_s, d_s, s_s, fx, gx, fy, gy, fz, gz, dg, a_s, b_s,
):
    nx, ny, nz = conc.shape
    nq = nx + 2 * H
    rows = ny + 2 * W
    fields = (u_s, d_s, s_s)
    for k, (own, ref) in enumerate(zip((conc, diff, source), fields)):
        ref[H : H + nx, 0:ny, :] = own[...]
        ref[H : H + nx, ny : ny + W, :] = yhi[k]
        ref[H : H + nx, ny + W :, :] = ylo[k]
        ref[0:H, 0:ny, :] = xlo[k * H : (k + 1) * H]
        ref[H + nx :, 0:ny, :] = xhi[k * H : (k + 1) * H]
        ref[0:H, ny:, :] = jnp.zeros((H, 2 * W, nz), F32)
        ref[H + nx :, ny:, :] = jnp.zeros((H, 2 * W, nz), F32)
    for k, dx, side, at in corner_slots():
        n = W - dx
        begin = ny if side == 0 else rows - n
        fields[k][H - dx, begin : begin + n, :] = clo[at : at + n]
        fields[k][H + nx - 1 + dx, begin : begin + n, :] = chi[at : at + n]

    first, last = positions((rows, nz), 1)

    def coefficients(q, carry):
        u, d = u_s[q], d_s[q]
        e = d + d * u

        def toward(un, dn):
            return e - d * un + dn

        fxq = toward(u_s[q + 1], d_s[q + 1])
        gxq = toward(u_s[q - 1], d_s[q - 1])
        fyq = toward(up(u, 0), up(d, 0))
        gyq = toward(down(u, 0), down(d, 0))
        fzq = toward(jnp.where(last, 0.0, up(u, 1)), jnp.where(last, 0.0, up(d, 1)))
        gzq = toward(jnp.where(first, 0.0, down(u, 1)), jnp.where(first, 0.0, down(d, 1)))
        dg[q] = 1.0 + ((fxq + gxq) + (fyq + gyq)) + (fzq + gzq)
        fx[q] = fxq
        gx[q] = gxq
        fy[q] = fyq
        gy[q] = gyq
        fz[q] = jnp.where(last, 0.0, fzq)
        gz[q] = jnp.where(first, 0.0, gzq)
        return carry

    lax.fori_loop(1, nq - 1, coefficients, 0, unroll=4)

    def across(q, inner):
        u, d = u_s[q], d_s[q]
        return d + d * u - d * u_s[inner] + d_s[inner]

    fx[0] = across(0, 1)
    gx[nq - 1] = across(nq - 1, nq - 2)

    def finish(q, part):
        def edge(here, there):
            u, d, w = (ref[q, here : here + 1] for ref in fields)
            un, dn, wn = (ref[q, there : there + 1] for ref in fields)
            return (d + d * u - d * un + dn) * (w - wn)

        a_s[q, 0:ny] = part
        a_s[q, ny:] = jnp.zeros((2 * W, nz), F32)
        a_s[q, 0:1] += edge(0, rows - 1)
        a_s[q, ny - 1 : ny] += edge(ny - 1, ny)

    finish(0, xlo[3 * H])
    finish(nq - 1, xhi[3 * H])

    def adjoint_at(w, q):
        v = w[q]
        total = dg[q] * v - fx[q] * w[q + 1] - gx[q] * w[q - 1]
        total = total - fy[q] * up(v, 0) - gy[q] * down(v, 0)
        total = total - fz[q] * up(v, 1) - gz[q] * down(v, 1)
        return jnp.where(d_s[q] > 0.0, total, 0.0)

    def forward_at(w, q):
        v = w[q]
        total = dg[q] * v - gx[q + 1] * w[q + 1] - fx[q - 1] * w[q - 1]
        total = total - up(gy[q] * v, 0) - down(fy[q] * v, 0)
        total = total - up(gz[q] * v, 1) - down(fz[q] * v, 1)
        return jnp.where(d_s[q] > 0.0, total, 0.0)

    def sweep(apply, w, margin, out_s, out):
        def edge(q, carry):
            out_s[q] = apply(w, q)
            return carry

        def middle(q, carry):
            value = apply(w, q)
            if out_s is not None:
                out_s[q] = value
            mine = value[0:ny]
            out[q - H] = mine
            return carry + jnp.sum((mine * mine).reshape(ny // 8, 8, nz), axis=0)

        if margin < H:
            for q in (*range(margin, H), *range(H + nx, nq - margin)):
                edge(q, 0)
        return lax.fori_loop(H, H + nx, middle, jnp.zeros((8, nz), F32), unroll=4)

    def source_norm(q, carry):
        mine = source[q]
        return carry + jnp.sum((mine * mine).reshape(ny // 8, 8, nz), axis=0)

    m0 = lax.fori_loop(0, nx, source_norm, jnp.zeros((8, nz), F32), unroll=True)
    m1 = sweep(adjoint_at, s_s, 1, a_s, p1)
    m2 = sweep(forward_at, a_s, 1, b_s, p2)
    m3 = sweep(adjoint_at, b_s, 2, a_s, p3)
    sweep(forward_at, a_s, 3, None, p4)

    slot = lax.broadcasted_iota(jnp.int32, (1, LANES), 1)
    row = jnp.zeros((1, LANES), F32)
    for k, m in enumerate((m0, m1, m2, m3)):
        row = jnp.where(slot == k, jnp.sum(m), row)
    moments[...] = jnp.broadcast_to(row, moments.shape)


def krylov(copies, conc, diff, source, *halos):
    nx, ny, nz = conc.shape
    whole = pl.BlockSpec(memory_space=pltpu.VMEM)
    block = jax.ShapeDtypeStruct((nx, ny, nz), F32)
    scratch = pltpu.VMEM((nx + 2 * H, ny + 2 * W, nz), F32)
    return pl.pallas_call(
        krylov_kernel,
        out_shape=(block,) * 4 + (jax.ShapeDtypeStruct((copies, 1, LANES), F32),),
        in_specs=[whole] * 9,
        out_specs=(whole,) * 5,
        scratch_shapes=[scratch] * 12,
        compiler_params=pltpu.CompilerParams(vmem_limit_bytes=32 << 20),
        name="krylov",
    )(conc, diff, source, *halos)


def combine_kernel(moments, source, p1, p2, p3, p4, adjoint, residual):
    m = jnp.sum(moments[...], axis=0)
    m0, m1, m2, m3 = (m[:, k : k + 1] for k in range(4))
    alpha = m0 / m1
    beta = alpha * (m2 / m1) - 1.0
    grow = 1.0 + beta
    image = grow * grow * m1 - 2.0 * grow * alpha * m2 + alpha * alpha * m3
    step = (beta * m0) / image
    near = alpha + step * grow
    far = step * alpha
    adjoint[...] = near[None] * p1[...] - far[None] * p3[...]
    residual[...] = source[...] - near[None] * p2[...] + far[None] * p4[...]


def combine(moments, source, p1, p2, p3, p4):
    whole = pl.BlockSpec(memory_space=pltpu.VMEM)
    block = jax.ShapeDtypeStruct(source.shape, F32)
    return pl.pallas_call(
        combine_kernel,
        out_shape=(block, block),
        in_specs=[whole] * 6,
        out_specs=(whole, whole),
        compiler_params=pltpu.CompilerParams(vmem_limit_bytes=16 << 20),
        name="combine",
    )(moments, source, p1, p2, p3, p4)


def forth(cells, axis):
    count = lax.axis_size(axis)
    return lax.ppermute(cells, axis, [(i, i + 1) for i in range(count - 1)])


def back(cells, axis):
    count = lax.axis_size(axis)
    return lax.ppermute(cells, axis, [(i + 1, i) for i in range(count - 1)])


def local(conc, labels, kappa, source):
    conc, source, diff, xtail = pack(conc, labels, kappa, source)
    xlo = forth(xtail, "gx")
    yhead, ytail = pack_rows(conc, diff, source)
    ylo = forth(ytail, "gy")
    yhi = back(yhead, "gy")
    xhi = back(pack_head(conc, diff, source, ylo), "gx")
    chead, ctail = pack_corners(ylo, yhi)
    clo = forth(ctail, "gx")
    chi = back(chead, "gx")
    count = lax.axis_size(("gx", "gy"))
    p1, p2, p3, p4, moments = krylov(
        count, conc, diff, source, xlo, xhi, ylo, yhi, clo, chi
    )
    moments = lax.all_to_all(moments, ("gx", "gy"), 0, 0, tiled=True)
    return combine(moments, source, p1, p2, p3, p4)


def solution(mesh):
    return jax.shard_map(
        local,
        mesh=mesh,
        in_specs=(P("gx", "gy", None), P("gx", "gy", None), P(), P("gx", "gy", None)),
        out_specs=(P("gx", "gy", None), P("gx", "gy", None)),
        check_vma=False,
    )
```

```python
import functools

import jax
import jax.numpy as jnp
from jax import lax
from jax.experimental import pallas as pl
from jax.experimental.pallas import tpu as pltpu
from jax.sharding import PartitionSpec as P

ITERS = 2
DT = 0.5
W = 2 * ITERS
H = W - 1
F32 = jnp.float32
LANES = 128


def up(v, axis):
    return pltpu.roll(v, v.shape[axis] - 1, axis)


def down(v, axis):
    return pltpu.roll(v, 1, axis)


def positions(shape, axis):
    index = lax.broadcasted_iota(jnp.int32, shape, axis)
    return index == 0, index == shape[axis] - 1


def pack_kernel(
    kappa_in, conc_in, labels_in, source_in,
    conc, source, diff, xtail,
    labels, kappa, sems,
):
    nx, ny, nz = conc.shape
    copies = [
        pltpu.make_async_copy(src, dst, sems.at[k])
        for k, (src, dst) in enumerate(
            (
                (kappa_in, kappa),
                (labels_in, labels),
                (conc_in, conc),
                (source_in, source),
            )
        )
    ]
    for copy in copies:
        copy.start()
    for copy in copies:
        copy.wait()
    k0, k1, k2 = ((0.5 * DT) * kappa[k] for k in range(3))

    def body(x, carry):
        lab = labels[x]
        base = jnp.where(lab == 0, k0, jnp.where(lab == 1, k1, k2))
        diff[x] = base * jnp.exp(conc[x])
        return carry

    lax.fori_loop(0, nx, body, 0, unroll=True)
    pack_face((conc, diff, source), nx - H, nx - H, xtail)


def pack_face(fields, begin, inner, slab):
    for k, ref in enumerate(fields):
        slab[k * H : (k + 1) * H] = ref[begin : begin + H]
    slab[3 * H] = partial_image(fields, inner)


def partial_image(fields, x):
    conc, diff, source = fields
    u, d, w = conc[x], diff[x], source[x]
    bottom, top = positions(u.shape, 0)
    first, last = positions(u.shape, 1)
    e = d + d * u

    def term(un, dn, wn):
        return (e - d * un + dn) * (w - wn)

    def shifted(move, edge, axis):
        return [jnp.where(edge, 0.0, move(v, axis)) for v in (u, d, w)]

    total = w + term(conc[x + 1], diff[x + 1], source[x + 1])
    total = total + term(conc[x - 1], diff[x - 1], source[x - 1])
    total = total + jnp.where(top, 0.0, term(*shifted(up, top, 0)))
    total = total + jnp.where(bottom, 0.0, term(*shifted(down, bottom, 0)))
    total = total + term(*shifted(up, last, 1))
    return total + term(*shifted(down, first, 1))


def pack(conc, labels, kappa, source):
    nx, ny, nz = conc.shape
    whole = pl.BlockSpec(memory_space=pltpu.VMEM)
    block = jax.ShapeDtypeStruct((nx, ny, nz), F32)
    slab = jax.ShapeDtypeStruct((3 * H + 1, ny, nz), F32)
    outside = [
        pltpu.with_memory_space_constraint(v, pltpu.HBM)
        for v in (kappa, conc, labels, source)
    ]
    return pl.pallas_call(
        pack_kernel,
        out_shape=(block, block, block, slab),
        in_specs=[pl.BlockSpec(memory_space=pltpu.HBM)] * 4,
        out_specs=(whole,) * 4,
        scratch_shapes=[
            pltpu.VMEM((nx, ny, nz), jnp.int32),
            pltpu.SMEM((3,), F32),
            pltpu.SemaphoreType.DMA((4,)),
        ],
        compiler_params=pltpu.CompilerParams(vmem_limit_bytes=16 << 20),
        name="pack",
    )(*outside)


def pack_rows_kernel(conc, diff, source, yhead, ytail):
    ny = conc.shape[1]
    for k, ref in enumerate((conc, diff, source)):
        yhead[k] = ref[:, 0:W, :]
        ytail[k] = ref[:, ny - W : ny, :]


def pack_rows(conc, diff, source):
    nx, ny, nz = conc.shape
    whole = pl.BlockSpec(memory_space=pltpu.VMEM)
    rows = jax.ShapeDtypeStruct((3, nx, W, nz), F32)
    return pl.pallas_call(
        pack_rows_kernel,
        out_shape=(rows, rows),
        in_specs=[whole] * 3,
        out_specs=(whole, whole),
        compiler_params=pltpu.CompilerParams(vmem_limit_bytes=16 << 20),
        cost_estimate=pl.CostEstimate(
            flops=1 << 22, bytes_accessed=1 << 24, transcendentals=0
        ),
        name="pack_rows",
    )(conc, diff, source)


def pack_head_kernel(conc, diff, source, after, xhead):
    pack_face((conc, diff, source), 0, H - 1, xhead)


def pack_head(conc, diff, source, after):
    nx, ny, nz = conc.shape
    whole = pl.BlockSpec(memory_space=pltpu.VMEM)
    return pl.pallas_call(
        pack_head_kernel,
        out_shape=jax.ShapeDtypeStruct((3 * H + 1, ny, nz), F32),
        in_specs=[whole] * 4,
        out_specs=whole,
        compiler_params=pltpu.CompilerParams(vmem_limit_bytes=16 << 20),
        name="pack_head",
    )(conc, diff, source, after)


def corner_slots():
    at = 0
    for k in range(3):
        for dx in range(1, H + 1):
            for side in range(2):
                yield k, dx, side, at
                at += W - dx


CORNER_ROWS = 3 * sum(2 * (W - dx) for dx in range(1, H + 1))


def pack_corners_kernel(ylo, yhi, chead, ctail):
    nx = ylo.shape[1]
    for k, dx, side, at in corner_slots():
        n = W - dx
        ref = yhi if side == 0 else ylo
        begin = 0 if side == 0 else W - n
        chead[at : at + n] = ref[k, dx - 1, begin : begin + n]
        ctail[at : at + n] = ref[k, nx - dx, begin : begin + n]


def pack_corners(ylo, yhi):
    nz = ylo.shape[3]
    whole = pl.BlockSpec(memory_space=pltpu.VMEM)
    rows = jax.ShapeDtypeStruct((CORNER_ROWS, nz), F32)
    return pl.pallas_call(
        pack_corners_kernel,
        out_shape=(rows, rows),
        in_specs=[whole] * 2,
        out_specs=(whole, whole),
        compiler_params=pltpu.CompilerParams(vmem_limit_bytes=16 << 20),
        name="pack_corners",
    )(ylo, yhi)


def krylov_kernel(
    conc, diff, source, xlo, xhi, ylo, yhi, clo, chi,
    p1, p2, p3, moments, a_s, dg, fx, gx, fy, gy, fz, gz,
    u_s, d_s, s_s, b_s,
):
    nx, ny, nz = conc.shape
    nq = nx + 2 * H
    rows = ny + 2 * W
    fields = (u_s, d_s, s_s)
    for k, (own, ref) in enumerate(zip((conc, diff, source), fields)):
        ref[H : H + nx, 0:ny, :] = own[...]
        ref[H : H + nx, ny : ny + W, :] = yhi[k]
        ref[H : H + nx, ny + W :, :] = ylo[k]
        ref[0:H, 0:ny, :] = xlo[k * H : (k + 1) * H]
        ref[H + nx :, 0:ny, :] = xhi[k * H : (k + 1) * H]
        ref[0:H, ny:, :] = jnp.zeros((H, 2 * W, nz), F32)
        ref[H + nx :, ny:, :] = jnp.zeros((H, 2 * W, nz), F32)
    for k, dx, side, at in corner_slots():
        n = W - dx
        begin = ny if side == 0 else rows - n
        fields[k][H - dx, begin : begin + n, :] = clo[at : at + n]
        fields[k][H + nx - 1 + dx, begin : begin + n, :] = chi[at : at + n]

    first, last = positions((rows, nz), 1)

    def coefficients(q, carry):
        u, d = u_s[q], d_s[q]
        e = d + d * u

        def toward(un, dn):
            return e - d * un + dn

        fxq = toward(u_s[q + 1], d_s[q + 1])
        gxq = toward(u_s[q - 1], d_s[q - 1])
        fyq = toward(up(u, 0), up(d, 0))
        gyq = toward(down(u, 0), down(d, 0))
        fzq = toward(jnp.where(last, 0.0, up(u, 1)), jnp.where(last, 0.0, up(d, 1)))
        gzq = toward(jnp.where(first, 0.0, down(u, 1)), jnp.where(first, 0.0, down(d, 1)))
        dg[q] = 1.0 + ((fxq + gxq) + (fyq + gyq)) + (fzq + gzq)
        fx[q] = fxq
        gx[q] = gxq
        fy[q] = fyq
        gy[q] = gyq
        fz[q] = jnp.where(last, 0.0, fzq)
        gz[q] = jnp.where(first, 0.0, gzq)
        return carry

    lax.fori_loop(1, nq - 1, coefficients, 0, unroll=4)

    def across(q, inner):
        u, d = u_s[q], d_s[q]
        return d + d * u - d * u_s[inner] + d_s[inner]

    fx[0] = across(0, 1)
    gx[nq - 1] = across(nq - 1, nq - 2)

    def finish(q, part):
        def edge(here, there):
            u, d, w = (ref[q, here : here + 1] for ref in fields)
            un, dn, wn = (ref[q, there : there + 1] for ref in fields)
            return (d + d * u - d * un + dn) * (w - wn)

        a_s[q, 0:ny] = part
        a_s[q, ny:] = jnp.zeros((2 * W, nz), F32)
        a_s[q, 0:1] += edge(0, rows - 1)
        a_s[q, ny - 1 : ny] += edge(ny - 1, ny)

    finish(0, xlo[3 * H])
    finish(nq - 1, xhi[3 * H])

    def adjoint_at(w, q):
        v = w[q]
        total = dg[q] * v - fx[q] * w[q + 1] - gx[q] * w[q - 1]
        total = total - fy[q] * up(v, 0) - gy[q] * down(v, 0)
        total = total - fz[q] * up(v, 1) - gz[q] * down(v, 1)
        return jnp.where(d_s[q] > 0.0, total, 0.0)

    def forward_at(w, q):
        total = forward(w, q, dg, fx, gx, fy, gy, fz, gz)
        return jnp.where(d_s[q] > 0.0, total, 0.0)

    def sweep(apply, w, margin, out_s, out):
        def edge(q, carry):
            out_s[q] = apply(w, q)
            return carry

        def middle(q, carry):
            value = apply(w, q)
            out_s[q] = value
            mine = value[0:ny]
            out[q - H] = mine
            return carry + jnp.sum((mine * mine).reshape(ny // 8, 8, nz), axis=0)

        if margin < H:
            for q in (*range(margin, H), *range(H + nx, nq - margin)):
                edge(q, 0)
        return lax.fori_loop(H, H + nx, middle, jnp.zeros((8, nz), F32), unroll=4)

    def source_norm(q, carry):
        mine = source[q]
        return carry + jnp.sum((mine * mine).reshape(ny // 8, 8, nz), axis=0)

    m0 = lax.fori_loop(0, nx, source_norm, jnp.zeros((8, nz), F32), unroll=True)
    m1 = sweep(adjoint_at, s_s, 1, a_s, p1)
    m2 = sweep(forward_at, a_s, 1, b_s, p2)
    m3 = sweep(adjoint_at, b_s, 2, a_s, p3)

    slot = lax.broadcasted_iota(jnp.int32, (1, LANES), 1)
    row = jnp.zeros((1, LANES), F32)
    for k, m in enumerate((m0, m1, m2, m3)):
        row = jnp.where(slot == k, jnp.sum(m), row)
    moments[...] = jnp.broadcast_to(row, moments.shape)


def forward(w, q, dg, fx, gx, fy, gy, fz, gz):
    v = w[q]
    total = dg[q] * v - gx[q + 1] * w[q + 1] - fx[q - 1] * w[q - 1]
    total = total - up(gy[q] * v, 0) - down(fy[q] * v, 0)
    return total - up(gz[q] * v, 1) - down(fz[q] * v, 1)


def last_apply_kernel(w, dg, fx, gx, fy, gy, fz, gz, out):
    nx, ny, _ = out.shape

    def plane(x, carry):
        out[x] = forward(w, x + H, dg, fx, gx, fy, gy, fz, gz)[0:ny]
        return carry

    lax.fori_loop(0, nx, plane, 0, unroll=4)


def last_apply(like, *fields):
    whole = pl.BlockSpec(memory_space=pltpu.VMEM)
    return pl.pallas_call(
        last_apply_kernel,
        out_shape=jax.ShapeDtypeStruct(like.shape, F32),
        in_specs=[whole] * 8,
        out_specs=whole,
        compiler_params=pltpu.CompilerParams(vmem_limit_bytes=16 << 20),
        cost_estimate=pl.CostEstimate(
            flops=1 << 22, bytes_accessed=1 << 24, transcendentals=0
        ),
        name="last_apply",
    )(*fields)


def krylov(copies, conc, diff, source, *halos):
    nx, ny, nz = conc.shape
    whole = pl.BlockSpec(memory_space=pltpu.VMEM)
    block = jax.ShapeDtypeStruct((nx, ny, nz), F32)
    padded = (nx + 2 * H, ny + 2 * W, nz)
    return pl.pallas_call(
        krylov_kernel,
        out_shape=(block,) * 3
        + (jax.ShapeDtypeStruct((copies, 1, LANES), F32),)
        + (jax.ShapeDtypeStruct(padded, F32),) * 8,
        in_specs=[whole] * 9,
        out_specs=(whole,) * 12,
        scratch_shapes=[pltpu.VMEM(padded, F32)] * 4,
        compiler_params=pltpu.CompilerParams(vmem_limit_bytes=32 << 20),
        name="krylov",
    )(conc, diff, source, *halos)


def combine_kernel(moments, source, p1, p2, p3, p4, adjoint, residual):
    m = jnp.sum(moments[...], axis=0)
    m0, m1, m2, m3 = (m[:, k : k + 1] for k in range(4))
    alpha = m0 / m1
    beta = alpha * (m2 / m1) - 1.0
    grow = 1.0 + beta
    image = grow * grow * m1 - 2.0 * grow * alpha * m2 + alpha * alpha * m3
    step = (beta * m0) / image
    near = alpha + step * grow
    far = step * alpha
    adjoint[...] = near[None] * p1[...] - far[None] * p3[...]
    residual[...] = source[...] - near[None] * p2[...] + far[None] * p4[...]


def combine(moments, source, p1, p2, p3, p4):
    whole = pl.BlockSpec(memory_space=pltpu.VMEM)
    block = jax.ShapeDtypeStruct(source.shape, F32)
    return pl.pallas_call(
        combine_kernel,
        out_shape=(block, block),
        in_specs=[whole] * 6,
        out_specs=(whole, whole),
        compiler_params=pltpu.CompilerParams(vmem_limit_bytes=16 << 20),
        name="combine",
    )(moments, source, p1, p2, p3, p4)


def forth(cells, axis):
    count = lax.axis_size(axis)
    return lax.ppermute(cells, axis, [(i, i + 1) for i in range(count - 1)])


def back(cells, axis):
    count = lax.axis_size(axis)
    return lax.ppermute(cells, axis, [(i + 1, i) for i in range(count - 1)])


def local(conc, labels, kappa, source):
    conc, source, diff, xtail = pack(conc, labels, kappa, source)
    xlo = forth(xtail, "gx")
    yhead, ytail = pack_rows(conc, diff, source)
    ylo = forth(ytail, "gy")
    yhi = back(yhead, "gy")
    xhi = back(pack_head(conc, diff, source, ylo), "gx")
    chead, ctail = pack_corners(ylo, yhi)
    clo = forth(ctail, "gx")
    chi = back(chead, "gx")
    p1, p2, p3, moments, *fields = krylov(
        1, conc, diff, source, xlo, xhi, ylo, yhi, clo, chi
    )
    moments = lax.all_gather(moments, ("gx", "gy"), axis=0, tiled=True)
    p4 = last_apply(p3, *fields)
    return combine(moments, source, p1, p2, p3, p4)


def solution(mesh):
    return jax.shard_map(
        local,
        mesh=mesh,
        in_specs=(P("gx", "gy", None), P("gx", "gy", None), P(), P("gx", "gy", None)),
        out_specs=(P("gx", "gy", None), P("gx", "gy", None)),
        check_vma=False,
    )
```

```python
import functools

import jax
import jax.numpy as jnp
from jax import lax
from jax.experimental import pallas as pl
from jax.experimental.pallas import tpu as pltpu
from jax.sharding import PartitionSpec as P

ITERS = 2
DT = 0.5
W = 2 * ITERS
H = W - 1
F32 = jnp.float32
LANES = 128


def up(v, axis):
    return pltpu.roll(v, v.shape[axis] - 1, axis)


def down(v, axis):
    return pltpu.roll(v, 1, axis)


def positions(shape, axis):
    index = lax.broadcasted_iota(jnp.int32, shape, axis)
    return index == 0, index == shape[axis] - 1


def low_first(axis):
    return lax.axis_index(axis) % 2 == 0


def pack_kernel(
    kappa_in, conc_in, labels_in, source_in,
    conc, source, diff, xone, xtwo,
    labels, kappa, sems,
):
    nx, ny, nz = conc.shape
    copies = [
        pltpu.make_async_copy(src, dst, sems.at[k])
        for k, (src, dst) in enumerate(
            (
                (kappa_in, kappa),
                (labels_in, labels),
                (conc_in, conc),
                (source_in, source),
            )
        )
    ]
    for copy in copies:
        copy.start()
    for copy in copies:
        copy.wait()
    k0, k1, k2 = ((0.5 * DT) * kappa[k] for k in range(3))

    def body(x, carry):
        lab = labels[x]
        base = jnp.where(lab == 0, k0, jnp.where(lab == 1, k1, k2))
        diff[x] = base * jnp.exp(conc[x])
        return carry

    lax.fori_loop(0, nx, body, 0, unroll=True)
    flip = low_first("gx")
    pack_face((conc, diff, source), ~flip, xone)
    pack_face((conc, diff, source), flip, xtwo)


def pack_face(fields, at_tail, slab):
    nx = fields[0].shape[0]
    begin = jnp.where(at_tail, nx - H, 0)
    for k, ref in enumerate(fields):
        slab[k * H : (k + 1) * H] = ref[pl.ds(begin, H)]
    slab[3 * H] = partial_image(fields, jnp.where(at_tail, nx - H, H - 1))


def partial_image(fields, x):
    conc, diff, source = fields
    u, d, w = conc[x], diff[x], source[x]
    bottom, top = positions(u.shape, 0)
    first, last = positions(u.shape, 1)
    e = d + d * u

    def term(un, dn, wn):
        return (e - d * un + dn) * (w - wn)

    def shifted(move, edge, axis):
        return [jnp.where(edge, 0.0, move(v, axis)) for v in (u, d, w)]

    total = w + term(conc[x + 1], diff[x + 1], source[x + 1])
    total = total + term(conc[x - 1], diff[x - 1], source[x - 1])
    total = total + jnp.where(top, 0.0, term(*shifted(up, top, 0)))
    total = total + jnp.where(bottom, 0.0, term(*shifted(down, bottom, 0)))
    total = total + term(*shifted(up, last, 1))
    return total + term(*shifted(down, first, 1))


def pack(conc, labels, kappa, source):
    nx, ny, nz = conc.shape
    whole = pl.BlockSpec(memory_space=pltpu.VMEM)
    block = jax.ShapeDtypeStruct((nx, ny, nz), F32)
    slab = jax.ShapeDtypeStruct((3 * H + 1, ny, nz), F32)
    outside = [
        pltpu.with_memory_space_constraint(v, pltpu.HBM)
        for v in (kappa, conc, labels, source)
    ]
    return pl.pallas_call(
        pack_kernel,
        out_shape=(block, block, block, slab, slab),
        in_specs=[pl.BlockSpec(memory_space=pltpu.HBM)] * 4,
        out_specs=(whole,) * 5,
        scratch_shapes=[
            pltpu.VMEM((nx, ny, nz), jnp.int32),
            pltpu.SMEM((3,), F32),
            pltpu.SemaphoreType.DMA((4,)),
        ],
        compiler_params=pltpu.CompilerParams(vmem_limit_bytes=16 << 20),
        name="pack",
    )(*outside)


def pack_rows_kernel(conc, diff, source, yone, ytwo):
    ny = conc.shape[1]
    flip = low_first("gy")
    for k, ref in enumerate((conc, diff, source)):
        head = ref[:, 0:W, :]
        tail = ref[:, ny - W : ny, :]
        yone[k] = jnp.where(flip, head, tail)
        ytwo[k] = jnp.where(flip, tail, head)


def pack_rows(conc, diff, source):
    nx, ny, nz = conc.shape
    whole = pl.BlockSpec(memory_space=pltpu.VMEM)
    rows = jax.ShapeDtypeStruct((3, nx, W, nz), F32)
    return pl.pallas_call(
        pack_rows_kernel,
        out_shape=(rows, rows),
        in_specs=[whole] * 3,
        out_specs=(whole, whole),
        compiler_params=pltpu.CompilerParams(vmem_limit_bytes=16 << 20),
        cost_estimate=pl.CostEstimate(
            flops=1 << 22, bytes_accessed=1 << 24, transcendentals=0
        ),
        name="pack_rows",
    )(conc, diff, source)


def corner_slots():
    at = 0
    for k in range(3):
        for dx in range(1, H + 1):
            for side in range(2):
                yield k, dx, side, at
                at += W - dx


CORNER_ROWS = 3 * sum(2 * (W - dx) for dx in range(1, H + 1))


def pack_corners_kernel(yone, ytwo, cone, ctwo):
    nx = yone.shape[1]
    flip_x, flip_y = low_first("gx"), low_first("gy")
    for k, dx, side, at in corner_slots():
        n = W - dx
        rows = slice(0, n) if side == 0 else slice(W - n, W)
        above = flip_y if side == 0 else ~flip_y
        for slab, at_tail in ((cone, ~flip_x), (ctwo, flip_x)):
            x = jnp.where(at_tail, nx - dx, dx - 1)
            slab[at : at + n] = jnp.where(above, ytwo[k, x, rows], yone[k, x, rows])


def pack_corners(yone, ytwo):
    nz = yone.shape[3]
    whole = pl.BlockSpec(memory_space=pltpu.VMEM)
    rows = jax.ShapeDtypeStruct((CORNER_ROWS, nz), F32)
    return pl.pallas_call(
        pack_corners_kernel,
        out_shape=(rows, rows),
        in_specs=[whole] * 2,
        out_specs=(whole, whole),
        compiler_params=pltpu.CompilerParams(vmem_limit_bytes=16 << 20),
        name="pack_corners",
    )(yone, ytwo)


def krylov_kernel(
    conc, diff, source, xone, xtwo, yone, ytwo, cone, ctwo,
    p1, p2, p3, p4, moments,
    u_s, d_s, s_s, fx, gx, fy, gy, fz, gz, dg, a_s, b_s,
):
    nx, ny, nz = conc.shape
    nq = nx + 2 * H
    rows = ny + 2 * W
    fields = (u_s, d_s, s_s)
    flip_x, flip_y = low_first("gx"), low_first("gy")
    sides = ((xone, cone, flip_x), (xtwo, ctwo, ~flip_x))
    for k, (own, ref) in enumerate(zip((conc, diff, source), fields)):
        ref[H : H + nx, 0:ny, :] = own[...]
        ref[H : H + nx, ny : ny + W, :] = jnp.where(flip_y, ytwo[k], yone[k])
        ref[H : H + nx, ny + W :, :] = jnp.where(flip_y, yone[k], ytwo[k])
        ref[0:H, ny:, :] = jnp.zeros((H, 2 * W, nz), F32)
        ref[H + nx :, ny:, :] = jnp.zeros((H, 2 * W, nz), F32)
        for face, _, low in sides:
            begin = jnp.where(low, 0, H + nx)
            ref[pl.ds(begin, H), 0:ny, :] = face[k * H : (k + 1) * H]
    for k, dx, side, at in corner_slots():
        n = W - dx
        begin = ny if side == 0 else rows - n
        for _, corner, low in sides:
            q = jnp.where(low, H - dx, H + nx - 1 + dx)
            fields[k][q, begin : begin + n, :] = corner[at : at + n]

    first, last = positions((rows, nz), 1)

    def coefficients(q, carry):
        u, d = u_s[q], d_s[q]
        e = d + d * u

        def toward(un, dn):
            return e - d * un + dn

        fxq = toward(u_s[q + 1], d_s[q + 1])
        gxq = toward(u_s[q - 1], d_s[q - 1])
        fyq = toward(up(u, 0), up(d, 0))
        gyq = toward(down(u, 0), down(d, 0))
        fzq = toward(jnp.where(last, 0.0, up(u, 1)), jnp.where(last, 0.0, up(d, 1)))
        gzq = toward(jnp.where(first, 0.0, down(u, 1)), jnp.where(first, 0.0, down(d, 1)))
        dg[q] = 1.0 + ((fxq + gxq) + (fyq + gyq)) + (fzq + gzq)
        fx[q] = fxq
        gx[q] = gxq
        fy[q] = fyq
        gy[q] = gyq
        fz[q] = jnp.where(last, 0.0, fzq)
        gz[q] = jnp.where(first, 0.0, gzq)
        return carry

    lax.fori_loop(1, nq - 1, coefficients, 0, unroll=4)

    def across(q, inner):
        u, d = u_s[q], d_s[q]
        return d + d * u - d * u_s[inner] + d_s[inner]

    fx[0] = across(0, 1)
    gx[nq - 1] = across(nq - 1, nq - 2)

    def finish(q, part):
        def edge(here, there):
            u, d, w = (ref[q, here : here + 1] for ref in fields)
            un, dn, wn = (ref[q, there : there + 1] for ref in fields)
            return (d + d * u - d * un + dn) * (w - wn)

        a_s[q, 0:ny] = part
        a_s[q, ny:] = jnp.zeros((2 * W, nz), F32)
        a_s[q, 0:1] += edge(0, rows - 1)
        a_s[q, ny - 1 : ny] += edge(ny - 1, ny)

    for face, _, low in sides:
        finish(jnp.where(low, 0, nq - 1), face[3 * H])

    def adjoint_at(w, q):
        v = w[q]
        total = dg[q] * v - fx[q] * w[q + 1] - gx[q] * w[q - 1]
        total = total - fy[q] * up(v, 0) - gy[q] * down(v, 0)
        total = total - fz[q] * up(v, 1) - gz[q] * down(v, 1)
        return jnp.where(d_s[q] > 0.0, total, 0.0)

    def forward_at(w, q):
        v = w[q]
        total = dg[q] * v - gx[q + 1] * w[q + 1] - fx[q - 1] * w[q - 1]
        total = total - up(gy[q] * v, 0) - down(fy[q] * v, 0)
        total = total - up(gz[q] * v, 1) - down(fz[q] * v, 1)
        return jnp.where(d_s[q] > 0.0, total, 0.0)

    def sweep(apply, w, margin, out_s, out):
        def edge(q, carry):
            out_s[q] = apply(w, q)
            return carry

        def middle(q, carry):
            value = apply(w, q)
            if out_s is not None:
                out_s[q] = value
            mine = value[0:ny]
            out[q - H] = mine
            return carry + jnp.sum((mine * mine).reshape(ny // 8, 8, nz), axis=0)

        if margin < H:
            for q in (*range(margin, H), *range(H + nx, nq - margin)):
                edge(q, 0)
        return lax.fori_loop(H, H + nx, middle, jnp.zeros((8, nz), F32), unroll=4)

    def source_norm(q, carry):
        mine = source[q]
        return carry + jnp.sum((mine * mine).reshape(ny // 8, 8, nz), axis=0)

    m0 = lax.fori_loop(0, nx, source_norm, jnp.zeros((8, nz), F32), unroll=True)
    m1 = sweep(adjoint_at, s_s, 1, a_s, p1)
    m2 = sweep(forward_at, a_s, 1, b_s, p2)
    m3 = sweep(adjoint_at, b_s, 2, a_s, p3)
    sweep(forward_at, a_s, 3, None, p4)

    slot = lax.broadcasted_iota(jnp.int32, (1, LANES), 1)
    row = jnp.zeros((1, LANES), F32)
    for k, m in enumerate((m0, m1, m2, m3)):
        row = jnp.where(slot == k, jnp.sum(m), row)
    moments[...] = jnp.broadcast_to(row, moments.shape)


def krylov(copies, conc, diff, source, *halos):
    nx, ny, nz = conc.shape
    whole = pl.BlockSpec(memory_space=pltpu.VMEM)
    block = jax.ShapeDtypeStruct((nx, ny, nz), F32)
    scratch = pltpu.VMEM((nx + 2 * H, ny + 2 * W, nz), F32)
    return pl.pallas_call(
        krylov_kernel,
        out_shape=(block,) * 4 + (jax.ShapeDtypeStruct((copies, 1, LANES), F32),),
        in_specs=[whole] * 9,
        out_specs=(whole,) * 5,
        scratch_shapes=[scratch] * 12,
        compiler_params=pltpu.CompilerParams(vmem_limit_bytes=32 << 20),
        name="krylov",
    )(conc, diff, source, *halos)


def combine_kernel(moments, source, p1, p2, p3, p4, adjoint, residual):
    m = jnp.sum(moments[...], axis=0)
    m0, m1, m2, m3 = (m[:, k : k + 1] for k in range(4))
    alpha = m0 / m1
    beta = alpha * (m2 / m1) - 1.0
    grow = 1.0 + beta
    image = grow * grow * m1 - 2.0 * grow * alpha * m2 + alpha * alpha * m3
    step = (beta * m0) / image
    near = alpha + step * grow
    far = step * alpha
    adjoint[...] = near[None] * p1[...] - far[None] * p3[...]
    residual[...] = source[...] - near[None] * p2[...] + far[None] * p4[...]


def combine(moments, source, p1, p2, p3, p4):
    whole = pl.BlockSpec(memory_space=pltpu.VMEM)
    block = jax.ShapeDtypeStruct(source.shape, F32)
    return pl.pallas_call(
        combine_kernel,
        out_shape=(block, block),
        in_specs=[whole] * 6,
        out_specs=(whole, whole),
        compiler_params=pltpu.CompilerParams(vmem_limit_bytes=16 << 20),
        name="combine",
    )(moments, source, p1, p2, p3, p4)


def swap(cells, axis, first):
    pairs = [(i, i + 1) for i in range(first, lax.axis_size(axis) - 1, 2)]
    return lax.ppermute(cells, axis, pairs + [(j, i) for i, j in pairs])


def local(conc, labels, kappa, source):
    conc, source, diff, xone, xtwo = pack(conc, labels, kappa, source)
    xone = swap(xone, "gx", 1)
    xtwo = swap(xtwo, "gx", 0)
    yone, ytwo = pack_rows(conc, diff, source)
    yone = swap(yone, "gy", 1)
    ytwo = swap(ytwo, "gy", 0)
    cone, ctwo = pack_corners(yone, ytwo)
    cone = swap(cone, "gx", 1)
    ctwo = swap(ctwo, "gx", 0)
    count = lax.axis_size(("gx", "gy"))
    p1, p2, p3, p4, moments = krylov(
        count, conc, diff, source, xone, xtwo, yone, ytwo, cone, ctwo
    )
    moments = lax.all_to_all(moments, ("gx", "gy"), 0, 0, tiled=True)
    return combine(moments, source, p1, p2, p3, p4)


def solution(mesh):
    return jax.shard_map(
        local,
        mesh=mesh,
        in_specs=(P("gx", "gy", None), P("gx", "gy", None), P(), P("gx", "gy", None)),
        out_specs=(P("gx", "gy", None), P("gx", "gy", None)),
        check_vma=False,
    )
```

```python
import jax
import jax.numpy as jnp
from jax import lax
from jax.experimental import pallas as pl
from jax.experimental.pallas import tpu as pltpu
from jax.sharding import PartitionSpec as P

ITERS = 2
DT = 0.5
W = 2 * ITERS
F32 = jnp.float32
LANES = 128
VMEM = pl.BlockSpec(memory_space=pltpu.VMEM)


def low_first(axis):
    return lax.axis_index(axis) % 2 == 0


def up(v, axis):
    return pltpu.roll(v, v.shape[axis] - 1, axis)


def down(v, axis):
    return pltpu.roll(v, 1, axis)


def z_ends(shape):
    index = lax.broadcasted_iota(jnp.int32, shape, 1)
    return index == 0, index == shape[1] - 1


def coupling(u, d, un, dn):
    return d + d * u - d * un + dn


def params(megabytes=16):
    return pltpu.CompilerParams(vmem_limit_bytes=megabytes << 20)


def f32(*shape):
    return jax.ShapeDtypeStruct(shape, F32)


HALO = ((0, 3), (1, 3), (2, 3), (3, 2), (4, 2))


def corner_slots(ny):
    at = 2 * ny + 2
    for field, n in HALO:
        for side in range(2):
            yield field, n, side, at
            at += n


def corner_rows(ny):
    rows = 2 * ny + 2 + sum(2 * n for _, n in HALO)
    return -(-rows // 8) * 8


def pack_kernel(
    kappa_in, conc_in, labels_in, source_in,
    conc, source, diff, xone, xtwo,
    labels, kappa, sems,
):
    nx, ny, nz = conc.shape
    copies = [
        pltpu.make_async_copy(src, dst, sems.at[k])
        for k, (src, dst) in enumerate(
            (
                (kappa_in, kappa),
                (labels_in, labels),
                (conc_in, conc),
                (source_in, source),
            )
        )
    ]
    for copy in copies:
        copy.start()
    for copy in copies:
        copy.wait()
    k0, k1, k2 = ((0.5 * DT) * kappa[k] for k in range(3))

    def body(x, carry):
        lab = labels[x]
        base = jnp.where(lab == 0, k0, jnp.where(lab == 1, k1, k2))
        diff[x] = base * jnp.exp(conc[x])
        return carry

    lax.fori_loop(0, nx, body, 0, unroll=True)
    flip = low_first("gx")
    for slab, at_head in ((xone, flip), (xtwo, ~flip)):
        edge = jnp.where(at_head, 0, nx - 1)
        inner = jnp.where(at_head, 1, nx - 2)
        slab[0] = conc[edge]
        slab[1] = diff[edge]
        slab[2] = source[edge]
        slab[3] = source[inner]
        slab[4] = coupling(conc[edge], diff[edge], conc[inner], diff[inner])


def pack(conc, labels, kappa, source):
    nx, ny, nz = conc.shape
    outside = [
        pltpu.with_memory_space_constraint(v, pltpu.HBM)
        for v in (kappa, conc, labels, source)
    ]
    return pl.pallas_call(
        pack_kernel,
        out_shape=(f32(nx, ny, nz),) * 3 + (f32(5, ny, nz),) * 2,
        in_specs=[pl.BlockSpec(memory_space=pltpu.HBM)] * 4,
        out_specs=(VMEM,) * 5,
        scratch_shapes=[
            pltpu.VMEM((nx, ny, nz), jnp.int32),
            pltpu.SMEM((3,), F32),
            pltpu.SemaphoreType.DMA((4,)),
        ],
        compiler_params=params(),
        name="pack",
    )(*outside)


def pack_rows_kernel(conc, diff, source, yone, ytwo):
    ny = conc.shape[1]
    flip = low_first("gy")
    for k, ref in enumerate((conc, diff, source)):
        head = ref[:, 0:W, :]
        tail = ref[:, ny - W : ny, :]
        yone[k] = jnp.where(flip, head, tail)
        ytwo[k] = jnp.where(flip, tail, head)


def pack_rows(conc, diff, source):
    nx, ny, nz = conc.shape
    return pl.pallas_call(
        pack_rows_kernel,
        out_shape=(f32(3, nx, W, nz),) * 2,
        in_specs=[VMEM] * 3,
        out_specs=(VMEM,) * 2,
        compiler_params=params(),
        cost_estimate=pl.CostEstimate(
            flops=1 << 22, bytes_accessed=1 << 24, transcendentals=0
        ),
        name="pack_rows",
    )(conc, diff, source)


def in_plane_adjoint(v, fy, gy, fz, gz):
    total = fy * up(v, 0) + gy * down(v, 0)
    return total + (fz * up(v, 1) + gz * down(v, 1))


def in_plane_forward(v, fy, gy, fz, gz):
    total = up(gy * v, 0) + down(fy * v, 0)
    return total + (up(gz * v, 1) + down(fz * v, 1))


def in_plane_couplings(u, d):
    first, last = z_ends(u.shape)
    fy = coupling(u, d, up(u, 0), up(d, 0))
    gy = coupling(u, d, down(u, 0), down(d, 0))
    fz = coupling(u, d, jnp.where(last, 0.0, up(u, 1)), jnp.where(last, 0.0, up(d, 1)))
    gz = coupling(
        u, d, jnp.where(first, 0.0, down(u, 1)), jnp.where(first, 0.0, down(d, 1))
    )
    return fy, gy, fz, gz


def own_kernel(
    conc, diff, source, yone, ytwo,
    u_s, d_s, s_s, fx, gx, fy, gy, fz, gz, dg, p1, cone, ctwo,
    slabs,
):
    nx, ny, nz = conc.shape
    rows = ny + 2 * W
    flip_x, flip_y = low_first("gx"), low_first("gy")
    for k, (own, ref) in enumerate(((conc, u_s), (diff, d_s), (source, s_s))):
        ref[:, 0:ny, :] = own[...]
        ref[:, ny : ny + W, :] = jnp.where(flip_y, ytwo[k], yone[k])
        ref[:, ny + W :, :] = jnp.where(flip_y, yone[k], ytwo[k])
    first, last = z_ends((rows, nz))

    order = [q for k in range(nx // 2) for q in (k, nx - 1 - k)]
    for q in order:
        u, d = u_s[q], d_s[q]
        fyq, gyq, fzq, gzq = in_plane_couplings(u, d)
        total = 1.0 + ((fyq + gyq) + (fzq + gzq))
        if q + 1 < nx:
            fxq = coupling(u, d, u_s[q + 1], d_s[q + 1])
            fx[q] = fxq
            total = total + fxq
        if q > 0:
            gxq = coupling(u, d, u_s[q - 1], d_s[q - 1])
            gx[q] = gxq
            total = total + gxq
        dg[q] = total
        fy[q] = fyq
        gy[q] = gyq
        fz[q] = jnp.where(last, 0.0, fzq)
        gz[q] = jnp.where(first, 0.0, gzq)

    for q in order[2:]:
        v = s_s[q]
        total = dg[q] * v - fx[q] * s_s[q + 1] - gx[q] * s_s[q - 1]
        total = total - in_plane_adjoint(v, fy[q], gy[q], fz[q], gz[q])
        p1[q] = jnp.where(d_s[q] > 0.0, total, 0.0)

    for at, edge, inner, beyond in ((0, 0, 1, 2), (1, nx - 1, nx - 2, nx - 3)):
        toward, away = (fx, gx) if at == 0 else (gx, fx)
        v = p1[inner]
        m = away[inner] * v
        q = dg[inner] * v - away[beyond] * p1[beyond]
        q = q - in_plane_forward(v, fy[inner], gy[inner], fz[inner], gz[inner])
        slabs[at, 0:ny] = m[0:ny]
        slabs[at, ny : 2 * ny] = q[0:ny]
        slabs[at, 2 * ny : 2 * ny + 1] = m[ny : ny + 1]
        slabs[at, 2 * ny + 1 : 2 * ny + 2] = m[rows - 1 : rows]
        kept = (u_s.at[edge], d_s.at[edge], s_s.at[edge], s_s.at[inner], toward.at[edge])
        used = 2 * ny + 2
        for field, n, side, row in corner_slots(ny):
            begin = ny if side == 0 else rows - n
            slabs[at, row : row + n] = kept[field][begin : begin + n, :]
            used = row + n
        if used < slabs.shape[1]:
            slabs[at, used:] = jnp.zeros((slabs.shape[1] - used, nz), F32)
    cone[...] = jnp.where(flip_x, slabs[0], slabs[1])
    ctwo[...] = jnp.where(flip_x, slabs[1], slabs[0])


def own(conc, diff, source, yone, ytwo):
    nx, ny, nz = conc.shape
    corner = f32(corner_rows(ny), nz)
    return pl.pallas_call(
        own_kernel,
        out_shape=(f32(nx, ny + 2 * W, nz),) * 11 + (corner,) * 2,
        in_specs=[VMEM] * 5,
        out_specs=(VMEM,) * 13,
        scratch_shapes=[pltpu.VMEM((2, corner_rows(ny), nz), F32)],
        compiler_params=params(),
        name="own",
    )(conc, diff, source, yone, ytwo)


def square(v, ny):
    mine = v[0:ny]
    return jnp.sum((mine * mine).reshape(ny // 8, 8, mine.shape[1]), axis=0)


def inside_kernel(d_s, s_s, fx, gx, fy, gy, fz, gz, dg, p1, p2, p3, part):
    nx, rows, nz = d_s.shape
    ny = rows - 2 * W
    sums = [jnp.zeros((8, nz), F32) for _ in range(4)]
    for q in range(nx):
        sums[0] = sums[0] + square(s_s[q], ny)
    for q in range(1, nx - 1):
        sums[1] = sums[1] + square(p1[q], ny)
    for q in range(2, nx - 2):
        v = p1[q]
        total = dg[q] * v - gx[q + 1] * p1[q + 1] - fx[q - 1] * p1[q - 1]
        total = total - in_plane_forward(v, fy[q], gy[q], fz[q], gz[q])
        total = jnp.where(d_s[q] > 0.0, total, 0.0)
        p2[q] = total
        sums[2] = sums[2] + square(total, ny)
    for q in range(3, nx - 3):
        v = p2[q]
        total = dg[q] * v - fx[q] * p2[q + 1] - gx[q] * p2[q - 1]
        total = total - in_plane_adjoint(v, fy[q], gy[q], fz[q], gz[q])
        total = jnp.where(d_s[q] > 0.0, total, 0.0)
        p3[q] = total
        sums[3] = sums[3] + square(total, ny)
    for k in range(4):
        part[k] = sums[k]


def inside(d_s, *fields):
    nx, rows, nz = d_s.shape
    return pl.pallas_call(
        inside_kernel,
        out_shape=(f32(nx, rows, nz),) * 2 + (f32(4, 8, nz),),
        in_specs=[VMEM] * 10,
        out_specs=(VMEM,) * 3,
        compiler_params=params(),
        cost_estimate=pl.CostEstimate(
            flops=1 << 22, bytes_accessed=1 << 23, transcendentals=0
        ),
        name="inside",
    )(d_s, *fields)


def finish_kernel(
    u_s, d_s, s_s, fx, gx, fy, gy, fz, gz, dg, p1_in, p2_in, p3_in, part,
    xone, xtwo, cone, ctwo,
    p1_out, p2_out, p3_out, p4_out, moments,
    side_s, edge_s, w_s,
):
    nx, rows, nz = d_s.shape
    ny = rows - 2 * W
    flip = low_first("gx")
    first, last = z_ends((rows, nz))

    for side, one in ((0, flip), (1, ~flip)):
        side_s[side, :, ny:, :] = jnp.zeros((7, 2 * W, nz), F32)
        for k in range(5):
            side_s[side, k, 0:ny] = jnp.where(one, xone[k], xtwo[k])
        corner = jnp.where(one, cone[...], ctwo[...])
        side_s[side, 5, 0:ny] = corner[0:ny]
        side_s[side, 6, 0:ny] = corner[ny : 2 * ny]
        side_s[side, 5, ny : ny + 1] = corner[2 * ny : 2 * ny + 1]
        side_s[side, 5, rows - 1 : rows] = corner[2 * ny + 1 : 2 * ny + 2]
        for field, n, half, row in corner_slots(ny):
            begin = ny if half == 0 else rows - n
            side_s[side, field, begin : begin + n] = corner[row : row + n]

    names = dict(
        u=u_s, d=d_s, s=s_s, fx=fx, gx=gx, fy=fy, gy=gy, fz=fz, gz=gz, dg=dg,
        p1=p1_in, p2=p2_in, p3=p3_in,
    )
    place = {(k, q): names[k].at[q] for k in names for q in range(nx)}
    spare = iter(range(w_s.shape[0]))

    def keep(name, q, value):
        place[name, q] = w_s.at[next(spare)]
        place[name, q][...] = value

    def get(name, q):
        return place[name, q][...]

    for side, (o, e, outward, inward) in enumerate(
        ((-1, 0, "gx", "fx"), (nx, nx - 1, "fx", "gx"))
    ):
        beyond = 2 * o - e
        for k, name in enumerate(("u", "d", "s")):
            place[name, o] = side_s.at[side, k]
        place["s", beyond] = side_s.at[side, 3]
        place[outward, o] = side_s.at[side, 4]
        place["m", o] = side_s.at[side, 5]
        place["q", o] = side_s.at[side, 6]
        u, d, ue, de = get("u", o), get("d", o), get("u", e), get("d", e)
        back = coupling(u, d, ue, de)
        out = coupling(ue, de, u, d)
        fyq, gyq, fzq, gzq = in_plane_couplings(u, d)
        total = 1.0 + get(outward, o) + back + ((fyq + gyq) + (fzq + gzq))
        new = {
            (inward, o): back,
            (outward, e): out,
            ("dg", o): total,
            ("dg", e): get("dg", e) + out,
            ("fy", o): fyq,
            ("gy", o): gyq,
            ("fz", o): jnp.where(last, 0.0, fzq),
            ("gz", o): jnp.where(first, 0.0, gzq),
        }
        for k, (key, value) in enumerate(new.items()):
            place[key] = edge_s.at[side, k]
            place[key][...] = value

    def masked(total, q):
        return jnp.where(get("d", q) > 0.0, total, 0.0)

    def in_plane(q):
        return [get(k, q) for k in ("fy", "gy", "fz", "gz")]

    def adjoint_at(w, q):
        v = get(w, q)
        total = get("dg", q) * v - get("fx", q) * get(w, q + 1)
        total = total - get("gx", q) * get(w, q - 1)
        return masked(total - in_plane_adjoint(v, *in_plane(q)), q)

    def forward_at(w, q):
        v = get(w, q)
        above = get("m", q) if q == nx else get("gx", q + 1) * get(w, q + 1)
        below = get("m", q) if q == -1 else get("fx", q - 1) * get(w, q - 1)
        total = get("dg", q) * v - above - below
        return masked(total - in_plane_forward(v, *in_plane(q)), q)

    sums = [part[k] for k in range(4)]

    def sweep(k, apply, w, name, out, ready):
        for q in range(-1, nx + 1):
            if ready <= q < nx - ready:
                out[q] = get(name, q)[0:ny]
                continue
            value = apply(w, q)
            keep(name, q, value)
            if 0 <= q < nx:
                out[q] = value[0:ny]
                sums[k] = sums[k] + square(value, ny)

    sweep(1, adjoint_at, "s", "p1", p1_out, 1)
    sweep(2, forward_at, "p1", "p2", p2_out, 2)
    for o, outward in ((-1, "gx"), (nx, "fx")):
        beyond = -2 if o == -1 else nx + 1
        keep("p2", beyond, get("q", o) - get(outward, o) * get("p1", o))
    sweep(3, adjoint_at, "p2", "p3", p3_out, 3)
    for q in range(nx):
        p4_out[q] = forward_at("p3", q)[0:ny]

    slot = lax.broadcasted_iota(jnp.int32, (1, LANES), 1)
    row = jnp.zeros((1, LANES), F32)
    for k in range(4):
        row = jnp.where(slot == k, jnp.sum(sums[k]), row)
    moments[...] = jnp.broadcast_to(row, moments.shape)


def finish(copies, ny, *fields):
    nx, rows, nz = fields[0].shape
    steps = 4 + 6 + 2 + 8
    return pl.pallas_call(
        finish_kernel,
        out_shape=(f32(nx, ny, nz),) * 4 + (f32(copies, 1, LANES),),
        in_specs=[VMEM] * len(fields),
        out_specs=(VMEM,) * 5,
        scratch_shapes=[
            pltpu.VMEM((2, 7, rows, nz), F32),
            pltpu.VMEM((2, 8, rows, nz), F32),
            pltpu.VMEM((steps, rows, nz), F32),
        ],
        compiler_params=params(),
        name="finish",
    )(*fields)


def combine_kernel(moments, source, p1, p2, p3, p4, adjoint, residual):
    m = jnp.sum(moments[...], axis=0)
    m0, m1, m2, m3 = (m[:, k : k + 1] for k in range(4))
    alpha = m0 / m1
    beta = alpha * (m2 / m1) - 1.0
    grow = 1.0 + beta
    image = grow * grow * m1 - 2.0 * grow * alpha * m2 + alpha * alpha * m3
    step = (beta * m0) / image
    near = alpha + step * grow
    far = step * alpha
    adjoint[...] = near[None] * p1[...] - far[None] * p3[...]
    residual[...] = source[...] - near[None] * p2[...] + far[None] * p4[...]


def combine(moments, source, p1, p2, p3, p4):
    return pl.pallas_call(
        combine_kernel,
        out_shape=(f32(*source.shape),) * 2,
        in_specs=[VMEM] * 6,
        out_specs=(VMEM,) * 2,
        compiler_params=params(),
        name="combine",
    )(moments, source, p1, p2, p3, p4)


def swap(cells, axis, first):
    pairs = [(i, i + 1) for i in range(first, lax.axis_size(axis) - 1, 2)]
    return lax.ppermute(cells, axis, pairs + [(j, i) for i, j in pairs])


def local(conc, labels, kappa, source):
    ny = conc.shape[1]
    conc, source, diff, xone, xtwo = pack(conc, labels, kappa, source)
    xone = swap(xone, "gx", 1)
    xtwo = swap(xtwo, "gx", 0)
    yone, ytwo = pack_rows(conc, diff, source)
    yone = swap(yone, "gy", 1)
    ytwo = swap(ytwo, "gy", 0)
    *fields, cone, ctwo = own(conc, diff, source, yone, ytwo)
    cone = swap(cone, "gx", 1)
    ctwo = swap(ctwo, "gx", 0)
    inner = inside(*fields[1:])
    p1, p2, p3, p4, moments = finish(
        lax.axis_size(("gx", "gy")), ny, *fields, *inner, xone, xtwo, cone, ctwo
    )
    moments = lax.all_to_all(moments, ("gx", "gy"), 0, 0, tiled=True)
    return combine(moments, source, p1, p2, p3, p4)


def solution(mesh):
    return jax.shard_map(
        local,
        mesh=mesh,
        in_specs=(P("gx", "gy", None), P("gx", "gy", None), P(), P("gx", "gy", None)),
        out_specs=(P("gx", "gy", None), P("gx", "gy", None)),
        check_vma=False,
    )
```

```python
import functools

import jax
import jax.numpy as jnp
from jax import lax
from jax.experimental import pallas as pl
from jax.experimental.pallas import tpu as pltpu
from jax.sharding import PartitionSpec as P

ITERS = 2
DT = 0.5
W = 2 * ITERS
F32 = jnp.float32
LANES = 128
VMEM = pl.BlockSpec(memory_space=pltpu.VMEM)


def low_first(axis):
    return lax.axis_index(axis) % 2 == 0


def up(v, axis):
    return pltpu.roll(v, v.shape[axis] - 1, axis)


def down(v, axis):
    return pltpu.roll(v, 1, axis)


def z_ends(shape):
    index = lax.broadcasted_iota(jnp.int32, shape, 1)
    return index == 0, index == shape[1] - 1


def coupling(u, d, un, dn):
    return d + d * u - d * un + dn


def params(megabytes=16):
    return pltpu.CompilerParams(vmem_limit_bytes=megabytes << 20)


def f32(*shape):
    return jax.ShapeDtypeStruct(shape, F32)


FIELDS = 7


def late_rows(ny):
    rows = ny + 2 * W
    for field, n in ((0, 3), (1, 3), (2, 3), (3, 2), (4, 2), (5, 1)):
        yield field, ny, n
        yield field, rows - n, n
    for field, n in ((5, 1), (6, 2)):
        yield field, 0, n
        yield field, ny - n, n


def late_count(ny):
    return sum(n for _, _, n in late_rows(ny))


def pack_kernel(
    kappa_in, conc_in, labels_in, source_in,
    conc, source, diff,
    labels, kappa, sems,
):
    nx, ny, nz = conc.shape
    copies = [
        pltpu.make_async_copy(src, dst, sems.at[k])
        for k, (src, dst) in enumerate(
            (
                (kappa_in, kappa),
                (labels_in, labels),
                (conc_in, conc),
                (source_in, source),
            )
        )
    ]
    for copy in copies:
        copy.start()
    for copy in copies:
        copy.wait()
    k0, k1, k2 = ((0.5 * DT) * kappa[k] for k in range(3))

    def body(x, carry):
        lab = labels[x]
        base = jnp.where(lab == 0, k0, jnp.where(lab == 1, k1, k2))
        diff[x] = base * jnp.exp(conc[x])
        return carry

    lax.fori_loop(0, nx, body, 0, unroll=True)


def pack(conc, labels, kappa, source):
    nx, ny, nz = conc.shape
    outside = [
        pltpu.with_memory_space_constraint(v, pltpu.HBM)
        for v in (kappa, conc, labels, source)
    ]
    return pl.pallas_call(
        pack_kernel,
        out_shape=(f32(nx, ny, nz),) * 3,
        in_specs=[pl.BlockSpec(memory_space=pltpu.HBM)] * 4,
        out_specs=(VMEM,) * 3,
        scratch_shapes=[
            pltpu.VMEM((nx, ny, nz), jnp.int32),
            pltpu.SMEM((3,), F32),
            pltpu.SemaphoreType.DMA((4,)),
        ],
        compiler_params=params(),
        name="pack",
    )(*outside)


def pack_rows_kernel(conc, diff, source, yone, ytwo):
    ny = conc.shape[1]
    flip = low_first("gy")
    for k, ref in enumerate((conc, diff, source)):
        head = ref[:, 0:W, :]
        tail = ref[:, ny - W : ny, :]
        yone[k] = jnp.where(flip, head, tail)
        ytwo[k] = jnp.where(flip, tail, head)


def pack_rows(conc, diff, source):
    nx, ny, nz = conc.shape
    return pl.pallas_call(
        pack_rows_kernel,
        out_shape=(f32(3, nx, W, nz),) * 2,
        in_specs=[VMEM] * 3,
        out_specs=(VMEM,) * 2,
        compiler_params=params(),
        cost_estimate=pl.CostEstimate(
            flops=1 << 22, bytes_accessed=1 << 24, transcendentals=0
        ),
        name="pack_rows",
    )(conc, diff, source)


def in_plane_adjoint(v, fy, gy, fz, gz):
    total = fy * up(v, 0) + gy * down(v, 0)
    return total + (fz * up(v, 1) + gz * down(v, 1))


def in_plane_forward(v, fy, gy, fz, gz):
    total = up(gy * v, 0) + down(fy * v, 0)
    return total + (up(gz * v, 1) + down(fz * v, 1))


def in_plane_couplings(u, d):
    first, last = z_ends(u.shape)
    fy = coupling(u, d, up(u, 0), up(d, 0))
    gy = coupling(u, d, down(u, 0), down(d, 0))
    fz = coupling(u, d, jnp.where(last, 0.0, up(u, 1)), jnp.where(last, 0.0, up(d, 1)))
    gz = coupling(
        u, d, jnp.where(first, 0.0, down(u, 1)), jnp.where(first, 0.0, down(d, 1))
    )
    return fy, gy, fz, gz


def pack_face_kernel(first_swap, conc, diff, source, slab):
    nx, ny, nz = conc.shape
    at_head = low_first("gx") if first_swap else ~low_first("gx")
    planes = [jnp.where(at_head, k, nx - 1 - k) for k in range(4)]
    u, d, s = ([ref[x] for x in planes] for ref in (conc, diff, source))
    first, last = z_ends((ny, nz))

    def between(i, j):
        return coupling(u[i], d[i], u[j], d[j])

    def image(i, before, after):
        fy, gy, fz, gz = in_plane_couplings(u[i], d[i])
        diagonal = 1.0 + ((fy + gy) + (fz + gz)) + (before + after)
        beside = (fy, gy, jnp.where(last, 0.0, fz), jnp.where(first, 0.0, gz))
        total = diagonal * s[i] - before * s[i - 1] - after * s[i + 1]
        return total - in_plane_adjoint(s[i], *beside), diagonal, beside

    back = between(1, 0)
    near, diagonal, beside = image(1, back, between(1, 2))
    inward = between(2, 1)
    far, _, _ = image(2, inward, between(2, 3))
    for k, v in enumerate((u[0], d[0], s[0], s[1], between(0, 1), back * near)):
        slab[k] = v
    slab[6] = diagonal * near - inward * far - in_plane_forward(near, *beside)


def pack_face(first_swap, conc, diff, source):
    return pl.pallas_call(
        functools.partial(pack_face_kernel, first_swap),
        out_shape=f32(FIELDS, *conc.shape[1:]),
        in_specs=[VMEM] * 3,
        out_specs=VMEM,
        compiler_params=params(),
        name="pack_face",
    )(conc, diff, source)


def own_kernel(
    conc, diff, source, yone, ytwo,
    u_s, d_s, s_s, fx, gx, fy, gy, fz, gz, dg, p1, cone, ctwo,
    slabs, mq_s,
):
    nx, ny, nz = conc.shape
    rows = ny + 2 * W
    flip_x, flip_y = low_first("gx"), low_first("gy")
    for k, (own, ref) in enumerate(((conc, u_s), (diff, d_s), (source, s_s))):
        ref[:, 0:ny, :] = own[...]
        ref[:, ny : ny + W, :] = jnp.where(flip_y, ytwo[k], yone[k])
        ref[:, ny + W :, :] = jnp.where(flip_y, yone[k], ytwo[k])
    first, last = z_ends((rows, nz))

    order = [q for k in range(nx // 2) for q in (k, nx - 1 - k)]
    for q in order:
        u, d = u_s[q], d_s[q]
        fyq, gyq, fzq, gzq = in_plane_couplings(u, d)
        total = 1.0 + ((fyq + gyq) + (fzq + gzq))
        if q + 1 < nx:
            fxq = coupling(u, d, u_s[q + 1], d_s[q + 1])
            fx[q] = fxq
            total = total + fxq
        if q > 0:
            gxq = coupling(u, d, u_s[q - 1], d_s[q - 1])
            gx[q] = gxq
            total = total + gxq
        dg[q] = total
        fy[q] = fyq
        gy[q] = gyq
        fz[q] = jnp.where(last, 0.0, fzq)
        gz[q] = jnp.where(first, 0.0, gzq)

    for q in order[2:]:
        v = s_s[q]
        total = dg[q] * v - fx[q] * s_s[q + 1] - gx[q] * s_s[q - 1]
        total = total - in_plane_adjoint(v, fy[q], gy[q], fz[q], gz[q])
        p1[q] = jnp.where(d_s[q] > 0.0, total, 0.0)

    for at, edge, inner, beyond in ((0, 0, 1, 2), (1, nx - 1, nx - 2, nx - 3)):
        toward, away = (fx, gx) if at == 0 else (gx, fx)
        v = p1[inner]
        m = away[inner] * v
        q = dg[inner] * v - away[beyond] * p1[beyond]
        q = q - in_plane_forward(v, fy[inner], gy[inner], fz[inner], gz[inner])
        mq_s[at, 0] = m
        mq_s[at, 1] = q
        kept = (
            u_s.at[edge], d_s.at[edge], s_s.at[edge], s_s.at[inner], toward.at[edge],
            mq_s.at[at, 0], mq_s.at[at, 1],
        )
        row = 0
        for field, begin, n in late_rows(ny):
            slabs[at, row : row + n] = kept[field][begin : begin + n, :]
            row += n
    cone[...] = jnp.where(flip_x, slabs[0], slabs[1])
    ctwo[...] = jnp.where(flip_x, slabs[1], slabs[0])


def own(conc, diff, source, yone, ytwo):
    nx, ny, nz = conc.shape
    late = f32(late_count(ny), nz)
    return pl.pallas_call(
        own_kernel,
        out_shape=(f32(nx, ny + 2 * W, nz),) * 11 + (late,) * 2,
        in_specs=[VMEM] * 5,
        out_specs=(VMEM,) * 13,
        scratch_shapes=[
            pltpu.VMEM((2, late_count(ny), nz), F32),
            pltpu.VMEM((2, 2, ny + 2 * W, nz), F32),
        ],
        compiler_params=params(),
        name="own",
    )(conc, diff, source, yone, ytwo)


def square(v, ny):
    mine = v[0:ny]
    return jnp.sum((mine * mine).reshape(ny // 8, 8, mine.shape[1]), axis=0)


def inside_kernel(d_s, s_s, fx, gx, fy, gy, fz, gz, dg, p1, p2, p3, part):
    nx, rows, nz = d_s.shape
    ny = rows - 2 * W
    sums = [jnp.zeros((8, nz), F32) for _ in range(4)]
    for q in range(nx):
        sums[0] = sums[0] + square(s_s[q], ny)
    for q in range(1, nx - 1):
        sums[1] = sums[1] + square(p1[q], ny)
    for q in range(2, nx - 2):
        v = p1[q]
        total = dg[q] * v - gx[q + 1] * p1[q + 1] - fx[q - 1] * p1[q - 1]
        total = total - in_plane_forward(v, fy[q], gy[q], fz[q], gz[q])
        total = jnp.where(d_s[q] > 0.0, total, 0.0)
        p2[q] = total
        sums[2] = sums[2] + square(total, ny)
    for q in range(3, nx - 3):
        v = p2[q]
        total = dg[q] * v - fx[q] * p2[q + 1] - gx[q] * p2[q - 1]
        total = total - in_plane_adjoint(v, fy[q], gy[q], fz[q], gz[q])
        total = jnp.where(d_s[q] > 0.0, total, 0.0)
        p3[q] = total
        sums[3] = sums[3] + square(total, ny)
    for k in range(4):
        part[k] = sums[k]


def inside(d_s, *fields):
    nx, rows, nz = d_s.shape
    return pl.pallas_call(
        inside_kernel,
        out_shape=(f32(nx, rows, nz),) * 2 + (f32(4, 8, nz),),
        in_specs=[VMEM] * 10,
        out_specs=(VMEM,) * 3,
        compiler_params=params(),
        cost_estimate=pl.CostEstimate(
            flops=1 << 22, bytes_accessed=1 << 23, transcendentals=0
        ),
        name="inside",
    )(d_s, *fields)


def finish_kernel(
    u_s, d_s, s_s, fx, gx, fy, gy, fz, gz, dg, p1_in, p2_in, p3_in, part,
    xone, xtwo, cone, ctwo,
    p1_out, p2_out, p3_out, p4_out, moments,
    side_s, edge_s, w_s,
):
    nx, rows, nz = d_s.shape
    ny = rows - 2 * W
    flip = low_first("gx")
    first, last = z_ends((rows, nz))

    for side, one in ((0, flip), (1, ~flip)):
        side_s[side, :, 0:ny] = jnp.where(one, xone[...], xtwo[...])
        side_s[side, :, ny:] = jnp.zeros((FIELDS, 2 * W, nz), F32)
        late = jnp.where(one, cone[...], ctwo[...])
        row = 0
        for field, begin, n in late_rows(ny):
            side_s[side, field, begin : begin + n] = late[row : row + n]
            row += n

    names = dict(
        u=u_s, d=d_s, s=s_s, fx=fx, gx=gx, fy=fy, gy=gy, fz=fz, gz=gz, dg=dg,
        p1=p1_in, p2=p2_in, p3=p3_in,
    )
    place = {(k, q): names[k].at[q] for k in names for q in range(nx)}
    spare = iter(range(w_s.shape[0]))

    def keep(name, q, value):
        place[name, q] = w_s.at[next(spare)]
        place[name, q][...] = value

    def get(name, q):
        return place[name, q][...]

    for side, (o, e, outward, inward) in enumerate(
        ((-1, 0, "gx", "fx"), (nx, nx - 1, "fx", "gx"))
    ):
        beyond = 2 * o - e
        for k, name in enumerate(("u", "d", "s")):
            place[name, o] = side_s.at[side, k]
        place["s", beyond] = side_s.at[side, 3]
        place[outward, o] = side_s.at[side, 4]
        place["m", o] = side_s.at[side, 5]
        place["q", o] = side_s.at[side, 6]
        u, d, ue, de = get("u", o), get("d", o), get("u", e), get("d", e)
        back = coupling(u, d, ue, de)
        out = coupling(ue, de, u, d)
        fyq, gyq, fzq, gzq = in_plane_couplings(u, d)
        total = 1.0 + get(outward, o) + back + ((fyq + gyq) + (fzq + gzq))
        new = {
            (inward, o): back,
            (outward, e): out,
            ("dg", o): total,
            ("dg", e): get("dg", e) + out,
            ("fy", o): fyq,
            ("gy", o): gyq,
            ("fz", o): jnp.where(last, 0.0, fzq),
            ("gz", o): jnp.where(first, 0.0, gzq),
        }
        for k, (key, value) in enumerate(new.items()):
            place[key] = edge_s.at[side, k]
            place[key][...] = value

    def masked(total, q):
        return jnp.where(get("d", q) > 0.0, total, 0.0)

    def in_plane(q):
        return [get(k, q) for k in ("fy", "gy", "fz", "gz")]

    def adjoint_at(w, q):
        v = get(w, q)
        total = get("dg", q) * v - get("fx", q) * get(w, q + 1)
        total = total - get("gx", q) * get(w, q - 1)
        return masked(total - in_plane_adjoint(v, *in_plane(q)), q)

    def forward_at(w, q):
        v = get(w, q)
        above = get("m", q) if q == nx else get("gx", q + 1) * get(w, q + 1)
        below = get("m", q) if q == -1 else get("fx", q - 1) * get(w, q - 1)
        total = get("dg", q) * v - above - below
        return masked(total - in_plane_forward(v, *in_plane(q)), q)

    sums = [part[k] for k in range(4)]

    def sweep(k, apply, w, name, out, ready):
        for q in range(-1, nx + 1):
            if ready <= q < nx - ready:
                out[q] = get(name, q)[0:ny]
                continue
            value = apply(w, q)
            keep(name, q, value)
            if 0 <= q < nx:
                out[q] = value[0:ny]
                sums[k] = sums[k] + square(value, ny)

    sweep(1, adjoint_at, "s", "p1", p1_out, 1)
    sweep(2, forward_at, "p1", "p2", p2_out, 2)
    for o, outward in ((-1, "gx"), (nx, "fx")):
        beyond = -2 if o == -1 else nx + 1
        keep("p2", beyond, get("q", o) - get(outward, o) * get("p1", o))
    sweep(3, adjoint_at, "p2", "p3", p3_out, 3)
    for q in range(nx):
        p4_out[q] = forward_at("p3", q)[0:ny]

    slot = lax.broadcasted_iota(jnp.int32, (1, LANES), 1)
    row = jnp.zeros((1, LANES), F32)
    for k in range(4):
        row = jnp.where(slot == k, jnp.sum(sums[k]), row)
    moments[...] = jnp.broadcast_to(row, moments.shape)


def finish(copies, ny, *fields):
    nx, rows, nz = fields[0].shape
    steps = 4 + 6 + 2 + 8
    return pl.pallas_call(
        finish_kernel,
        out_shape=(f32(nx, ny, nz),) * 4 + (f32(copies, 1, LANES),),
        in_specs=[VMEM] * len(fields),
        out_specs=(VMEM,) * 5,
        scratch_shapes=[
            pltpu.VMEM((2, FIELDS, rows, nz), F32),
            pltpu.VMEM((2, 8, rows, nz), F32),
            pltpu.VMEM((steps, rows, nz), F32),
        ],
        compiler_params=params(),
        name="finish",
    )(*fields)


def combine_kernel(moments, source, p1, p2, p3, p4, adjoint, residual):
    m = jnp.sum(moments[...], axis=0)
    m0, m1, m2, m3 = (m[:, k : k + 1] for k in range(4))
    alpha = m0 / m1
    beta = alpha * (m2 / m1) - 1.0
    grow = 1.0 + beta
    image = grow * grow * m1 - 2.0 * grow * alpha * m2 + alpha * alpha * m3
    step = (beta * m0) / image
    near = alpha + step * grow
    far = step * alpha
    adjoint[...] = near[None] * p1[...] - far[None] * p3[...]
    residual[...] = source[...] - near[None] * p2[...] + far[None] * p4[...]


def combine(moments, source, p1, p2, p3, p4):
    return pl.pallas_call(
        combine_kernel,
        out_shape=(f32(*source.shape),) * 2,
        in_specs=[VMEM] * 6,
        out_specs=(VMEM,) * 2,
        compiler_params=params(),
        name="combine",
    )(moments, source, p1, p2, p3, p4)


def swap(cells, axis, first):
    pairs = [(i, i + 1) for i in range(first, lax.axis_size(axis) - 1, 2)]
    return lax.ppermute(cells, axis, pairs + [(j, i) for i, j in pairs])


def local(conc, labels, kappa, source):
    ny = conc.shape[1]
    conc, source, diff = pack(conc, labels, kappa, source)
    xone = swap(pack_face(True, conc, diff, source), "gx", 1)
    xtwo = swap(pack_face(False, conc, diff, source), "gx", 0)
    yone, ytwo = pack_rows(conc, diff, source)
    yone = swap(yone, "gy", 1)
    ytwo = swap(ytwo, "gy", 0)
    *fields, cone, ctwo = own(conc, diff, source, yone, ytwo)
    cone = swap(cone, "gx", 1)
    ctwo = swap(ctwo, "gx", 0)
    inner = inside(*fields[1:])
    p1, p2, p3, p4, moments = finish(
        lax.axis_size(("gx", "gy")), ny, *fields, *inner, xone, xtwo, cone, ctwo
    )
    moments = lax.all_to_all(moments, ("gx", "gy"), 0, 0, tiled=True)
    return combine(moments, source, p1, p2, p3, p4)


def solution(mesh):
    return jax.shard_map(
        local,
        mesh=mesh,
        in_specs=(P("gx", "gy", None), P("gx", "gy", None), P(), P("gx", "gy", None)),
        out_specs=(P("gx", "gy", None), P("gx", "gy", None)),
        check_vma=False,
    )
```

```python
import functools

import jax
import jax.numpy as jnp
from jax import lax
from jax.experimental import pallas as pl
from jax.experimental.pallas import tpu as pltpu
from jax.sharding import PartitionSpec as P

ITERS = 2
DT = 0.5
W = 2 * ITERS
F32 = jnp.float32
LANES = 128
TILE = 8
VMEM = pl.BlockSpec(memory_space=pltpu.VMEM)


def low_first(axis):
    return lax.axis_index(axis) % 2 == 0


def up(v, axis):
    return pltpu.roll(v, v.shape[axis] - 1, axis)


def down(v, axis):
    return pltpu.roll(v, 1, axis)


def z_ends(shape):
    index = lax.broadcasted_iota(jnp.int32, shape, 1)
    return index == 0, index == shape[1] - 1


def coupling(u, d, un, dn):
    return d + d * u - d * un + dn


def params(megabytes=16):
    return pltpu.CompilerParams(vmem_limit_bytes=megabytes << 20)


def f32(*shape):
    return jax.ShapeDtypeStruct(shape, F32)


FIELDS = 7


def late_rows(ny):
    rows = ny + 2 * W
    for field, n in ((0, 3), (1, 3), (2, 3), (3, 2), (4, 2), (5, 1)):
        yield field, ny, n
        yield field, rows - n, n
    for field, n in ((5, 1), (6, 2)):
        yield field, 0, n
        yield field, ny - n, n


def late_count(ny):
    return sum(n for _, _, n in late_rows(ny))


def pack_kernel(
    kappa_in, conc_in, labels_in, source_in,
    conc, source, diff,
    labels, kappa, sems,
):
    nx, ny, nz = conc.shape
    copies = [
        pltpu.make_async_copy(src, dst, sems.at[k])
        for k, (src, dst) in enumerate(
            (
                (kappa_in, kappa),
                (labels_in, labels),
                (conc_in, conc),
                (source_in, source),
            )
        )
    ]
    for copy in copies:
        copy.start()
    for copy in copies:
        copy.wait()
    k0, k1, k2 = ((0.5 * DT) * kappa[k] for k in range(3))

    def body(x, carry):
        lab = labels[x]
        base = jnp.where(lab == 0, k0, jnp.where(lab == 1, k1, k2))
        diff[x] = base * jnp.exp(conc[x])
        return carry

    lax.fori_loop(0, nx, body, 0, unroll=True)


def pack(conc, labels, kappa, source):
    nx, ny, nz = conc.shape
    outside = [
        pltpu.with_memory_space_constraint(v, pltpu.HBM)
        for v in (kappa, conc, labels, source)
    ]
    return pl.pallas_call(
        pack_kernel,
        out_shape=(f32(nx, ny, nz),) * 3,
        in_specs=[pl.BlockSpec(memory_space=pltpu.HBM)] * 4,
        out_specs=(VMEM,) * 3,
        scratch_shapes=[
            pltpu.VMEM((nx, ny, nz), jnp.int32),
            pltpu.SMEM((3,), F32),
            pltpu.SemaphoreType.DMA((4,)),
        ],
        compiler_params=params(),
        name="pack",
    )(*outside)


def pack_rows_kernel(conc, diff, source, yone, ytwo):
    ny = conc.shape[1]
    flip = low_first("gy")
    for k, ref in enumerate((conc, diff, source)):
        yone[k] = jnp.where(flip, ref[:, 0:TILE, :], ref[:, ny - TILE : ny, :])
        ytwo[k] = jnp.where(flip, ref[:, ny - W : ny, :], ref[:, 0:W, :])


def pack_rows(conc, diff, source):
    nx, ny, nz = conc.shape
    return pl.pallas_call(
        pack_rows_kernel,
        out_shape=(f32(3, nx, TILE, nz), f32(3, nx, W, nz)),
        in_specs=[VMEM] * 3,
        out_specs=(VMEM,) * 2,
        compiler_params=params(),
        name="pack_rows",
    )(conc, diff, source)


def rows_beside(yone, ytwo, k, x):
    flip = low_first("gy")
    below = jnp.where(flip, yone[k, x, TILE - W :], ytwo[k, x])
    return below, jnp.where(flip, ytwo[k, x], yone[k, x, 0:W])


def in_plane_adjoint(v, fy, gy, fz, gz):
    total = fy * up(v, 0) + gy * down(v, 0)
    return total + (fz * up(v, 1) + gz * down(v, 1))


def in_plane_forward(v, fy, gy, fz, gz):
    total = up(gy * v, 0) + down(fy * v, 0)
    return total + (up(gz * v, 1) + down(fz * v, 1))


def in_plane_couplings(u, d):
    first, last = z_ends(u.shape)
    fy = coupling(u, d, up(u, 0), up(d, 0))
    gy = coupling(u, d, down(u, 0), down(d, 0))
    fz = coupling(u, d, jnp.where(last, 0.0, up(u, 1)), jnp.where(last, 0.0, up(d, 1)))
    gz = coupling(
        u, d, jnp.where(first, 0.0, down(u, 1)), jnp.where(first, 0.0, down(d, 1))
    )
    return fy, gy, fz, gz


def face_planes(first_swap, nx):
    at_head = low_first("gx") if first_swap else ~low_first("gx")
    return [jnp.where(at_head, k, nx - 1 - k) for k in range(4)]


def face_fields(u, d, s):
    first, last = z_ends(u[0].shape)

    def between(i, j):
        return coupling(u[i], d[i], u[j], d[j])

    def image(i, before, after):
        fy, gy, fz, gz = in_plane_couplings(u[i], d[i])
        diagonal = 1.0 + ((fy + gy) + (fz + gz)) + (before + after)
        beside = (fy, gy, jnp.where(last, 0.0, fz), jnp.where(first, 0.0, gz))
        total = diagonal * s[i] - before * s[i - 1] - after * s[i + 1]
        total = total - in_plane_adjoint(s[i], *beside)
        return jnp.where(d[i] > 0.0, total, 0.0), diagonal, beside

    back, inward = between(1, 0), between(2, 1)
    near, diagonal, beside = image(1, back, between(1, 2))
    far, _, _ = image(2, inward, between(2, 3))
    rest = diagonal * near - inward * far - in_plane_forward(near, *beside)
    return u[0], d[0], s[0], s[1], between(0, 1), back * near, rest


def pack_face_kernel(first_swap, conc, diff, source, slab):
    planes = face_planes(first_swap, conc.shape[0])
    u, d, s = ([ref[x] for x in planes] for ref in (conc, diff, source))
    for k, v in enumerate(face_fields(u, d, s)):
        slab[k] = v


def pack_face(first_swap, conc, diff, source):
    return pl.pallas_call(
        functools.partial(pack_face_kernel, first_swap),
        out_shape=f32(FIELDS, *conc.shape[1:]),
        in_specs=[VMEM] * 3,
        out_specs=VMEM,
        compiler_params=params(),
        name="pack_face",
    )(conc, diff, source)


def pack_late_kernel(conc, diff, source, yone, ytwo, cone, ctwo, near_s, out_s):
    nx, ny, nz = conc.shape
    rows = ny + 2 * W

    def narrow(row):
        if row < ny:
            return row + W if row < W else row - ny + 3 * W
        return row - ny + 3 * W if row < ny + W else row - ny - W

    for first_swap, late in ((True, cone), (False, ctwo)):
        for j, x in enumerate(face_planes(first_swap, nx)):
            for k, ref in enumerate((conc, diff, source)):
                below, above = rows_beside(yone, ytwo, k, x)
                near_s[k, j, 0:W] = below
                near_s[k, j, W : 2 * W] = ref[x, 0:W]
                near_s[k, j, 2 * W : 3 * W] = ref[x, ny - W : ny]
                near_s[k, j, 3 * W :] = above
        fields = face_fields(*([near_s[k, j] for j in range(4)] for k in range(3)))
        for k, v in enumerate(fields):
            out_s[k] = v
        row = 0
        for k, begin, n in late_rows(ny):
            at = narrow(begin)
            late[row : row + n] = out_s[k, at : at + n]
            row += n


def pack_late(conc, diff, source, yone, ytwo):
    nx, ny, nz = conc.shape
    return pl.pallas_call(
        pack_late_kernel,
        out_shape=(f32(late_count(ny), nz),) * 2,
        in_specs=[VMEM] * 5,
        out_specs=(VMEM,) * 2,
        scratch_shapes=[
            pltpu.VMEM((3, 4, 4 * W, nz), F32),
            pltpu.VMEM((FIELDS, 4 * W, nz), F32),
        ],
        compiler_params=params(),
        name="pack_late",
    )(conc, diff, source, yone, ytwo)


def own_kernel(
    conc, diff, source, yone, ytwo,
    u_s, d_s, s_s, fx, gx, fy, gy, fz, gz, dg, p1,
):
    nx, ny, nz = conc.shape
    rows = ny + 2 * W
    for k, (own, ref) in enumerate(((conc, u_s), (diff, d_s), (source, s_s))):
        below, above = rows_beside(yone, ytwo, k, slice(0, nx))
        ref[:, 0:ny, :] = own[...]
        ref[:, ny : ny + W, :] = above
        ref[:, ny + W :, :] = below
    first, last = z_ends((rows, nz))

    for q in range(nx):
        u, d = u_s[q], d_s[q]
        fyq, gyq, fzq, gzq = in_plane_couplings(u, d)
        total = 1.0 + ((fyq + gyq) + (fzq + gzq))
        if q + 1 < nx:
            fxq = coupling(u, d, u_s[q + 1], d_s[q + 1])
            fx[q] = fxq
            total = total + fxq
        if q > 0:
            gxq = coupling(u, d, u_s[q - 1], d_s[q - 1])
            gx[q] = gxq
            total = total + gxq
        dg[q] = total
        fy[q] = fyq
        gy[q] = gyq
        fz[q] = jnp.where(last, 0.0, fzq)
        gz[q] = jnp.where(first, 0.0, gzq)

    for q in range(1, nx - 1):
        v = s_s[q]
        total = dg[q] * v - fx[q] * s_s[q + 1] - gx[q] * s_s[q - 1]
        total = total - in_plane_adjoint(v, fy[q], gy[q], fz[q], gz[q])
        p1[q] = jnp.where(d_s[q] > 0.0, total, 0.0)


def own(conc, diff, source, yone, ytwo):
    nx, ny, nz = conc.shape
    return pl.pallas_call(
        own_kernel,
        out_shape=(f32(nx, ny + 2 * W, nz),) * 11,
        in_specs=[VMEM] * 5,
        out_specs=(VMEM,) * 11,
        compiler_params=params(),
        name="own",
    )(conc, diff, source, yone, ytwo)


def square(v, ny):
    mine = v[0:ny]
    return jnp.sum((mine * mine).reshape(ny // 8, 8, mine.shape[1]), axis=0)


def inside_kernel(d_s, s_s, fx, gx, fy, gy, fz, gz, dg, p1, p2, p3, part):
    nx, rows, nz = d_s.shape
    ny = rows - 2 * W
    sums = [jnp.zeros((8, nz), F32) for _ in range(4)]
    for q in range(nx):
        sums[0] = sums[0] + square(s_s[q], ny)
    for q in range(1, nx - 1):
        sums[1] = sums[1] + square(p1[q], ny)
    for q in range(2, nx - 2):
        v = p1[q]
        total = dg[q] * v - gx[q + 1] * p1[q + 1] - fx[q - 1] * p1[q - 1]
        total = total - in_plane_forward(v, fy[q], gy[q], fz[q], gz[q])
        total = jnp.where(d_s[q] > 0.0, total, 0.0)
        p2[q] = total
        sums[2] = sums[2] + square(total, ny)
    for q in range(3, nx - 3):
        v = p2[q]
        total = dg[q] * v - fx[q] * p2[q + 1] - gx[q] * p2[q - 1]
        total = total - in_plane_adjoint(v, fy[q], gy[q], fz[q], gz[q])
        total = jnp.where(d_s[q] > 0.0, total, 0.0)
        p3[q] = total
        sums[3] = sums[3] + square(total, ny)
    for k in range(4):
        part[k] = sums[k]


def inside(d_s, *fields):
    nx, rows, nz = d_s.shape
    return pl.pallas_call(
        inside_kernel,
        out_shape=(f32(nx, rows, nz),) * 2 + (f32(4, 8, nz),),
        in_specs=[VMEM] * 10,
        out_specs=(VMEM,) * 3,
        compiler_params=params(),
        cost_estimate=pl.CostEstimate(
            flops=1 << 22, bytes_accessed=1 << 23, transcendentals=0
        ),
        name="inside",
    )(d_s, *fields)


def finish_kernel(
    u_s, d_s, s_s, fx, gx, fy, gy, fz, gz, dg, p1_in, p2_in, p3_in, part,
    xone, xtwo, cone, ctwo,
    p1_out, p2_out, p3_out, p4_out, moments,
    side_s, edge_s, w_s,
):
    nx, rows, nz = d_s.shape
    ny = rows - 2 * W
    flip = low_first("gx")
    first, last = z_ends((rows, nz))

    for side, one in ((0, flip), (1, ~flip)):
        side_s[side, :, 0:ny] = jnp.where(one, xone[...], xtwo[...])
        side_s[side, :, ny:] = jnp.zeros((FIELDS, 2 * W, nz), F32)
        late = jnp.where(one, cone[...], ctwo[...])
        row = 0
        for field, begin, n in late_rows(ny):
            side_s[side, field, begin : begin + n] = late[row : row + n]
            row += n

    names = dict(
        u=u_s, d=d_s, s=s_s, fx=fx, gx=gx, fy=fy, gy=gy, fz=fz, gz=gz, dg=dg,
        p1=p1_in, p2=p2_in, p3=p3_in,
    )
    place = {(k, q): names[k].at[q] for k in names for q in range(nx)}
    spare = iter(range(w_s.shape[0]))

    def keep(name, q, value):
        place[name, q] = w_s.at[next(spare)]
        place[name, q][...] = value

    def get(name, q):
        return place[name, q][...]

    for side, (o, e, outward, inward) in enumerate(
        ((-1, 0, "gx", "fx"), (nx, nx - 1, "fx", "gx"))
    ):
        beyond = 2 * o - e
        for k, name in enumerate(("u", "d", "s")):
            place[name, o] = side_s.at[side, k]
        place["s", beyond] = side_s.at[side, 3]
        place[outward, o] = side_s.at[side, 4]
        place["m", o] = side_s.at[side, 5]
        place["q", o] = side_s.at[side, 6]
        u, d, ue, de = get("u", o), get("d", o), get("u", e), get("d", e)
        back = coupling(u, d, ue, de)
        out = coupling(ue, de, u, d)
        fyq, gyq, fzq, gzq = in_plane_couplings(u, d)
        total = 1.0 + get(outward, o) + back + ((fyq + gyq) + (fzq + gzq))
        new = {
            (inward, o): back,
            (outward, e): out,
            ("dg", o): total,
            ("dg", e): get("dg", e) + out,
            ("fy", o): fyq,
            ("gy", o): gyq,
            ("fz", o): jnp.where(last, 0.0, fzq),
            ("gz", o): jnp.where(first, 0.0, gzq),
        }
        for k, (key, value) in enumerate(new.items()):
            place[key] = edge_s.at[side, k]
            place[key][...] = value

    def masked(total, q):
        return jnp.where(get("d", q) > 0.0, total, 0.0)

    def in_plane(q):
        return [get(k, q) for k in ("fy", "gy", "fz", "gz")]

    def adjoint_at(w, q):
        v = get(w, q)
        total = get("dg", q) * v - get("fx", q) * get(w, q + 1)
        total = total - get("gx", q) * get(w, q - 1)
        return masked(total - in_plane_adjoint(v, *in_plane(q)), q)

    def forward_at(w, q):
        v = get(w, q)
        above = get("m", q) if q == nx else get("gx", q + 1) * get(w, q + 1)
        below = get("m", q) if q == -1 else get("fx", q - 1) * get(w, q - 1)
        total = get("dg", q) * v - above - below
        return masked(total - in_plane_forward(v, *in_plane(q)), q)

    sums = [part[k] for k in range(4)]

    def sweep(k, apply, w, name, out, ready):
        for q in range(-1, nx + 1):
            if ready <= q < nx - ready:
                out[q] = get(name, q)[0:ny]
                continue
            value = apply(w, q)
            keep(name, q, value)
            if 0 <= q < nx:
                out[q] = value[0:ny]
                sums[k] = sums[k] + square(value, ny)

    sweep(1, adjoint_at, "s", "p1", p1_out, 1)
    sweep(2, forward_at, "p1", "p2", p2_out, 2)
    for o, outward in ((-1, "gx"), (nx, "fx")):
        beyond = -2 if o == -1 else nx + 1
        keep("p2", beyond, get("q", o) - get(outward, o) * get("p1", o))
    sweep(3, adjoint_at, "p2", "p3", p3_out, 3)
    for q in range(nx):
        p4_out[q] = forward_at("p3", q)[0:ny]

    slot = lax.broadcasted_iota(jnp.int32, (1, LANES), 1)
    row = jnp.zeros((1, LANES), F32)
    for k in range(4):
        row = jnp.where(slot == k, jnp.sum(sums[k]), row)
    moments[...] = jnp.broadcast_to(row, moments.shape)


def finish(copies, ny, *fields):
    nx, rows, nz = fields[0].shape
    steps = 4 + 6 + 2 + 8
    return pl.pallas_call(
        finish_kernel,
        out_shape=(f32(nx, ny, nz),) * 4 + (f32(copies, 1, LANES),),
        in_specs=[VMEM] * len(fields),
        out_specs=(VMEM,) * 5,
        scratch_shapes=[
            pltpu.VMEM((2, FIELDS, rows, nz), F32),
            pltpu.VMEM((2, 8, rows, nz), F32),
            pltpu.VMEM((steps, rows, nz), F32),
        ],
        compiler_params=params(),
        name="finish",
    )(*fields)


def combine_kernel(moments, source, p1, p2, p3, p4, adjoint, residual):
    m = jnp.sum(moments[...], axis=0)
    m0, m1, m2, m3 = (m[:, k : k + 1] for k in range(4))
    alpha = m0 / m1
    beta = alpha * (m2 / m1) - 1.0
    grow = 1.0 + beta
    image = grow * grow * m1 - 2.0 * grow * alpha * m2 + alpha * alpha * m3
    step = (beta * m0) / image
    near = alpha + step * grow
    far = step * alpha
    adjoint[...] = near[None] * p1[...] - far[None] * p3[...]
    residual[...] = source[...] - near[None] * p2[...] + far[None] * p4[...]


def combine(moments, source, p1, p2, p3, p4):
    return pl.pallas_call(
        combine_kernel,
        out_shape=(f32(*source.shape),) * 2,
        in_specs=[VMEM] * 6,
        out_specs=(VMEM,) * 2,
        compiler_params=params(),
        name="combine",
    )(moments, source, p1, p2, p3, p4)


def swap(cells, axis, first):
    pairs = [(i, i + 1) for i in range(first, lax.axis_size(axis) - 1, 2)]
    return lax.ppermute(cells, axis, pairs + [(j, i) for i, j in pairs])


def local(conc, labels, kappa, source):
    ny = conc.shape[1]
    conc, source, diff = pack(conc, labels, kappa, source)
    xone = swap(pack_face(True, conc, diff, source), "gx", 1)
    xtwo = swap(pack_face(False, conc, diff, source), "gx", 0)
    yone, ytwo = pack_rows(conc, diff, source)
    yone = swap(yone, "gy", 1)
    ytwo = swap(ytwo, "gy", 0)
    cone, ctwo = pack_late(conc, diff, source, yone, ytwo)
    cone = swap(cone, "gx", 1)
    ctwo = swap(ctwo, "gx", 0)
    fields = own(conc, diff, source, yone, ytwo)
    inner = inside(*fields[1:])
    p1, p2, p3, p4, moments = finish(
        lax.axis_size(("gx", "gy")), ny, *fields, *inner, xone, xtwo, cone, ctwo
    )
    moments = lax.all_to_all(moments, ("gx", "gy"), 0, 0, tiled=True)
    return combine(moments, source, p1, p2, p3, p4)


def solution(mesh):
    return jax.shard_map(
        local,
        mesh=mesh,
        in_specs=(P("gx", "gy", None), P("gx", "gy", None), P(), P("gx", "gy", None)),
        out_specs=(P("gx", "gy", None), P("gx", "gy", None)),
        check_vma=False,
    )
```

```python
import functools

import jax
import jax.numpy as jnp
from jax import lax
from jax.experimental import pallas as pl
from jax.experimental.pallas import tpu as pltpu
from jax.sharding import PartitionSpec as P

ITERS = 2
DT = 0.5
W = 2 * ITERS
F32 = jnp.float32
LANES = 128
TILE = 8
VMEM = pl.BlockSpec(memory_space=pltpu.VMEM)


def low_first(axis):
    return lax.axis_index(axis) % 2 == 0


def up(v, axis):
    return pltpu.roll(v, v.shape[axis] - 1, axis)


def down(v, axis):
    return pltpu.roll(v, 1, axis)


def z_ends(shape):
    index = lax.broadcasted_iota(jnp.int32, shape, 1)
    return index == 0, index == shape[1] - 1


def coupling(u, d, un, dn):
    return d + d * u - d * un + dn


def params(megabytes=16):
    return pltpu.CompilerParams(vmem_limit_bytes=megabytes << 20)


def f32(*shape):
    return jax.ShapeDtypeStruct(shape, F32)


FIELDS = 7


def late_rows(ny):
    rows = ny + 2 * W
    for field, n in ((0, 3), (1, 3), (2, 3), (3, 2), (4, 2), (5, 1)):
        yield field, ny, n
        yield field, rows - n, n
    for field, n in ((5, 1), (6, 2)):
        yield field, 0, n
        yield field, ny - n, n


def late_count(ny):
    return sum(n for _, _, n in late_rows(ny))


def pack_kernel(
    kappa_in, conc_in, labels_in, source_in,
    conc, source, diff,
    labels, kappa, sems,
):
    nx, ny, nz = conc.shape
    copies = [
        pltpu.make_async_copy(src, dst, sems.at[k])
        for k, (src, dst) in enumerate(
            (
                (kappa_in, kappa),
                (labels_in, labels),
                (conc_in, conc),
                (source_in, source),
            )
        )
    ]
    for copy in copies:
        copy.start()
    for copy in copies:
        copy.wait()
    k0, k1, k2 = ((0.5 * DT) * kappa[k] for k in range(3))

    def body(x, carry):
        lab = labels[x]
        base = jnp.where(lab == 0, k0, jnp.where(lab == 1, k1, k2))
        diff[x] = base * jnp.exp(conc[x])
        return carry

    lax.fori_loop(0, nx, body, 0, unroll=True)


def pack(conc, labels, kappa, source):
    nx, ny, nz = conc.shape
    outside = [
        pltpu.with_memory_space_constraint(v, pltpu.HBM)
        for v in (kappa, conc, labels, source)
    ]
    return pl.pallas_call(
        pack_kernel,
        out_shape=(f32(nx, ny, nz),) * 3,
        in_specs=[pl.BlockSpec(memory_space=pltpu.HBM)] * 4,
        out_specs=(VMEM,) * 3,
        scratch_shapes=[
            pltpu.VMEM((nx, ny, nz), jnp.int32),
            pltpu.SMEM((3,), F32),
            pltpu.SemaphoreType.DMA((4,)),
        ],
        compiler_params=params(),
        name="pack",
    )(*outside)


def pack_rows_kernel(conc, diff, source, yone, ytwo):
    ny = conc.shape[1]
    flip = low_first("gy")
    for k, ref in enumerate((conc, diff, source)):
        yone[k] = jnp.where(flip, ref[:, 0:TILE, :], ref[:, ny - TILE : ny, :])
        ytwo[k] = jnp.where(flip, ref[:, ny - W : ny, :], ref[:, 0:W, :])


def pack_rows(conc, diff, source):
    nx, ny, nz = conc.shape
    return pl.pallas_call(
        pack_rows_kernel,
        out_shape=(f32(3, nx, TILE, nz), f32(3, nx, W, nz)),
        in_specs=[VMEM] * 3,
        out_specs=(VMEM,) * 2,
        compiler_params=params(),
        name="pack_rows",
    )(conc, diff, source)


def rows_beside(yone, ytwo, k, x):
    flip = low_first("gy")
    below = jnp.where(flip, yone[k, x, TILE - W :], ytwo[k, x])
    return below, jnp.where(flip, ytwo[k, x], yone[k, x, 0:W])


def in_plane_adjoint(v, fy, gy, fz, gz):
    total = fy * up(v, 0) + gy * down(v, 0)
    return total + (fz * up(v, 1) + gz * down(v, 1))


def in_plane_forward(v, fy, gy, fz, gz):
    total = up(gy * v, 0) + down(fy * v, 0)
    return total + (up(gz * v, 1) + down(fz * v, 1))


def in_plane_couplings(u, d):
    first, last = z_ends(u.shape)
    fy = coupling(u, d, up(u, 0), up(d, 0))
    gy = coupling(u, d, down(u, 0), down(d, 0))
    fz = coupling(u, d, jnp.where(last, 0.0, up(u, 1)), jnp.where(last, 0.0, up(d, 1)))
    gz = coupling(
        u, d, jnp.where(first, 0.0, down(u, 1)), jnp.where(first, 0.0, down(d, 1))
    )
    return fy, gy, fz, gz


def face_planes(first_swap, nx):
    at_head = low_first("gx") if first_swap else ~low_first("gx")
    return [jnp.where(at_head, k, nx - 1 - k) for k in range(4)]


def face_fields(u, d, s):
    first, last = z_ends(u[0].shape)

    def between(i, j):
        return coupling(u[i], d[i], u[j], d[j])

    def image(i, before, after):
        fy, gy, fz, gz = in_plane_couplings(u[i], d[i])
        diagonal = 1.0 + ((fy + gy) + (fz + gz)) + (before + after)
        beside = (fy, gy, jnp.where(last, 0.0, fz), jnp.where(first, 0.0, gz))
        total = diagonal * s[i] - before * s[i - 1] - after * s[i + 1]
        total = total - in_plane_adjoint(s[i], *beside)
        return jnp.where(d[i] > 0.0, total, 0.0), diagonal, beside

    back, inward = between(1, 0), between(2, 1)
    near, diagonal, beside = image(1, back, between(1, 2))
    far, _, _ = image(2, inward, between(2, 3))
    rest = diagonal * near - inward * far - in_plane_forward(near, *beside)
    return u[0], d[0], s[0], s[1], between(0, 1), back * near, rest


def pack_face_kernel(first_swap, conc, diff, source, slab):
    planes = face_planes(first_swap, conc.shape[0])
    u, d, s = ([ref[x] for x in planes] for ref in (conc, diff, source))
    for k, v in enumerate(face_fields(u, d, s)):
        slab[k] = v


def pack_face(first_swap, conc, diff, source):
    return pl.pallas_call(
        functools.partial(pack_face_kernel, first_swap),
        out_shape=f32(FIELDS, *conc.shape[1:]),
        in_specs=[VMEM] * 3,
        out_specs=VMEM,
        compiler_params=params(),
        name="pack_face",
    )(conc, diff, source)


def pack_late_kernel(conc, diff, source, yone, ytwo, cone, ctwo, near_s, out_s):
    nx, ny, nz = conc.shape
    rows = ny + 2 * W

    def narrow(row):
        if row < ny:
            return row + W if row < W else row - ny + 3 * W
        return row - ny + 3 * W if row < ny + W else row - ny - W

    for first_swap, late in ((True, cone), (False, ctwo)):
        for j, x in enumerate(face_planes(first_swap, nx)):
            for k, ref in enumerate((conc, diff, source)):
                below, above = rows_beside(yone, ytwo, k, x)
                near_s[k, j, 0:W] = below
                near_s[k, j, W : 2 * W] = ref[x, 0:W]
                near_s[k, j, 2 * W : 3 * W] = ref[x, ny - W : ny]
                near_s[k, j, 3 * W :] = above
        fields = face_fields(*([near_s[k, j] for j in range(4)] for k in range(3)))
        for k, v in enumerate(fields):
            out_s[k] = v
        row = 0
        for k, begin, n in late_rows(ny):
            at = narrow(begin)
            late[row : row + n] = out_s[k, at : at + n]
            row += n


def pack_late(conc, diff, source, yone, ytwo):
    nx, ny, nz = conc.shape
    return pl.pallas_call(
        pack_late_kernel,
        out_shape=(f32(late_count(ny), nz),) * 2,
        in_specs=[VMEM] * 5,
        out_specs=(VMEM,) * 2,
        scratch_shapes=[
            pltpu.VMEM((3, 4, 4 * W, nz), F32),
            pltpu.VMEM((FIELDS, 4 * W, nz), F32),
        ],
        compiler_params=params(),
        name="pack_late",
    )(conc, diff, source, yone, ytwo)


def own_kernel(
    conc, diff, source, yone, ytwo,
    u_s, d_s, s_s, fx, gx, fy, gy, fz, gz, dg, p1,
):
    nx, ny, nz = conc.shape
    rows = ny + 2 * W
    for k, (own, ref) in enumerate(((conc, u_s), (diff, d_s), (source, s_s))):
        below, above = rows_beside(yone, ytwo, k, slice(0, nx))
        ref[:, 0:ny, :] = own[...]
        ref[:, ny : ny + W, :] = above
        ref[:, ny + W :, :] = below
    first, last = z_ends((rows, nz))

    for q in range(nx):
        u, d = u_s[q], d_s[q]
        fyq, gyq, fzq, gzq = in_plane_couplings(u, d)
        total = 1.0 + ((fyq + gyq) + (fzq + gzq))
        if q + 1 < nx:
            fxq = coupling(u, d, u_s[q + 1], d_s[q + 1])
            fx[q] = fxq
            total = total + fxq
        if q > 0:
            gxq = coupling(u, d, u_s[q - 1], d_s[q - 1])
            gx[q] = gxq
            total = total + gxq
        dg[q] = total
        fy[q] = fyq
        gy[q] = gyq
        fz[q] = jnp.where(last, 0.0, fzq)
        gz[q] = jnp.where(first, 0.0, gzq)

    for q in range(1, nx - 1):
        v = s_s[q]
        total = dg[q] * v - fx[q] * s_s[q + 1] - gx[q] * s_s[q - 1]
        total = total - in_plane_adjoint(v, fy[q], gy[q], fz[q], gz[q])
        p1[q] = jnp.where(d_s[q] > 0.0, total, 0.0)


def own(conc, diff, source, yone, ytwo):
    nx, ny, nz = conc.shape
    return pl.pallas_call(
        own_kernel,
        out_shape=(f32(nx, ny + 2 * W, nz),) * 11,
        in_specs=[VMEM] * 5,
        out_specs=(VMEM,) * 11,
        compiler_params=params(),
        name="own",
    )(conc, diff, source, yone, ytwo)


def square(v, ny):
    mine = v[0:ny]
    return jnp.sum((mine * mine).reshape(ny // 8, 8, mine.shape[1]), axis=0)


def inside_kernel(d_s, s_s, fx, gx, fy, gy, fz, gz, dg, p1, p2, p3, part):
    nx, rows, nz = d_s.shape
    ny = rows - 2 * W
    sums = [jnp.zeros((8, nz), F32) for _ in range(4)]
    for q in range(nx):
        sums[0] = sums[0] + square(s_s[q], ny)
    for q in range(1, nx - 1):
        sums[1] = sums[1] + square(p1[q], ny)
    for q in range(2, nx - 2):
        v = p1[q]
        total = dg[q] * v - gx[q + 1] * p1[q + 1] - fx[q - 1] * p1[q - 1]
        total = total - in_plane_forward(v, fy[q], gy[q], fz[q], gz[q])
        total = jnp.where(d_s[q] > 0.0, total, 0.0)
        p2[q] = total
        sums[2] = sums[2] + square(total, ny)
    for q in range(3, nx - 3):
        v = p2[q]
        total = dg[q] * v - fx[q] * p2[q + 1] - gx[q] * p2[q - 1]
        total = total - in_plane_adjoint(v, fy[q], gy[q], fz[q], gz[q])
        total = jnp.where(d_s[q] > 0.0, total, 0.0)
        p3[q] = total
        sums[3] = sums[3] + square(total, ny)
    for k in range(4):
        part[k] = sums[k]


def inside(d_s, *fields):
    nx, rows, nz = d_s.shape
    return pl.pallas_call(
        inside_kernel,
        out_shape=(f32(nx, rows, nz),) * 2 + (f32(4, 8, nz),),
        in_specs=[VMEM] * 10,
        out_specs=(VMEM,) * 3,
        compiler_params=params(),
        cost_estimate=pl.CostEstimate(
            flops=1 << 22, bytes_accessed=1 << 23, transcendentals=0
        ),
        name="inside",
    )(d_s, *fields)


def finish_kernel(
    u_s, d_s, s_s, fx, gx, fy, gy, fz, gz, dg, p1_in, p2_in, p3_in, part,
    xone, xtwo, cone, ctwo,
    p1_out, p2_out, p3_out, p4_out, moments,
    side_s, edge_s, w_s,
):
    nx, rows, nz = d_s.shape
    ny = rows - 2 * W
    flip = low_first("gx")
    first, last = z_ends((rows, nz))

    for side, one in ((0, flip), (1, ~flip)):
        side_s[side, :, 0:ny] = jnp.where(one, xone[...], xtwo[...])
        side_s[side, :, ny:] = jnp.zeros((FIELDS, 2 * W, nz), F32)
        late = jnp.where(one, cone[...], ctwo[...])
        row = 0
        for field, begin, n in late_rows(ny):
            side_s[side, field, begin : begin + n] = late[row : row + n]
            row += n

    names = dict(
        u=u_s, d=d_s, s=s_s, fx=fx, gx=gx, fy=fy, gy=gy, fz=fz, gz=gz, dg=dg,
        p1=p1_in, p2=p2_in, p3=p3_in,
    )
    place = {(k, q): names[k].at[q] for k in names for q in range(nx)}
    spare = iter(range(w_s.shape[0]))

    def keep(name, q, value):
        place[name, q] = w_s.at[next(spare)]
        place[name, q][...] = value

    def get(name, q):
        return place[name, q][...]

    for side, (o, e, outward, inward) in enumerate(
        ((-1, 0, "gx", "fx"), (nx, nx - 1, "fx", "gx"))
    ):
        beyond = 2 * o - e
        for k, name in enumerate(("u", "d", "s")):
            place[name, o] = side_s.at[side, k]
        place["s", beyond] = side_s.at[side, 3]
        place[outward, o] = side_s.at[side, 4]
        place["m", o] = side_s.at[side, 5]
        place["q", o] = side_s.at[side, 6]
        u, d, ue, de = get("u", o), get("d", o), get("u", e), get("d", e)
        back = coupling(u, d, ue, de)
        out = coupling(ue, de, u, d)
        fyq, gyq, fzq, gzq = in_plane_couplings(u, d)
        total = 1.0 + get(outward, o) + back + ((fyq + gyq) + (fzq + gzq))
        new = {
            (inward, o): back,
            (outward, e): out,
            ("dg", o): total,
            ("dg", e): get("dg", e) + out,
            ("fy", o): fyq,
            ("gy", o): gyq,
            ("fz", o): jnp.where(last, 0.0, fzq),
            ("gz", o): jnp.where(first, 0.0, gzq),
        }
        for k, (key, value) in enumerate(new.items()):
            place[key] = edge_s.at[side, k]
            place[key][...] = value

    def masked(total, q):
        return jnp.where(get("d", q) > 0.0, total, 0.0)

    def in_plane(q):
        return [get(k, q) for k in ("fy", "gy", "fz", "gz")]

    def adjoint_at(w, q):
        v = get(w, q)
        total = get("dg", q) * v - get("fx", q) * get(w, q + 1)
        total = total - get("gx", q) * get(w, q - 1)
        return masked(total - in_plane_adjoint(v, *in_plane(q)), q)

    def forward_at(w, q):
        v = get(w, q)
        above = get("m", q) if q == nx else get("gx", q + 1) * get(w, q + 1)
        below = get("m", q) if q == -1 else get("fx", q - 1) * get(w, q - 1)
        total = get("dg", q) * v - above - below
        return masked(total - in_plane_forward(v, *in_plane(q)), q)

    sums = [part[k] for k in range(4)]

    def sweep(k, apply, w, name, out, ready):
        for q in range(-1, nx + 1):
            if ready <= q < nx - ready:
                out[q] = get(name, q)[0:ny]
                continue
            value = apply(w, q)
            keep(name, q, value)
            if 0 <= q < nx:
                out[q] = value[0:ny]
                sums[k] = sums[k] + square(value, ny)

    sweep(1, adjoint_at, "s", "p1", p1_out, 1)
    sweep(2, forward_at, "p1", "p2", p2_out, 2)
    for o, outward in ((-1, "gx"), (nx, "fx")):
        beyond = -2 if o == -1 else nx + 1
        keep("p2", beyond, get("q", o) - get(outward, o) * get("p1", o))
    sweep(3, adjoint_at, "p2", "p3", p3_out, 3)
    for q in range(nx):
        p4_out[q] = forward_at("p3", q)[0:ny]

    slot = lax.broadcasted_iota(jnp.int32, (1, LANES), 1)
    row = jnp.zeros((1, LANES), F32)
    for k in range(4):
        row = jnp.where(slot == k, jnp.sum(sums[k]), row)
    moments[...] = jnp.broadcast_to(row, moments.shape)


def finish(copies, ny, *fields):
    nx, rows, nz = fields[0].shape
    steps = 4 + 6 + 2 + 8
    return pl.pallas_call(
        finish_kernel,
        out_shape=(f32(nx, ny, nz),) * 4 + (f32(copies, 1, LANES),),
        in_specs=[VMEM] * len(fields),
        out_specs=(VMEM,) * 5,
        scratch_shapes=[
            pltpu.VMEM((2, FIELDS, rows, nz), F32),
            pltpu.VMEM((2, 8, rows, nz), F32),
            pltpu.VMEM((steps, rows, nz), F32),
        ],
        compiler_params=params(),
        name="finish",
    )(*fields)


def combine_kernel(moments, source, p1, p2, p3, p4, adjoint, residual):
    m = jnp.sum(moments[...], axis=0)
    m0, m1, m2, m3 = (m[:, k : k + 1] for k in range(4))
    alpha = m0 / m1
    beta = alpha * (m2 / m1) - 1.0
    grow = 1.0 + beta
    image = grow * grow * m1 - 2.0 * grow * alpha * m2 + alpha * alpha * m3
    step = (beta * m0) / image
    near = alpha + step * grow
    far = step * alpha
    adjoint[...] = near[None] * p1[...] - far[None] * p3[...]
    residual[...] = source[...] - near[None] * p2[...] + far[None] * p4[...]


def combine(moments, source, p1, p2, p3, p4):
    return pl.pallas_call(
        combine_kernel,
        out_shape=(f32(*source.shape),) * 2,
        in_specs=[VMEM] * 6,
        out_specs=(VMEM,) * 2,
        compiler_params=params(),
        name="combine",
    )(moments, source, p1, p2, p3, p4)


def swap(cells, axis, first):
    pairs = [(i, i + 1) for i in range(first, lax.axis_size(axis) - 1, 2)]
    return lax.ppermute(cells, axis, pairs + [(j, i) for i, j in pairs])


def local(conc, labels, kappa, source):
    ny = conc.shape[1]
    conc, source, diff = pack(conc, labels, kappa, source)
    xtwo = swap(pack_face(False, conc, diff, source), "gx", 0)
    xone = swap(pack_face(True, conc, diff, source), "gx", 1)
    yone, ytwo = pack_rows(conc, diff, source)
    yone = swap(yone, "gy", 1)
    ytwo = swap(ytwo, "gy", 0)
    cone, ctwo = pack_late(conc, diff, source, yone, ytwo)
    cone = swap(cone, "gx", 1)
    ctwo = swap(ctwo, "gx", 0)
    fields = own(conc, diff, source, yone, ytwo)
    inner = inside(*fields[1:])
    p1, p2, p3, p4, moments = finish(
        lax.axis_size(("gx", "gy")), ny, *fields, *inner, xone, xtwo, cone, ctwo
    )
    moments = lax.all_to_all(moments, ("gx", "gy"), 0, 0, tiled=True)
    return combine(moments, source, p1, p2, p3, p4)


def solution(mesh):
    return jax.shard_map(
        local,
        mesh=mesh,
        in_specs=(P("gx", "gy", None), P("gx", "gy", None), P(), P("gx", "gy", None)),
        out_specs=(P("gx", "gy", None), P("gx", "gy", None)),
        check_vma=False,
    )
```

```python
import functools

import jax
import jax.numpy as jnp
from jax import lax
from jax.experimental import pallas as pl
from jax.experimental.pallas import tpu as pltpu
from jax.sharding import PartitionSpec as P

ITERS = 2
DT = 0.5
W = 2 * ITERS
F32 = jnp.float32
LANES = 128
TILE = 8
VMEM = pl.BlockSpec(memory_space=pltpu.VMEM)


def low_first(axis):
    return lax.axis_index(axis) % 2 == 0


def up(v, axis):
    return pltpu.roll(v, v.shape[axis] - 1, axis)


def down(v, axis):
    return pltpu.roll(v, 1, axis)


def z_ends(shape):
    index = lax.broadcasted_iota(jnp.int32, shape, 1)
    return index == 0, index == shape[1] - 1


def coupling(u, d, un, dn):
    return d + d * u - d * un + dn


def params(megabytes=16):
    return pltpu.CompilerParams(vmem_limit_bytes=megabytes << 20)


def f32(*shape):
    return jax.ShapeDtypeStruct(shape, F32)


FIELDS = 7


def late_rows(ny):
    rows = ny + 2 * W
    for field, n in ((0, 3), (1, 3), (2, 3), (3, 2), (4, 2), (5, 1)):
        yield field, ny, n
        yield field, rows - n, n
    for field, n in ((5, 1), (6, 2)):
        yield field, 0, n
        yield field, ny - n, n


def late_count(ny):
    return sum(n for _, _, n in late_rows(ny))


def pack_kernel(
    kappa_in, conc_in, labels_in, source_in,
    conc, source, diff,
    labels, kappa, sems,
):
    nx, ny, nz = conc.shape
    copies = [
        pltpu.make_async_copy(src, dst, sems.at[k])
        for k, (src, dst) in enumerate(
            (
                (kappa_in, kappa),
                (labels_in, labels),
                (conc_in, conc),
                (source_in, source),
            )
        )
    ]
    for copy in copies:
        copy.start()
    for copy in copies:
        copy.wait()
    k0, k1, k2 = ((0.5 * DT) * kappa[k] for k in range(3))

    def body(x, carry):
        lab = labels[x]
        base = jnp.where(lab == 0, k0, jnp.where(lab == 1, k1, k2))
        diff[x] = base * jnp.exp(conc[x])
        return carry

    lax.fori_loop(0, nx, body, 0, unroll=True)


def pack(conc, labels, kappa, source):
    nx, ny, nz = conc.shape
    outside = [
        pltpu.with_memory_space_constraint(v, pltpu.HBM)
        for v in (kappa, conc, labels, source)
    ]
    return pl.pallas_call(
        pack_kernel,
        out_shape=(f32(nx, ny, nz),) * 3,
        in_specs=[pl.BlockSpec(memory_space=pltpu.HBM)] * 4,
        out_specs=(VMEM,) * 3,
        scratch_shapes=[
            pltpu.VMEM((nx, ny, nz), jnp.int32),
            pltpu.SMEM((3,), F32),
            pltpu.SemaphoreType.DMA((4,)),
        ],
        compiler_params=params(),
        name="pack",
    )(*outside)


def pack_rows_kernel(conc, diff, source, yone, ytwo):
    ny = conc.shape[1]
    flip = low_first("gy")
    for k, ref in enumerate((conc, diff, source)):
        yone[k] = jnp.where(flip, ref[:, 0:TILE, :], ref[:, ny - TILE : ny, :])
        ytwo[k] = jnp.where(flip, ref[:, ny - W : ny, :], ref[:, 0:W, :])


def pack_rows(conc, diff, source):
    nx, ny, nz = conc.shape
    return pl.pallas_call(
        pack_rows_kernel,
        out_shape=(f32(3, nx, TILE, nz), f32(3, nx, W, nz)),
        in_specs=[VMEM] * 3,
        out_specs=(VMEM,) * 2,
        compiler_params=params(),
        name="pack_rows",
    )(conc, diff, source)


def rows_beside(yone, ytwo, k, x):
    flip = low_first("gy")
    below = jnp.where(flip, yone[k, x, TILE - W :], ytwo[k, x])
    return below, jnp.where(flip, ytwo[k, x], yone[k, x, 0:W])


def in_plane_adjoint(v, fy, gy, fz, gz):
    total = fy * up(v, 0) + gy * down(v, 0)
    return total + (fz * up(v, 1) + gz * down(v, 1))


def in_plane_forward(v, fy, gy, fz, gz):
    total = up(gy * v, 0) + down(fy * v, 0)
    return total + (up(gz * v, 1) + down(fz * v, 1))


def in_plane_couplings(u, d):
    first, last = z_ends(u.shape)
    fy = coupling(u, d, up(u, 0), up(d, 0))
    gy = coupling(u, d, down(u, 0), down(d, 0))
    fz = coupling(u, d, jnp.where(last, 0.0, up(u, 1)), jnp.where(last, 0.0, up(d, 1)))
    gz = coupling(
        u, d, jnp.where(first, 0.0, down(u, 1)), jnp.where(first, 0.0, down(d, 1))
    )
    return fy, gy, fz, gz


def face_planes(first_swap, nx):
    at_head = low_first("gx") if first_swap else ~low_first("gx")
    return [jnp.where(at_head, k, nx - 1 - k) for k in range(4)]


def face_fields(u, d, s):
    first, last = z_ends(u[0].shape)

    def between(i, j):
        return coupling(u[i], d[i], u[j], d[j])

    def image(i, before, after):
        fy, gy, fz, gz = in_plane_couplings(u[i], d[i])
        diagonal = 1.0 + ((fy + gy) + (fz + gz)) + (before + after)
        beside = (fy, gy, jnp.where(last, 0.0, fz), jnp.where(first, 0.0, gz))
        total = diagonal * s[i] - before * s[i - 1] - after * s[i + 1]
        total = total - in_plane_adjoint(s[i], *beside)
        return jnp.where(d[i] > 0.0, total, 0.0), diagonal, beside

    back, inward = between(1, 0), between(2, 1)
    near, diagonal, beside = image(1, back, between(1, 2))
    far, _, _ = image(2, inward, between(2, 3))
    rest = diagonal * near - inward * far - in_plane_forward(near, *beside)
    return u[0], d[0], s[0], s[1], between(0, 1), back * near, rest


def pack_face_kernel(first_swap, conc, diff, source, slab):
    planes = face_planes(first_swap, conc.shape[0])
    u, d, s = ([ref[x] for x in planes] for ref in (conc, diff, source))
    for k, v in enumerate(face_fields(u, d, s)):
        slab[k] = v


def pack_face(first_swap, conc, diff, source):
    return pl.pallas_call(
        functools.partial(pack_face_kernel, first_swap),
        out_shape=f32(FIELDS, *conc.shape[1:]),
        in_specs=[VMEM] * 3,
        out_specs=VMEM,
        compiler_params=params(),
        name="pack_face",
    )(conc, diff, source)


def pack_late_kernel(conc, diff, source, yone, ytwo, cone, ctwo, near_s, out_s):
    nx, ny, nz = conc.shape
    rows = ny + 2 * W

    def narrow(row):
        if row < ny:
            return row + W if row < W else row - ny + 3 * W
        return row - ny + 3 * W if row < ny + W else row - ny - W

    for first_swap, late in ((True, cone), (False, ctwo)):
        for j, x in enumerate(face_planes(first_swap, nx)):
            for k, ref in enumerate((conc, diff, source)):
                below, above = rows_beside(yone, ytwo, k, x)
                near_s[k, j, 0:W] = below
                near_s[k, j, W : 2 * W] = ref[x, 0:W]
                near_s[k, j, 2 * W : 3 * W] = ref[x, ny - W : ny]
                near_s[k, j, 3 * W :] = above
        fields = face_fields(*([near_s[k, j] for j in range(4)] for k in range(3)))
        for k, v in enumerate(fields):
            out_s[k] = v
        row = 0
        for k, begin, n in late_rows(ny):
            at = narrow(begin)
            late[row : row + n] = out_s[k, at : at + n]
            row += n


def pack_late(conc, diff, source, yone, ytwo):
    nx, ny, nz = conc.shape
    return pl.pallas_call(
        pack_late_kernel,
        out_shape=(f32(late_count(ny), nz),) * 2,
        in_specs=[VMEM] * 5,
        out_specs=(VMEM,) * 2,
        scratch_shapes=[
            pltpu.VMEM((3, 4, 4 * W, nz), F32),
            pltpu.VMEM((FIELDS, 4 * W, nz), F32),
        ],
        compiler_params=params(),
        name="pack_late",
    )(conc, diff, source, yone, ytwo)


def own_kernel(
    conc, diff, source, yone, ytwo,
    u_s, d_s, s_s, fx, gx, fy, gy, fz, gz, dg, p1,
):
    nx, ny, nz = conc.shape
    rows = ny + 2 * W
    for k, (own, ref) in enumerate(((conc, u_s), (diff, d_s), (source, s_s))):
        below, above = rows_beside(yone, ytwo, k, slice(0, nx))
        ref[:, 0:ny, :] = own[...]
        ref[:, ny : ny + W, :] = above
        ref[:, ny + W :, :] = below
    first, last = z_ends((rows, nz))

    for q in range(nx):
        u, d = u_s[q], d_s[q]
        fyq, gyq, fzq, gzq = in_plane_couplings(u, d)
        total = 1.0 + ((fyq + gyq) + (fzq + gzq))
        if q + 1 < nx:
            fxq = coupling(u, d, u_s[q + 1], d_s[q + 1])
            fx[q] = fxq
            total = total + fxq
        if q > 0:
            gxq = coupling(u, d, u_s[q - 1], d_s[q - 1])
            gx[q] = gxq
            total = total + gxq
        dg[q] = total
        fy[q] = fyq
        gy[q] = gyq
        fz[q] = jnp.where(last, 0.0, fzq)
        gz[q] = jnp.where(first, 0.0, gzq)

    for q in range(1, nx - 1):
        v = s_s[q]
        total = dg[q] * v - fx[q] * s_s[q + 1] - gx[q] * s_s[q - 1]
        total = total - in_plane_adjoint(v, fy[q], gy[q], fz[q], gz[q])
        p1[q] = jnp.where(d_s[q] > 0.0, total, 0.0)


def own(conc, diff, source, yone, ytwo):
    nx, ny, nz = conc.shape
    return pl.pallas_call(
        own_kernel,
        out_shape=(f32(nx, ny + 2 * W, nz),) * 11,
        in_specs=[VMEM] * 5,
        out_specs=(VMEM,) * 11,
        compiler_params=params(),
        name="own",
    )(conc, diff, source, yone, ytwo)


def square(v, ny):
    mine = v[0:ny]
    return jnp.sum((mine * mine).reshape(ny // 8, 8, mine.shape[1]), axis=0)


def inside_kernel(d_s, s_s, fx, gx, fy, gy, fz, gz, dg, p1, p2, p3, part):
    nx, rows, nz = d_s.shape
    ny = rows - 2 * W
    sums = [jnp.zeros((8, nz), F32) for _ in range(4)]
    for q in range(nx):
        sums[0] = sums[0] + square(s_s[q], ny)
    for q in range(1, nx - 1):
        sums[1] = sums[1] + square(p1[q], ny)
    for q in range(2, nx - 2):
        v = p1[q]
        total = dg[q] * v - gx[q + 1] * p1[q + 1] - fx[q - 1] * p1[q - 1]
        total = total - in_plane_forward(v, fy[q], gy[q], fz[q], gz[q])
        total = jnp.where(d_s[q] > 0.0, total, 0.0)
        p2[q] = total
        sums[2] = sums[2] + square(total, ny)
    for q in range(3, nx - 3):
        v = p2[q]
        total = dg[q] * v - fx[q] * p2[q + 1] - gx[q] * p2[q - 1]
        total = total - in_plane_adjoint(v, fy[q], gy[q], fz[q], gz[q])
        total = jnp.where(d_s[q] > 0.0, total, 0.0)
        p3[q] = total
        sums[3] = sums[3] + square(total, ny)
    for k in range(4):
        part[k] = sums[k]


def inside(d_s, *fields):
    nx, rows, nz = d_s.shape
    return pl.pallas_call(
        inside_kernel,
        out_shape=(f32(nx, rows, nz),) * 2 + (f32(4, 8, nz),),
        in_specs=[VMEM] * 10,
        out_specs=(VMEM,) * 3,
        compiler_params=params(),
        cost_estimate=pl.CostEstimate(
            flops=1 << 22, bytes_accessed=1 << 23, transcendentals=0
        ),
        name="inside",
    )(d_s, *fields)


def finish_kernel(
    u_s, d_s, s_s, fx, gx, fy, gy, fz, gz, dg, p1_in, p2_in, p3_in, part,
    xtwo, xone, cone, ctwo,
    p1_out, p2_out, p3_out, p4_out, moments,
    side_s, edge_s, w_s,
):
    nx, rows, nz = d_s.shape
    ny = rows - 2 * W
    flip = low_first("gx")
    first, last = z_ends((rows, nz))

    for side, one in ((0, flip), (1, ~flip)):
        side_s[side, :, 0:ny] = jnp.where(one, xone[...], xtwo[...])
        side_s[side, :, ny:] = jnp.zeros((FIELDS, 2 * W, nz), F32)
        late = jnp.where(one, cone[...], ctwo[...])
        row = 0
        for field, begin, n in late_rows(ny):
            side_s[side, field, begin : begin + n] = late[row : row + n]
            row += n

    names = dict(
        u=u_s, d=d_s, s=s_s, fx=fx, gx=gx, fy=fy, gy=gy, fz=fz, gz=gz, dg=dg,
        p1=p1_in, p2=p2_in, p3=p3_in,
    )
    place = {(k, q): names[k].at[q] for k in names for q in range(nx)}
    spare = iter(range(w_s.shape[0]))

    def keep(name, q, value):
        place[name, q] = w_s.at[next(spare)]
        place[name, q][...] = value

    def get(name, q):
        return place[name, q][...]

    for side, (o, e, outward, inward) in enumerate(
        ((-1, 0, "gx", "fx"), (nx, nx - 1, "fx", "gx"))
    ):
        beyond = 2 * o - e
        for k, name in enumerate(("u", "d", "s")):
            place[name, o] = side_s.at[side, k]
        place["s", beyond] = side_s.at[side, 3]
        place[outward, o] = side_s.at[side, 4]
        place["m", o] = side_s.at[side, 5]
        place["q", o] = side_s.at[side, 6]
        u, d, ue, de = get("u", o), get("d", o), get("u", e), get("d", e)
        back = coupling(u, d, ue, de)
        out = coupling(ue, de, u, d)
        fyq, gyq, fzq, gzq = in_plane_couplings(u, d)
        total = 1.0 + get(outward, o) + back + ((fyq + gyq) + (fzq + gzq))
        new = {
            (inward, o): back,
            (outward, e): out,
            ("dg", o): total,
            ("dg", e): get("dg", e) + out,
            ("fy", o): fyq,
            ("gy", o): gyq,
            ("fz", o): jnp.where(last, 0.0, fzq),
            ("gz", o): jnp.where(first, 0.0, gzq),
        }
        for k, (key, value) in enumerate(new.items()):
            place[key] = edge_s.at[side, k]
            place[key][...] = value

    def masked(total, q):
        return jnp.where(get("d", q) > 0.0, total, 0.0)

    def in_plane(q):
        return [get(k, q) for k in ("fy", "gy", "fz", "gz")]

    def adjoint_at(w, q):
        v = get(w, q)
        total = get("dg", q) * v - get("fx", q) * get(w, q + 1)
        total = total - get("gx", q) * get(w, q - 1)
        return masked(total - in_plane_adjoint(v, *in_plane(q)), q)

    def forward_at(w, q):
        v = get(w, q)
        above = get("m", q) if q == nx else get("gx", q + 1) * get(w, q + 1)
        below = get("m", q) if q == -1 else get("fx", q - 1) * get(w, q - 1)
        total = get("dg", q) * v - above - below
        return masked(total - in_plane_forward(v, *in_plane(q)), q)

    sums = [part[k] for k in range(4)]

    def sweep(k, apply, w, name, out, ready):
        for q in range(-1, nx + 1):
            if ready <= q < nx - ready:
                out[q] = get(name, q)[0:ny]
                continue
            value = apply(w, q)
            keep(name, q, value)
            if 0 <= q < nx:
                out[q] = value[0:ny]
                sums[k] = sums[k] + square(value, ny)

    sweep(1, adjoint_at, "s", "p1", p1_out, 1)
    sweep(2, forward_at, "p1", "p2", p2_out, 2)
    for o, outward in ((-1, "gx"), (nx, "fx")):
        beyond = -2 if o == -1 else nx + 1
        keep("p2", beyond, get("q", o) - get(outward, o) * get("p1", o))
    sweep(3, adjoint_at, "p2", "p3", p3_out, 3)
    for q in range(nx):
        p4_out[q] = forward_at("p3", q)[0:ny]

    slot = lax.broadcasted_iota(jnp.int32, (1, LANES), 1)
    row = jnp.zeros((1, LANES), F32)
    for k in range(4):
        row = jnp.where(slot == k, jnp.sum(sums[k]), row)
    moments[...] = jnp.broadcast_to(row, moments.shape)


def finish(copies, ny, *fields):
    nx, rows, nz = fields[0].shape
    steps = 4 + 6 + 2 + 8
    return pl.pallas_call(
        finish_kernel,
        out_shape=(f32(nx, ny, nz),) * 4 + (f32(copies, 1, LANES),),
        in_specs=[VMEM] * len(fields),
        out_specs=(VMEM,) * 5,
        scratch_shapes=[
            pltpu.VMEM((2, FIELDS, rows, nz), F32),
            pltpu.VMEM((2, 8, rows, nz), F32),
            pltpu.VMEM((steps, rows, nz), F32),
        ],
        compiler_params=params(),
        name="finish",
    )(*fields)


def combine_kernel(moments, source, p1, p2, p3, p4, adjoint, residual):
    m = jnp.sum(moments[...], axis=0)
    m0, m1, m2, m3 = (m[:, k : k + 1] for k in range(4))
    alpha = m0 / m1
    beta = alpha * (m2 / m1) - 1.0
    grow = 1.0 + beta
    image = grow * grow * m1 - 2.0 * grow * alpha * m2 + alpha * alpha * m3
    step = (beta * m0) / image
    near = alpha + step * grow
    far = step * alpha
    adjoint[...] = near[None] * p1[...] - far[None] * p3[...]
    residual[...] = source[...] - near[None] * p2[...] + far[None] * p4[...]


def combine(moments, source, p1, p2, p3, p4):
    return pl.pallas_call(
        combine_kernel,
        out_shape=(f32(*source.shape),) * 2,
        in_specs=[VMEM] * 6,
        out_specs=(VMEM,) * 2,
        compiler_params=params(),
        name="combine",
    )(moments, source, p1, p2, p3, p4)


def swap(cells, axis, first):
    pairs = [(i, i + 1) for i in range(first, lax.axis_size(axis) - 1, 2)]
    return lax.ppermute(cells, axis, pairs + [(j, i) for i, j in pairs])


def local(conc, labels, kappa, source):
    ny = conc.shape[1]
    conc, source, diff = pack(conc, labels, kappa, source)
    xtwo = swap(pack_face(False, conc, diff, source), "gx", 0)
    xone = swap(pack_face(True, conc, diff, source), "gx", 1)
    yone, ytwo = pack_rows(conc, diff, source)
    yone = swap(yone, "gy", 1)
    ytwo = swap(ytwo, "gy", 0)
    cone, ctwo = pack_late(conc, diff, source, yone, ytwo)
    cone = swap(cone, "gx", 1)
    ctwo = swap(ctwo, "gx", 0)
    fields = own(conc, diff, source, yone, ytwo)
    inner = inside(*fields[1:])
    p1, p2, p3, p4, moments = finish(
        lax.axis_size(("gx", "gy")), ny, *fields, *inner, xtwo, xone, cone, ctwo
    )
    moments = lax.all_to_all(moments, ("gx", "gy"), 0, 0, tiled=True)
    return combine(moments, source, p1, p2, p3, p4)


def solution(mesh):
    return jax.shard_map(
        local,
        mesh=mesh,
        in_specs=(P("gx", "gy", None), P("gx", "gy", None), P(), P("gx", "gy", None)),
        out_specs=(P("gx", "gy", None), P("gx", "gy", None)),
        check_vma=False,
    )
```

```python
import functools

import jax
import jax.numpy as jnp
from jax import lax
from jax.experimental import pallas as pl
from jax.experimental.pallas import tpu as pltpu
from jax.sharding import PartitionSpec as P

ITERS = 2
DT = 0.5
W = 2 * ITERS
F32 = jnp.float32
LANES = 128
YROWS = (8, 6)
VMEM = pl.BlockSpec(memory_space=pltpu.VMEM)


def low_first(axis):
    return lax.axis_index(axis) % 2 == 0


def up(v, axis):
    return pltpu.roll(v, v.shape[axis] - 1, axis)


def down(v, axis):
    return pltpu.roll(v, 1, axis)


def z_ends(shape):
    index = lax.broadcasted_iota(jnp.int32, shape, 1)
    return index == 0, index == shape[1] - 1


def coupling(u, d, un, dn):
    return d + d * u - d * un + dn


def params(megabytes=16):
    return pltpu.CompilerParams(vmem_limit_bytes=megabytes << 20)


def f32(*shape):
    return jax.ShapeDtypeStruct(shape, F32)


FIELDS = 7


def late_rows(ny):
    rows = ny + 2 * W
    for field, n in ((0, 3), (1, 3), (2, 3), (3, 2), (4, 2), (5, 1)):
        yield field, ny, n
        yield field, rows - n, n
    for field, n in ((5, 1), (6, 2)):
        yield field, 0, n
        yield field, ny - n, n


def late_count(ny):
    return sum(n for _, _, n in late_rows(ny))


def pack_kernel(
    kappa_in, conc_in, labels_in, source_in,
    conc, source, diff,
    labels, kappa, sems,
):
    nx, ny, nz = conc.shape
    copies = [
        pltpu.make_async_copy(src, dst, sems.at[k])
        for k, (src, dst) in enumerate(
            (
                (kappa_in, kappa),
                (labels_in, labels),
                (conc_in, conc),
                (source_in, source),
            )
        )
    ]
    for copy in copies:
        copy.start()
    for copy in copies:
        copy.wait()
    k0, k1, k2 = ((0.5 * DT) * kappa[k] for k in range(3))

    def body(x, carry):
        lab = labels[x]
        base = jnp.where(lab == 0, k0, jnp.where(lab == 1, k1, k2))
        diff[x] = base * jnp.exp(conc[x])
        return carry

    lax.fori_loop(0, nx, body, 0, unroll=True)


def pack(conc, labels, kappa, source):
    nx, ny, nz = conc.shape
    outside = [
        pltpu.with_memory_space_constraint(v, pltpu.HBM)
        for v in (kappa, conc, labels, source)
    ]
    return pl.pallas_call(
        pack_kernel,
        out_shape=(f32(nx, ny, nz),) * 3,
        in_specs=[pl.BlockSpec(memory_space=pltpu.HBM)] * 4,
        out_specs=(VMEM,) * 3,
        scratch_shapes=[
            pltpu.VMEM((nx, ny, nz), jnp.int32),
            pltpu.SMEM((3,), F32),
            pltpu.SemaphoreType.DMA((4,)),
        ],
        compiler_params=params(),
        name="pack",
    )(*outside)


def pack_rows_kernel(conc, diff, source, yone, ytwo):
    ny = conc.shape[1]
    flip = low_first("gy")
    for k, ref in enumerate((conc, diff, source)):
        for out, n, head in ((yone, YROWS[0], flip), (ytwo, YROWS[1], ~flip)):
            out[k] = jnp.where(head, ref[:, 0:n, :], ref[:, ny - n : ny, :])


def pack_rows(conc, diff, source):
    nx, ny, nz = conc.shape
    return pl.pallas_call(
        pack_rows_kernel,
        out_shape=tuple(f32(3, nx, n, nz) for n in YROWS),
        in_specs=[VMEM] * 3,
        out_specs=(VMEM,) * 2,
        compiler_params=params(),
        name="pack_rows",
    )(conc, diff, source)


def rows_beside(yone, ytwo, k, x):
    flip = low_first("gy")
    one, two = (slice(n - W, n) for n in YROWS)
    below = jnp.where(flip, yone[k, x, one], ytwo[k, x, two])
    return below, jnp.where(flip, ytwo[k, x, 0:W], yone[k, x, 0:W])


def in_plane_adjoint(v, fy, gy, fz, gz):
    total = fy * up(v, 0) + gy * down(v, 0)
    return total + (fz * up(v, 1) + gz * down(v, 1))


def in_plane_forward(v, fy, gy, fz, gz):
    total = up(gy * v, 0) + down(fy * v, 0)
    return total + (up(gz * v, 1) + down(fz * v, 1))


def in_plane_couplings(u, d):
    first, last = z_ends(u.shape)
    fy = coupling(u, d, up(u, 0), up(d, 0))
    gy = coupling(u, d, down(u, 0), down(d, 0))
    fz = coupling(u, d, jnp.where(last, 0.0, up(u, 1)), jnp.where(last, 0.0, up(d, 1)))
    gz = coupling(
        u, d, jnp.where(first, 0.0, down(u, 1)), jnp.where(first, 0.0, down(d, 1))
    )
    return fy, gy, fz, gz


def face_planes(first_swap, nx):
    at_head = low_first("gx") if first_swap else ~low_first("gx")
    return [jnp.where(at_head, k, nx - 1 - k) for k in range(4)]


def face_fields(u, d, s):
    first, last = z_ends(u[0].shape)

    def between(i, j):
        return coupling(u[i], d[i], u[j], d[j])

    def image(i, before, after):
        fy, gy, fz, gz = in_plane_couplings(u[i], d[i])
        diagonal = 1.0 + ((fy + gy) + (fz + gz)) + (before + after)
        beside = (fy, gy, jnp.where(last, 0.0, fz), jnp.where(first, 0.0, gz))
        total = diagonal * s[i] - before * s[i - 1] - after * s[i + 1]
        total = total - in_plane_adjoint(s[i], *beside)
        return jnp.where(d[i] > 0.0, total, 0.0), diagonal, beside

    back, inward = between(1, 0), between(2, 1)
    near, diagonal, beside = image(1, back, between(1, 2))
    far, _, _ = image(2, inward, between(2, 3))
    rest = diagonal * near - inward * far - in_plane_forward(near, *beside)
    return u[0], d[0], s[0], s[1], between(0, 1), back * near, rest


def pack_face_kernel(first_swap, conc, diff, source, *slabs):
    planes = face_planes(first_swap, conc.shape[0])
    u, d, s = ([ref[x] for x in planes] for ref in (conc, diff, source))
    for k, v in enumerate(face_fields(u, d, s)):
        if k < slabs[0].shape[0]:
            slabs[0][k] = v
        else:
            slabs[1][...] = v


def pack_face(first_swap, conc, diff, source):
    plane = conc.shape[1:]
    return pl.pallas_call(
        functools.partial(pack_face_kernel, first_swap),
        out_shape=(f32(FIELDS - 1, *plane), f32(*plane))
        if first_swap
        else f32(FIELDS, *plane),
        in_specs=[VMEM] * 3,
        out_specs=(VMEM, VMEM) if first_swap else VMEM,
        compiler_params=params(),
        name="pack_face",
    )(conc, diff, source)


def pack_late_kernel(
    conc, diff, source, yone, ytwo, rest, cone, ctwo, near_s, out_s
):
    nx, ny, nz = conc.shape
    rows = ny + 2 * W

    def narrow(row):
        if row < ny:
            return row + W if row < W else row - ny + 3 * W
        return row - ny + 3 * W if row < ny + W else row - ny - W

    for first_swap, late in ((True, cone), (False, ctwo)):
        for j, x in enumerate(face_planes(first_swap, nx)):
            for k, ref in enumerate((conc, diff, source)):
                below, above = rows_beside(yone, ytwo, k, x)
                near_s[k, j, 0:W] = below
                near_s[k, j, W : 2 * W] = ref[x, 0:W]
                near_s[k, j, 2 * W : 3 * W] = ref[x, ny - W : ny]
                near_s[k, j, 3 * W :] = above
        fields = face_fields(*([near_s[k, j] for j in range(4)] for k in range(3)))
        for k, v in enumerate(fields):
            out_s[k] = v
        row = 0
        if first_swap:
            late[0:ny] = rest[...]
            row = ny
        for k, begin, n in late_rows(ny):
            at = narrow(begin)
            late[row : row + n] = out_s[k, at : at + n]
            row += n


def pack_late(conc, diff, source, yone, ytwo, rest):
    nx, ny, nz = conc.shape
    return pl.pallas_call(
        pack_late_kernel,
        out_shape=(f32(ny + late_count(ny), nz), f32(late_count(ny), nz)),
        in_specs=[VMEM] * 6,
        out_specs=(VMEM,) * 2,
        scratch_shapes=[
            pltpu.VMEM((3, 4, 4 * W, nz), F32),
            pltpu.VMEM((FIELDS, 4 * W, nz), F32),
        ],
        compiler_params=params(),
        name="pack_late",
    )(conc, diff, source, yone, ytwo, rest)


def own_kernel(
    conc, diff, source, yone, ytwo,
    u_s, d_s, s_s, fx, gx, fy, gy, fz, gz, dg, p1,
):
    nx, ny, nz = conc.shape
    rows = ny + 2 * W
    for k, (own, ref) in enumerate(((conc, u_s), (diff, d_s), (source, s_s))):
        below, above = rows_beside(yone, ytwo, k, slice(0, nx))
        ref[:, 0:ny, :] = own[...]
        ref[:, ny : ny + W, :] = above
        ref[:, ny + W :, :] = below
    first, last = z_ends((rows, nz))

    for q in range(nx):
        u, d = u_s[q], d_s[q]
        fyq, gyq, fzq, gzq = in_plane_couplings(u, d)
        total = 1.0 + ((fyq + gyq) + (fzq + gzq))
        if q + 1 < nx:
            fxq = coupling(u, d, u_s[q + 1], d_s[q + 1])
            fx[q] = fxq
            total = total + fxq
        if q > 0:
            gxq = coupling(u, d, u_s[q - 1], d_s[q - 1])
            gx[q] = gxq
            total = total + gxq
        dg[q] = total
        fy[q] = fyq
        gy[q] = gyq
        fz[q] = jnp.where(last, 0.0, fzq)
        gz[q] = jnp.where(first, 0.0, gzq)

    for q in range(1, nx - 1):
        v = s_s[q]
        total = dg[q] * v - fx[q] * s_s[q + 1] - gx[q] * s_s[q - 1]
        total = total - in_plane_adjoint(v, fy[q], gy[q], fz[q], gz[q])
        p1[q] = jnp.where(d_s[q] > 0.0, total, 0.0)


def own(conc, diff, source, yone, ytwo):
    nx, ny, nz = conc.shape
    return pl.pallas_call(
        own_kernel,
        out_shape=(f32(nx, ny + 2 * W, nz),) * 11,
        in_specs=[VMEM] * 5,
        out_specs=(VMEM,) * 11,
        compiler_params=params(),
        name="own",
    )(conc, diff, source, yone, ytwo)


def square(v, ny):
    mine = v[0:ny]
    return jnp.sum((mine * mine).reshape(ny // 8, 8, mine.shape[1]), axis=0)


def inside_kernel(d_s, s_s, fx, gx, fy, gy, fz, gz, dg, p1, p2, p3, part):
    nx, rows, nz = d_s.shape
    ny = rows - 2 * W
    sums = [jnp.zeros((8, nz), F32) for _ in range(4)]
    for q in range(nx):
        sums[0] = sums[0] + square(s_s[q], ny)
    for q in range(1, nx - 1):
        sums[1] = sums[1] + square(p1[q], ny)
    for q in range(2, nx - 2):
        v = p1[q]
        total = dg[q] * v - gx[q + 1] * p1[q + 1] - fx[q - 1] * p1[q - 1]
        total = total - in_plane_forward(v, fy[q], gy[q], fz[q], gz[q])
        total = jnp.where(d_s[q] > 0.0, total, 0.0)
        p2[q] = total
        sums[2] = sums[2] + square(total, ny)
    for q in range(3, nx - 3):
        v = p2[q]
        total = dg[q] * v - fx[q] * p2[q + 1] - gx[q] * p2[q - 1]
        total = total - in_plane_adjoint(v, fy[q], gy[q], fz[q], gz[q])
        total = jnp.where(d_s[q] > 0.0, total, 0.0)
        p3[q] = total
        sums[3] = sums[3] + square(total, ny)
    for k in range(4):
        part[k] = sums[k]


def inside(d_s, *fields):
    nx, rows, nz = d_s.shape
    return pl.pallas_call(
        inside_kernel,
        out_shape=(f32(nx, rows, nz),) * 2 + (f32(4, 8, nz),),
        in_specs=[VMEM] * 10,
        out_specs=(VMEM,) * 3,
        compiler_params=params(),
        cost_estimate=pl.CostEstimate(
            flops=1 << 22, bytes_accessed=1 << 23, transcendentals=0
        ),
        name="inside",
    )(d_s, *fields)


def finish_kernel(
    u_s, d_s, s_s, fx, gx, fy, gy, fz, gz, dg, p1_in, p2_in, p3_in, part,
    xtwo, xone, cone, ctwo,
    p1_out, p2_out, p3_out, p4_out, moments,
    side_s, edge_s, w_s,
):
    nx, rows, nz = d_s.shape
    ny = rows - 2 * W
    flip = low_first("gx")
    first, last = z_ends((rows, nz))

    for side, one in ((0, flip), (1, ~flip)):
        side_s[side, 0 : FIELDS - 1, 0:ny] = jnp.where(
            one, xone[...], xtwo[0 : FIELDS - 1]
        )
        side_s[side, FIELDS - 1, 0:ny] = jnp.where(one, cone[0:ny], xtwo[FIELDS - 1])
        side_s[side, :, ny:] = jnp.zeros((FIELDS, 2 * W, nz), F32)
        late = jnp.where(one, cone[ny:], ctwo[...])
        row = 0
        for field, begin, n in late_rows(ny):
            side_s[side, field, begin : begin + n] = late[row : row + n]
            row += n

    names = dict(
        u=u_s, d=d_s, s=s_s, fx=fx, gx=gx, fy=fy, gy=gy, fz=fz, gz=gz, dg=dg,
        p1=p1_in, p2=p2_in, p3=p3_in,
    )
    place = {(k, q): names[k].at[q] for k in names for q in range(nx)}
    spare = iter(range(w_s.shape[0]))

    def keep(name, q, value):
        place[name, q] = w_s.at[next(spare)]
        place[name, q][...] = value

    def get(name, q):
        return place[name, q][...]

    for side, (o, e, outward, inward) in enumerate(
        ((-1, 0, "gx", "fx"), (nx, nx - 1, "fx", "gx"))
    ):
        beyond = 2 * o - e
        for k, name in enumerate(("u", "d", "s")):
            place[name, o] = side_s.at[side, k]
        place["s", beyond] = side_s.at[side, 3]
        place[outward, o] = side_s.at[side, 4]
        place["m", o] = side_s.at[side, 5]
        place["q", o] = side_s.at[side, 6]
        u, d, ue, de = get("u", o), get("d", o), get("u", e), get("d", e)
        back = coupling(u, d, ue, de)
        out = coupling(ue, de, u, d)
        fyq, gyq, fzq, gzq = in_plane_couplings(u, d)
        total = 1.0 + get(outward, o) + back + ((fyq + gyq) + (fzq + gzq))
        new = {
            (inward, o): back,
            (outward, e): out,
            ("dg", o): total,
            ("dg", e): get("dg", e) + out,
            ("fy", o): fyq,
            ("gy", o): gyq,
            ("fz", o): jnp.where(last, 0.0, fzq),
            ("gz", o): jnp.where(first, 0.0, gzq),
        }
        for k, (key, value) in enumerate(new.items()):
            place[key] = edge_s.at[side, k]
            place[key][...] = value

    def masked(total, q):
        return jnp.where(get("d", q) > 0.0, total, 0.0)

    def in_plane(q):
        return [get(k, q) for k in ("fy", "gy", "fz", "gz")]

    def adjoint_at(w, q):
        v = get(w, q)
        total = get("dg", q) * v - get("fx", q) * get(w, q + 1)
        total = total - get("gx", q) * get(w, q - 1)
        return masked(total - in_plane_adjoint(v, *in_plane(q)), q)

    def forward_at(w, q):
        v = get(w, q)
        above = get("m", q) if q == nx else get("gx", q + 1) * get(w, q + 1)
        below = get("m", q) if q == -1 else get("fx", q - 1) * get(w, q - 1)
        total = get("dg", q) * v - above - below
        return masked(total - in_plane_forward(v, *in_plane(q)), q)

    sums = [part[k] for k in range(4)]

    def sweep(k, apply, w, name, out, ready):
        for q in range(-1, nx + 1):
            if ready <= q < nx - ready:
                out[q] = get(name, q)[0:ny]
                continue
            value = apply(w, q)
            keep(name, q, value)
            if 0 <= q < nx:
                out[q] = value[0:ny]
                sums[k] = sums[k] + square(value, ny)

    sweep(1, adjoint_at, "s", "p1", p1_out, 1)
    sweep(2, forward_at, "p1", "p2", p2_out, 2)
    for o, outward in ((-1, "gx"), (nx, "fx")):
        beyond = -2 if o == -1 else nx + 1
        keep("p2", beyond, get("q", o) - get(outward, o) * get("p1", o))
    sweep(3, adjoint_at, "p2", "p3", p3_out, 3)
    for q in range(nx):
        p4_out[q] = forward_at("p3", q)[0:ny]

    slot = lax.broadcasted_iota(jnp.int32, (1, LANES), 1)
    row = jnp.zeros((1, LANES), F32)
    for k in range(4):
        row = jnp.where(slot == k, jnp.sum(sums[k]), row)
    moments[...] = jnp.broadcast_to(row, moments.shape)


def finish(copies, ny, *fields):
    nx, rows, nz = fields[0].shape
    steps = 4 + 6 + 2 + 8
    return pl.pallas_call(
        finish_kernel,
        out_shape=(f32(nx, ny, nz),) * 4 + (f32(copies, 1, LANES),),
        in_specs=[VMEM] * len(fields),
        out_specs=(VMEM,) * 5,
        scratch_shapes=[
            pltpu.VMEM((2, FIELDS, rows, nz), F32),
            pltpu.VMEM((2, 8, rows, nz), F32),
            pltpu.VMEM((steps, rows, nz), F32),
        ],
        compiler_params=params(),
        name="finish",
    )(*fields)


def combine_kernel(moments, source, p1, p2, p3, p4, adjoint, residual):
    m = jnp.sum(moments[...], axis=0)
    m0, m1, m2, m3 = (m[:, k : k + 1] for k in range(4))
    alpha = m0 / m1
    beta = alpha * (m2 / m1) - 1.0
    grow = 1.0 + beta
    image = grow * grow * m1 - 2.0 * grow * alpha * m2 + alpha * alpha * m3
    step = (beta * m0) / image
    near = alpha + step * grow
    far = step * alpha
    adjoint[...] = near[None] * p1[...] - far[None] * p3[...]
    residual[...] = source[...] - near[None] * p2[...] + far[None] * p4[...]


def combine(moments, source, p1, p2, p3, p4):
    return pl.pallas_call(
        combine_kernel,
        out_shape=(f32(*source.shape),) * 2,
        in_specs=[VMEM] * 6,
        out_specs=(VMEM,) * 2,
        compiler_params=params(),
        name="combine",
    )(moments, source, p1, p2, p3, p4)


def swap(cells, axis, first):
    pairs = [(i, i + 1) for i in range(first, lax.axis_size(axis) - 1, 2)]
    return lax.ppermute(cells, axis, pairs + [(j, i) for i, j in pairs])


def local(conc, labels, kappa, source):
    ny = conc.shape[1]
    conc, source, diff = pack(conc, labels, kappa, source)
    xtwo = swap(pack_face(False, conc, diff, source), "gx", 0)
    xone, rest = pack_face(True, conc, diff, source)
    xone = swap(xone, "gx", 1)
    yone, ytwo = pack_rows(conc, diff, source)
    yone = swap(yone, "gy", 1)
    ytwo = swap(ytwo, "gy", 0)
    cone, ctwo = pack_late(conc, diff, source, yone, ytwo, rest)
    cone = swap(cone, "gx", 1)
    ctwo = swap(ctwo, "gx", 0)
    fields = own(conc, diff, source, yone, ytwo)
    inner = inside(*fields[1:])
    p1, p2, p3, p4, moments = finish(
        lax.axis_size(("gx", "gy")), ny, *fields, *inner, xtwo, xone, cone, ctwo
    )
    moments = lax.all_to_all(moments, ("gx", "gy"), 0, 0, tiled=True)
    return combine(moments, source, p1, p2, p3, p4)


def solution(mesh):
    return jax.shard_map(
        local,
        mesh=mesh,
        in_specs=(P("gx", "gy", None), P("gx", "gy", None), P(), P("gx", "gy", None)),
        out_specs=(P("gx", "gy", None), P("gx", "gy", None)),
        check_vma=False,
    )
```

```python
import functools

import jax
import jax.numpy as jnp
from jax import lax
from jax.experimental import pallas as pl
from jax.experimental.pallas import tpu as pltpu
from jax.sharding import PartitionSpec as P

ITERS = 2
DT = 0.5
W = 2 * ITERS
F32 = jnp.float32
LANES = 128
VMEM = pl.BlockSpec(memory_space=pltpu.VMEM)


def low_first(axis):
    return lax.axis_index(axis) % 2 == 0


def up(v, axis):
    return pltpu.roll(v, v.shape[axis] - 1, axis)


def down(v, axis):
    return pltpu.roll(v, 1, axis)


def z_ends(shape):
    index = lax.broadcasted_iota(jnp.int32, shape, 1)
    return index == 0, index == shape[1] - 1


def coupling(u, d, un, dn):
    return d + d * u - d * un + dn


def params(megabytes=16):
    return pltpu.CompilerParams(vmem_limit_bytes=megabytes << 20)


def f32(*shape):
    return jax.ShapeDtypeStruct(shape, F32)


FIELDS = 7


def late_rows(ny):
    rows = ny + 2 * W
    for field, n in ((0, 3), (1, 3), (2, 3), (3, 2), (4, 2), (5, 1)):
        yield field, ny, n
        yield field, rows - n, n
    for field, n in ((5, 1), (6, 2)):
        yield field, 0, n
        yield field, ny - n, n


def late_count(ny):
    return sum(n for _, _, n in late_rows(ny))


def pack_kernel(
    kappa_in, conc_in, labels_in, source_in,
    conc, source, diff,
    labels, kappa, sems,
):
    nx, ny, nz = conc.shape
    copies = [
        pltpu.make_async_copy(src, dst, sems.at[k])
        for k, (src, dst) in enumerate(
            (
                (kappa_in, kappa),
                (labels_in, labels),
                (conc_in, conc),
                (source_in, source),
            )
        )
    ]
    for copy in copies:
        copy.start()
    for copy in copies:
        copy.wait()
    k0, k1, k2 = ((0.5 * DT) * kappa[k] for k in range(3))

    def body(x, carry):
        lab = labels[x]
        base = jnp.where(lab == 0, k0, jnp.where(lab == 1, k1, k2))
        diff[x] = base * jnp.exp(conc[x])
        return carry

    lax.fori_loop(0, nx, body, 0, unroll=True)


def pack(conc, labels, kappa, source):
    nx, ny, nz = conc.shape
    outside = [
        pltpu.with_memory_space_constraint(v, pltpu.HBM)
        for v in (kappa, conc, labels, source)
    ]
    return pl.pallas_call(
        pack_kernel,
        out_shape=(f32(nx, ny, nz),) * 3,
        in_specs=[pl.BlockSpec(memory_space=pltpu.HBM)] * 4,
        out_specs=(VMEM,) * 3,
        scratch_shapes=[
            pltpu.VMEM((nx, ny, nz), jnp.int32),
            pltpu.SMEM((3,), F32),
            pltpu.SemaphoreType.DMA((4,)),
        ],
        compiler_params=params(),
        name="pack",
    )(*outside)


def pack_rows_kernel(conc, diff, source, out):
    ny = conc.shape[1]
    for k, ref in enumerate((conc, diff, source)):
        out[k, :, 0:W] = ref[:, 0:W, :]
        out[k, :, W:] = ref[:, ny - W : ny, :]


def pack_rows(conc, diff, source):
    nx, ny, nz = conc.shape
    return pl.pallas_call(
        pack_rows_kernel,
        out_shape=f32(3, nx, 2 * W, nz),
        in_specs=[VMEM] * 3,
        out_specs=VMEM,
        compiler_params=params(),
        name="pack_rows",
    )(conc, diff, source)


def relay_rows_kernel(near, out):
    even = low_first("gy")
    out[...] = jnp.where(even, near[:, :, W:], near[:, :, 0:W])


def relay_rows(near):
    return pl.pallas_call(
        relay_rows_kernel,
        out_shape=f32(*near.shape[:2], W, near.shape[3]),
        in_specs=[VMEM],
        out_specs=VMEM,
        compiler_params=params(),
        name="relay_rows",
    )(near)


def rows_beside(near, far, k, x):
    even = low_first("gy")
    below = jnp.where(even, far[k, x], near[k, x, W:])
    return below, jnp.where(even, near[k, x, 0:W], far[k, x])


def in_plane_adjoint(v, fy, gy, fz, gz):
    total = fy * up(v, 0) + gy * down(v, 0)
    return total + (fz * up(v, 1) + gz * down(v, 1))


def in_plane_forward(v, fy, gy, fz, gz):
    total = up(gy * v, 0) + down(fy * v, 0)
    return total + (up(gz * v, 1) + down(fz * v, 1))


def in_plane_couplings(u, d):
    first, last = z_ends(u.shape)
    fy = coupling(u, d, up(u, 0), up(d, 0))
    gy = coupling(u, d, down(u, 0), down(d, 0))
    fz = coupling(u, d, jnp.where(last, 0.0, up(u, 1)), jnp.where(last, 0.0, up(d, 1)))
    gz = coupling(
        u, d, jnp.where(first, 0.0, down(u, 1)), jnp.where(first, 0.0, down(d, 1))
    )
    return fy, gy, fz, gz


def face_planes(first_swap, nx):
    at_head = low_first("gx") if first_swap else ~low_first("gx")
    return [jnp.where(at_head, k, nx - 1 - k) for k in range(4)]


def face_fields(u, d, s):
    first, last = z_ends(u[0].shape)

    def between(i, j):
        return coupling(u[i], d[i], u[j], d[j])

    def image(i, before, after):
        fy, gy, fz, gz = in_plane_couplings(u[i], d[i])
        diagonal = 1.0 + ((fy + gy) + (fz + gz)) + (before + after)
        beside = (fy, gy, jnp.where(last, 0.0, fz), jnp.where(first, 0.0, gz))
        total = diagonal * s[i] - before * s[i - 1] - after * s[i + 1]
        total = total - in_plane_adjoint(s[i], *beside)
        return jnp.where(d[i] > 0.0, total, 0.0), diagonal, beside

    back, inward = between(1, 0), between(2, 1)
    near, diagonal, beside = image(1, back, between(1, 2))
    far, _, _ = image(2, inward, between(2, 3))
    rest = diagonal * near - inward * far - in_plane_forward(near, *beside)
    return u[0], d[0], s[0], s[1], between(0, 1), back * near, rest


def pack_face_kernel(first_swap, conc, diff, source, slab):
    planes = face_planes(first_swap, conc.shape[0])
    u, d, s = ([ref[x] for x in planes] for ref in (conc, diff, source))
    for k, v in enumerate(face_fields(u, d, s)):
        slab[k] = v


def pack_face(first_swap, conc, diff, source):
    return pl.pallas_call(
        functools.partial(pack_face_kernel, first_swap),
        out_shape=f32(FIELDS, *conc.shape[1:]),
        in_specs=[VMEM] * 3,
        out_specs=VMEM,
        compiler_params=params(),
        name="pack_face",
    )(conc, diff, source)


def pack_late_kernel(conc, diff, source, near, far, cone, ctwo, near_s, out_s):
    nx, ny, nz = conc.shape
    rows = ny + 2 * W

    def narrow(row):
        if row < ny:
            return row + W if row < W else row - ny + 3 * W
        return row - ny + 3 * W if row < ny + W else row - ny - W

    for first_swap, late in ((True, cone), (False, ctwo)):
        for j, x in enumerate(face_planes(first_swap, nx)):
            for k, ref in enumerate((conc, diff, source)):
                below, above = rows_beside(near, far, k, x)
                near_s[k, j, 0:W] = below
                near_s[k, j, W : 2 * W] = ref[x, 0:W]
                near_s[k, j, 2 * W : 3 * W] = ref[x, ny - W : ny]
                near_s[k, j, 3 * W :] = above
        fields = face_fields(*([near_s[k, j] for j in range(4)] for k in range(3)))
        for k, v in enumerate(fields):
            out_s[k] = v
        row = 0
        for k, begin, n in late_rows(ny):
            at = narrow(begin)
            late[row : row + n] = out_s[k, at : at + n]
            row += n


def pack_late(conc, diff, source, near, far):
    nx, ny, nz = conc.shape
    return pl.pallas_call(
        pack_late_kernel,
        out_shape=(f32(late_count(ny), nz),) * 2,
        in_specs=[VMEM] * 5,
        out_specs=(VMEM,) * 2,
        scratch_shapes=[
            pltpu.VMEM((3, 4, 4 * W, nz), F32),
            pltpu.VMEM((FIELDS, 4 * W, nz), F32),
        ],
        compiler_params=params(),
        name="pack_late",
    )(conc, diff, source, near, far)


def own_kernel(
    conc, diff, source, near, far,
    u_s, d_s, s_s, fx, gx, fy, gy, fz, gz, dg, p1,
):
    nx, ny, nz = conc.shape
    rows = ny + 2 * W
    for k, (own, ref) in enumerate(((conc, u_s), (diff, d_s), (source, s_s))):
        below, above = rows_beside(near, far, k, slice(0, nx))
        ref[:, 0:ny, :] = own[...]
        ref[:, ny : ny + W, :] = above
        ref[:, ny + W :, :] = below
    first, last = z_ends((rows, nz))

    for q in range(nx):
        u, d = u_s[q], d_s[q]
        fyq, gyq, fzq, gzq = in_plane_couplings(u, d)
        total = 1.0 + ((fyq + gyq) + (fzq + gzq))
        if q + 1 < nx:
            fxq = coupling(u, d, u_s[q + 1], d_s[q + 1])
            fx[q] = fxq
            total = total + fxq
        if q > 0:
            gxq = coupling(u, d, u_s[q - 1], d_s[q - 1])
            gx[q] = gxq
            total = total + gxq
        dg[q] = total
        fy[q] = fyq
        gy[q] = gyq
        fz[q] = jnp.where(last, 0.0, fzq)
        gz[q] = jnp.where(first, 0.0, gzq)

    for q in range(1, nx - 1):
        v = s_s[q]
        total = dg[q] * v - fx[q] * s_s[q + 1] - gx[q] * s_s[q - 1]
        total = total - in_plane_adjoint(v, fy[q], gy[q], fz[q], gz[q])
        p1[q] = jnp.where(d_s[q] > 0.0, total, 0.0)


def own(conc, diff, source, near, far):
    nx, ny, nz = conc.shape
    return pl.pallas_call(
        own_kernel,
        out_shape=(f32(nx, ny + 2 * W, nz),) * 11,
        in_specs=[VMEM] * 5,
        out_specs=(VMEM,) * 11,
        compiler_params=params(),
        name="own",
    )(conc, diff, source, near, far)


def square(v, ny):
    mine = v[0:ny]
    return jnp.sum((mine * mine).reshape(ny // 8, 8, mine.shape[1]), axis=0)


def inside_kernel(d_s, s_s, fx, gx, fy, gy, fz, gz, dg, p1, p2, p3, part):
    nx, rows, nz = d_s.shape
    ny = rows - 2 * W
    sums = [jnp.zeros((8, nz), F32) for _ in range(4)]
    for q in range(nx):
        sums[0] = sums[0] + square(s_s[q], ny)
    for q in range(1, nx - 1):
        sums[1] = sums[1] + square(p1[q], ny)
    for q in range(2, nx - 2):
        v = p1[q]
        total = dg[q] * v - gx[q + 1] * p1[q + 1] - fx[q - 1] * p1[q - 1]
        total = total - in_plane_forward(v, fy[q], gy[q], fz[q], gz[q])
        total = jnp.where(d_s[q] > 0.0, total, 0.0)
        p2[q] = total
        sums[2] = sums[2] + square(total, ny)
    for q in range(3, nx - 3):
        v = p2[q]
        total = dg[q] * v - fx[q] * p2[q + 1] - gx[q] * p2[q - 1]
        total = total - in_plane_adjoint(v, fy[q], gy[q], fz[q], gz[q])
        total = jnp.where(d_s[q] > 0.0, total, 0.0)
        p3[q] = total
        sums[3] = sums[3] + square(total, ny)
    for k in range(4):
        part[k] = sums[k]


def inside(d_s, *fields):
    nx, rows, nz = d_s.shape
    return pl.pallas_call(
        inside_kernel,
        out_shape=(f32(nx, rows, nz),) * 2 + (f32(4, 8, nz),),
        in_specs=[VMEM] * 10,
        out_specs=(VMEM,) * 3,
        compiler_params=params(),
        cost_estimate=pl.CostEstimate(
            flops=1 << 22, bytes_accessed=1 << 23, transcendentals=0
        ),
        name="inside",
    )(d_s, *fields)


def finish_kernel(
    u_s, d_s, s_s, fx, gx, fy, gy, fz, gz, dg, p1_in, p2_in, p3_in, part,
    xtwo, xone, cone, ctwo,
    p1_out, p2_out, p3_out, p4_out, moments,
    side_s, edge_s, w_s,
):
    nx, rows, nz = d_s.shape
    ny = rows - 2 * W
    flip = low_first("gx")
    first, last = z_ends((rows, nz))

    for side, one in ((0, flip), (1, ~flip)):
        side_s[side, :, 0:ny] = jnp.where(one, xone[...], xtwo[...])
        side_s[side, :, ny:] = jnp.zeros((FIELDS, 2 * W, nz), F32)
        late = jnp.where(one, cone[...], ctwo[...])
        row = 0
        for field, begin, n in late_rows(ny):
            side_s[side, field, begin : begin + n] = late[row : row + n]
            row += n

    names = dict(
        u=u_s, d=d_s, s=s_s, fx=fx, gx=gx, fy=fy, gy=gy, fz=fz, gz=gz, dg=dg,
        p1=p1_in, p2=p2_in, p3=p3_in,
    )
    place = {(k, q): names[k].at[q] for k in names for q in range(nx)}
    spare = iter(range(w_s.shape[0]))

    def keep(name, q, value):
        place[name, q] = w_s.at[next(spare)]
        place[name, q][...] = value

    def get(name, q):
        return place[name, q][...]

    for side, (o, e, outward, inward) in enumerate(
        ((-1, 0, "gx", "fx"), (nx, nx - 1, "fx", "gx"))
    ):
        beyond = 2 * o - e
        for k, name in enumerate(("u", "d", "s")):
            place[name, o] = side_s.at[side, k]
        place["s", beyond] = side_s.at[side, 3]
        place[outward, o] = side_s.at[side, 4]
        place["m", o] = side_s.at[side, 5]
        place["q", o] = side_s.at[side, 6]
        u, d, ue, de = get("u", o), get("d", o), get("u", e), get("d", e)
        back = coupling(u, d, ue, de)
        out = coupling(ue, de, u, d)
        fyq, gyq, fzq, gzq = in_plane_couplings(u, d)
        total = 1.0 + get(outward, o) + back + ((fyq + gyq) + (fzq + gzq))
        new = {
            (inward, o): back,
            (outward, e): out,
            ("dg", o): total,
            ("dg", e): get("dg", e) + out,
            ("fy", o): fyq,
            ("gy", o): gyq,
            ("fz", o): jnp.where(last, 0.0, fzq),
            ("gz", o): jnp.where(first, 0.0, gzq),
        }
        for k, (key, value) in enumerate(new.items()):
            place[key] = edge_s.at[side, k]
            place[key][...] = value

    def masked(total, q):
        return jnp.where(get("d", q) > 0.0, total, 0.0)

    def in_plane(q):
        return [get(k, q) for k in ("fy", "gy", "fz", "gz")]

    def adjoint_at(w, q):
        v = get(w, q)
        total = get("dg", q) * v - get("fx", q) * get(w, q + 1)
        total = total - get("gx", q) * get(w, q - 1)
        return masked(total - in_plane_adjoint(v, *in_plane(q)), q)

    def forward_at(w, q):
        v = get(w, q)
        above = get("m", q) if q == nx else get("gx", q + 1) * get(w, q + 1)
        below = get("m", q) if q == -1 else get("fx", q - 1) * get(w, q - 1)
        total = get("dg", q) * v - above - below
        return masked(total - in_plane_forward(v, *in_plane(q)), q)

    sums = [part[k] for k in range(4)]

    def sweep(k, apply, w, name, out, ready):
        for q in range(-1, nx + 1):
            if ready <= q < nx - ready:
                out[q] = get(name, q)[0:ny]
                continue
            value = apply(w, q)
            keep(name, q, value)
            if 0 <= q < nx:
                out[q] = value[0:ny]
                sums[k] = sums[k] + square(value, ny)

    sweep(1, adjoint_at, "s", "p1", p1_out, 1)
    sweep(2, forward_at, "p1", "p2", p2_out, 2)
    for o, outward in ((-1, "gx"), (nx, "fx")):
        beyond = -2 if o == -1 else nx + 1
        keep("p2", beyond, get("q", o) - get(outward, o) * get("p1", o))
    sweep(3, adjoint_at, "p2", "p3", p3_out, 3)
    for q in range(nx):
        p4_out[q] = forward_at("p3", q)[0:ny]

    slot = lax.broadcasted_iota(jnp.int32, (1, LANES), 1)
    row = jnp.zeros((1, LANES), F32)
    for k in range(4):
        row = jnp.where(slot == k, jnp.sum(sums[k]), row)
    moments[...] = jnp.broadcast_to(row, moments.shape)


def finish(copies, ny, *fields):
    nx, rows, nz = fields[0].shape
    steps = 4 + 6 + 2 + 8
    return pl.pallas_call(
        finish_kernel,
        out_shape=(f32(nx, ny, nz),) * 4 + (f32(copies, 1, LANES),),
        in_specs=[VMEM] * len(fields),
        out_specs=(VMEM,) * 5,
        scratch_shapes=[
            pltpu.VMEM((2, FIELDS, rows, nz), F32),
            pltpu.VMEM((2, 8, rows, nz), F32),
            pltpu.VMEM((steps, rows, nz), F32),
        ],
        compiler_params=params(),
        name="finish",
    )(*fields)


def combine_kernel(moments, source, p1, p2, p3, p4, adjoint, residual):
    m = jnp.sum(moments[...], axis=0)
    m0, m1, m2, m3 = (m[:, k : k + 1] for k in range(4))
    alpha = m0 / m1
    beta = alpha * (m2 / m1) - 1.0
    grow = 1.0 + beta
    image = grow * grow * m1 - 2.0 * grow * alpha * m2 + alpha * alpha * m3
    step = (beta * m0) / image
    near = alpha + step * grow
    far = step * alpha
    adjoint[...] = near[None] * p1[...] - far[None] * p3[...]
    residual[...] = source[...] - near[None] * p2[...] + far[None] * p4[...]


def combine(moments, source, p1, p2, p3, p4):
    return pl.pallas_call(
        combine_kernel,
        out_shape=(f32(*source.shape),) * 2,
        in_specs=[VMEM] * 6,
        out_specs=(VMEM,) * 2,
        compiler_params=params(),
        name="combine",
    )(moments, source, p1, p2, p3, p4)


def swap(cells, axis, first):
    pairs = [(i, i + 1) for i in range(first, lax.axis_size(axis) - 1, 2)]
    return lax.ppermute(cells, axis, pairs + [(j, i) for i, j in pairs])


def second_neighbours(cells, axis):
    count = lax.axis_size(axis)
    pairs = [(i, i + 2) for i in range(0, count - 2, 2)]
    return lax.ppermute(cells, axis, pairs + [(i, i - 2) for i in range(3, count, 2)])


def local(conc, labels, kappa, source):
    ny = conc.shape[1]
    conc, source, diff = pack(conc, labels, kappa, source)
    xtwo = swap(pack_face(False, conc, diff, source), "gx", 0)
    xone = swap(pack_face(True, conc, diff, source), "gx", 1)
    near = swap(pack_rows(conc, diff, source), "gy", 0)
    far = second_neighbours(relay_rows(near), "gy")
    cone, ctwo = pack_late(conc, diff, source, near, far)
    cone = swap(cone, "gx", 1)
    ctwo = swap(ctwo, "gx", 0)
    fields = own(conc, diff, source, near, far)
    inner = inside(*fields[1:])
    p1, p2, p3, p4, moments = finish(
        lax.axis_size(("gx", "gy")), ny, *fields, *inner, xtwo, xone, cone, ctwo
    )
    moments = lax.all_to_all(moments, ("gx", "gy"), 0, 0, tiled=True)
    return combine(moments, source, p1, p2, p3, p4)


def solution(mesh):
    return jax.shard_map(
        local,
        mesh=mesh,
        in_specs=(P("gx", "gy", None), P("gx", "gy", None), P(), P("gx", "gy", None)),
        out_specs=(P("gx", "gy", None), P("gx", "gy", None)),
        check_vma=False,
    )
```

```python
import functools

import jax
import jax.numpy as jnp
from jax import lax
from jax.experimental import pallas as pl
from jax.experimental.pallas import tpu as pltpu
from jax.sharding import PartitionSpec as P

ITERS = 2
DT = 0.5
W = 2 * ITERS
F32 = jnp.float32
LANES = 128
TILE = 8
VMEM = pl.BlockSpec(memory_space=pltpu.VMEM)


def low_first(axis):
    return lax.axis_index(axis) % 2 == 0


def up(v, axis):
    return pltpu.roll(v, v.shape[axis] - 1, axis)


def down(v, axis):
    return pltpu.roll(v, 1, axis)


def z_ends(shape):
    index = lax.broadcasted_iota(jnp.int32, shape, 1)
    return index == 0, index == shape[1] - 1


def coupling(u, d, un, dn):
    return d + d * u - d * un + dn


def params(megabytes=16):
    return pltpu.CompilerParams(vmem_limit_bytes=megabytes << 20)


def f32(*shape):
    return jax.ShapeDtypeStruct(shape, F32)


FIELDS = 7


def late_rows(ny):
    rows = ny + 2 * W
    for field, n in ((0, 3), (1, 3), (2, 3), (3, 2), (4, 2), (5, 1)):
        yield field, ny, n
        yield field, rows - n, n
    for field, n in ((5, 1), (6, 2)):
        yield field, 0, n
        yield field, ny - n, n


def late_count(ny):
    return sum(n for _, _, n in late_rows(ny))


def pack_kernel(
    kappa_in, conc_in, labels_in, source_in,
    conc, source, diff,
    labels, kappa, sems,
):
    nx, ny, nz = conc.shape
    copies = [
        pltpu.make_async_copy(src, dst, sems.at[k])
        for k, (src, dst) in enumerate(
            (
                (kappa_in, kappa),
                (labels_in, labels),
                (conc_in, conc),
                (source_in, source),
            )
        )
    ]
    for copy in copies:
        copy.start()
    for copy in copies:
        copy.wait()
    k0, k1, k2 = ((0.5 * DT) * kappa[k] for k in range(3))

    def body(x, carry):
        lab = labels[x]
        base = jnp.where(lab == 0, k0, jnp.where(lab == 1, k1, k2))
        diff[x] = base * jnp.exp(conc[x])
        return carry

    lax.fori_loop(0, nx, body, 0, unroll=True)


def pack(conc, labels, kappa, source):
    nx, ny, nz = conc.shape
    outside = [
        pltpu.with_memory_space_constraint(v, pltpu.HBM)
        for v in (kappa, conc, labels, source)
    ]
    return pl.pallas_call(
        pack_kernel,
        out_shape=(f32(nx, ny, nz),) * 3,
        in_specs=[pl.BlockSpec(memory_space=pltpu.HBM)] * 4,
        out_specs=(VMEM,) * 3,
        scratch_shapes=[
            pltpu.VMEM((nx, ny, nz), jnp.int32),
            pltpu.SMEM((3,), F32),
            pltpu.SemaphoreType.DMA((4,)),
        ],
        compiler_params=params(),
        name="pack",
    )(*outside)


def pack_rows_kernel(conc, diff, source, yone, ytwo):
    ny = conc.shape[1]
    nx = conc.shape[0]
    flip = low_first("gy")
    for k, ref in enumerate((conc, diff, source)):
        head = ref[:, 0:TILE, :]
        tail = ref[:, ny - TILE : ny, :]
        yone[k, 0:nx] = jnp.where(flip, head, tail)
        yone[k, nx:] = jnp.zeros((1, TILE, conc.shape[2]), F32)
        ytwo[k] = jnp.where(flip, tail, head)


def pack_rows(conc, diff, source):
    nx, ny, nz = conc.shape
    return pl.pallas_call(
        pack_rows_kernel,
        out_shape=(f32(3, nx + 1, TILE, nz), f32(3, nx, TILE, nz)),
        in_specs=[VMEM] * 3,
        out_specs=(VMEM,) * 2,
        compiler_params=params(),
        name="pack_rows",
    )(conc, diff, source)


def rows_beside(yone, ytwo, k, x):
    flip = low_first("gy")
    low, high = slice(0, W), slice(TILE - W, TILE)
    below = jnp.where(flip, yone[k, x, high], ytwo[k, x, high])
    return below, jnp.where(flip, ytwo[k, x, low], yone[k, x, low])


def in_plane_adjoint(v, fy, gy, fz, gz):
    total = fy * up(v, 0) + gy * down(v, 0)
    return total + (fz * up(v, 1) + gz * down(v, 1))


def in_plane_forward(v, fy, gy, fz, gz):
    total = up(gy * v, 0) + down(fy * v, 0)
    return total + (up(gz * v, 1) + down(fz * v, 1))


def in_plane_couplings(u, d):
    first, last = z_ends(u.shape)
    fy = coupling(u, d, up(u, 0), up(d, 0))
    gy = coupling(u, d, down(u, 0), down(d, 0))
    fz = coupling(u, d, jnp.where(last, 0.0, up(u, 1)), jnp.where(last, 0.0, up(d, 1)))
    gz = coupling(
        u, d, jnp.where(first, 0.0, down(u, 1)), jnp.where(first, 0.0, down(d, 1))
    )
    return fy, gy, fz, gz


def face_planes(first_swap, nx):
    at_head = low_first("gx") if first_swap else ~low_first("gx")
    return [jnp.where(at_head, k, nx - 1 - k) for k in range(4)]


def face_fields(u, d, s):
    first, last = z_ends(u[0].shape)

    def between(i, j):
        return coupling(u[i], d[i], u[j], d[j])

    def image(i, before, after):
        fy, gy, fz, gz = in_plane_couplings(u[i], d[i])
        diagonal = 1.0 + ((fy + gy) + (fz + gz)) + (before + after)
        beside = (fy, gy, jnp.where(last, 0.0, fz), jnp.where(first, 0.0, gz))
        total = diagonal * s[i] - before * s[i - 1] - after * s[i + 1]
        total = total - in_plane_adjoint(s[i], *beside)
        return jnp.where(d[i] > 0.0, total, 0.0), diagonal, beside

    back, inward = between(1, 0), between(2, 1)
    near, diagonal, beside = image(1, back, between(1, 2))
    far, _, _ = image(2, inward, between(2, 3))
    rest = diagonal * near - inward * far - in_plane_forward(near, *beside)
    return u[0], d[0], s[0], s[1], between(0, 1), back * near, rest


def pack_face_kernel(first_swap, conc, diff, source, slab):
    nx, ny, nz = conc.shape
    planes = face_planes(first_swap, nx)
    u, d, s = ([ref[x] for x in planes] for ref in (conc, diff, source))
    for k, v in enumerate(face_fields(u, d, s)):
        slab[k * ny : (k + 1) * ny] = v
    if not first_swap:
        slab[FIELDS * ny :] = jnp.zeros((TILE, nz), F32)


def pack_face(first_swap, conc, diff, source):
    _, ny, nz = conc.shape
    return pl.pallas_call(
        functools.partial(pack_face_kernel, first_swap),
        out_shape=f32(FIELDS * ny + (0 if first_swap else TILE), nz),
        in_specs=[VMEM] * 3,
        out_specs=VMEM,
        compiler_params=params(),
        name="pack_face",
    )(conc, diff, source)


def pack_late_kernel(conc, diff, source, yone, ytwo, cone, ctwo, near_s, out_s):
    nx, ny, nz = conc.shape
    rows = ny + 2 * W

    def narrow(row):
        if row < ny:
            return row + W if row < W else row - ny + 3 * W
        return row - ny + 3 * W if row < ny + W else row - ny - W

    for first_swap, late in ((True, cone), (False, ctwo)):
        for j, x in enumerate(face_planes(first_swap, nx)):
            for k, ref in enumerate((conc, diff, source)):
                below, above = rows_beside(yone, ytwo, k, x)
                near_s[k, j, 0:W] = below
                near_s[k, j, W : 2 * W] = ref[x, 0:W]
                near_s[k, j, 2 * W : 3 * W] = ref[x, ny - W : ny]
                near_s[k, j, 3 * W :] = above
        fields = face_fields(*([near_s[k, j] for j in range(4)] for k in range(3)))
        for k, v in enumerate(fields):
            out_s[k] = v
        row = 0
        for k, begin, n in late_rows(ny):
            at = narrow(begin)
            late[row : row + n] = out_s[k, at : at + n]
            row += n


def pack_late(conc, diff, source, yone, ytwo):
    nx, ny, nz = conc.shape
    return pl.pallas_call(
        pack_late_kernel,
        out_shape=(f32(late_count(ny), nz),) * 2,
        in_specs=[VMEM] * 5,
        out_specs=(VMEM,) * 2,
        scratch_shapes=[
            pltpu.VMEM((3, 4, 4 * W, nz), F32),
            pltpu.VMEM((FIELDS, 4 * W, nz), F32),
        ],
        compiler_params=params(),
        name="pack_late",
    )(conc, diff, source, yone, ytwo)


def own_kernel(
    conc, diff, source, yone, ytwo,
    u_s, d_s, s_s, fx, gx, fy, gy, fz, gz, dg, p1,
):
    nx, ny, nz = conc.shape
    rows = ny + 2 * W
    for k, (own, ref) in enumerate(((conc, u_s), (diff, d_s), (source, s_s))):
        below, above = rows_beside(yone, ytwo, k, slice(0, nx))
        ref[:, 0:ny, :] = own[...]
        ref[:, ny : ny + W, :] = above
        ref[:, ny + W :, :] = below
    first, last = z_ends((rows, nz))

    for q in range(nx):
        u, d = u_s[q], d_s[q]
        fyq, gyq, fzq, gzq = in_plane_couplings(u, d)
        total = 1.0 + ((fyq + gyq) + (fzq + gzq))
        if q + 1 < nx:
            fxq = coupling(u, d, u_s[q + 1], d_s[q + 1])
            fx[q] = fxq
            total = total + fxq
        if q > 0:
            gxq = coupling(u, d, u_s[q - 1], d_s[q - 1])
            gx[q] = gxq
            total = total + gxq
        dg[q] = total
        fy[q] = fyq
        gy[q] = gyq
        fz[q] = jnp.where(last, 0.0, fzq)
        gz[q] = jnp.where(first, 0.0, gzq)

    for q in range(1, nx - 1):
        v = s_s[q]
        total = dg[q] * v - fx[q] * s_s[q + 1] - gx[q] * s_s[q - 1]
        total = total - in_plane_adjoint(v, fy[q], gy[q], fz[q], gz[q])
        p1[q] = jnp.where(d_s[q] > 0.0, total, 0.0)


def own(conc, diff, source, yone, ytwo):
    nx, ny, nz = conc.shape
    return pl.pallas_call(
        own_kernel,
        out_shape=(f32(nx, ny + 2 * W, nz),) * 11,
        in_specs=[VMEM] * 5,
        out_specs=(VMEM,) * 11,
        compiler_params=params(),
        name="own",
    )(conc, diff, source, yone, ytwo)


def square(v, ny):
    mine = v[0:ny]
    return jnp.sum((mine * mine).reshape(ny // 8, 8, mine.shape[1]), axis=0)


def inside_kernel(d_s, s_s, fx, gx, fy, gy, fz, gz, dg, p1, p2, p3, part):
    nx, rows, nz = d_s.shape
    ny = rows - 2 * W
    sums = [jnp.zeros((8, nz), F32) for _ in range(4)]
    for q in range(nx):
        sums[0] = sums[0] + square(s_s[q], ny)
    for q in range(1, nx - 1):
        sums[1] = sums[1] + square(p1[q], ny)
    for q in range(2, nx - 2):
        v = p1[q]
        total = dg[q] * v - gx[q + 1] * p1[q + 1] - fx[q - 1] * p1[q - 1]
        total = total - in_plane_forward(v, fy[q], gy[q], fz[q], gz[q])
        total = jnp.where(d_s[q] > 0.0, total, 0.0)
        p2[q] = total
        sums[2] = sums[2] + square(total, ny)
    for q in range(3, nx - 3):
        v = p2[q]
        total = dg[q] * v - fx[q] * p2[q + 1] - gx[q] * p2[q - 1]
        total = total - in_plane_adjoint(v, fy[q], gy[q], fz[q], gz[q])
        total = jnp.where(d_s[q] > 0.0, total, 0.0)
        p3[q] = total
        sums[3] = sums[3] + square(total, ny)
    for k in range(4):
        part[k] = sums[k]


def inside(d_s, *fields):
    nx, rows, nz = d_s.shape
    return pl.pallas_call(
        inside_kernel,
        out_shape=(f32(nx, rows, nz),) * 2 + (f32(4, 8, nz),),
        in_specs=[VMEM] * 10,
        out_specs=(VMEM,) * 3,
        compiler_params=params(),
        cost_estimate=pl.CostEstimate(
            flops=1 << 22, bytes_accessed=1 << 23, transcendentals=0
        ),
        name="inside",
    )(d_s, *fields)


def finish_kernel(
    u_s, d_s, s_s, fx, gx, fy, gy, fz, gz, dg, p1_in, p2_in, p3_in, part,
    xtwo, xone, cone, ctwo,
    p1_out, p2_out, p3_out, p4_out, moments,
    side_s, edge_s, w_s,
):
    nx, rows, nz = d_s.shape
    ny = rows - 2 * W
    flip = low_first("gx")
    first, last = z_ends((rows, nz))

    for side, one in ((0, flip), (1, ~flip)):
        for k in range(FIELDS):
            plane = slice(k * ny, (k + 1) * ny)
            side_s[side, k, 0:ny] = jnp.where(one, xone[plane], xtwo[plane])
        side_s[side, :, ny:] = jnp.zeros((FIELDS, 2 * W, nz), F32)
        late = jnp.where(one, cone[...], ctwo[...])
        row = 0
        for field, begin, n in late_rows(ny):
            side_s[side, field, begin : begin + n] = late[row : row + n]
            row += n

    names = dict(
        u=u_s, d=d_s, s=s_s, fx=fx, gx=gx, fy=fy, gy=gy, fz=fz, gz=gz, dg=dg,
        p1=p1_in, p2=p2_in, p3=p3_in,
    )
    place = {(k, q): names[k].at[q] for k in names for q in range(nx)}
    spare = iter(range(w_s.shape[0]))

    def keep(name, q, value):
        place[name, q] = w_s.at[next(spare)]
        place[name, q][...] = value

    def get(name, q):
        return place[name, q][...]

    for side, (o, e, outward, inward) in enumerate(
        ((-1, 0, "gx", "fx"), (nx, nx - 1, "fx", "gx"))
    ):
        beyond = 2 * o - e
        for k, name in enumerate(("u", "d", "s")):
            place[name, o] = side_s.at[side, k]
        place["s", beyond] = side_s.at[side, 3]
        place[outward, o] = side_s.at[side, 4]
        place["m", o] = side_s.at[side, 5]
        place["q", o] = side_s.at[side, 6]
        u, d, ue, de = get("u", o), get("d", o), get("u", e), get("d", e)
        back = coupling(u, d, ue, de)
        out = coupling(ue, de, u, d)
        fyq, gyq, fzq, gzq = in_plane_couplings(u, d)
        total = 1.0 + get(outward, o) + back + ((fyq + gyq) + (fzq + gzq))
        new = {
            (inward, o): back,
            (outward, e): out,
            ("dg", o): total,
            ("dg", e): get("dg", e) + out,
            ("fy", o): fyq,
            ("gy", o): gyq,
            ("fz", o): jnp.where(last, 0.0, fzq),
            ("gz", o): jnp.where(first, 0.0, gzq),
        }
        for k, (key, value) in enumerate(new.items()):
            place[key] = edge_s.at[side, k]
            place[key][...] = value

    def masked(total, q):
        return jnp.where(get("d", q) > 0.0, total, 0.0)

    def in_plane(q):
        return [get(k, q) for k in ("fy", "gy", "fz", "gz")]

    def adjoint_at(w, q):
        v = get(w, q)
        total = get("dg", q) * v - get("fx", q) * get(w, q + 1)
        total = total - get("gx", q) * get(w, q - 1)
        return masked(total - in_plane_adjoint(v, *in_plane(q)), q)

    def forward_at(w, q):
        v = get(w, q)
        above = get("m", q) if q == nx else get("gx", q + 1) * get(w, q + 1)
        below = get("m", q) if q == -1 else get("fx", q - 1) * get(w, q - 1)
        total = get("dg", q) * v - above - below
        return masked(total - in_plane_forward(v, *in_plane(q)), q)

    sums = [part[k] for k in range(4)]

    def sweep(k, apply, w, name, out, ready):
        for q in range(-1, nx + 1):
            if ready <= q < nx - ready:
                out[q] = get(name, q)[0:ny]
                continue
            value = apply(w, q)
            keep(name, q, value)
            if 0 <= q < nx:
                out[q] = value[0:ny]
                sums[k] = sums[k] + square(value, ny)

    sweep(1, adjoint_at, "s", "p1", p1_out, 1)
    sweep(2, forward_at, "p1", "p2", p2_out, 2)
    for o, outward in ((-1, "gx"), (nx, "fx")):
        beyond = -2 if o == -1 else nx + 1
        keep("p2", beyond, get("q", o) - get(outward, o) * get("p1", o))
    sweep(3, adjoint_at, "p2", "p3", p3_out, 3)
    for q in range(nx):
        p4_out[q] = forward_at("p3", q)[0:ny]

    slot = lax.broadcasted_iota(jnp.int32, (1, LANES), 1)
    row = jnp.zeros((1, LANES), F32)
    for k in range(4):
        row = jnp.where(slot == k, jnp.sum(sums[k]), row)
    moments[...] = jnp.broadcast_to(row, moments.shape)


def finish(copies, ny, *fields):
    nx, rows, nz = fields[0].shape
    steps = 4 + 6 + 2 + 8
    return pl.pallas_call(
        finish_kernel,
        out_shape=(f32(nx, ny, nz),) * 4 + (f32(copies, 1, LANES),),
        in_specs=[VMEM] * len(fields),
        out_specs=(VMEM,) * 5,
        scratch_shapes=[
            pltpu.VMEM((2, FIELDS, rows, nz), F32),
            pltpu.VMEM((2, 8, rows, nz), F32),
            pltpu.VMEM((steps, rows, nz), F32),
        ],
        compiler_params=params(),
        name="finish",
    )(*fields)


def combine_kernel(moments, source, p1, p2, p3, p4, adjoint, residual):
    m = jnp.sum(moments[...], axis=0)
    m0, m1, m2, m3 = (m[:, k : k + 1] for k in range(4))
    alpha = m0 / m1
    beta = alpha * (m2 / m1) - 1.0
    grow = 1.0 + beta
    image = grow * grow * m1 - 2.0 * grow * alpha * m2 + alpha * alpha * m3
    step = (beta * m0) / image
    near = alpha + step * grow
    far = step * alpha
    adjoint[...] = near[None] * p1[...] - far[None] * p3[...]
    residual[...] = source[...] - near[None] * p2[...] + far[None] * p4[...]


def combine(moments, source, p1, p2, p3, p4):
    return pl.pallas_call(
        combine_kernel,
        out_shape=(f32(*source.shape),) * 2,
        in_specs=[VMEM] * 6,
        out_specs=(VMEM,) * 2,
        compiler_params=params(),
        name="combine",
    )(moments, source, p1, p2, p3, p4)


def swap(cells, axis, first):
    pairs = [(i, i + 1) for i in range(first, lax.axis_size(axis) - 1, 2)]
    return lax.ppermute(cells, axis, pairs + [(j, i) for i, j in pairs])


def local(conc, labels, kappa, source):
    ny = conc.shape[1]
    conc, source, diff = pack(conc, labels, kappa, source)
    xtwo = swap(pack_face(False, conc, diff, source), "gx", 0)
    xone = swap(pack_face(True, conc, diff, source), "gx", 1)
    yone, ytwo = pack_rows(conc, diff, source)
    yone = swap(yone, "gy", 1)
    ytwo = swap(ytwo, "gy", 0)
    cone, ctwo = pack_late(conc, diff, source, yone, ytwo)
    cone = swap(cone, "gx", 1)
    ctwo = swap(ctwo, "gx", 0)
    fields = own(conc, diff, source, yone, ytwo)
    inner = inside(*fields[1:])
    p1, p2, p3, p4, moments = finish(
        lax.axis_size(("gx", "gy")), ny, *fields, *inner, xtwo, xone, cone, ctwo
    )
    moments = lax.all_to_all(moments, ("gx", "gy"), 0, 0, tiled=True)
    return combine(moments, source, p1, p2, p3, p4)


def solution(mesh):
    return jax.shard_map(
        local,
        mesh=mesh,
        in_specs=(P("gx", "gy", None), P("gx", "gy", None), P(), P("gx", "gy", None)),
        out_specs=(P("gx", "gy", None), P("gx", "gy", None)),
        check_vma=False,
    )
```

```python
import functools

import jax
import jax.numpy as jnp
from jax import lax
from jax.experimental import pallas as pl
from jax.experimental.pallas import tpu as pltpu
from jax.sharding import PartitionSpec as P

ITERS = 2
DT = 0.5
W = 2 * ITERS
F32 = jnp.float32
LANES = 128
TILE = 8
VMEM = pl.BlockSpec(memory_space=pltpu.VMEM)


def low_first(axis):
    return lax.axis_index(axis) % 2 == 0


def up(v, axis):
    return pltpu.roll(v, v.shape[axis] - 1, axis)


def down(v, axis):
    return pltpu.roll(v, 1, axis)


def z_ends(shape):
    index = lax.broadcasted_iota(jnp.int32, shape, 1)
    return index == 0, index == shape[1] - 1


def coupling(u, d, un, dn):
    return d + d * u - d * un + dn


def params(megabytes=16):
    return pltpu.CompilerParams(vmem_limit_bytes=megabytes << 20)


def f32(*shape):
    return jax.ShapeDtypeStruct(shape, F32)


FIELDS = 7


def late_rows(ny):
    rows = ny + 2 * W
    for field, n in ((0, 3), (1, 3), (2, 3), (3, 2), (4, 2), (5, 1)):
        yield field, ny, n
        yield field, rows - n, n
    for field, n in ((5, 1), (6, 2)):
        yield field, 0, n
        yield field, ny - n, n


def late_count(ny):
    return sum(n for _, _, n in late_rows(ny))


def pack_kernel(
    kappa_in, conc_in, labels_in, source_in,
    conc, source, diff,
    labels, kappa, sems,
):
    nx, ny, nz = conc.shape
    copies = [
        pltpu.make_async_copy(src, dst, sems.at[k])
        for k, (src, dst) in enumerate(
            (
                (kappa_in, kappa),
                (labels_in, labels),
                (conc_in, conc),
                (source_in, source),
            )
        )
    ]
    for copy in copies:
        copy.start()
    for copy in copies:
        copy.wait()
    k0, k1, k2 = ((0.5 * DT) * kappa[k] for k in range(3))

    def body(x, carry):
        lab = labels[x]
        base = jnp.where(lab == 0, k0, jnp.where(lab == 1, k1, k2))
        diff[x] = base * jnp.exp(conc[x])
        return carry

    lax.fori_loop(0, nx, body, 0, unroll=True)


def pack(conc, labels, kappa, source):
    nx, ny, nz = conc.shape
    outside = [
        pltpu.with_memory_space_constraint(v, pltpu.HBM)
        for v in (kappa, conc, labels, source)
    ]
    return pl.pallas_call(
        pack_kernel,
        out_shape=(f32(nx, ny, nz),) * 3,
        in_specs=[pl.BlockSpec(memory_space=pltpu.HBM)] * 4,
        out_specs=(VMEM,) * 3,
        scratch_shapes=[
            pltpu.VMEM((nx, ny, nz), jnp.int32),
            pltpu.SMEM((3,), F32),
            pltpu.SemaphoreType.DMA((4,)),
        ],
        compiler_params=params(),
        name="pack",
    )(*outside)


def pack_rows_kernel(conc, diff, source, yone, ytwo):
    ny = conc.shape[1]
    flip = low_first("gy")
    for k, ref in enumerate((conc, diff, source)):
        head = ref[:, 0:TILE, :]
        tail = ref[:, ny - TILE : ny, :]
        yone[k] = jnp.where(flip, head, tail)
        ytwo[k] = jnp.where(flip, tail, head)


def pack_rows(conc, diff, source):
    nx, ny, nz = conc.shape
    return pl.pallas_call(
        pack_rows_kernel,
        out_shape=(f32(3, nx, TILE, nz),) * 2,
        in_specs=[VMEM] * 3,
        out_specs=(VMEM,) * 2,
        compiler_params=params(),
        name="pack_rows",
    )(conc, diff, source)


def rows_beside(yone, ytwo, k, x):
    flip = low_first("gy")
    low, high = slice(0, W), slice(TILE - W, TILE)
    below = jnp.where(flip, yone[k, x, high], ytwo[k, x, high])
    return below, jnp.where(flip, ytwo[k, x, low], yone[k, x, low])


def in_plane_adjoint(v, fy, gy, fz, gz):
    total = fy * up(v, 0) + gy * down(v, 0)
    return total + (fz * up(v, 1) + gz * down(v, 1))


def in_plane_forward(v, fy, gy, fz, gz):
    total = up(gy * v, 0) + down(fy * v, 0)
    return total + (up(gz * v, 1) + down(fz * v, 1))


def in_plane_couplings(u, d):
    first, last = z_ends(u.shape)
    fy = coupling(u, d, up(u, 0), up(d, 0))
    gy = coupling(u, d, down(u, 0), down(d, 0))
    fz = coupling(u, d, jnp.where(last, 0.0, up(u, 1)), jnp.where(last, 0.0, up(d, 1)))
    gz = coupling(
        u, d, jnp.where(first, 0.0, down(u, 1)), jnp.where(first, 0.0, down(d, 1))
    )
    return fy, gy, fz, gz


def face_planes(first_swap, nx):
    at_head = low_first("gx") if first_swap else ~low_first("gx")
    return [jnp.where(at_head, k, nx - 1 - k) for k in range(4)]


def face_fields(u, d, s):
    first, last = z_ends(u[0].shape)

    def between(i, j):
        return coupling(u[i], d[i], u[j], d[j])

    def image(i, before, after):
        fy, gy, fz, gz = in_plane_couplings(u[i], d[i])
        diagonal = 1.0 + ((fy + gy) + (fz + gz)) + (before + after)
        beside = (fy, gy, jnp.where(last, 0.0, fz), jnp.where(first, 0.0, gz))
        total = diagonal * s[i] - before * s[i - 1] - after * s[i + 1]
        total = total - in_plane_adjoint(s[i], *beside)
        return jnp.where(d[i] > 0.0, total, 0.0), diagonal, beside

    back, inward = between(1, 0), between(2, 1)
    near, diagonal, beside = image(1, back, between(1, 2))
    far, _, _ = image(2, inward, between(2, 3))
    rest = diagonal * near - inward * far - in_plane_forward(near, *beside)
    return u[0], d[0], s[0], s[1], between(0, 1), back * near, rest


def pack_face_kernel(first_swap, conc, diff, source, slab):
    nx, ny, nz = conc.shape
    planes = face_planes(first_swap, nx)
    u, d, s = ([ref[x] for x in planes] for ref in (conc, diff, source))
    for k, v in enumerate(face_fields(u, d, s)):
        slab[k * ny : (k + 1) * ny] = v
    if not first_swap:
        slab[FIELDS * ny :] = jnp.zeros((TILE, nz), F32)


def pack_face(first_swap, conc, diff, source):
    _, ny, nz = conc.shape
    return pl.pallas_call(
        functools.partial(pack_face_kernel, first_swap),
        out_shape=f32(FIELDS * ny + (0 if first_swap else TILE), nz),
        in_specs=[VMEM] * 3,
        out_specs=VMEM,
        compiler_params=params(),
        name="pack_face",
    )(conc, diff, source)


def pack_late_kernel(conc, diff, source, yone, ytwo, cone, ctwo, near_s, out_s):
    nx, ny, nz = conc.shape
    rows = ny + 2 * W

    def narrow(row):
        if row < ny:
            return row + W if row < W else row - ny + 3 * W
        return row - ny + 3 * W if row < ny + W else row - ny - W

    for first_swap, late in ((True, cone), (False, ctwo)):
        for j, x in enumerate(face_planes(first_swap, nx)):
            for k, ref in enumerate((conc, diff, source)):
                below, above = rows_beside(yone, ytwo, k, x)
                near_s[k, j, 0:W] = below
                near_s[k, j, W : 2 * W] = ref[x, 0:W]
                near_s[k, j, 2 * W : 3 * W] = ref[x, ny - W : ny]
                near_s[k, j, 3 * W :] = above
        fields = face_fields(*([near_s[k, j] for j in range(4)] for k in range(3)))
        for k, v in enumerate(fields):
            out_s[k] = v
        row = 0
        for k, begin, n in late_rows(ny):
            at = narrow(begin)
            late[row : row + n] = out_s[k, at : at + n]
            row += n


def pack_late(conc, diff, source, yone, ytwo):
    nx, ny, nz = conc.shape
    return pl.pallas_call(
        pack_late_kernel,
        out_shape=(f32(late_count(ny), nz),) * 2,
        in_specs=[VMEM] * 5,
        out_specs=(VMEM,) * 2,
        scratch_shapes=[
            pltpu.VMEM((3, 4, 4 * W, nz), F32),
            pltpu.VMEM((FIELDS, 4 * W, nz), F32),
        ],
        compiler_params=params(),
        name="pack_late",
    )(conc, diff, source, yone, ytwo)


def own_kernel(
    conc, diff, source, yone, ytwo,
    u_s, d_s, s_s, fx, gx, fy, gy, fz, gz, dg, p1,
):
    nx, ny, nz = conc.shape
    rows = ny + 2 * W
    for k, (own, ref) in enumerate(((conc, u_s), (diff, d_s), (source, s_s))):
        below, above = rows_beside(yone, ytwo, k, slice(0, nx))
        ref[:, 0:ny, :] = own[...]
        ref[:, ny : ny + W, :] = above
        ref[:, ny + W :, :] = below
    first, last = z_ends((rows, nz))

    for q in range(nx):
        u, d = u_s[q], d_s[q]
        fyq, gyq, fzq, gzq = in_plane_couplings(u, d)
        total = 1.0 + ((fyq + gyq) + (fzq + gzq))
        if q + 1 < nx:
            fxq = coupling(u, d, u_s[q + 1], d_s[q + 1])
            fx[q] = fxq
            total = total + fxq
        if q > 0:
            gxq = coupling(u, d, u_s[q - 1], d_s[q - 1])
            gx[q] = gxq
            total = total + gxq
        dg[q] = total
        fy[q] = fyq
        gy[q] = gyq
        fz[q] = jnp.where(last, 0.0, fzq)
        gz[q] = jnp.where(first, 0.0, gzq)

    for q in range(1, nx - 1):
        v = s_s[q]
        total = dg[q] * v - fx[q] * s_s[q + 1] - gx[q] * s_s[q - 1]
        total = total - in_plane_adjoint(v, fy[q], gy[q], fz[q], gz[q])
        p1[q] = jnp.where(d_s[q] > 0.0, total, 0.0)


def own(conc, diff, source, yone, ytwo):
    nx, ny, nz = conc.shape
    return pl.pallas_call(
        own_kernel,
        out_shape=(f32(nx, ny + 2 * W, nz),) * 11,
        in_specs=[VMEM] * 5,
        out_specs=(VMEM,) * 11,
        compiler_params=params(),
        name="own",
    )(conc, diff, source, yone, ytwo)


def mask_halo(total, d, ny):
    return jnp.concatenate([total[0:ny], jnp.where(d > 0.0, total[ny:], 0.0)], axis=0)


def square(v, ny):
    mine = v[0:ny]
    return jnp.sum((mine * mine).reshape(ny // 8, 8, mine.shape[1]), axis=0)


def inside_kernel(d_s, s_s, fx, gx, fy, gy, fz, gz, dg, p1, p2, p3, part):
    nx, rows, nz = d_s.shape
    ny = rows - 2 * W
    sums = [jnp.zeros((8, nz), F32) for _ in range(4)]
    for q in range(nx):
        sums[0] = sums[0] + square(s_s[q], ny)
    for q in range(1, nx - 1):
        sums[1] = sums[1] + square(p1[q], ny)
    for q in range(2, nx - 2):
        v = p1[q]
        total = dg[q] * v - gx[q + 1] * p1[q + 1] - fx[q - 1] * p1[q - 1]
        total = total - in_plane_forward(v, fy[q], gy[q], fz[q], gz[q])
        total = jnp.where(d_s[q] > 0.0, total, 0.0)
        p2[q] = total
        sums[2] = sums[2] + square(total, ny)
    for q in range(3, nx - 3):
        v = p2[q]
        total = dg[q] * v - fx[q] * p2[q + 1] - gx[q] * p2[q - 1]
        total = total - in_plane_adjoint(v, fy[q], gy[q], fz[q], gz[q])
        total = jnp.where(d_s[q] > 0.0, total, 0.0)
        p3[q] = total
        sums[3] = sums[3] + square(total, ny)
    for k in range(4):
        part[k] = sums[k]


def inside(d_s, *fields):
    nx, rows, nz = d_s.shape
    return pl.pallas_call(
        inside_kernel,
        out_shape=(f32(nx, rows, nz),) * 2 + (f32(4, 8, nz),),
        in_specs=[VMEM] * 10,
        out_specs=(VMEM,) * 3,
        compiler_params=params(),
        cost_estimate=pl.CostEstimate(
            flops=1 << 22, bytes_accessed=1 << 23, transcendentals=0
        ),
        name="inside",
    )(d_s, *fields)


def finish_kernel(
    u_s, d_s, s_s, fx, gx, fy, gy, fz, gz, dg, p1_in, p2_in, p3_in, part,
    xtwo, xone, cone, ctwo,
    p1_out, p2_out, p3_out, p4_out, moments,
    side_s, edge_s, w_s,
):
    nx, rows, nz = d_s.shape
    ny = rows - 2 * W
    flip = low_first("gx")
    first, last = z_ends((rows, nz))

    side_s[:, :, ny:] = jnp.zeros((2, FIELDS, 2 * W, nz), F32)
    for side, slab, late in (
        (jnp.where(flip, 0, 1), xone, cone),
        (jnp.where(flip, 1, 0), xtwo, ctwo),
    ):
        for k in range(FIELDS):
            side_s[side, k, 0:ny] = slab[k * ny : (k + 1) * ny]
        row = 0
        for field, begin, n in late_rows(ny):
            side_s[side, field, begin : begin + n] = late[row : row + n]
            row += n

    names = dict(
        u=u_s, d=d_s, s=s_s, fx=fx, gx=gx, fy=fy, gy=gy, fz=fz, gz=gz, dg=dg,
        p1=p1_in, p2=p2_in, p3=p3_in,
    )
    place = {(k, q): names[k].at[q] for k in names for q in range(nx)}
    spare = iter(range(w_s.shape[0]))

    def keep(name, q, value):
        place[name, q] = w_s.at[next(spare)]
        place[name, q][...] = value

    def get(name, q):
        return place[name, q][...]

    for side, (o, e, outward, inward) in enumerate(
        ((-1, 0, "gx", "fx"), (nx, nx - 1, "fx", "gx"))
    ):
        beyond = 2 * o - e
        for k, name in enumerate(("u", "d", "s")):
            place[name, o] = side_s.at[side, k]
        place["s", beyond] = side_s.at[side, 3]
        place[outward, o] = side_s.at[side, 4]
        place["m", o] = side_s.at[side, 5]
        place["q", o] = side_s.at[side, 6]
        u, d, ue, de = get("u", o), get("d", o), get("u", e), get("d", e)
        back = coupling(u, d, ue, de)
        out = coupling(ue, de, u, d)
        fyq, gyq, fzq, gzq = in_plane_couplings(u, d)
        total = 1.0 + get(outward, o) + back + ((fyq + gyq) + (fzq + gzq))
        new = {
            (inward, o): back,
            (outward, e): out,
            ("dg", o): total,
            ("dg", e): get("dg", e) + out,
            ("fy", o): fyq,
            ("gy", o): gyq,
            ("fz", o): jnp.where(last, 0.0, fzq),
            ("gz", o): jnp.where(first, 0.0, gzq),
        }
        for k, (key, value) in enumerate(new.items()):
            place[key] = edge_s.at[side, k]
            place[key][...] = value

    def masked(total, q):
        if q in (-1, nx):
            return jnp.where(get("d", q) > 0.0, total, 0.0)
        return mask_halo(total, place["d", q][ny:], ny)

    def in_plane(q):
        return [get(k, q) for k in ("fy", "gy", "fz", "gz")]

    def adjoint_at(w, q):
        v = get(w, q)
        total = get("dg", q) * v - get("fx", q) * get(w, q + 1)
        total = total - get("gx", q) * get(w, q - 1)
        return masked(total - in_plane_adjoint(v, *in_plane(q)), q)

    def forward_at(w, q):
        v = get(w, q)
        above = get("m", q) if q == nx else get("gx", q + 1) * get(w, q + 1)
        below = get("m", q) if q == -1 else get("fx", q - 1) * get(w, q - 1)
        total = get("dg", q) * v - above - below
        return masked(total - in_plane_forward(v, *in_plane(q)), q)

    sums = [part[k] for k in range(4)]

    def sweep(k, apply, w, name, out, ready):
        for q in range(-1, nx + 1):
            if ready <= q < nx - ready:
                out[q] = get(name, q)[0:ny]
                continue
            value = apply(w, q)
            keep(name, q, value)
            if 0 <= q < nx:
                out[q] = value[0:ny]
                sums[k] = sums[k] + square(value, ny)

    sweep(1, adjoint_at, "s", "p1", p1_out, 1)
    sweep(2, forward_at, "p1", "p2", p2_out, 2)
    for o, outward in ((-1, "gx"), (nx, "fx")):
        beyond = -2 if o == -1 else nx + 1
        keep("p2", beyond, get("q", o) - get(outward, o) * get("p1", o))
    sweep(3, adjoint_at, "p2", "p3", p3_out, 3)
    for q in range(nx):
        p4_out[q] = forward_at("p3", q)[0:ny]

    slot = lax.broadcasted_iota(jnp.int32, (1, LANES), 1)
    row = jnp.zeros((1, LANES), F32)
    for k in range(4):
        row = jnp.where(slot == k, jnp.sum(sums[k]), row)
    moments[...] = jnp.broadcast_to(row, moments.shape)


def finish(copies, ny, *fields):
    nx, rows, nz = fields[0].shape
    steps = 4 + 6 + 2 + 8
    return pl.pallas_call(
        finish_kernel,
        out_shape=(f32(nx, ny, nz),) * 4 + (f32(copies, 1, LANES),),
        in_specs=[VMEM] * len(fields),
        out_specs=(VMEM,) * 5,
        scratch_shapes=[
            pltpu.VMEM((2, FIELDS, rows, nz), F32),
            pltpu.VMEM((2, 8, rows, nz), F32),
            pltpu.VMEM((steps, rows, nz), F32),
        ],
        compiler_params=params(),
        name="finish",
    )(*fields)


def combine_kernel(moments, source, p1, p2, p3, p4, adjoint, residual):
    m = jnp.sum(moments[...], axis=0)
    m0, m1, m2, m3 = (m[:, k : k + 1] for k in range(4))
    alpha = m0 / m1
    beta = alpha * (m2 / m1) - 1.0
    grow = 1.0 + beta
    image = grow * grow * m1 - 2.0 * grow * alpha * m2 + alpha * alpha * m3
    step = (beta * m0) / image
    near = alpha + step * grow
    far = step * alpha
    adjoint[...] = near[None] * p1[...] - far[None] * p3[...]
    residual[...] = source[...] - near[None] * p2[...] + far[None] * p4[...]


def combine(moments, source, p1, p2, p3, p4):
    return pl.pallas_call(
        combine_kernel,
        out_shape=(f32(*source.shape),) * 2,
        in_specs=[VMEM] * 6,
        out_specs=(VMEM,) * 2,
        compiler_params=params(),
        name="combine",
    )(moments, source, p1, p2, p3, p4)


def swap(cells, axis, first):
    pairs = [(i, i + 1) for i in range(first, lax.axis_size(axis) - 1, 2)]
    return lax.ppermute(cells, axis, pairs + [(j, i) for i, j in pairs])


def local(conc, labels, kappa, source):
    ny = conc.shape[1]
    conc, source, diff = pack(conc, labels, kappa, source)
    xtwo = swap(pack_face(False, conc, diff, source), "gx", 0)
    xone = swap(pack_face(True, conc, diff, source), "gx", 1)
    yone, ytwo = pack_rows(conc, diff, source)
    yone = swap(yone, "gy", 1)
    ytwo = swap(ytwo, "gy", 0)
    cone, ctwo = pack_late(conc, diff, source, yone, ytwo)
    cone = swap(cone, "gx", 1)
    ctwo = swap(ctwo, "gx", 0)
    fields = own(conc, diff, source, yone, ytwo)
    inner = inside(*fields[1:])
    p1, p2, p3, p4, moments = finish(
        lax.axis_size(("gx", "gy")), ny, *fields, *inner, xtwo, xone, cone, ctwo
    )
    moments = lax.all_to_all(moments, ("gx", "gy"), 0, 0, tiled=True)
    return combine(moments, source, p1, p2, p3, p4)


def solution(mesh):
    return jax.shard_map(
        local,
        mesh=mesh,
        in_specs=(P("gx", "gy", None), P("gx", "gy", None), P(), P("gx", "gy", None)),
        out_specs=(P("gx", "gy", None), P("gx", "gy", None)),
        check_vma=False,
    )
```

```python
import functools

import jax
import jax.numpy as jnp
from jax import lax
from jax.experimental import pallas as pl
from jax.experimental.pallas import tpu as pltpu
from jax.sharding import PartitionSpec as P

ITERS = 2
DT = 0.5
W = 2 * ITERS
F32 = jnp.float32
LANES = 128
YROWS = (8, 6)
VMEM = pl.BlockSpec(memory_space=pltpu.VMEM)


def low_first(axis):
    return lax.axis_index(axis) % 2 == 0


def up(v, axis):
    return pltpu.roll(v, v.shape[axis] - 1, axis)


def down(v, axis):
    return pltpu.roll(v, 1, axis)


def z_ends(shape):
    index = lax.broadcasted_iota(jnp.int32, shape, 1)
    return index == 0, index == shape[1] - 1


def coupling(u, d, un, dn):
    return d + d * u - d * un + dn


def params(megabytes=16):
    return pltpu.CompilerParams(vmem_limit_bytes=megabytes << 20)


def f32(*shape):
    return jax.ShapeDtypeStruct(shape, F32)


FIELDS = 7


def late_rows(ny):
    rows = ny + 2 * W
    for field, n in ((0, 3), (1, 3), (2, 3), (3, 2), (4, 2), (5, 1)):
        yield field, ny, n
        yield field, rows - n, n
    for field, n in ((5, 1), (6, 2)):
        yield field, 0, n
        yield field, ny - n, n


def late_count(ny):
    return sum(n for _, _, n in late_rows(ny))


def pack_kernel(
    kappa_in, conc_in, labels_in, source_in,
    conc, source, diff,
    labels, kappa, sems,
):
    nx, ny, nz = conc.shape
    copies = [
        pltpu.make_async_copy(src, dst, sems.at[k])
        for k, (src, dst) in enumerate(
            (
                (kappa_in, kappa),
                (labels_in, labels),
                (conc_in, conc),
                (source_in, source),
            )
        )
    ]
    for copy in copies:
        copy.start()
    for copy in copies:
        copy.wait()
    k0, k1, k2 = ((0.5 * DT) * kappa[k] for k in range(3))

    def body(x, carry):
        lab = labels[x]
        base = jnp.where(lab == 0, k0, jnp.where(lab == 1, k1, k2))
        diff[x] = base * jnp.exp(conc[x])
        return carry

    lax.fori_loop(0, nx, body, 0, unroll=True)


def pack(conc, labels, kappa, source):
    nx, ny, nz = conc.shape
    outside = [
        pltpu.with_memory_space_constraint(v, pltpu.HBM)
        for v in (kappa, conc, labels, source)
    ]
    return pl.pallas_call(
        pack_kernel,
        out_shape=(f32(nx, ny, nz),) * 3,
        in_specs=[pl.BlockSpec(memory_space=pltpu.HBM)] * 4,
        out_specs=(VMEM,) * 3,
        scratch_shapes=[
            pltpu.VMEM((nx, ny, nz), jnp.int32),
            pltpu.SMEM((3,), F32),
            pltpu.SemaphoreType.DMA((4,)),
        ],
        compiler_params=params(),
        name="pack",
    )(*outside)


def pack_rows_kernel(conc, diff, source, yone, ytwo):
    ny = conc.shape[1]
    flip = low_first("gy")
    for k, ref in enumerate((conc, diff, source)):
        for out, n, head in ((yone, YROWS[0], flip), (ytwo, YROWS[1], ~flip)):
            out[k] = jnp.where(head, ref[:, 0:n, :], ref[:, ny - n : ny, :])


def pack_rows(conc, diff, source):
    nx, ny, nz = conc.shape
    return pl.pallas_call(
        pack_rows_kernel,
        out_shape=tuple(f32(3, nx, n, nz) for n in YROWS),
        in_specs=[VMEM] * 3,
        out_specs=(VMEM,) * 2,
        compiler_params=params(),
        name="pack_rows",
    )(conc, diff, source)


def rows_beside(yone, ytwo, k, x):
    flip = low_first("gy")
    one, two = (slice(n - W, n) for n in YROWS)
    below = jnp.where(flip, yone[k, x, one], ytwo[k, x, two])
    return below, jnp.where(flip, ytwo[k, x, 0:W], yone[k, x, 0:W])


def in_plane_adjoint(v, fy, gy, fz, gz):
    total = fy * up(v, 0) + gy * down(v, 0)
    return total + (fz * up(v, 1) + gz * down(v, 1))


def in_plane_forward(v, fy, gy, fz, gz):
    total = up(gy * v, 0) + down(fy * v, 0)
    return total + (up(gz * v, 1) + down(fz * v, 1))


def in_plane_couplings(u, d):
    first, last = z_ends(u.shape)
    fy = coupling(u, d, up(u, 0), up(d, 0))
    gy = coupling(u, d, down(u, 0), down(d, 0))
    fz = coupling(u, d, jnp.where(last, 0.0, up(u, 1)), jnp.where(last, 0.0, up(d, 1)))
    gz = coupling(
        u, d, jnp.where(first, 0.0, down(u, 1)), jnp.where(first, 0.0, down(d, 1))
    )
    return fy, gy, fz, gz


def face_planes(first_swap, nx):
    at_head = low_first("gx") if first_swap else ~low_first("gx")
    return [jnp.where(at_head, k, nx - 1 - k) for k in range(4)]


def face_fields(u, d, s):
    first, last = z_ends(u[0].shape)

    def between(i, j):
        return coupling(u[i], d[i], u[j], d[j])

    def image(i, before, after):
        fy, gy, fz, gz = in_plane_couplings(u[i], d[i])
        diagonal = 1.0 + ((fy + gy) + (fz + gz)) + (before + after)
        beside = (fy, gy, jnp.where(last, 0.0, fz), jnp.where(first, 0.0, gz))
        total = diagonal * s[i] - before * s[i - 1] - after * s[i + 1]
        total = total - in_plane_adjoint(s[i], *beside)
        return jnp.where(d[i] > 0.0, total, 0.0), diagonal, beside

    back, inward = between(1, 0), between(2, 1)
    near, diagonal, beside = image(1, back, between(1, 2))
    far, _, _ = image(2, inward, between(2, 3))
    rest = diagonal * near - inward * far - in_plane_forward(near, *beside)
    return u[0], d[0], s[0], s[1], between(0, 1), back * near, rest


def pack_face_kernel(first_swap, conc, diff, source, *slabs):
    planes = face_planes(first_swap, conc.shape[0])
    u, d, s = ([ref[x] for x in planes] for ref in (conc, diff, source))
    for k, v in enumerate(face_fields(u, d, s)):
        if k < slabs[0].shape[0]:
            slabs[0][k] = v
        else:
            slabs[1][...] = v


def pack_face(first_swap, conc, diff, source):
    plane = conc.shape[1:]
    return pl.pallas_call(
        functools.partial(pack_face_kernel, first_swap),
        out_shape=(f32(FIELDS - 1, *plane), f32(*plane))
        if first_swap
        else f32(FIELDS, *plane),
        in_specs=[VMEM] * 3,
        out_specs=(VMEM, VMEM) if first_swap else VMEM,
        compiler_params=params(),
        name="pack_face",
    )(conc, diff, source)


def pack_late_kernel(
    conc, diff, source, yone, ytwo, rest, cone, ctwo, near_s, out_s
):
    nx, ny, nz = conc.shape
    rows = ny + 2 * W

    def narrow(row):
        if row < ny:
            return row + W if row < W else row - ny + 3 * W
        return row - ny + 3 * W if row < ny + W else row - ny - W

    for first_swap, late in ((True, cone), (False, ctwo)):
        for j, x in enumerate(face_planes(first_swap, nx)):
            for k, ref in enumerate((conc, diff, source)):
                below, above = rows_beside(yone, ytwo, k, x)
                near_s[k, j, 0:W] = below
                near_s[k, j, W : 2 * W] = ref[x, 0:W]
                near_s[k, j, 2 * W : 3 * W] = ref[x, ny - W : ny]
                near_s[k, j, 3 * W :] = above
        fields = face_fields(*([near_s[k, j] for j in range(4)] for k in range(3)))
        for k, v in enumerate(fields):
            out_s[k] = v
        row = 0
        if first_swap:
            late[0:ny] = rest[...]
            row = ny
        for k, begin, n in late_rows(ny):
            at = narrow(begin)
            late[row : row + n] = out_s[k, at : at + n]
            row += n


def pack_late(conc, diff, source, yone, ytwo, rest):
    nx, ny, nz = conc.shape
    return pl.pallas_call(
        pack_late_kernel,
        out_shape=(f32(ny + late_count(ny), nz), f32(late_count(ny), nz)),
        in_specs=[VMEM] * 6,
        out_specs=(VMEM,) * 2,
        scratch_shapes=[
            pltpu.VMEM((3, 4, 4 * W, nz), F32),
            pltpu.VMEM((FIELDS, 4 * W, nz), F32),
        ],
        compiler_params=params(),
        name="pack_late",
    )(conc, diff, source, yone, ytwo, rest)


def own_kernel(
    conc, diff, source, yone, ytwo,
    u_s, d_s, s_s, fx, gx, fy, gy, fz, gz, dg, p1,
):
    nx, ny, nz = conc.shape
    rows = ny + 2 * W
    for k, (own, ref) in enumerate(((conc, u_s), (diff, d_s), (source, s_s))):
        below, above = rows_beside(yone, ytwo, k, slice(0, nx))
        ref[:, 0:ny, :] = own[...]
        ref[:, ny : ny + W, :] = above
        ref[:, ny + W :, :] = below
    first, last = z_ends((rows, nz))

    for q in range(nx):
        u, d = u_s[q], d_s[q]
        fyq, gyq, fzq, gzq = in_plane_couplings(u, d)
        total = 1.0 + ((fyq + gyq) + (fzq + gzq))
        if q + 1 < nx:
            fxq = coupling(u, d, u_s[q + 1], d_s[q + 1])
            fx[q] = fxq
            total = total + fxq
        if q > 0:
            gxq = coupling(u, d, u_s[q - 1], d_s[q - 1])
            gx[q] = gxq
            total = total + gxq
        dg[q] = total
        fy[q] = fyq
        gy[q] = gyq
        fz[q] = jnp.where(last, 0.0, fzq)
        gz[q] = jnp.where(first, 0.0, gzq)

    for q in range(1, nx - 1):
        v = s_s[q]
        total = dg[q] * v - fx[q] * s_s[q + 1] - gx[q] * s_s[q - 1]
        total = total - in_plane_adjoint(v, fy[q], gy[q], fz[q], gz[q])
        p1[q] = jnp.where(d_s[q] > 0.0, total, 0.0)


def own(conc, diff, source, yone, ytwo):
    nx, ny, nz = conc.shape
    return pl.pallas_call(
        own_kernel,
        out_shape=(f32(nx, ny + 2 * W, nz),) * 11,
        in_specs=[VMEM] * 5,
        out_specs=(VMEM,) * 11,
        compiler_params=params(),
        name="own",
    )(conc, diff, source, yone, ytwo)


def mask_halo(total, d, ny):
    return jnp.concatenate([total[0:ny], jnp.where(d > 0.0, total[ny:], 0.0)], axis=0)


def square(v, ny):
    mine = v[0:ny]
    return jnp.sum((mine * mine).reshape(ny // 8, 8, mine.shape[1]), axis=0)


def inside_kernel(d_s, s_s, fx, gx, fy, gy, fz, gz, dg, p1, p2, p3, part):
    nx, rows, nz = d_s.shape
    ny = rows - 2 * W
    sums = [jnp.zeros((8, nz), F32) for _ in range(4)]
    for q in range(nx):
        sums[0] = sums[0] + square(s_s[q], ny)
    for q in range(1, nx - 1):
        sums[1] = sums[1] + square(p1[q], ny)
    for q in range(2, nx - 2):
        v = p1[q]
        total = dg[q] * v - gx[q + 1] * p1[q + 1] - fx[q - 1] * p1[q - 1]
        total = total - in_plane_forward(v, fy[q], gy[q], fz[q], gz[q])
        total = jnp.where(d_s[q] > 0.0, total, 0.0)
        p2[q] = total
        sums[2] = sums[2] + square(total, ny)
    for q in range(3, nx - 3):
        v = p2[q]
        total = dg[q] * v - fx[q] * p2[q + 1] - gx[q] * p2[q - 1]
        total = total - in_plane_adjoint(v, fy[q], gy[q], fz[q], gz[q])
        total = jnp.where(d_s[q] > 0.0, total, 0.0)
        p3[q] = total
        sums[3] = sums[3] + square(total, ny)
    for k in range(4):
        part[k] = sums[k]


def inside(d_s, *fields):
    nx, rows, nz = d_s.shape
    return pl.pallas_call(
        inside_kernel,
        out_shape=(f32(nx, rows, nz),) * 2 + (f32(4, 8, nz),),
        in_specs=[VMEM] * 10,
        out_specs=(VMEM,) * 3,
        compiler_params=params(),
        cost_estimate=pl.CostEstimate(
            flops=1 << 22, bytes_accessed=1 << 23, transcendentals=0
        ),
        name="inside",
    )(d_s, *fields)


def finish_kernel(
    u_s, d_s, s_s, fx, gx, fy, gy, fz, gz, dg, p1_in, p2_in, p3_in, part,
    xtwo, xone, cone, ctwo,
    p1_out, p2_out, p3_out, edge_s, moments,
    side_s, w_s,
):
    nx, rows, nz = d_s.shape
    ny = rows - 2 * W
    flip = low_first("gx")
    first, last = z_ends((rows, nz))

    for side, one in ((0, flip), (1, ~flip)):
        side_s[side, 0 : FIELDS - 1, 0:ny] = jnp.where(
            one, xone[...], xtwo[0 : FIELDS - 1]
        )
        side_s[side, FIELDS - 1, 0:ny] = jnp.where(one, cone[0:ny], xtwo[FIELDS - 1])
        side_s[side, :, ny:] = jnp.zeros((FIELDS, 2 * W, nz), F32)
        late = jnp.where(one, cone[ny:], ctwo[...])
        row = 0
        for field, begin, n in late_rows(ny):
            side_s[side, field, begin : begin + n] = late[row : row + n]
            row += n

    names = dict(
        u=u_s, d=d_s, s=s_s, fx=fx, gx=gx, fy=fy, gy=gy, fz=fz, gz=gz, dg=dg,
        p1=p1_in, p2=p2_in, p3=p3_in,
    )
    place = {(k, q): names[k].at[q] for k in names for q in range(nx)}
    spare = iter(range(w_s.shape[0]))

    def keep(name, q, value):
        place[name, q] = w_s.at[next(spare)]
        place[name, q][...] = value

    def get(name, q):
        return place[name, q][...]

    for side, (o, e, outward, inward) in enumerate(
        ((-1, 0, "gx", "fx"), (nx, nx - 1, "fx", "gx"))
    ):
        beyond = 2 * o - e
        for k, name in enumerate(("u", "d", "s")):
            place[name, o] = side_s.at[side, k]
        place["s", beyond] = side_s.at[side, 3]
        place[outward, o] = side_s.at[side, 4]
        place["m", o] = side_s.at[side, 5]
        place["q", o] = side_s.at[side, 6]
        u, d, ue, de = get("u", o), get("d", o), get("u", e), get("d", e)
        back = coupling(u, d, ue, de)
        out = coupling(ue, de, u, d)
        fyq, gyq, fzq, gzq = in_plane_couplings(u, d)
        total = 1.0 + get(outward, o) + back + ((fyq + gyq) + (fzq + gzq))
        new = {
            (inward, o): back,
            (outward, e): out,
            ("dg", o): total,
            ("dg", e): get("dg", e) + out,
            ("fy", o): fyq,
            ("gy", o): gyq,
            ("fz", o): jnp.where(last, 0.0, fzq),
            ("gz", o): jnp.where(first, 0.0, gzq),
        }
        for k, (key, value) in enumerate(new.items()):
            place[key] = edge_s.at[side, k]
            place[key][...] = value

    def masked(total, q):
        if q in (-1, nx):
            return jnp.where(get("d", q) > 0.0, total, 0.0)
        return mask_halo(total, place["d", q][ny:], ny)

    def in_plane(q):
        return [get(k, q) for k in ("fy", "gy", "fz", "gz")]

    def adjoint_at(w, q):
        v = get(w, q)
        total = get("dg", q) * v - get("fx", q) * get(w, q + 1)
        total = total - get("gx", q) * get(w, q - 1)
        return masked(total - in_plane_adjoint(v, *in_plane(q)), q)

    def forward_at(w, q):
        v = get(w, q)
        above = get("m", q) if q == nx else get("gx", q + 1) * get(w, q + 1)
        below = get("m", q) if q == -1 else get("fx", q - 1) * get(w, q - 1)
        total = get("dg", q) * v - above - below
        return masked(total - in_plane_forward(v, *in_plane(q)), q)

    sums = [part[k] for k in range(4)]

    def sweep(k, apply, w, name, out, ready):
        for q in range(-1, nx + 1):
            if ready <= q < nx - ready:
                out[q] = get(name, q)[0:ny]
                continue
            value = apply(w, q)
            keep(name, q, value)
            if 0 <= q < nx:
                out[q] = value[0:ny]
                sums[k] = sums[k] + square(value, ny)

    sweep(1, adjoint_at, "s", "p1", p1_out, 1)
    sweep(2, forward_at, "p1", "p2", p2_out, 2)
    for o, outward in ((-1, "gx"), (nx, "fx")):
        beyond = -2 if o == -1 else nx + 1
        keep("p2", beyond, get("q", o) - get(outward, o) * get("p1", o))
    for q in range(-1, nx + 1):
        if 3 <= q < nx - 3:
            p3_out[q + 1] = get("p3", q)
            continue
        value = adjoint_at("p2", q)
        p3_out[q + 1] = value
        if 0 <= q < nx:
            sums[3] = sums[3] + square(value, ny)

    slot = lax.broadcasted_iota(jnp.int32, (1, LANES), 1)
    row = jnp.zeros((1, LANES), F32)
    for k in range(4):
        row = jnp.where(slot == k, jnp.sum(sums[k]), row)
    moments[...] = jnp.broadcast_to(row, moments.shape)


def finish(copies, ny, *fields):
    nx, rows, nz = fields[0].shape
    steps = 4 + 6 + 2
    return pl.pallas_call(
        finish_kernel,
        out_shape=(
            f32(nx, ny, nz),
            f32(nx, ny, nz),
            f32(nx + 2, rows, nz),
            f32(2, 8, rows, nz),
            f32(copies, 1, LANES),
        ),
        in_specs=[VMEM] * len(fields),
        out_specs=(VMEM,) * 5,
        scratch_shapes=[
            pltpu.VMEM((2, FIELDS, rows, nz), F32),
            pltpu.VMEM((steps, rows, nz), F32),
        ],
        compiler_params=params(),
        name="finish",
    )(*fields)


def combine_kernel(
    moments, source, p1, p2, p3, edge, fx, gx, fy, gy, fz, gz, dg,
    adjoint_out, residual_out,
    adjoint, residual, sems,
):
    nx, ny, nz = source.shape
    m = jnp.sum(moments[...], axis=0)
    m0, m1, m2, m3 = (m[:, k : k + 1] for k in range(4))
    alpha = m0 / m1
    beta = alpha * (m2 / m1) - 1.0
    grow = 1.0 + beta
    image = grow * grow * m1 - 2.0 * grow * alpha * m2 + alpha * alpha * m3
    step = (beta * m0) / image
    near = alpha + step * grow
    far = step * alpha
    copies = []

    def send(src, dst, begin, end):
        planes = pl.ds(begin, end - begin)
        copies.append(
            pltpu.make_async_copy(src.at[planes], dst.at[planes], sems.at[len(copies)])
        )
        copies[-1].start()

    half = nx // 2
    for begin in (0, half):
        for x in range(begin, begin + half):
            adjoint[x] = near * p1[x] - far * p3[x + 1, 0:ny]
        send(adjoint, adjoint_out, begin, begin + half)
    for x in range(nx):
        v = p3[x + 1]
        above = edge[1, 0] if x == nx - 1 else gx[x + 1]
        below = edge[0, 0] if x == 0 else fx[x - 1]
        diagonal = edge[0, 3] if x == 0 else edge[1, 3] if x == nx - 1 else dg[x]
        p4 = diagonal * v - above * p3[x + 2] - below * p3[x]
        p4 = p4 - in_plane_forward(v, fy[x], gy[x], fz[x], gz[x])
        residual[x] = source[x] - near * p2[x] + far * p4[0:ny]
        if x % 2 == 1:
            send(residual, residual_out, x - 1, x + 1)
    for copy in copies:
        copy.wait()


def combine(moments, source, p1, p2, p3, edge, *couplings):
    nx, ny, nz = source.shape
    return pl.pallas_call(
        combine_kernel,
        out_shape=(f32(nx, ny, nz),) * 2,
        in_specs=[VMEM] * (6 + len(couplings)),
        out_specs=(pl.BlockSpec(memory_space=pltpu.HBM),) * 2,
        scratch_shapes=[
            pltpu.VMEM((nx, ny, nz), F32),
            pltpu.VMEM((nx, ny, nz), F32),
            pltpu.SemaphoreType.DMA((2 + nx // 2,)),
        ],
        compiler_params=params(),
        name="combine",
    )(moments, source, p1, p2, p3, edge, *couplings)


def swap(cells, axis, first):
    pairs = [(i, i + 1) for i in range(first, lax.axis_size(axis) - 1, 2)]
    return lax.ppermute(cells, axis, pairs + [(j, i) for i, j in pairs])


def local(conc, labels, kappa, source):
    ny = conc.shape[1]
    conc, source, diff = pack(conc, labels, kappa, source)
    xtwo = swap(pack_face(False, conc, diff, source), "gx", 0)
    xone, rest = pack_face(True, conc, diff, source)
    xone = swap(xone, "gx", 1)
    yone, ytwo = pack_rows(conc, diff, source)
    yone = swap(yone, "gy", 1)
    ytwo = swap(ytwo, "gy", 0)
    cone, ctwo = pack_late(conc, diff, source, yone, ytwo, rest)
    cone = swap(cone, "gx", 1)
    ctwo = swap(ctwo, "gx", 0)
    fields = own(conc, diff, source, yone, ytwo)
    inner = inside(*fields[1:])
    p1, p2, p3, edge, moments = finish(
        lax.axis_size(("gx", "gy")), ny, *fields, *inner, xtwo, xone, cone, ctwo
    )
    moments = lax.all_to_all(moments, ("gx", "gy"), 0, 0, tiled=True)
    return combine(moments, source, p1, p2, p3, edge, *fields[3:10])


def solution(mesh):
    return jax.shard_map(
        local,
        mesh=mesh,
        in_specs=(P("gx", "gy", None), P("gx", "gy", None), P(), P("gx", "gy", None)),
        out_specs=(P("gx", "gy", None), P("gx", "gy", None)),
        check_vma=False,
    )
```

```python
import functools

import jax
import jax.numpy as jnp
from jax import lax
from jax.experimental import pallas as pl
from jax.experimental.pallas import tpu as pltpu
from jax.sharding import PartitionSpec as P

ITERS = 2
DT = 0.5
W = 2 * ITERS
F32 = jnp.float32
LANES = 128
YROWS = (8, 6)
VMEM = pl.BlockSpec(memory_space=pltpu.VMEM)


def low_first(axis):
    return lax.axis_index(axis) % 2 == 0


def up(v, axis):
    return pltpu.roll(v, v.shape[axis] - 1, axis)


def down(v, axis):
    return pltpu.roll(v, 1, axis)


def z_ends(shape):
    index = lax.broadcasted_iota(jnp.int32, shape, 1)
    return index == 0, index == shape[1] - 1


def coupling(u, d, un, dn):
    return d + d * u - d * un + dn


def params(megabytes=16):
    return pltpu.CompilerParams(vmem_limit_bytes=megabytes << 20)


def f32(*shape):
    return jax.ShapeDtypeStruct(shape, F32)


FIELDS = 7


def late_rows(ny):
    rows = ny + 2 * W
    for field, n in ((0, 3), (1, 3), (2, 3), (3, 2), (4, 2), (5, 1)):
        yield field, ny, n
        yield field, rows - n, n
    for field, n in ((5, 1), (6, 2)):
        yield field, 0, n
        yield field, ny - n, n


def late_count(ny):
    return sum(n for _, _, n in late_rows(ny))


def pack_kernel(
    kappa_in, conc_in, labels_in, source_in,
    conc, source, diff,
    labels, kappa, sems,
):
    nx, ny, nz = conc.shape
    copies = [
        pltpu.make_async_copy(src, dst, sems.at[k])
        for k, (src, dst) in enumerate(
            (
                (labels_in, labels),
                (conc_in, conc),
                (kappa_in, kappa),
                (source_in, source),
            )
        )
    ]
    for copy in copies:
        copy.start()
    for copy in copies[:3]:
        copy.wait()
    k0, k1, k2 = ((0.5 * DT) * kappa[k] for k in range(3))

    def body(x, carry):
        lab = labels[x]
        base = jnp.where(lab == 0, k0, jnp.where(lab == 1, k1, k2))
        diff[x] = base * jnp.exp(conc[x])
        return carry

    lax.fori_loop(0, nx, body, 0, unroll=True)
    copies[3].wait()


def pack(conc, labels, kappa, source):
    nx, ny, nz = conc.shape
    outside = [
        pltpu.with_memory_space_constraint(v, pltpu.HBM)
        for v in (kappa, conc, labels, source)
    ]
    return pl.pallas_call(
        pack_kernel,
        out_shape=(f32(nx, ny, nz),) * 3,
        in_specs=[pl.BlockSpec(memory_space=pltpu.HBM)] * 4,
        out_specs=(VMEM,) * 3,
        scratch_shapes=[
            pltpu.VMEM((nx, ny, nz), jnp.int32),
            pltpu.SMEM((3,), F32),
            pltpu.SemaphoreType.DMA((4,)),
        ],
        compiler_params=params(),
        name="pack",
    )(*outside)


def pack_rows_kernel(conc, diff, source, yone, ytwo):
    ny = conc.shape[1]
    flip = low_first("gy")
    for k, ref in enumerate((conc, diff, source)):
        for out, n, head in ((yone, YROWS[0], flip), (ytwo, YROWS[1], ~flip)):
            out[k] = jnp.where(head, ref[:, 0:n, :], ref[:, ny - n : ny, :])


def pack_rows(conc, diff, source):
    nx, ny, nz = conc.shape
    return pl.pallas_call(
        pack_rows_kernel,
        out_shape=tuple(f32(3, nx, n, nz) for n in YROWS),
        in_specs=[VMEM] * 3,
        out_specs=(VMEM,) * 2,
        compiler_params=params(),
        name="pack_rows",
    )(conc, diff, source)


def rows_beside(yone, ytwo, k, x):
    flip = low_first("gy")
    one, two = (slice(n - W, n) for n in YROWS)
    below = jnp.where(flip, yone[k, x, one], ytwo[k, x, two])
    return below, jnp.where(flip, ytwo[k, x, 0:W], yone[k, x, 0:W])


def in_plane_adjoint(v, fy, gy, fz, gz):
    total = fy * up(v, 0) + gy * down(v, 0)
    return total + (fz * up(v, 1) + gz * down(v, 1))


def in_plane_forward(v, fy, gy, fz, gz):
    total = up(gy * v, 0) + down(fy * v, 0)
    return total + (up(gz * v, 1) + down(fz * v, 1))


def in_plane_couplings(u, d):
    first, last = z_ends(u.shape)
    fy = coupling(u, d, up(u, 0), up(d, 0))
    gy = coupling(u, d, down(u, 0), down(d, 0))
    fz = coupling(u, d, jnp.where(last, 0.0, up(u, 1)), jnp.where(last, 0.0, up(d, 1)))
    gz = coupling(
        u, d, jnp.where(first, 0.0, down(u, 1)), jnp.where(first, 0.0, down(d, 1))
    )
    return fy, gy, fz, gz


def face_planes(first_swap, nx):
    at_head = low_first("gx") if first_swap else ~low_first("gx")
    return [jnp.where(at_head, k, nx - 1 - k) for k in range(4)]


def face_fields(u, d, s):
    first, last = z_ends(u[0].shape)

    def between(i, j):
        return coupling(u[i], d[i], u[j], d[j])

    def image(i, before, after):
        fy, gy, fz, gz = in_plane_couplings(u[i], d[i])
        diagonal = 1.0 + ((fy + gy) + (fz + gz)) + (before + after)
        beside = (fy, gy, jnp.where(last, 0.0, fz), jnp.where(first, 0.0, gz))
        total = diagonal * s[i] - before * s[i - 1] - after * s[i + 1]
        total = total - in_plane_adjoint(s[i], *beside)
        return jnp.where(d[i] > 0.0, total, 0.0), diagonal, beside

    back, inward = between(1, 0), between(2, 1)
    near, diagonal, beside = image(1, back, between(1, 2))
    far, _, _ = image(2, inward, between(2, 3))
    rest = diagonal * near - inward * far - in_plane_forward(near, *beside)
    return u[0], d[0], s[0], s[1], between(0, 1), back * near, rest


def pack_face_kernel(first_swap, conc, diff, source, *slabs):
    planes = face_planes(first_swap, conc.shape[0])
    u, d, s = ([ref[x] for x in planes] for ref in (conc, diff, source))
    for k, v in enumerate(face_fields(u, d, s)):
        if k < slabs[0].shape[0]:
            slabs[0][k] = v
        else:
            slabs[1][...] = v


def pack_face(first_swap, conc, diff, source):
    plane = conc.shape[1:]
    return pl.pallas_call(
        functools.partial(pack_face_kernel, first_swap),
        out_shape=(f32(FIELDS - 1, *plane), f32(*plane))
        if first_swap
        else f32(FIELDS, *plane),
        in_specs=[VMEM] * 3,
        out_specs=(VMEM, VMEM) if first_swap else VMEM,
        compiler_params=params(),
        name="pack_face",
    )(conc, diff, source)


def pack_late_kernel(
    conc, diff, source, yone, ytwo, rest, cone, ctwo, near_s, out_s
):
    nx, ny, nz = conc.shape
    rows = ny + 2 * W

    def narrow(row):
        if row < ny:
            return row + W if row < W else row - ny + 3 * W
        return row - ny + 3 * W if row < ny + W else row - ny - W

    for first_swap, late in ((True, cone), (False, ctwo)):
        for j, x in enumerate(face_planes(first_swap, nx)):
            for k, ref in enumerate((conc, diff, source)):
                below, above = rows_beside(yone, ytwo, k, x)
                near_s[k, j, 0:W] = below
                near_s[k, j, W : 2 * W] = ref[x, 0:W]
                near_s[k, j, 2 * W : 3 * W] = ref[x, ny - W : ny]
                near_s[k, j, 3 * W :] = above
        fields = face_fields(*([near_s[k, j] for j in range(4)] for k in range(3)))
        for k, v in enumerate(fields):
            out_s[k] = v
        row = 0
        if first_swap:
            late[0:ny] = rest[...]
            row = ny
        for k, begin, n in late_rows(ny):
            at = narrow(begin)
            if first_swap and k == FIELDS - 1:
                late[begin : begin + n] = out_s[k, at : at + n]
                continue
            late[row : row + n] = out_s[k, at : at + n]
            row += n


def pack_late(conc, diff, source, yone, ytwo, rest):
    nx, ny, nz = conc.shape
    return pl.pallas_call(
        pack_late_kernel,
        out_shape=(f32(ny + late_count(ny) - 4, nz), f32(late_count(ny), nz)),
        in_specs=[VMEM] * 6,
        out_specs=(VMEM,) * 2,
        scratch_shapes=[
            pltpu.VMEM((3, 4, 4 * W, nz), F32),
            pltpu.VMEM((FIELDS, 4 * W, nz), F32),
        ],
        compiler_params=params(),
        name="pack_late",
    )(conc, diff, source, yone, ytwo, rest)


def own_kernel(
    conc, diff, source, yone, ytwo,
    u_s, d_s, s_s, fx, gx, fy, gy, fz, gz, dg, p1,
):
    nx, ny, nz = conc.shape
    rows = ny + 2 * W
    for k, (own, ref) in enumerate(((conc, u_s), (diff, d_s), (source, s_s))):
        below, above = rows_beside(yone, ytwo, k, slice(0, nx))
        ref[:, 0:ny, :] = own[...]
        ref[:, ny : ny + W, :] = above
        ref[:, ny + W :, :] = below
    first, last = z_ends((rows, nz))

    for q in range(nx):
        u, d = u_s[q], d_s[q]
        fyq, gyq, fzq, gzq = in_plane_couplings(u, d)
        total = 1.0 + ((fyq + gyq) + (fzq + gzq))
        if q + 1 < nx:
            fxq = coupling(u, d, u_s[q + 1], d_s[q + 1])
            fx[q] = fxq
            total = total + fxq
        if q > 0:
            gxq = coupling(u, d, u_s[q - 1], d_s[q - 1])
            gx[q] = gxq
            total = total + gxq
        dg[q] = total
        fy[q] = fyq
        gy[q] = gyq
        fz[q] = jnp.where(last, 0.0, fzq)
        gz[q] = jnp.where(first, 0.0, gzq)

    for q in range(1, nx - 1):
        v = s_s[q]
        total = dg[q] * v - fx[q] * s_s[q + 1] - gx[q] * s_s[q - 1]
        total = total - in_plane_adjoint(v, fy[q], gy[q], fz[q], gz[q])
        p1[q] = jnp.where(d_s[q] > 0.0, total, 0.0)


def own(conc, diff, source, yone, ytwo):
    nx, ny, nz = conc.shape
    return pl.pallas_call(
        own_kernel,
        out_shape=(f32(nx, ny + 2 * W, nz),) * 11,
        in_specs=[VMEM] * 5,
        out_specs=(VMEM,) * 11,
        compiler_params=params(),
        name="own",
    )(conc, diff, source, yone, ytwo)


def mask_halo(total, d, ny):
    return jnp.concatenate([total[0:ny], jnp.where(d > 0.0, total[ny:], 0.0)], axis=0)


def square(v, ny):
    mine = v[0:ny]
    return jnp.sum((mine * mine).reshape(ny // 8, 8, mine.shape[1]), axis=0)


def inside_kernel(d_s, s_s, fx, gx, fy, gy, fz, gz, dg, p1, p2, p3, part):
    nx, rows, nz = d_s.shape
    ny = rows - 2 * W
    sums = [jnp.zeros((8, nz), F32) for _ in range(4)]
    for q in range(nx):
        sums[0] = sums[0] + square(s_s[q], ny)
    for q in range(1, nx - 1):
        sums[1] = sums[1] + square(p1[q], ny)
    for q in range(2, nx - 2):
        v = p1[q]
        total = dg[q] * v - gx[q + 1] * p1[q + 1] - fx[q - 1] * p1[q - 1]
        total = total - in_plane_forward(v, fy[q], gy[q], fz[q], gz[q])
        total = jnp.where(d_s[q] > 0.0, total, 0.0)
        p2[q] = total
        sums[2] = sums[2] + square(total, ny)
    for q in range(3, nx - 3):
        v = p2[q]
        total = dg[q] * v - fx[q] * p2[q + 1] - gx[q] * p2[q - 1]
        total = total - in_plane_adjoint(v, fy[q], gy[q], fz[q], gz[q])
        total = jnp.where(d_s[q] > 0.0, total, 0.0)
        p3[q] = total
        sums[3] = sums[3] + square(total, ny)
    for k in range(4):
        part[k] = sums[k]


def inside(d_s, *fields):
    nx, rows, nz = d_s.shape
    return pl.pallas_call(
        inside_kernel,
        out_shape=(f32(nx, rows, nz),) * 2 + (f32(4, 8, nz),),
        in_specs=[VMEM] * 10,
        out_specs=(VMEM,) * 3,
        compiler_params=params(),
        cost_estimate=pl.CostEstimate(
            flops=1 << 22, bytes_accessed=1 << 23, transcendentals=0
        ),
        name="inside",
    )(d_s, *fields)


def finish_kernel(
    u_s, d_s, s_s, fx, gx, fy, gy, fz, gz, dg, p1_in, p2_in, p3_in, part,
    xtwo, xone, cone, ctwo,
    p1_out, p2_out, p3_out, edge_s, moments,
    side_s, w_s,
):
    nx, rows, nz = d_s.shape
    ny = rows - 2 * W
    flip = low_first("gx")
    first, last = z_ends((rows, nz))

    for side, one in ((0, flip), (1, ~flip)):
        side_s[side, 0 : FIELDS - 1, 0:ny] = jnp.where(
            one, xone[...], xtwo[0 : FIELDS - 1]
        )
        side_s[side, FIELDS - 1, 0:ny] = jnp.where(one, cone[0:ny], xtwo[FIELDS - 1])
        side_s[side, :, ny:] = jnp.zeros((FIELDS, 2 * W, nz), F32)
        common = late_count(ny) - 4
        late = jnp.where(one, cone[ny:], ctwo[0:common])
        row = 0
        for field, begin, n in late_rows(ny):
            if field == FIELDS - 1:
                rows_q = jnp.where(one, cone[begin : begin + n], ctwo[row : row + n])
                side_s[side, field, begin : begin + n] = rows_q
            else:
                side_s[side, field, begin : begin + n] = late[row : row + n]
            row += n

    names = dict(
        u=u_s, d=d_s, s=s_s, fx=fx, gx=gx, fy=fy, gy=gy, fz=fz, gz=gz, dg=dg,
        p1=p1_in, p2=p2_in, p3=p3_in,
    )
    place = {(k, q): names[k].at[q] for k in names for q in range(nx)}
    spare = iter(range(w_s.shape[0]))

    def keep(name, q, value):
        place[name, q] = w_s.at[next(spare)]
        place[name, q][...] = value

    def get(name, q):
        return place[name, q][...]

    for side, (o, e, outward, inward) in enumerate(
        ((-1, 0, "gx", "fx"), (nx, nx - 1, "fx", "gx"))
    ):
        beyond = 2 * o - e
        for k, name in enumerate(("u", "d", "s")):
            place[name, o] = side_s.at[side, k]
        place["s", beyond] = side_s.at[side, 3]
        place[outward, o] = side_s.at[side, 4]
        place["m", o] = side_s.at[side, 5]
        place["q", o] = side_s.at[side, 6]
        u, d, ue, de = get("u", o), get("d", o), get("u", e), get("d", e)
        back = coupling(u, d, ue, de)
        out = coupling(ue, de, u, d)
        fyq, gyq, fzq, gzq = in_plane_couplings(u, d)
        total = 1.0 + get(outward, o) + back + ((fyq + gyq) + (fzq + gzq))
        new = {
            (inward, o): back,
            (outward, e): out,
            ("dg", o): total,
            ("dg", e): get("dg", e) + out,
            ("fy", o): fyq,
            ("gy", o): gyq,
            ("fz", o): jnp.where(last, 0.0, fzq),
            ("gz", o): jnp.where(first, 0.0, gzq),
        }
        for k, (key, value) in enumerate(new.items()):
            place[key] = edge_s.at[side, k]
            place[key][...] = value

    def masked(total, q):
        if q in (-1, nx):
            return jnp.where(get("d", q) > 0.0, total, 0.0)
        return mask_halo(total, place["d", q][ny:], ny)

    def in_plane(q):
        return [get(k, q) for k in ("fy", "gy", "fz", "gz")]

    def adjoint_at(w, q):
        v = get(w, q)
        total = get("dg", q) * v - get("fx", q) * get(w, q + 1)
        total = total - get("gx", q) * get(w, q - 1)
        return masked(total - in_plane_adjoint(v, *in_plane(q)), q)

    def forward_at(w, q):
        v = get(w, q)
        above = get("m", q) if q == nx else get("gx", q + 1) * get(w, q + 1)
        below = get("m", q) if q == -1 else get("fx", q - 1) * get(w, q - 1)
        total = get("dg", q) * v - above - below
        return masked(total - in_plane_forward(v, *in_plane(q)), q)

    sums = [part[k] for k in range(4)]

    def sweep(k, apply, w, name, out, ready):
        for q in range(-1, nx + 1):
            if ready <= q < nx - ready:
                out[q] = get(name, q)[0:ny]
                continue
            value = apply(w, q)
            keep(name, q, value)
            if 0 <= q < nx:
                out[q] = value[0:ny]
                sums[k] = sums[k] + square(value, ny)

    sweep(1, adjoint_at, "s", "p1", p1_out, 1)
    sweep(2, forward_at, "p1", "p2", p2_out, 2)
    for o, outward in ((-1, "gx"), (nx, "fx")):
        beyond = -2 if o == -1 else nx + 1
        keep("p2", beyond, get("q", o) - get(outward, o) * get("p1", o))
    for q in range(-1, nx + 1):
        if 3 <= q < nx - 3:
            p3_out[q + 1] = get("p3", q)
            continue
        value = adjoint_at("p2", q)
        p3_out[q + 1] = value
        if 0 <= q < nx:
            sums[3] = sums[3] + square(value, ny)

    slot = lax.broadcasted_iota(jnp.int32, (1, LANES), 1)
    row = jnp.zeros((1, LANES), F32)
    for k in range(4):
        row = jnp.where(slot == k, jnp.sum(sums[k]), row)
    moments[...] = jnp.broadcast_to(row, moments.shape)


def finish(copies, ny, *fields):
    nx, rows, nz = fields[0].shape
    steps = 4 + 6 + 2
    return pl.pallas_call(
        finish_kernel,
        out_shape=(
            f32(nx, ny, nz),
            f32(nx, ny, nz),
            f32(nx + 2, rows, nz),
            f32(2, 8, rows, nz),
            f32(copies, 1, LANES),
        ),
        in_specs=[VMEM] * len(fields),
        out_specs=(VMEM,) * 5,
        scratch_shapes=[
            pltpu.VMEM((2, FIELDS, rows, nz), F32),
            pltpu.VMEM((steps, rows, nz), F32),
        ],
        compiler_params=params(),
        name="finish",
    )(*fields)


def combine_kernel(
    moments, source, p1, p2, p3, edge, fx, gx, fy, gy, fz, gz, dg,
    adjoint_out, residual_out,
    adjoint, residual, sems,
):
    nx, ny, nz = source.shape
    m = jnp.sum(moments[...], axis=0)
    m0, m1, m2, m3 = (m[:, k : k + 1] for k in range(4))
    alpha = m0 / m1
    beta = alpha * (m2 / m1) - 1.0
    grow = 1.0 + beta
    image = grow * grow * m1 - 2.0 * grow * alpha * m2 + alpha * alpha * m3
    step = (beta * m0) / image
    near = alpha + step * grow
    far = step * alpha
    for x in range(nx):
        v = p3[x + 1]
        above = edge[1, 0] if x == nx - 1 else gx[x + 1]
        below = edge[0, 0] if x == 0 else fx[x - 1]
        diagonal = edge[0, 3] if x == 0 else edge[1, 3] if x == nx - 1 else dg[x]
        p4 = diagonal * v - above * p3[x + 2] - below * p3[x]
        p4 = p4 - in_plane_forward(v, fy[x], gy[x], fz[x], gz[x])
        residual[x] = p4[0:ny]
    copies = []
    half = nx // 2
    for begin in (0, half):
        for x in range(begin, begin + half):
            adjoint[x] = near * p1[x] - far * p3[x + 1, 0:ny]
            residual[x] = source[x] - near * p2[x] + far * residual[x]
        planes = pl.ds(begin, half)
        for src, dst in ((adjoint, adjoint_out), (residual, residual_out)):
            copies.append(
                pltpu.make_async_copy(
                    src.at[planes], dst.at[planes], sems.at[len(copies)]
                )
            )
            copies[-1].start()
    for copy in copies:
        copy.wait()


def combine(moments, source, p1, p2, p3, edge, *couplings):
    nx, ny, nz = source.shape
    return pl.pallas_call(
        combine_kernel,
        out_shape=(f32(nx, ny, nz),) * 2,
        in_specs=[VMEM] * (6 + len(couplings)),
        out_specs=(pl.BlockSpec(memory_space=pltpu.HBM),) * 2,
        scratch_shapes=[
            pltpu.VMEM((nx, ny, nz), F32),
            pltpu.VMEM((nx, ny, nz), F32),
            pltpu.SemaphoreType.DMA((4,)),
        ],
        compiler_params=params(),
        name="combine",
    )(moments, source, p1, p2, p3, edge, *couplings)


def swap(cells, axis, first):
    pairs = [(i, i + 1) for i in range(first, lax.axis_size(axis) - 1, 2)]
    return lax.ppermute(cells, axis, pairs + [(j, i) for i, j in pairs])


def local(conc, labels, kappa, source):
    ny = conc.shape[1]
    conc, source, diff = pack(conc, labels, kappa, source)
    xtwo = swap(pack_face(False, conc, diff, source), "gx", 0)
    xone, rest = pack_face(True, conc, diff, source)
    xone = swap(xone, "gx", 1)
    yone, ytwo = pack_rows(conc, diff, source)
    yone = swap(yone, "gy", 1)
    ytwo = swap(ytwo, "gy", 0)
    cone, ctwo = pack_late(conc, diff, source, yone, ytwo, rest)
    cone = swap(cone, "gx", 1)
    ctwo = swap(ctwo, "gx", 0)
    fields = own(conc, diff, source, yone, ytwo)
    inner = inside(*fields[1:])
    p1, p2, p3, edge, moments = finish(
        lax.axis_size(("gx", "gy")), ny, *fields, *inner, xtwo, xone, cone, ctwo
    )
    moments = lax.all_to_all(moments, ("gx", "gy"), 0, 0, tiled=True)
    return combine(moments, source, p1, p2, p3, edge, *fields[3:10])


def solution(mesh):
    return jax.shard_map(
        local,
        mesh=mesh,
        in_specs=(P("gx", "gy", None), P("gx", "gy", None), P(), P("gx", "gy", None)),
        out_specs=(P("gx", "gy", None), P("gx", "gy", None)),
        check_vma=False,
    )
```

```python
import functools

import jax
import jax.numpy as jnp
from jax import lax
from jax.experimental import pallas as pl
from jax.experimental.pallas import tpu as pltpu
from jax.sharding import PartitionSpec as P

ITERS = 2
DT = 0.5
W = 2 * ITERS
F32 = jnp.float32
LANES = 128
SPARE = 1
YROWS = (8, 6)
VMEM = pl.BlockSpec(memory_space=pltpu.VMEM)


def low_first(axis):
    return lax.axis_index(axis) % 2 == 0


def up(v, axis):
    return pltpu.roll(v, v.shape[axis] - 1, axis)


def down(v, axis):
    return pltpu.roll(v, 1, axis)


def z_ends(shape):
    index = lax.broadcasted_iota(jnp.int32, shape, 1)
    return index == 0, index == shape[1] - 1


def coupling(u, d, un, dn):
    return d + d * u - d * un + dn


def params(megabytes=16):
    return pltpu.CompilerParams(vmem_limit_bytes=megabytes << 20)


def f32(*shape):
    return jax.ShapeDtypeStruct(shape, F32)


FIELDS = 7


def late_rows(ny):
    rows = ny + 2 * W
    for field, n in ((0, 3), (1, 3), (2, 3), (3, 2), (4, 2), (5, 1)):
        yield field, ny, n
        yield field, rows - n, n
    for field, n in ((5, 1), (6, 2)):
        yield field, 0, n
        yield field, ny - n, n


def late_count(ny):
    return sum(n for _, _, n in late_rows(ny))


def pack_kernel(
    kappa_in, conc_in, labels_in, source_in,
    conc, source, diff,
    labels, kappa, sems,
):
    nx, ny, nz = conc.shape
    copies = [
        pltpu.make_async_copy(src, dst, sems.at[k])
        for k, (src, dst) in enumerate(
            (
                (labels_in, labels),
                (conc_in, conc),
                (kappa_in, kappa),
                (source_in, source),
            )
        )
    ]
    for copy in copies:
        copy.start()
    for copy in copies[:3]:
        copy.wait()
    k0, k1, k2 = ((0.5 * DT) * kappa[k] for k in range(3))

    def body(x, carry):
        lab = labels[x]
        base = jnp.where(lab == 0, k0, jnp.where(lab == 1, k1, k2))
        diff[x] = base * jnp.exp(conc[x])
        return carry

    lax.fori_loop(0, nx, body, 0, unroll=True)
    copies[3].wait()


def pack(conc, labels, kappa, source):
    nx, ny, nz = conc.shape
    outside = [
        pltpu.with_memory_space_constraint(v, pltpu.HBM)
        for v in (kappa, conc, labels, source)
    ]
    return pl.pallas_call(
        pack_kernel,
        out_shape=(f32(nx, ny, nz),) * 3,
        in_specs=[pl.BlockSpec(memory_space=pltpu.HBM)] * 4,
        out_specs=(VMEM,) * 3,
        scratch_shapes=[
            pltpu.VMEM((nx, ny, nz), jnp.int32),
            pltpu.SMEM((3,), F32),
            pltpu.SemaphoreType.DMA((4,)),
        ],
        compiler_params=params(),
        name="pack",
    )(*outside)


def pack_rows_kernel(conc, diff, source, yone, ytwo):
    ny = conc.shape[1]
    flip = low_first("gy")
    for k, ref in enumerate((conc, diff, source)):
        for out, n, head in ((yone, YROWS[0], flip), (ytwo, YROWS[1], ~flip)):
            out[k] = jnp.where(head, ref[:, 0:n, :], ref[:, ny - n : ny, :])


def pack_rows(conc, diff, source):
    nx, ny, nz = conc.shape
    return pl.pallas_call(
        pack_rows_kernel,
        out_shape=tuple(f32(3, nx, n, nz) for n in YROWS),
        in_specs=[VMEM] * 3,
        out_specs=(VMEM,) * 2,
        compiler_params=params(),
        name="pack_rows",
    )(conc, diff, source)


def rows_beside(yone, ytwo, k, x):
    flip = low_first("gy")
    one, two = (slice(n - W, n) for n in YROWS)
    below = jnp.where(flip, yone[k, x, one], ytwo[k, x, two])
    return below, jnp.where(flip, ytwo[k, x, 0:W], yone[k, x, 0:W])


def in_plane_adjoint(v, fy, gy, fz, gz):
    total = fy * up(v, 0) + gy * down(v, 0)
    return total + (fz * up(v, 1) + gz * down(v, 1))


def in_plane_forward(v, fy, gy, fz, gz):
    total = up(gy * v, 0) + down(fy * v, 0)
    return total + (up(gz * v, 1) + down(fz * v, 1))


def in_plane_couplings(u, d):
    first, last = z_ends(u.shape)
    fy = coupling(u, d, up(u, 0), up(d, 0))
    gy = coupling(u, d, down(u, 0), down(d, 0))
    fz = coupling(u, d, jnp.where(last, 0.0, up(u, 1)), jnp.where(last, 0.0, up(d, 1)))
    gz = coupling(
        u, d, jnp.where(first, 0.0, down(u, 1)), jnp.where(first, 0.0, down(d, 1))
    )
    return fy, gy, fz, gz


def face_planes(first_swap, nx):
    at_head = low_first("gx") if first_swap else ~low_first("gx")
    return [jnp.where(at_head, k, nx - 1 - k) for k in range(4)]


def face_fields(u, d, s):
    first, last = z_ends(u[0].shape)

    def between(i, j):
        return coupling(u[i], d[i], u[j], d[j])

    def image(i, before, after):
        fy, gy, fz, gz = in_plane_couplings(u[i], d[i])
        diagonal = 1.0 + ((fy + gy) + (fz + gz)) + (before + after)
        beside = (fy, gy, jnp.where(last, 0.0, fz), jnp.where(first, 0.0, gz))
        total = diagonal * s[i] - before * s[i - 1] - after * s[i + 1]
        total = total - in_plane_adjoint(s[i], *beside)
        return jnp.where(d[i] > 0.0, total, 0.0), diagonal, beside

    back, inward = between(1, 0), between(2, 1)
    near, diagonal, beside = image(1, back, between(1, 2))
    far, _, _ = image(2, inward, between(2, 3))
    rest = diagonal * near - inward * far - in_plane_forward(near, *beside)
    return u[0], d[0], s[0], s[1], between(0, 1), back * near, rest


def pack_face_kernel(first_swap, conc, diff, source, *slabs):
    planes = face_planes(first_swap, conc.shape[0])
    u, d, s = ([ref[x] for x in planes] for ref in (conc, diff, source))
    for k, v in enumerate(face_fields(u, d, s)):
        if k < slabs[0].shape[0]:
            slabs[0][k] = v
        else:
            slabs[1][...] = v


def pack_face(first_swap, conc, diff, source):
    plane = conc.shape[1:]
    return pl.pallas_call(
        functools.partial(pack_face_kernel, first_swap),
        out_shape=(f32(FIELDS - 1, *plane), f32(*plane))
        if first_swap
        else f32(FIELDS, *plane),
        in_specs=[VMEM] * 3,
        out_specs=(VMEM, VMEM) if first_swap else VMEM,
        compiler_params=params(),
        name="pack_face",
    )(conc, diff, source)


def pack_late_kernel(
    conc, diff, source, yone, ytwo, rest, cone, ctwo, near_s, out_s
):
    nx, ny, nz = conc.shape
    rows = ny + 2 * W

    def narrow(row):
        if row < ny:
            return row + W if row < W else row - ny + 3 * W
        return row - ny + 3 * W if row < ny + W else row - ny - W

    for first_swap, late in ((True, cone), (False, ctwo)):
        for j, x in enumerate(face_planes(first_swap, nx)):
            for k, ref in enumerate((conc, diff, source)):
                below, above = rows_beside(yone, ytwo, k, x)
                near_s[k, j, 0:W] = below
                near_s[k, j, W : 2 * W] = ref[x, 0:W]
                near_s[k, j, 2 * W : 3 * W] = ref[x, ny - W : ny]
                near_s[k, j, 3 * W :] = above
        fields = face_fields(*([near_s[k, j] for j in range(4)] for k in range(3)))
        for k, v in enumerate(fields):
            out_s[k] = v
        row = 0
        if first_swap:
            late[0:ny] = rest[...]
            row = ny
        for k, begin, n in late_rows(ny):
            at = narrow(begin)
            if first_swap and k == FIELDS - 1:
                late[begin : begin + n] = out_s[k, at : at + n]
                continue
            late[row : row + n] = out_s[k, at : at + n]
            row += n


def pack_late(conc, diff, source, yone, ytwo, rest):
    nx, ny, nz = conc.shape
    return pl.pallas_call(
        pack_late_kernel,
        out_shape=(f32(ny + late_count(ny) - 4, nz), f32(late_count(ny), nz)),
        in_specs=[VMEM] * 6,
        out_specs=(VMEM,) * 2,
        scratch_shapes=[
            pltpu.VMEM((3, 4, 4 * W, nz), F32),
            pltpu.VMEM((FIELDS, 4 * W, nz), F32),
        ],
        compiler_params=params(),
        name="pack_late",
    )(conc, diff, source, yone, ytwo, rest)


def own_kernel(
    conc, diff, source, yone, ytwo,
    u_s, d_s, s_s, fx, gx, fy, gy, fz, gz, dg, p1,
):
    nx, ny, nz = conc.shape
    rows = ny + 2 * W
    for k, (own, ref) in enumerate(((conc, u_s), (diff, d_s), (source, s_s))):
        below, above = rows_beside(yone, ytwo, k, slice(0, nx))
        ref[0:nx, 0:ny, :] = own[...]
        ref[0:nx, ny : ny + W, :] = above
        ref[0:nx, ny + W :, :] = below
    first, last = z_ends((rows, nz))

    for q in range(nx):
        u, d = u_s[q], d_s[q]
        fyq, gyq, fzq, gzq = in_plane_couplings(u, d)
        total = 1.0 + ((fyq + gyq) + (fzq + gzq))
        if q + 1 < nx:
            fxq = coupling(u, d, u_s[q + 1], d_s[q + 1])
            fx[q] = fxq
            total = total + fxq
        if q > 0:
            gxq = coupling(u, d, u_s[q - 1], d_s[q - 1])
            gx[q] = gxq
            total = total + gxq
        dg[q] = total
        fy[q] = fyq
        gy[q] = gyq
        fz[q] = jnp.where(last, 0.0, fzq)
        gz[q] = jnp.where(first, 0.0, gzq)

    for q in range(1, nx - 1):
        v = s_s[q]
        total = dg[q] * v - fx[q] * s_s[q + 1] - gx[q] * s_s[q - 1]
        total = total - in_plane_adjoint(v, fy[q], gy[q], fz[q], gz[q])
        p1[q] = jnp.where(d_s[q] > 0.0, total, 0.0)


def own(conc, diff, source, yone, ytwo):
    nx, ny, nz = conc.shape
    return pl.pallas_call(
        own_kernel,
        out_shape=(f32(nx + SPARE, ny + 2 * W, nz),) * 11,
        in_specs=[VMEM] * 5,
        out_specs=(VMEM,) * 11,
        compiler_params=params(),
        name="own",
    )(conc, diff, source, yone, ytwo)


def mask_halo(total, d, ny):
    return jnp.concatenate([total[0:ny], jnp.where(d > 0.0, total[ny:], 0.0)], axis=0)


def square(v, ny):
    mine = v[0:ny]
    return jnp.sum((mine * mine).reshape(ny // 8, 8, mine.shape[1]), axis=0)


def inside_kernel(d_s, s_s, fx, gx, fy, gy, fz, gz, dg, p1, p2, p3, part):
    nx, rows, nz = d_s.shape
    nx = nx - SPARE
    ny = rows - 2 * W
    sums = [jnp.zeros((8, nz), F32) for _ in range(4)]
    for q in range(nx):
        sums[0] = sums[0] + square(s_s[q], ny)
    for q in range(1, nx - 1):
        sums[1] = sums[1] + square(p1[q], ny)
    for q in range(2, nx - 2):
        v = p1[q]
        total = dg[q] * v - gx[q + 1] * p1[q + 1] - fx[q - 1] * p1[q - 1]
        total = total - in_plane_forward(v, fy[q], gy[q], fz[q], gz[q])
        total = jnp.where(d_s[q] > 0.0, total, 0.0)
        p2[q] = total
        sums[2] = sums[2] + square(total, ny)
    for q in range(3, nx - 3):
        v = p2[q]
        total = dg[q] * v - fx[q] * p2[q + 1] - gx[q] * p2[q - 1]
        total = total - in_plane_adjoint(v, fy[q], gy[q], fz[q], gz[q])
        total = jnp.where(d_s[q] > 0.0, total, 0.0)
        p3[q] = total
        sums[3] = sums[3] + square(total, ny)
    for k in range(4):
        part[k] = sums[k]


def inside(d_s, *fields):
    nx, rows, nz = d_s.shape
    return pl.pallas_call(
        inside_kernel,
        out_shape=(f32(nx, rows, nz),) * 2 + (f32(4, 8, nz),),
        in_specs=[VMEM] * 10,
        out_specs=(VMEM,) * 3,
        compiler_params=params(),
        cost_estimate=pl.CostEstimate(
            flops=1 << 22, bytes_accessed=1 << 23, transcendentals=0
        ),
        name="inside",
    )(d_s, *fields)


def finish_kernel(
    u_s, d_s, s_s, fx, gx, fy, gy, fz, gz, dg, p1_in, p2_in, p3_in, part,
    xtwo, xone, cone, ctwo,
    p1_out, p2_out, p3_out, edge_s, moments,
    side_s, w_s,
):
    nx, rows, nz = d_s.shape
    nx, ny = nx - SPARE, rows - 2 * W
    flip = low_first("gx")
    first, last = z_ends((rows, nz))

    for side, one in ((0, flip), (1, ~flip)):
        side_s[side, 0 : FIELDS - 1, 0:ny] = jnp.where(
            one, xone[...], xtwo[0 : FIELDS - 1]
        )
        side_s[side, FIELDS - 1, 0:ny] = jnp.where(one, cone[0:ny], xtwo[FIELDS - 1])
        side_s[side, :, ny:] = jnp.zeros((FIELDS, 2 * W, nz), F32)
        common = late_count(ny) - 4
        late = jnp.where(one, cone[ny:], ctwo[0:common])
        row = 0
        for field, begin, n in late_rows(ny):
            if field == FIELDS - 1:
                rows_q = jnp.where(one, cone[begin : begin + n], ctwo[row : row + n])
                side_s[side, field, begin : begin + n] = rows_q
            else:
                side_s[side, field, begin : begin + n] = late[row : row + n]
            row += n

    names = dict(
        u=u_s, d=d_s, s=s_s, fx=fx, gx=gx, fy=fy, gy=gy, fz=fz, gz=gz, dg=dg,
        p1=p1_in, p2=p2_in, p3=p3_in,
    )
    place = {(k, q): names[k].at[q] for k in names for q in range(nx)}
    spare = iter(range(w_s.shape[0]))

    def keep(name, q, value):
        place[name, q] = w_s.at[next(spare)]
        place[name, q][...] = value

    def get(name, q):
        return place[name, q][...]

    for side, (o, e, outward, inward) in enumerate(
        ((-1, 0, "gx", "fx"), (nx, nx - 1, "fx", "gx"))
    ):
        beyond = 2 * o - e
        for k, name in enumerate(("u", "d", "s")):
            place[name, o] = side_s.at[side, k]
        place["s", beyond] = side_s.at[side, 3]
        place[outward, o] = side_s.at[side, 4]
        place["m", o] = side_s.at[side, 5]
        place["q", o] = side_s.at[side, 6]
        u, d, ue, de = get("u", o), get("d", o), get("u", e), get("d", e)
        back = coupling(u, d, ue, de)
        out = coupling(ue, de, u, d)
        fyq, gyq, fzq, gzq = in_plane_couplings(u, d)
        total = 1.0 + get(outward, o) + back + ((fyq + gyq) + (fzq + gzq))
        new = {
            (inward, o): back,
            (outward, e): out,
            ("dg", o): total,
            ("dg", e): get("dg", e) + out,
            ("fy", o): fyq,
            ("gy", o): gyq,
            ("fz", o): jnp.where(last, 0.0, fzq),
            ("gz", o): jnp.where(first, 0.0, gzq),
        }
        for k, (key, value) in enumerate(new.items()):
            place[key] = edge_s.at[side, k]
            place[key][...] = value

    def masked(total, q):
        if q in (-1, nx):
            return jnp.where(get("d", q) > 0.0, total, 0.0)
        return mask_halo(total, place["d", q][ny:], ny)

    def in_plane(q):
        return [get(k, q) for k in ("fy", "gy", "fz", "gz")]

    def adjoint_at(w, q):
        v = get(w, q)
        total = get("dg", q) * v - get("fx", q) * get(w, q + 1)
        total = total - get("gx", q) * get(w, q - 1)
        return masked(total - in_plane_adjoint(v, *in_plane(q)), q)

    def forward_at(w, q):
        v = get(w, q)
        above = get("m", q) if q == nx else get("gx", q + 1) * get(w, q + 1)
        below = get("m", q) if q == -1 else get("fx", q - 1) * get(w, q - 1)
        total = get("dg", q) * v - above - below
        return masked(total - in_plane_forward(v, *in_plane(q)), q)

    sums = [part[k] for k in range(4)]

    def sweep(k, apply, w, name, out, ready):
        for q in range(-1, nx + 1):
            if ready <= q < nx - ready:
                out[q] = get(name, q)[0:ny]
                continue
            value = apply(w, q)
            keep(name, q, value)
            if 0 <= q < nx:
                out[q] = value[0:ny]
                sums[k] = sums[k] + square(value, ny)

    sweep(1, adjoint_at, "s", "p1", p1_out, 1)
    sweep(2, forward_at, "p1", "p2", p2_out, 2)
    for o, outward in ((-1, "gx"), (nx, "fx")):
        beyond = -2 if o == -1 else nx + 1
        keep("p2", beyond, get("q", o) - get(outward, o) * get("p1", o))
    for q in range(-1, nx + 1):
        if 3 <= q < nx - 3:
            p3_out[q + 1] = get("p3", q)
            continue
        value = adjoint_at("p2", q)
        p3_out[q + 1] = value
        if 0 <= q < nx:
            sums[3] = sums[3] + square(value, ny)

    slot = lax.broadcasted_iota(jnp.int32, (1, LANES), 1)
    row = jnp.zeros((1, LANES), F32)
    for k in range(4):
        row = jnp.where(slot == k, jnp.sum(sums[k]), row)
    moments[...] = jnp.broadcast_to(row, moments.shape)


def finish(copies, ny, *fields):
    nx, rows, nz = fields[0].shape
    nx = nx - SPARE
    steps = 4 + 6 + 2
    return pl.pallas_call(
        finish_kernel,
        out_shape=(
            f32(nx, ny, nz),
            f32(nx, ny, nz),
            f32(nx + 2, rows, nz),
            f32(2, 8, rows, nz),
            f32(copies, 1, LANES),
        ),
        in_specs=[VMEM] * len(fields),
        out_specs=(VMEM,) * 5,
        scratch_shapes=[
            pltpu.VMEM((2, FIELDS, rows, nz), F32),
            pltpu.VMEM((steps, rows, nz), F32),
        ],
        compiler_params=params(),
        name="finish",
    )(*fields)


def combine_kernel(
    moments, source, p1, p2, p3, edge, fx, gx, fy, gy, fz, gz, dg,
    adjoint_out, residual_out,
    adjoint, residual, sems,
):
    nx, ny, nz = source.shape
    m = jnp.sum(moments[...], axis=0)
    m0, m1, m2, m3 = (m[:, k : k + 1] for k in range(4))
    alpha = m0 / m1
    beta = alpha * (m2 / m1) - 1.0
    grow = 1.0 + beta
    image = grow * grow * m1 - 2.0 * grow * alpha * m2 + alpha * alpha * m3
    step = (beta * m0) / image
    near = alpha + step * grow
    far = step * alpha
    for x in range(nx):
        v = p3[x + 1]
        above = edge[1, 0] if x == nx - 1 else gx[x + 1]
        below = edge[0, 0] if x == 0 else fx[x - 1]
        diagonal = edge[0, 3] if x == 0 else edge[1, 3] if x == nx - 1 else dg[x]
        p4 = diagonal * v - above * p3[x + 2] - below * p3[x]
        p4 = p4 - in_plane_forward(v, fy[x], gy[x], fz[x], gz[x])
        residual[x] = p4[0:ny]
    copies = []
    half = nx // 2
    for begin in (0, half):
        for x in range(begin, begin + half):
            adjoint[x] = near * p1[x] - far * p3[x + 1, 0:ny]
            residual[x] = source[x] - near * p2[x] + far * residual[x]
        planes = pl.ds(begin, half)
        for src, dst in ((adjoint, adjoint_out), (residual, residual_out)):
            copies.append(
                pltpu.make_async_copy(
                    src.at[planes], dst.at[planes], sems.at[len(copies)]
                )
            )
            copies[-1].start()
    for copy in copies:
        copy.wait()


def combine(moments, source, p1, p2, p3, edge, *couplings):
    nx, ny, nz = source.shape
    return pl.pallas_call(
        combine_kernel,
        out_shape=(f32(nx, ny, nz),) * 2,
        in_specs=[VMEM] * (6 + len(couplings)),
        out_specs=(pl.BlockSpec(memory_space=pltpu.HBM),) * 2,
        scratch_shapes=[
            pltpu.VMEM((nx, ny, nz), F32),
            pltpu.VMEM((nx, ny, nz), F32),
            pltpu.SemaphoreType.DMA((4,)),
        ],
        compiler_params=params(),
        name="combine",
    )(moments, source, p1, p2, p3, edge, *couplings)


def swap(cells, axis, first):
    pairs = [(i, i + 1) for i in range(first, lax.axis_size(axis) - 1, 2)]
    return lax.ppermute(cells, axis, pairs + [(j, i) for i, j in pairs])


def local(conc, labels, kappa, source):
    ny = conc.shape[1]
    conc, source, diff = pack(conc, labels, kappa, source)
    xtwo = swap(pack_face(False, conc, diff, source), "gx", 0)
    xone, rest = pack_face(True, conc, diff, source)
    xone = swap(xone, "gx", 1)
    yone, ytwo = pack_rows(conc, diff, source)
    yone = swap(yone, "gy", 1)
    ytwo = swap(ytwo, "gy", 0)
    cone, ctwo = pack_late(conc, diff, source, yone, ytwo, rest)
    cone = swap(cone, "gx", 1)
    ctwo = swap(ctwo, "gx", 0)
    fields = own(conc, diff, source, yone, ytwo)
    inner = inside(*fields[1:])
    p1, p2, p3, edge, moments = finish(
        lax.axis_size(("gx", "gy")), ny, *fields, *inner, xtwo, xone, cone, ctwo
    )
    moments = lax.all_to_all(moments, ("gx", "gy"), 0, 0, tiled=True)
    return combine(moments, source, p1, p2, p3, edge, *fields[3:10])


def solution(mesh):
    return jax.shard_map(
        local,
        mesh=mesh,
        in_specs=(P("gx", "gy", None), P("gx", "gy", None), P(), P("gx", "gy", None)),
        out_specs=(P("gx", "gy", None), P("gx", "gy", None)),
        check_vma=False,
    )
```

```python
import functools

import jax
import jax.numpy as jnp
from jax import lax
from jax.experimental import pallas as pl
from jax.experimental.pallas import tpu as pltpu
from jax.sharding import PartitionSpec as P

ITERS = 2
DT = 0.5
W = 2 * ITERS
F32 = jnp.float32
LANES = 128
YROWS = (8, 6)
VMEM = pl.BlockSpec(memory_space=pltpu.VMEM)


def low_first(axis):
    return lax.axis_index(axis) % 2 == 0


def up(v, axis):
    return pltpu.roll(v, v.shape[axis] - 1, axis)


def down(v, axis):
    return pltpu.roll(v, 1, axis)


def z_ends(shape):
    index = lax.broadcasted_iota(jnp.int32, shape, 1)
    return index == 0, index == shape[1] - 1


def coupling(u, d, un, dn):
    return d + d * u - d * un + dn


def params(megabytes=16):
    return pltpu.CompilerParams(vmem_limit_bytes=megabytes << 20)


def f32(*shape):
    return jax.ShapeDtypeStruct(shape, F32)


FIELDS = 7


def late_rows(ny):
    rows = ny + 2 * W
    for field, n in ((0, 3), (1, 3), (2, 3), (3, 2), (4, 2), (5, 1)):
        yield field, ny, n
        yield field, rows - n, n
    for field, n in ((5, 1), (6, 2)):
        yield field, 0, n
        yield field, ny - n, n


def late_count(ny):
    return sum(n for _, _, n in late_rows(ny))


def pack_kernel(
    kappa_in, conc_in, labels_in, source_in,
    conc, source, diff,
    labels, kappa, sems,
):
    nx, ny, nz = conc.shape
    copies = [
        pltpu.make_async_copy(src, dst, sems.at[k])
        for k, (src, dst) in enumerate(
            (
                (labels_in, labels),
                (conc_in, conc),
                (kappa_in, kappa),
                (source_in, source),
            )
        )
    ]
    for copy in copies:
        copy.start()
    for copy in copies[:3]:
        copy.wait()
    k0, k1, k2 = ((0.5 * DT) * kappa[k] for k in range(3))

    def body(x, carry):
        lab = labels[x]
        base = jnp.where(lab == 0, k0, jnp.where(lab == 1, k1, k2))
        diff[x] = base * jnp.exp(conc[x])
        return carry

    lax.fori_loop(0, nx, body, 0, unroll=True)
    copies[3].wait()


def pack(conc, labels, kappa, source):
    nx, ny, nz = conc.shape
    outside = [
        pltpu.with_memory_space_constraint(v, pltpu.HBM)
        for v in (kappa, conc, labels, source)
    ]
    return pl.pallas_call(
        pack_kernel,
        out_shape=(f32(nx, ny, nz),) * 3,
        in_specs=[pl.BlockSpec(memory_space=pltpu.HBM)] * 4,
        out_specs=(VMEM,) * 3,
        scratch_shapes=[
            pltpu.VMEM((nx, ny, nz), jnp.int32),
            pltpu.SMEM((3,), F32),
            pltpu.SemaphoreType.DMA((4,)),
        ],
        compiler_params=params(),
        name="pack",
    )(*outside)


def pack_rows_kernel(conc, diff, source, yone, ytwo):
    ny = conc.shape[1]
    flip = low_first("gy")
    for k, ref in enumerate((conc, diff, source)):
        for out, n, head in ((yone, YROWS[0], flip), (ytwo, YROWS[1], ~flip)):
            out[k] = jnp.where(head, ref[:, 0:n, :], ref[:, ny - n : ny, :])


def pack_rows(conc, diff, source):
    nx, ny, nz = conc.shape
    return pl.pallas_call(
        pack_rows_kernel,
        out_shape=tuple(f32(3, nx, n, nz) for n in YROWS),
        in_specs=[VMEM] * 3,
        out_specs=(VMEM,) * 2,
        compiler_params=params(),
        name="pack_rows",
    )(conc, diff, source)


def rows_beside(yone, ytwo, k, x):
    flip = low_first("gy")
    one, two = (slice(n - W, n) for n in YROWS)
    below = jnp.where(flip, yone[k, x, one], ytwo[k, x, two])
    return below, jnp.where(flip, ytwo[k, x, 0:W], yone[k, x, 0:W])


def in_plane_adjoint(v, fy, gy, fz, gz):
    total = fy * up(v, 0) + gy * down(v, 0)
    return total + (fz * up(v, 1) + gz * down(v, 1))


def in_plane_forward(v, fy, gy, fz, gz):
    total = up(gy * v, 0) + down(fy * v, 0)
    return total + (up(gz * v, 1) + down(fz * v, 1))


def in_plane_couplings(u, d):
    first, last = z_ends(u.shape)
    fy = coupling(u, d, up(u, 0), up(d, 0))
    gy = coupling(u, d, down(u, 0), down(d, 0))
    fz = coupling(u, d, jnp.where(last, 0.0, up(u, 1)), jnp.where(last, 0.0, up(d, 1)))
    gz = coupling(
        u, d, jnp.where(first, 0.0, down(u, 1)), jnp.where(first, 0.0, down(d, 1))
    )
    return fy, gy, fz, gz


def face_planes(first_swap, nx):
    at_head = low_first("gx") if first_swap else ~low_first("gx")
    return [jnp.where(at_head, k, nx - 1 - k) for k in range(4)]


def face_fields(u, d, s):
    first, last = z_ends(u[0].shape)

    def between(i, j):
        return coupling(u[i], d[i], u[j], d[j])

    def image(i, before, after):
        fy, gy, fz, gz = in_plane_couplings(u[i], d[i])
        diagonal = 1.0 + ((fy + gy) + (fz + gz)) + (before + after)
        beside = (fy, gy, jnp.where(last, 0.0, fz), jnp.where(first, 0.0, gz))
        total = diagonal * s[i] - before * s[i - 1] - after * s[i + 1]
        total = total - in_plane_adjoint(s[i], *beside)
        return jnp.where(d[i] > 0.0, total, 0.0), diagonal, beside

    back, inward = between(1, 0), between(2, 1)
    near, diagonal, beside = image(1, back, between(1, 2))
    far, _, _ = image(2, inward, between(2, 3))
    rest = diagonal * near - inward * far - in_plane_forward(near, *beside)
    return u[0], d[0], s[0], s[1], between(0, 1), back * near, rest


def pack_face_kernel(first_swap, conc, diff, source, *slabs):
    planes = face_planes(first_swap, conc.shape[0])
    u, d, s = ([ref[x] for x in planes] for ref in (conc, diff, source))
    for k, v in enumerate(face_fields(u, d, s)):
        if k < slabs[0].shape[0]:
            slabs[0][k] = v
        else:
            slabs[1][...] = v


def pack_face(first_swap, conc, diff, source):
    plane = conc.shape[1:]
    return pl.pallas_call(
        functools.partial(pack_face_kernel, first_swap),
        out_shape=(f32(FIELDS - 1, *plane), f32(*plane))
        if first_swap
        else f32(FIELDS, *plane),
        in_specs=[VMEM] * 3,
        out_specs=(VMEM, VMEM) if first_swap else VMEM,
        compiler_params=params(),
        name="pack_face",
    )(conc, diff, source)


def pack_late_kernel(
    conc, diff, source, yone, ytwo, rest, cone, ctwo, near_s, out_s
):
    nx, ny, nz = conc.shape
    rows = ny + 2 * W

    def narrow(row):
        if row < ny:
            return row + W if row < W else row - ny + 3 * W
        return row - ny + 3 * W if row < ny + W else row - ny - W

    for first_swap, late in ((True, cone), (False, ctwo)):
        for j, x in enumerate(face_planes(first_swap, nx)):
            for k, ref in enumerate((conc, diff, source)):
                below, above = rows_beside(yone, ytwo, k, x)
                near_s[k, j, 0:W] = below
                near_s[k, j, W : 2 * W] = ref[x, 0:W]
                near_s[k, j, 2 * W : 3 * W] = ref[x, ny - W : ny]
                near_s[k, j, 3 * W :] = above
        fields = face_fields(*([near_s[k, j] for j in range(4)] for k in range(3)))
        for k, v in enumerate(fields):
            out_s[k] = v
        row = 0
        if first_swap:
            late[0:ny] = rest[...]
            row = ny
        for k, begin, n in late_rows(ny):
            at = narrow(begin)
            if first_swap and k == FIELDS - 1:
                late[begin : begin + n] = out_s[k, at : at + n]
                continue
            late[row : row + n] = out_s[k, at : at + n]
            row += n


def pack_late(conc, diff, source, yone, ytwo, rest):
    nx, ny, nz = conc.shape
    return pl.pallas_call(
        pack_late_kernel,
        out_shape=(f32(ny + late_count(ny) - 4, nz), f32(late_count(ny), nz)),
        in_specs=[VMEM] * 6,
        out_specs=(VMEM,) * 2,
        scratch_shapes=[
            pltpu.VMEM((3, 4, 4 * W, nz), F32),
            pltpu.VMEM((FIELDS, 4 * W, nz), F32),
        ],
        compiler_params=params(),
        name="pack_late",
    )(conc, diff, source, yone, ytwo, rest)


def own_kernel(
    conc, diff, source, yone, ytwo,
    u_s, d_s, s_s, fg, fy, gy, fz, gz, dg, p1,
):
    nx, ny, nz = conc.shape
    rows = ny + 2 * W
    fx, gx = fg.at[0], fg.at[1]
    for k, (own, ref) in enumerate(((conc, u_s), (diff, d_s), (source, s_s))):
        below, above = rows_beside(yone, ytwo, k, slice(0, nx))
        ref[:, 0:ny, :] = own[...]
        ref[:, ny : ny + W, :] = above
        ref[:, ny + W :, :] = below
    first, last = z_ends((rows, nz))

    def couplings(q, carry, first_plane=False, last_plane=False):
        u, d = u_s[q], d_s[q]
        fyq, gyq, fzq, gzq = in_plane_couplings(u, d)
        total = 1.0 + ((fyq + gyq) + (fzq + gzq))
        if not last_plane:
            fxq = coupling(u, d, u_s[q + 1], d_s[q + 1])
            fx[q] = fxq
            total = total + fxq
        if not first_plane:
            gxq = coupling(u, d, u_s[q - 1], d_s[q - 1])
            gx[q] = gxq
            total = total + gxq
        dg[q] = total
        fy[q] = fyq
        gy[q] = gyq
        fz[q] = jnp.where(last, 0.0, fzq)
        gz[q] = jnp.where(first, 0.0, gzq)
        return carry

    def image(q, carry):
        v = s_s[q]
        total = dg[q] * v - fx[q] * s_s[q + 1] - gx[q] * s_s[q - 1]
        total = total - in_plane_adjoint(v, fy[q], gy[q], fz[q], gz[q])
        p1[q] = jnp.where(d_s[q] > 0.0, total, 0.0)
        return carry

    couplings(0, 0, first_plane=True)
    lax.fori_loop(1, nx - 1, couplings, 0, unroll=2)
    couplings(nx - 1, 0, last_plane=True)
    lax.fori_loop(1, nx - 1, image, 0, unroll=2)


def own(conc, diff, source, yone, ytwo):
    nx, ny, nz = conc.shape
    return pl.pallas_call(
        own_kernel,
        out_shape=(f32(nx, ny + 2 * W, nz),) * 3
        + (f32(2, nx, ny + 2 * W, nz),)
        + (f32(nx, ny + 2 * W, nz),) * 6,
        in_specs=[VMEM] * 5,
        out_specs=(VMEM,) * 10,
        compiler_params=params(),
        name="own",
    )(conc, diff, source, yone, ytwo)


def mask_halo(total, d, ny):
    return jnp.concatenate([total[0:ny], jnp.where(d > 0.0, total[ny:], 0.0)], axis=0)


def square(v, ny):
    mine = v[0:ny]
    return jnp.sum((mine * mine).reshape(ny // 8, 8, mine.shape[1]), axis=0)


def inside_kernel(d_s, s_s, fg, fy, gy, fz, gz, dg, p1, p2, p3, part):
    nx, rows, nz = d_s.shape
    fx, gx = fg.at[0], fg.at[1]
    ny = rows - 2 * W
    sums = [jnp.zeros((8, nz), F32) for _ in range(4)]
    for q in range(nx):
        sums[0] = sums[0] + square(s_s[q], ny)
    for q in range(1, nx - 1):
        sums[1] = sums[1] + square(p1[q], ny)
    for q in range(2, nx - 2):
        v = p1[q]
        total = dg[q] * v - gx[q + 1] * p1[q + 1] - fx[q - 1] * p1[q - 1]
        total = total - in_plane_forward(v, fy[q], gy[q], fz[q], gz[q])
        total = jnp.where(d_s[q] > 0.0, total, 0.0)
        p2[q] = total
        sums[2] = sums[2] + square(total, ny)
    for q in range(3, nx - 3):
        v = p2[q]
        total = dg[q] * v - fx[q] * p2[q + 1] - gx[q] * p2[q - 1]
        total = total - in_plane_adjoint(v, fy[q], gy[q], fz[q], gz[q])
        total = jnp.where(d_s[q] > 0.0, total, 0.0)
        p3[q] = total
        sums[3] = sums[3] + square(total, ny)
    for k in range(4):
        part[k] = sums[k]


def inside(d_s, *fields):
    nx, rows, nz = d_s.shape
    return pl.pallas_call(
        inside_kernel,
        out_shape=(f32(nx, rows, nz),) * 2 + (f32(4, 8, nz),),
        in_specs=[VMEM] * 9,
        out_specs=(VMEM,) * 3,
        compiler_params=params(),
        cost_estimate=pl.CostEstimate(
            flops=1 << 22, bytes_accessed=1 << 23, transcendentals=0
        ),
        name="inside",
    )(d_s, *fields)


def finish_kernel(
    u_s, d_s, s_s, fg, fy, gy, fz, gz, dg, p1, p2, p3, part,
    xone, xtwo, cone, ctwo,
    p1_e, p2_e, p3_e, edge, moments,
    side_s, o_s, w_s,
):
    nx, rows, nz = d_s.shape
    ny = rows - 2 * W
    flip = low_first("gx")
    first, last = z_ends((rows, nz))

    def half(side, sums):
        one = (side == 0) == flip
        e, a, b, c = (jnp.where(side == 0, k, nx - 1 - k) for k in range(4))
        side_s[0 : FIELDS - 1, 0:ny] = jnp.where(one, xone[...], xtwo[0 : FIELDS - 1])
        side_s[FIELDS - 1, 0:ny] = jnp.where(one, cone[0:ny], xtwo[FIELDS - 1])
        side_s[:, ny:] = jnp.zeros((FIELDS, 2 * W, nz), F32)
        late = jnp.where(one, cone[ny:], ctwo[0 : late_count(ny) - 4])
        row = 0
        for field, begin, n in late_rows(ny):
            if field == FIELDS - 1:
                rows_q = jnp.where(one, cone[begin : begin + n], ctwo[row : row + n])
                side_s[field, begin : begin + n] = rows_q
            else:
                side_s[field, begin : begin + n] = late[row : row + n]
            row += n

        u, d = side_s[0], side_s[1]
        ue, de = u_s[e], d_s[e]
        back = coupling(u, d, ue, de)
        out = coupling(ue, de, u, d)
        fyq, gyq, fzq, gzq = in_plane_couplings(u, d)
        total = 1.0 + side_s[4] + back + ((fyq + gyq) + (fzq + gzq))
        edge[side, 0] = back
        edge[side, 1] = dg[e] + out
        ends = (jnp.where(last, 0.0, fzq), jnp.where(first, 0.0, gzq))
        for k, value in enumerate((fyq, gyq, *ends, total, out)):
            o_s[k] = value

        def inside_o(total):
            return jnp.where(side_s[1] > 0.0, total, 0.0)

        def inside_own(total, q):
            return mask_halo(total, d_s[q, ny:], ny)

        def beside(q):
            if q is None:
                return [o_s[k] for k in range(4)]
            return [k[q] for k in (fy, gy, fz, gz)]

        v, ve = side_s[2], s_s[e]
        total = o_s[4] * v - side_s[4] * side_s[3] - edge[side, 0] * ve
        w_s[0] = inside_o(total - in_plane_adjoint(v, *beside(None)))
        total = edge[side, 1] * ve - o_s[5] * v - fg[side, e] * s_s[a]
        p1_e[side] = inside_own(total - in_plane_adjoint(ve, *beside(e)), e)
        v, ve, va = w_s[0], p1_e[side], p1[a]
        total = o_s[4] * v - side_s[5] - o_s[5] * ve
        w_s[1] = inside_o(total - in_plane_forward(v, *beside(None)))
        w_s[2] = side_s[6] - side_s[4] * v
        total = edge[side, 1] * ve - edge[side, 0] * v - fg[1 - side, a] * va
        p2_e[side, 0] = inside_own(total - in_plane_forward(ve, *beside(e)), e)
        total = dg[a] * va - fg[side, e] * ve - fg[1 - side, b] * p1[b]
        p2_e[side, 1] = inside_own(total - in_plane_forward(va, *beside(a)), a)
        v, ve, va, vb = w_s[1], p2_e[side, 0], p2_e[side, 1], p2[b]
        total = o_s[4] * v - side_s[4] * w_s[2] - edge[side, 0] * ve
        p3_e[side, 0] = inside_o(total - in_plane_adjoint(v, *beside(None)))
        total = edge[side, 1] * ve - o_s[5] * v - fg[side, e] * va
        p3_e[side, 1] = inside_own(total - in_plane_adjoint(ve, *beside(e)), e)
        total = dg[a] * va - fg[1 - side, a] * ve - fg[side, a] * vb
        p3_e[side, 2] = inside_own(total - in_plane_adjoint(va, *beside(a)), a)
        total = dg[b] * vb - fg[1 - side, b] * va - fg[side, b] * p2[c]
        p3_e[side, 3] = inside_own(total - in_plane_adjoint(vb, *beside(b)), b)
        return (
            sums[0] + square(p1_e[side], ny),
            sums[1] + square(p2_e[side, 0], ny) + square(p2_e[side, 1], ny),
            sums[2]
            + square(p3_e[side, 1], ny)
            + square(p3_e[side, 2], ny)
            + square(p3_e[side, 3], ny),
        )

    sums = lax.fori_loop(0, 2, half, tuple(part[k] for k in range(1, 4)))
    slot = lax.broadcasted_iota(jnp.int32, (1, LANES), 1)
    row = jnp.zeros((1, LANES), F32)
    for k, total in enumerate((part[0], *sums)):
        row = jnp.where(slot == k, jnp.sum(total), row)
    moments[...] = jnp.broadcast_to(row, moments.shape)


def finish(copies, *fields):
    nx, rows, nz = fields[0].shape
    return pl.pallas_call(
        finish_kernel,
        out_shape=(
            f32(2, rows, nz),
            f32(2, 2, rows, nz),
            f32(2, 4, rows, nz),
            f32(2, 2, rows, nz),
            f32(copies, 1, LANES),
        ),
        in_specs=[VMEM] * len(fields),
        out_specs=(VMEM,) * 5,
        scratch_shapes=[
            pltpu.VMEM((FIELDS, rows, nz), F32),
            pltpu.VMEM((6, rows, nz), F32),
            pltpu.VMEM((3, rows, nz), F32),
        ],
        compiler_params=params(),
        name="finish",
    )(*fields)


def combine_kernel(
    moments, source, p1, p2, p3, p1_e, p2_e, p3_e, edge, fg, fy, gy, fz, gz, dg,
    adjoint_out, residual_out,
    adjoint, residual, sems,
):
    nx, ny, nz = source.shape
    fx, gx = fg.at[0], fg.at[1]
    one = [p1_e.at[0], *(p1.at[x] for x in range(1, nx - 1)), p1_e.at[1]]
    two = [p2_e.at[0, 0], p2_e.at[0, 1], *(p2.at[x] for x in range(2, nx - 2))]
    two += [p2_e.at[1, 1], p2_e.at[1, 0]]
    three = [*(p3_e.at[0, k] for k in range(4)), *(p3.at[x] for x in range(3, nx - 3))]
    three += [p3_e.at[1, k] for k in range(3, -1, -1)]
    m = jnp.sum(moments[...], axis=0)
    m0, m1, m2, m3 = (m[:, k : k + 1] for k in range(4))
    alpha = m0 / m1
    beta = alpha * (m2 / m1) - 1.0
    grow = 1.0 + beta
    image = grow * grow * m1 - 2.0 * grow * alpha * m2 + alpha * alpha * m3
    step = (beta * m0) / image
    near = alpha + step * grow
    far = step * alpha
    for x in range(nx):
        v = three[x + 1][...]
        above = edge[1, 0] if x == nx - 1 else gx[x + 1]
        below = edge[0, 0] if x == 0 else fx[x - 1]
        diagonal = edge[0, 1] if x == 0 else edge[1, 1] if x == nx - 1 else dg[x]
        p4 = diagonal * v - above * three[x + 2][...] - below * three[x][...]
        p4 = p4 - in_plane_forward(v, fy[x], gy[x], fz[x], gz[x])
        residual[x] = p4[0:ny]
    copies = []
    half = nx // 2
    for begin in (0, half):
        for x in range(begin, begin + half):
            adjoint[x] = near * one[x][0:ny] - far * three[x + 1][0:ny]
            residual[x] = source[x] - near * two[x][0:ny] + far * residual[x]
        planes = pl.ds(begin, half)
        for src, dst in ((adjoint, adjoint_out), (residual, residual_out)):
            copies.append(
                pltpu.make_async_copy(
                    src.at[planes], dst.at[planes], sems.at[len(copies)]
                )
            )
            copies[-1].start()
    for copy in copies:
        copy.wait()


def combine(moments, source, *fields):
    nx, ny, nz = source.shape
    return pl.pallas_call(
        combine_kernel,
        out_shape=(f32(nx, ny, nz),) * 2,
        in_specs=[VMEM] * (2 + len(fields)),
        out_specs=(pl.BlockSpec(memory_space=pltpu.HBM),) * 2,
        scratch_shapes=[
            pltpu.VMEM((nx, ny, nz), F32),
            pltpu.VMEM((nx, ny, nz), F32),
            pltpu.SemaphoreType.DMA((4,)),
        ],
        compiler_params=params(),
        name="combine",
    )(moments, source, *fields)


def swap(cells, axis, first):
    pairs = [(i, i + 1) for i in range(first, lax.axis_size(axis) - 1, 2)]
    return lax.ppermute(cells, axis, pairs + [(j, i) for i, j in pairs])


def local(conc, labels, kappa, source):
    conc, source, diff = pack(conc, labels, kappa, source)
    xtwo = swap(pack_face(False, conc, diff, source), "gx", 0)
    xone, rest = pack_face(True, conc, diff, source)
    xone = swap(xone, "gx", 1)
    yone, ytwo = pack_rows(conc, diff, source)
    yone = swap(yone, "gy", 1)
    ytwo = swap(ytwo, "gy", 0)
    cone, ctwo = pack_late(conc, diff, source, yone, ytwo, rest)
    cone = swap(cone, "gx", 1)
    ctwo = swap(ctwo, "gx", 0)
    fields = own(conc, diff, source, yone, ytwo)
    p2, p3, part = inside(*fields[1:])
    *outer, moments = finish(
        lax.axis_size(("gx", "gy")), *fields, p2, p3, part, xone, xtwo, cone, ctwo
    )
    moments = lax.all_to_all(moments, ("gx", "gy"), 0, 0, tiled=True)
    return combine(moments, source, fields[9], p2, p3, *outer, *fields[3:9])


def solution(mesh):
    return jax.shard_map(
        local,
        mesh=mesh,
        in_specs=(P("gx", "gy", None), P("gx", "gy", None), P(), P("gx", "gy", None)),
        out_specs=(P("gx", "gy", None), P("gx", "gy", None)),
        check_vma=False,
    )
```

```python
import functools

import jax
import jax.numpy as jnp
from jax import lax
from jax.experimental import pallas as pl
from jax.experimental.pallas import tpu as pltpu
from jax.sharding import PartitionSpec as P

ITERS = 2
DT = 0.5
W = 2 * ITERS
F32 = jnp.float32
LANES = 128
YROWS = (8, 6)
VMEM = pl.BlockSpec(memory_space=pltpu.VMEM)


def low_first(axis):
    return lax.axis_index(axis) % 2 == 0


def up(v, axis):
    return pltpu.roll(v, v.shape[axis] - 1, axis)


def down(v, axis):
    return pltpu.roll(v, 1, axis)


def z_ends(shape):
    index = lax.broadcasted_iota(jnp.int32, shape, 1)
    return index == 0, index == shape[1] - 1


def coupling(u, d, un, dn):
    return d + d * u - d * un + dn


def params(megabytes=16):
    return pltpu.CompilerParams(vmem_limit_bytes=megabytes << 20)


def f32(*shape):
    return jax.ShapeDtypeStruct(shape, F32)


FIELDS = 7


def late_rows(ny):
    rows = ny + 2 * W
    for field, n in ((0, 3), (1, 3), (2, 3), (3, 2), (4, 1), (5, 1)):
        yield field, ny, n
        yield field, rows - n, n
    for field, n in ((5, 1), (6, 2)):
        yield field, 0, n
        yield field, ny - n, n


def late_count(ny):
    return sum(n for _, _, n in late_rows(ny))


def pack_kernel(
    kappa_in, conc_in, labels_in, source_in,
    conc, source, diff,
    labels, kappa, sems,
):
    nx, ny, nz = conc.shape
    copies = [
        pltpu.make_async_copy(src, dst, sems.at[k])
        for k, (src, dst) in enumerate(
            (
                (labels_in, labels),
                (conc_in, conc),
                (kappa_in, kappa),
                (source_in, source),
            )
        )
    ]
    for copy in copies:
        copy.start()
    for copy in copies[:3]:
        copy.wait()
    k0, k1, k2 = ((0.5 * DT) * kappa[k] for k in range(3))

    def body(x, carry):
        lab = labels[x]
        base = jnp.where(lab == 0, k0, jnp.where(lab == 1, k1, k2))
        diff[x] = base * jnp.exp(conc[x])
        return carry

    lax.fori_loop(0, nx, body, 0, unroll=True)
    copies[3].wait()


def pack(conc, labels, kappa, source):
    nx, ny, nz = conc.shape
    outside = [
        pltpu.with_memory_space_constraint(v, pltpu.HBM)
        for v in (kappa, conc, labels, source)
    ]
    return pl.pallas_call(
        pack_kernel,
        out_shape=(f32(nx, ny, nz),) * 3,
        in_specs=[pl.BlockSpec(memory_space=pltpu.HBM)] * 4,
        out_specs=(VMEM,) * 3,
        scratch_shapes=[
            pltpu.VMEM((nx, ny, nz), jnp.int32),
            pltpu.SMEM((3,), F32),
            pltpu.SemaphoreType.DMA((4,)),
        ],
        compiler_params=params(),
        name="pack",
    )(*outside)


def pack_rows_kernel(conc, diff, source, yone, ytwo):
    ny = conc.shape[1]
    flip = low_first("gy")
    for k, ref in enumerate((conc, diff, source)):
        for out, n, head in ((yone, YROWS[0], flip), (ytwo, YROWS[1], ~flip)):
            out[k] = jnp.where(head, ref[:, 0:n, :], ref[:, ny - n : ny, :])


def pack_rows(conc, diff, source):
    nx, ny, nz = conc.shape
    return pl.pallas_call(
        pack_rows_kernel,
        out_shape=tuple(f32(3, nx, n, nz) for n in YROWS),
        in_specs=[VMEM] * 3,
        out_specs=(VMEM,) * 2,
        compiler_params=params(),
        name="pack_rows",
    )(conc, diff, source)


def rows_beside(yone, ytwo, k, x):
    flip = low_first("gy")
    one, two = (slice(n - W, n) for n in YROWS)
    below = jnp.where(flip, yone[k, x, one], ytwo[k, x, two])
    return below, jnp.where(flip, ytwo[k, x, 0:W], yone[k, x, 0:W])


def in_plane_adjoint(v, fy, gy, fz, gz):
    total = fy * up(v, 0) + gy * down(v, 0)
    return total + (fz * up(v, 1) + gz * down(v, 1))


def in_plane_forward(v, fy, gy, fz, gz):
    total = up(gy * v, 0) + down(fy * v, 0)
    return total + (up(gz * v, 1) + down(fz * v, 1))


def in_plane_couplings(u, d):
    first, last = z_ends(u.shape)
    fy = coupling(u, d, up(u, 0), up(d, 0))
    gy = coupling(u, d, down(u, 0), down(d, 0))
    fz = coupling(u, d, jnp.where(last, 0.0, up(u, 1)), jnp.where(last, 0.0, up(d, 1)))
    gz = coupling(
        u, d, jnp.where(first, 0.0, down(u, 1)), jnp.where(first, 0.0, down(d, 1))
    )
    return fy, gy, fz, gz


def face_planes(first_swap, nx):
    at_head = low_first("gx") if first_swap else ~low_first("gx")
    return [jnp.where(at_head, k, nx - 1 - k) for k in range(4)]


def face_fields(u, d, s):
    first, last = z_ends(u[0].shape)

    def between(i, j):
        return coupling(u[i], d[i], u[j], d[j])

    def image(i, before, after):
        fy, gy, fz, gz = in_plane_couplings(u[i], d[i])
        diagonal = 1.0 + ((fy + gy) + (fz + gz)) + (before + after)
        beside = (fy, gy, jnp.where(last, 0.0, fz), jnp.where(first, 0.0, gz))
        total = diagonal * s[i] - before * s[i - 1] - after * s[i + 1]
        total = total - in_plane_adjoint(s[i], *beside)
        return jnp.where(d[i] > 0.0, total, 0.0), diagonal, beside

    back, inward = between(1, 0), between(2, 1)
    near, diagonal, beside = image(1, back, between(1, 2))
    far, _, _ = image(2, inward, between(2, 3))
    rest = diagonal * near - inward * far - in_plane_forward(near, *beside)
    return u[0], d[0], s[0], s[1], between(0, 1), back * near, rest


def pack_face_kernel(first_swap, conc, diff, source, *slabs):
    planes = face_planes(first_swap, conc.shape[0])
    u, d, s = ([ref[x] for x in planes] for ref in (conc, diff, source))
    for k, v in enumerate(face_fields(u, d, s)):
        if k < slabs[0].shape[0]:
            slabs[0][k] = v
        else:
            slabs[1][...] = v


def pack_face(first_swap, conc, diff, source):
    plane = conc.shape[1:]
    return pl.pallas_call(
        functools.partial(pack_face_kernel, first_swap),
        out_shape=(f32(FIELDS - 1, *plane), f32(*plane))
        if first_swap
        else f32(FIELDS, *plane),
        in_specs=[VMEM] * 3,
        out_specs=(VMEM, VMEM) if first_swap else VMEM,
        compiler_params=params(),
        name="pack_face",
    )(conc, diff, source)


def pack_late_kernel(
    conc, diff, source, yone, ytwo, rest, cone, ctwo, near_s, out_s
):
    nx, ny, nz = conc.shape
    rows = ny + 2 * W

    def narrow(row):
        if row < ny:
            return row + W if row < W else row - ny + 3 * W
        return row - ny + 3 * W if row < ny + W else row - ny - W

    for first_swap, late in ((True, cone), (False, ctwo)):
        for j, x in enumerate(face_planes(first_swap, nx)):
            for k, ref in enumerate((conc, diff, source)):
                below, above = rows_beside(yone, ytwo, k, x)
                near_s[k, j, 0:W] = below
                near_s[k, j, W : 2 * W] = ref[x, 0:W]
                near_s[k, j, 2 * W : 3 * W] = ref[x, ny - W : ny]
                near_s[k, j, 3 * W :] = above
        fields = face_fields(*([near_s[k, j] for j in range(4)] for k in range(3)))
        for k, v in enumerate(fields):
            out_s[k] = v
        for at in (W - 2, 3 * W + 1):
            mine, following, k = (out_s[j, at : at + 1] for j in (2, 3, 4))
            out_s[3, at : at + 1] = mine - k * (mine - following)
        row = 0
        if first_swap:
            late[0:ny] = rest[...]
            row = ny
        for k, begin, n in late_rows(ny):
            at = narrow(begin)
            if first_swap and k == FIELDS - 1:
                late[begin : begin + n] = out_s[k, at : at + n]
                continue
            late[row : row + n] = out_s[k, at : at + n]
            row += n


def pack_late(conc, diff, source, yone, ytwo, rest):
    nx, ny, nz = conc.shape
    return pl.pallas_call(
        pack_late_kernel,
        out_shape=(f32(ny + late_count(ny) - 4, nz), f32(late_count(ny), nz)),
        in_specs=[VMEM] * 6,
        out_specs=(VMEM,) * 2,
        scratch_shapes=[
            pltpu.VMEM((3, 4, 4 * W, nz), F32),
            pltpu.VMEM((FIELDS, 4 * W, nz), F32),
        ],
        compiler_params=params(),
        name="pack_late",
    )(conc, diff, source, yone, ytwo, rest)


def own_kernel(
    conc, diff, source, yone, ytwo,
    u_s, d_s, s_s, fx, gx, fy, gy, fz, gz, dg, p1,
):
    nx, ny, nz = conc.shape
    rows = ny + 2 * W
    for k, (own, ref) in enumerate(((conc, u_s), (diff, d_s), (source, s_s))):
        below, above = rows_beside(yone, ytwo, k, slice(0, nx))
        ref[:, 0:ny, :] = own[...]
        ref[:, ny : ny + W, :] = above
        ref[:, ny + W :, :] = below
    first, last = z_ends((rows, nz))

    for q in range(nx):
        u, d = u_s[q], d_s[q]
        fyq, gyq, fzq, gzq = in_plane_couplings(u, d)
        total = 1.0 + ((fyq + gyq) + (fzq + gzq))
        if q + 1 < nx:
            fxq = coupling(u, d, u_s[q + 1], d_s[q + 1])
            fx[q] = fxq
            total = total + fxq
        if q > 0:
            gxq = coupling(u, d, u_s[q - 1], d_s[q - 1])
            gx[q] = gxq
            total = total + gxq
        dg[q] = total
        fy[q] = fyq
        gy[q] = gyq
        fz[q] = jnp.where(last, 0.0, fzq)
        gz[q] = jnp.where(first, 0.0, gzq)

    for q in range(1, nx - 1):
        v = s_s[q]
        total = dg[q] * v - fx[q] * s_s[q + 1] - gx[q] * s_s[q - 1]
        total = total - in_plane_adjoint(v, fy[q], gy[q], fz[q], gz[q])
        p1[q] = jnp.where(d_s[q] > 0.0, total, 0.0)


def own(conc, diff, source, yone, ytwo):
    nx, ny, nz = conc.shape
    return pl.pallas_call(
        own_kernel,
        out_shape=(f32(nx, ny + 2 * W, nz),) * 11,
        in_specs=[VMEM] * 5,
        out_specs=(VMEM,) * 11,
        compiler_params=params(),
        name="own",
    )(conc, diff, source, yone, ytwo)


def mask_halo(total, d, ny):
    return jnp.concatenate([total[0:ny], jnp.where(d > 0.0, total[ny:], 0.0)], axis=0)


def square(v, ny):
    mine = v[0:ny]
    return jnp.sum((mine * mine).reshape(ny // 8, 8, mine.shape[1]), axis=0)


def inside_kernel(d_s, s_s, fx, gx, fy, gy, fz, gz, dg, p1, p2, p3, part):
    nx, rows, nz = d_s.shape
    ny = rows - 2 * W
    sums = [jnp.zeros((8, nz), F32) for _ in range(4)]
    for q in range(nx):
        sums[0] = sums[0] + square(s_s[q], ny)
    for q in range(1, nx - 1):
        sums[1] = sums[1] + square(p1[q], ny)
    for q in range(2, nx - 2):
        v = p1[q]
        total = dg[q] * v - gx[q + 1] * p1[q + 1] - fx[q - 1] * p1[q - 1]
        total = total - in_plane_forward(v, fy[q], gy[q], fz[q], gz[q])
        total = jnp.where(d_s[q] > 0.0, total, 0.0)
        p2[q] = total
        sums[2] = sums[2] + square(total, ny)
    for q in range(3, nx - 3):
        v = p2[q]
        total = dg[q] * v - fx[q] * p2[q + 1] - gx[q] * p2[q - 1]
        total = total - in_plane_adjoint(v, fy[q], gy[q], fz[q], gz[q])
        total = jnp.where(d_s[q] > 0.0, total, 0.0)
        p3[q] = total
        sums[3] = sums[3] + square(total, ny)
    for k in range(4):
        part[k] = sums[k]


def inside(d_s, *fields):
    nx, rows, nz = d_s.shape
    return pl.pallas_call(
        inside_kernel,
        out_shape=(f32(nx, rows, nz),) * 2 + (f32(4, 8, nz),),
        in_specs=[VMEM] * 10,
        out_specs=(VMEM,) * 3,
        compiler_params=params(),
        cost_estimate=pl.CostEstimate(
            flops=1 << 22, bytes_accessed=1 << 23, transcendentals=0
        ),
        name="inside",
    )(d_s, *fields)


def finish_kernel(
    u_s, d_s, s_s, fx, gx, fy, gy, fz, gz, dg, p1_in, p2_in, p3_in, part,
    xtwo, xone, cone, ctwo,
    p1_out, p2_out, p3_out, edge_s, moments,
    side_s, w_s,
):
    nx, rows, nz = d_s.shape
    ny = rows - 2 * W
    flip = low_first("gx")
    first, last = z_ends((rows, nz))

    for side, one in ((0, flip), (1, ~flip)):
        side_s[side, 0 : FIELDS - 1, 0:ny] = jnp.where(
            one, xone[...], xtwo[0 : FIELDS - 1]
        )
        side_s[side, FIELDS - 1, 0:ny] = jnp.where(one, cone[0:ny], xtwo[FIELDS - 1])
        side_s[side, :, ny:] = jnp.zeros((FIELDS, 2 * W, nz), F32)
        for at in (ny + 1, rows - 2):
            side_s[side, 4, at : at + 1] = jnp.ones((1, nz), F32)
        common = late_count(ny) - 4
        late = jnp.where(one, cone[ny:], ctwo[0:common])
        row = 0
        for field, begin, n in late_rows(ny):
            if field == FIELDS - 1:
                rows_q = jnp.where(one, cone[begin : begin + n], ctwo[row : row + n])
                side_s[side, field, begin : begin + n] = rows_q
            else:
                side_s[side, field, begin : begin + n] = late[row : row + n]
            row += n

    names = dict(
        u=u_s, d=d_s, s=s_s, fx=fx, gx=gx, fy=fy, gy=gy, fz=fz, gz=gz, dg=dg,
        p1=p1_in, p2=p2_in, p3=p3_in,
    )
    place = {(k, q): names[k].at[q] for k in names for q in range(nx)}
    spare = iter(range(w_s.shape[0]))

    def keep(name, q, value):
        place[name, q] = w_s.at[next(spare)]
        place[name, q][...] = value

    def get(name, q):
        return place[name, q][...]

    for side, (o, e, outward, inward) in enumerate(
        ((-1, 0, "gx", "fx"), (nx, nx - 1, "fx", "gx"))
    ):
        beyond = 2 * o - e
        for k, name in enumerate(("u", "d", "s")):
            place[name, o] = side_s.at[side, k]
        place["s", beyond] = side_s.at[side, 3]
        place[outward, o] = side_s.at[side, 4]
        place["m", o] = side_s.at[side, 5]
        place["q", o] = side_s.at[side, 6]
        u, d, ue, de = get("u", o), get("d", o), get("u", e), get("d", e)
        back = coupling(u, d, ue, de)
        out = coupling(ue, de, u, d)
        fyq, gyq, fzq, gzq = in_plane_couplings(u, d)
        total = 1.0 + get(outward, o) + back + ((fyq + gyq) + (fzq + gzq))
        new = {
            (inward, o): back,
            (outward, e): out,
            ("dg", o): total,
            ("dg", e): get("dg", e) + out,
            ("fy", o): fyq,
            ("gy", o): gyq,
            ("fz", o): jnp.where(last, 0.0, fzq),
            ("gz", o): jnp.where(first, 0.0, gzq),
        }
        for k, (key, value) in enumerate(new.items()):
            place[key] = edge_s.at[side, k]
            place[key][...] = value

    def masked(total, q):
        if q in (-1, nx):
            return jnp.where(get("d", q) > 0.0, total, 0.0)
        return mask_halo(total, place["d", q][ny:], ny)

    def in_plane(q):
        return [get(k, q) for k in ("fy", "gy", "fz", "gz")]

    def adjoint_at(w, q):
        v = get(w, q)
        total = get("dg", q) * v - get("fx", q) * get(w, q + 1)
        total = total - get("gx", q) * get(w, q - 1)
        return masked(total - in_plane_adjoint(v, *in_plane(q)), q)

    def forward_at(w, q):
        v = get(w, q)
        above = get("m", q) if q == nx else get("gx", q + 1) * get(w, q + 1)
        below = get("m", q) if q == -1 else get("fx", q - 1) * get(w, q - 1)
        total = get("dg", q) * v - above - below
        return masked(total - in_plane_forward(v, *in_plane(q)), q)

    sums = [part[k] for k in range(4)]

    def sweep(k, apply, w, name, out, ready):
        for q in range(-1, nx + 1):
            if ready <= q < nx - ready:
                out[q] = get(name, q)[0:ny]
                continue
            value = apply(w, q)
            keep(name, q, value)
            if 0 <= q < nx:
                out[q] = value[0:ny]
                sums[k] = sums[k] + square(value, ny)

    sweep(1, adjoint_at, "s", "p1", p1_out, 1)
    sweep(2, forward_at, "p1", "p2", p2_out, 2)
    for o, outward in ((-1, "gx"), (nx, "fx")):
        beyond = -2 if o == -1 else nx + 1
        keep("p2", beyond, get("q", o) - get(outward, o) * get("p1", o))
    for q in range(-1, nx + 1):
        if 3 <= q < nx - 3:
            p3_out[q + 1] = get("p3", q)
            continue
        value = adjoint_at("p2", q)
        p3_out[q + 1] = value
        if 0 <= q < nx:
            sums[3] = sums[3] + square(value, ny)

    slot = lax.broadcasted_iota(jnp.int32, (1, LANES), 1)
    row = jnp.zeros((1, LANES), F32)
    for k in range(4):
        row = jnp.where(slot == k, jnp.sum(sums[k]), row)
    moments[...] = jnp.broadcast_to(row, moments.shape)


def finish(copies, ny, *fields):
    nx, rows, nz = fields[0].shape
    steps = 4 + 6 + 2
    return pl.pallas_call(
        finish_kernel,
        out_shape=(
            f32(nx, ny, nz),
            f32(nx, ny, nz),
            f32(nx + 2, rows, nz),
            f32(2, 8, rows, nz),
            f32(copies, 1, LANES),
        ),
        in_specs=[VMEM] * len(fields),
        out_specs=(VMEM,) * 5,
        scratch_shapes=[
            pltpu.VMEM((2, FIELDS, rows, nz), F32),
            pltpu.VMEM((steps, rows, nz), F32),
        ],
        compiler_params=params(),
        name="finish",
    )(*fields)


def combine_kernel(
    moments, source, p1, p2, p3, edge, fx, gx, fy, gy, fz, gz, dg,
    adjoint_out, residual_out,
    adjoint, residual, sems,
):
    nx, ny, nz = source.shape
    m = jnp.sum(moments[...], axis=0)
    m0, m1, m2, m3 = (m[:, k : k + 1] for k in range(4))
    alpha = m0 / m1
    beta = alpha * (m2 / m1) - 1.0
    grow = 1.0 + beta
    image = grow * grow * m1 - 2.0 * grow * alpha * m2 + alpha * alpha * m3
    step = (beta * m0) / image
    near = alpha + step * grow
    far = step * alpha
    copies = []

    def send(src, dst, begin, end):
        planes = pl.ds(begin, end - begin)
        copies.append(
            pltpu.make_async_copy(src.at[planes], dst.at[planes], sems.at[len(copies)])
        )
        copies[-1].start()

    half = nx // 2
    for begin in (0, half):
        for x in range(begin, begin + half):
            adjoint[x] = near * p1[x] - far * p3[x + 1, 0:ny]
        send(adjoint, adjoint_out, begin, begin + half)
    for x in range(nx):
        v = p3[x + 1]
        above = edge[1, 0] if x == nx - 1 else gx[x + 1]
        below = edge[0, 0] if x == 0 else fx[x - 1]
        diagonal = edge[0, 3] if x == 0 else edge[1, 3] if x == nx - 1 else dg[x]
        p4 = diagonal * v - above * p3[x + 2] - below * p3[x]
        p4 = p4 - in_plane_forward(v, fy[x], gy[x], fz[x], gz[x])
        residual[x] = source[x] - near * p2[x] + far * p4[0:ny]
        if x % 2 == 1:
            send(residual, residual_out, x - 1, x + 1)
    for copy in copies:
        copy.wait()


def combine(moments, source, p1, p2, p3, edge, *couplings):
    nx, ny, nz = source.shape
    return pl.pallas_call(
        combine_kernel,
        out_shape=(f32(nx, ny, nz),) * 2,
        in_specs=[VMEM] * (6 + len(couplings)),
        out_specs=(pl.BlockSpec(memory_space=pltpu.HBM),) * 2,
        scratch_shapes=[
            pltpu.VMEM((nx, ny, nz), F32),
            pltpu.VMEM((nx, ny, nz), F32),
            pltpu.SemaphoreType.DMA((2 + nx // 2,)),
        ],
        compiler_params=params(),
        name="combine",
    )(moments, source, p1, p2, p3, edge, *couplings)


def swap(cells, axis, first):
    pairs = [(i, i + 1) for i in range(first, lax.axis_size(axis) - 1, 2)]
    return lax.ppermute(cells, axis, pairs + [(j, i) for i, j in pairs])


def local(conc, labels, kappa, source):
    ny = conc.shape[1]
    conc, source, diff = pack(conc, labels, kappa, source)
    xtwo = swap(pack_face(False, conc, diff, source), "gx", 0)
    xone, rest = pack_face(True, conc, diff, source)
    xone = swap(xone, "gx", 1)
    yone, ytwo = pack_rows(conc, diff, source)
    yone = swap(yone, "gy", 1)
    ytwo = swap(ytwo, "gy", 0)
    cone, ctwo = pack_late(conc, diff, source, yone, ytwo, rest)
    cone = swap(cone, "gx", 1)
    ctwo = swap(ctwo, "gx", 0)
    fields = own(conc, diff, source, yone, ytwo)
    inner = inside(*fields[1:])
    p1, p2, p3, edge, moments = finish(
        lax.axis_size(("gx", "gy")), ny, *fields, *inner, xtwo, xone, cone, ctwo
    )
    moments = lax.all_to_all(moments, ("gx", "gy"), 0, 0, tiled=True)
    return combine(moments, source, p1, p2, p3, edge, *fields[3:10])


def solution(mesh):
    return jax.shard_map(
        local,
        mesh=mesh,
        in_specs=(P("gx", "gy", None), P("gx", "gy", None), P(), P("gx", "gy", None)),
        out_specs=(P("gx", "gy", None), P("gx", "gy", None)),
        check_vma=False,
    )
```

```python
import functools

import jax
import jax.numpy as jnp
from jax import lax
from jax.experimental import pallas as pl
from jax.experimental.pallas import tpu as pltpu
from jax.sharding import PartitionSpec as P

ITERS = 2
DT = 0.5
W = 2 * ITERS
F32 = jnp.float32
LANES = 128
YROWS = (8, 8)
VMEM = pl.BlockSpec(memory_space=pltpu.VMEM)


def low_first(axis):
    return lax.axis_index(axis) % 2 == 0


def up(v, axis):
    return pltpu.roll(v, v.shape[axis] - 1, axis)


def down(v, axis):
    return pltpu.roll(v, 1, axis)


def z_ends(shape):
    index = lax.broadcasted_iota(jnp.int32, shape, 1)
    return index == 0, index == shape[1] - 1


def coupling(u, d, un, dn):
    return d + d * u - d * un + dn


def params(megabytes=16):
    return pltpu.CompilerParams(vmem_limit_bytes=megabytes << 20)


def f32(*shape):
    return jax.ShapeDtypeStruct(shape, F32)


FIELDS = 7


def late_rows(ny):
    rows = ny + 2 * W
    for field, n in ((0, 3), (1, 3), (2, 3), (3, 2), (4, 1), (5, 1)):
        yield field, ny, n
        yield field, rows - n, n
    for field, n in ((5, 1), (6, 2)):
        yield field, 0, n
        yield field, ny - n, n


def late_count(ny):
    return sum(n for _, _, n in late_rows(ny))


def pack_kernel(
    kappa_in, conc_in, labels_in, source_in,
    conc, source, diff,
    labels, kappa, sems,
):
    nx, ny, nz = conc.shape
    copies = [
        pltpu.make_async_copy(src, dst, sems.at[k])
        for k, (src, dst) in enumerate(
            (
                (labels_in, labels),
                (conc_in, conc),
                (kappa_in, kappa),
                (source_in, source),
            )
        )
    ]
    for copy in copies:
        copy.start()
    for copy in copies[:3]:
        copy.wait()
    k0, k1, k2 = ((0.5 * DT) * kappa[k] for k in range(3))

    def body(x, carry):
        lab = labels[x]
        base = jnp.where(lab == 0, k0, jnp.where(lab == 1, k1, k2))
        diff[x] = base * jnp.exp(conc[x])
        return carry

    lax.fori_loop(0, nx, body, 0, unroll=True)
    copies[3].wait()


def pack(conc, labels, kappa, source):
    nx, ny, nz = conc.shape
    outside = [
        pltpu.with_memory_space_constraint(v, pltpu.HBM)
        for v in (kappa, conc, labels, source)
    ]
    return pl.pallas_call(
        pack_kernel,
        out_shape=(f32(nx, ny, nz),) * 3,
        in_specs=[pl.BlockSpec(memory_space=pltpu.HBM)] * 4,
        out_specs=(VMEM,) * 3,
        scratch_shapes=[
            pltpu.VMEM((nx, ny, nz), jnp.int32),
            pltpu.SMEM((3,), F32),
            pltpu.SemaphoreType.DMA((4,)),
        ],
        compiler_params=params(),
        name="pack",
    )(*outside)


def pack_rows_kernel(conc, diff, source, yone, ytwo):
    nx, ny, nz = conc.shape
    flip = low_first("gy")
    for k, ref in enumerate((conc, diff, source)):
        for out, n, head in ((yone, YROWS[0], flip), (ytwo, YROWS[1], ~flip)):
            out[k, 0:nx] = jnp.where(head, ref[:, 0:n, :], ref[:, ny - n : ny, :])
        yone[k, nx] = jnp.zeros((YROWS[0], nz), F32)


def pack_rows(conc, diff, source):
    nx, ny, nz = conc.shape
    return pl.pallas_call(
        pack_rows_kernel,
        out_shape=(f32(3, nx + 1, YROWS[0], nz), f32(3, nx, YROWS[1], nz)),
        in_specs=[VMEM] * 3,
        out_specs=(VMEM,) * 2,
        compiler_params=params(),
        name="pack_rows",
    )(conc, diff, source)


def rows_beside(yone, ytwo, k, x):
    flip = low_first("gy")
    one, two = (slice(n - W, n) for n in YROWS)
    below = jnp.where(flip, yone[k, x, one], ytwo[k, x, two])
    return below, jnp.where(flip, ytwo[k, x, 0:W], yone[k, x, 0:W])


def in_plane_adjoint(v, fy, gy, fz, gz):
    total = fy * up(v, 0) + gy * down(v, 0)
    return total + (fz * up(v, 1) + gz * down(v, 1))


def in_plane_forward(v, fy, gy, fz, gz):
    total = up(gy * v, 0) + down(fy * v, 0)
    return total + (up(gz * v, 1) + down(fz * v, 1))


def in_plane_couplings(u, d):
    first, last = z_ends(u.shape)
    fy = coupling(u, d, up(u, 0), up(d, 0))
    gy = coupling(u, d, down(u, 0), down(d, 0))
    fz = coupling(u, d, jnp.where(last, 0.0, up(u, 1)), jnp.where(last, 0.0, up(d, 1)))
    gz = coupling(
        u, d, jnp.where(first, 0.0, down(u, 1)), jnp.where(first, 0.0, down(d, 1))
    )
    return fy, gy, fz, gz


def face_planes(first_swap, nx):
    at_head = low_first("gx") if first_swap else ~low_first("gx")
    return [jnp.where(at_head, k, nx - 1 - k) for k in range(4)]


def face_fields(u, d, s):
    first, last = z_ends(u[0].shape)

    def between(i, j):
        return coupling(u[i], d[i], u[j], d[j])

    def image(i, before, after):
        fy, gy, fz, gz = in_plane_couplings(u[i], d[i])
        diagonal = 1.0 + ((fy + gy) + (fz + gz)) + (before + after)
        beside = (fy, gy, jnp.where(last, 0.0, fz), jnp.where(first, 0.0, gz))
        total = diagonal * s[i] - before * s[i - 1] - after * s[i + 1]
        total = total - in_plane_adjoint(s[i], *beside)
        return jnp.where(d[i] > 0.0, total, 0.0), diagonal, beside

    back, inward = between(1, 0), between(2, 1)
    near, diagonal, beside = image(1, back, between(1, 2))
    far, _, _ = image(2, inward, between(2, 3))
    rest = diagonal * near - inward * far - in_plane_forward(near, *beside)
    return u[0], d[0], s[0], s[1], between(0, 1), back * near, rest


def face_rows(first_swap, ny):
    return FIELDS * ny + (-1 if first_swap else 1)


def pack_face_kernel(first_swap, conc, diff, source, slab):
    nx, ny, nz = conc.shape
    planes = face_planes(first_swap, nx)
    u, d, s = ([ref[x] for x in planes] for ref in (conc, diff, source))
    for k, v in enumerate(face_fields(u, d, s)):
        n = min(ny, slab.shape[0] - k * ny)
        slab[k * ny : k * ny + n] = v[0:n]
    if not first_swap:
        slab[FIELDS * ny :] = jnp.zeros((1, nz), F32)


def pack_face(first_swap, conc, diff, source):
    _, ny, nz = conc.shape
    return pl.pallas_call(
        functools.partial(pack_face_kernel, first_swap),
        out_shape=f32(face_rows(first_swap, ny), nz),
        in_specs=[VMEM] * 3,
        out_specs=VMEM,
        compiler_params=params(),
        name="pack_face",
    )(conc, diff, source)


def pack_late_kernel(
    conc, diff, source, yone, ytwo, cone, ctwo, near_s, out_s
):
    nx, ny, nz = conc.shape
    rows = ny + 2 * W

    def narrow(row):
        if row < ny:
            return row + W if row < W else row - ny + 3 * W
        return row - ny + 3 * W if row < ny + W else row - ny - W

    for first_swap, late in ((True, cone), (False, ctwo)):
        for j, x in enumerate(face_planes(first_swap, nx)):
            for k, ref in enumerate((conc, diff, source)):
                below, above = rows_beside(yone, ytwo, k, x)
                near_s[k, j, 0:W] = below
                near_s[k, j, W : 2 * W] = ref[x, 0:W]
                near_s[k, j, 2 * W : 3 * W] = ref[x, ny - W : ny]
                near_s[k, j, 3 * W :] = above
        fields = face_fields(*([near_s[k, j] for j in range(4)] for k in range(3)))
        for k, v in enumerate(fields):
            out_s[k] = v
        for at in (W - 2, 3 * W + 1):
            mine, following, k = (out_s[j, at : at + 1] for j in (2, 3, 4))
            out_s[3, at : at + 1] = mine - k * (mine - following)
        row = 0
        for k, begin, n in late_rows(ny):
            at = narrow(begin)
            late[row : row + n] = out_s[k, at : at + n]
            row += n


def pack_late(conc, diff, source, yone, ytwo):
    nx, ny, nz = conc.shape
    return pl.pallas_call(
        pack_late_kernel,
        out_shape=(f32(late_count(ny), nz),) * 2,
        in_specs=[VMEM] * 5,
        out_specs=(VMEM,) * 2,
        scratch_shapes=[
            pltpu.VMEM((3, 4, 4 * W, nz), F32),
            pltpu.VMEM((FIELDS, 4 * W, nz), F32),
        ],
        compiler_params=params(),
        name="pack_late",
    )(conc, diff, source, yone, ytwo)


def own_kernel(
    conc, diff, source, yone, ytwo,
    u_s, d_s, s_s, fx, gx, fy, gy, fz, gz, dg, p1,
):
    nx, ny, nz = conc.shape
    rows = ny + 2 * W
    for k, (own, ref) in enumerate(((conc, u_s), (diff, d_s), (source, s_s))):
        below, above = rows_beside(yone, ytwo, k, slice(0, nx))
        ref[:, 0:ny, :] = own[...]
        ref[:, ny : ny + W, :] = above
        ref[:, ny + W :, :] = below
    first, last = z_ends((rows, nz))

    for q in range(nx):
        u, d = u_s[q], d_s[q]
        fyq, gyq, fzq, gzq = in_plane_couplings(u, d)
        total = 1.0 + ((fyq + gyq) + (fzq + gzq))
        if q + 1 < nx:
            fxq = coupling(u, d, u_s[q + 1], d_s[q + 1])
            fx[q] = fxq
            total = total + fxq
        if q > 0:
            gxq = coupling(u, d, u_s[q - 1], d_s[q - 1])
            gx[q] = gxq
            total = total + gxq
        dg[q] = total
        fy[q] = fyq
        gy[q] = gyq
        fz[q] = jnp.where(last, 0.0, fzq)
        gz[q] = jnp.where(first, 0.0, gzq)

    for q in range(1, nx - 1):
        v = s_s[q]
        total = dg[q] * v - fx[q] * s_s[q + 1] - gx[q] * s_s[q - 1]
        total = total - in_plane_adjoint(v, fy[q], gy[q], fz[q], gz[q])
        p1[q] = jnp.where(d_s[q] > 0.0, total, 0.0)


def own(conc, diff, source, yone, ytwo):
    nx, ny, nz = conc.shape
    return pl.pallas_call(
        own_kernel,
        out_shape=(f32(nx, ny + 2 * W, nz),) * 11,
        in_specs=[VMEM] * 5,
        out_specs=(VMEM,) * 11,
        compiler_params=params(),
        name="own",
    )(conc, diff, source, yone, ytwo)


def mask_halo(total, d, ny):
    return jnp.concatenate([total[0:ny], jnp.where(d > 0.0, total[ny:], 0.0)], axis=0)


def square(v, ny):
    mine = v[0:ny]
    return jnp.sum((mine * mine).reshape(ny // 8, 8, mine.shape[1]), axis=0)


def inside_kernel(d_s, s_s, fx, gx, fy, gy, fz, gz, dg, p1, p2, p3, part):
    nx, rows, nz = d_s.shape
    ny = rows - 2 * W
    sums = [jnp.zeros((8, nz), F32) for _ in range(4)]
    for q in range(nx):
        sums[0] = sums[0] + square(s_s[q], ny)
    for q in range(1, nx - 1):
        sums[1] = sums[1] + square(p1[q], ny)
    for q in range(2, nx - 2):
        v = p1[q]
        total = dg[q] * v - gx[q + 1] * p1[q + 1] - fx[q - 1] * p1[q - 1]
        total = total - in_plane_forward(v, fy[q], gy[q], fz[q], gz[q])
        total = jnp.where(d_s[q] > 0.0, total, 0.0)
        p2[q] = total
        sums[2] = sums[2] + square(total, ny)
    for q in range(3, nx - 3):
        v = p2[q]
        total = dg[q] * v - fx[q] * p2[q + 1] - gx[q] * p2[q - 1]
        total = total - in_plane_adjoint(v, fy[q], gy[q], fz[q], gz[q])
        total = jnp.where(d_s[q] > 0.0, total, 0.0)
        p3[q] = total
        sums[3] = sums[3] + square(total, ny)
    for k in range(4):
        part[k] = sums[k]


def inside(d_s, *fields):
    nx, rows, nz = d_s.shape
    return pl.pallas_call(
        inside_kernel,
        out_shape=(f32(nx, rows, nz),) * 2 + (f32(4, 8, nz),),
        in_specs=[VMEM] * 10,
        out_specs=(VMEM,) * 3,
        compiler_params=params(),
        cost_estimate=pl.CostEstimate(
            flops=1 << 22, bytes_accessed=1 << 23, transcendentals=0
        ),
        name="inside",
    )(d_s, *fields)


def finish_kernel(
    u_s, d_s, s_s, fx, gx, fy, gy, fz, gz, dg, p1_in, p2_in, p3_in, part,
    xtwo, xone, ctwo, cone,
    p1_out, p2_out, p3_out, edge_s, moments,
    side_s, w_s,
):
    nx, rows, nz = d_s.shape
    ny = rows - 2 * W
    flip = low_first("gx")
    first, last = z_ends((rows, nz))

    for side, one in ((0, flip), (1, ~flip)):
        for k in range(FIELDS):
            n = min(ny, xone.shape[0] - k * ny)
            held = slice(k * ny, k * ny + n)
            side_s[side, k, 0:n] = jnp.where(one, xone[held], xtwo[held])
        side_s[side, :, ny:] = jnp.zeros((FIELDS, 2 * W, nz), F32)
        for at in (ny + 1, rows - 2):
            side_s[side, 4, at : at + 1] = jnp.ones((1, nz), F32)
        late = jnp.where(one, cone[...], ctwo[...])
        row = 0
        for field, begin, n in late_rows(ny):
            side_s[side, field, begin : begin + n] = late[row : row + n]
            row += n

    names = dict(
        u=u_s, d=d_s, s=s_s, fx=fx, gx=gx, fy=fy, gy=gy, fz=fz, gz=gz, dg=dg,
        p1=p1_in, p2=p2_in, p3=p3_in,
    )
    place = {(k, q): names[k].at[q] for k in names for q in range(nx)}
    spare = iter(range(w_s.shape[0]))

    def keep(name, q, value):
        place[name, q] = w_s.at[next(spare)]
        place[name, q][...] = value

    def get(name, q):
        return place[name, q][...]

    for side, (o, e, outward, inward) in enumerate(
        ((-1, 0, "gx", "fx"), (nx, nx - 1, "fx", "gx"))
    ):
        beyond = 2 * o - e
        for k, name in enumerate(("u", "d", "s")):
            place[name, o] = side_s.at[side, k]
        place["s", beyond] = side_s.at[side, 3]
        place[outward, o] = side_s.at[side, 4]
        place["m", o] = side_s.at[side, 5]
        place["q", o] = side_s.at[side, 6]
        u, d, ue, de = get("u", o), get("d", o), get("u", e), get("d", e)
        back = coupling(u, d, ue, de)
        out = coupling(ue, de, u, d)
        fyq, gyq, fzq, gzq = in_plane_couplings(u, d)
        total = 1.0 + get(outward, o) + back + ((fyq + gyq) + (fzq + gzq))
        new = {
            (inward, o): back,
            (outward, e): out,
            ("dg", o): total,
            ("dg", e): get("dg", e) + out,
            ("fy", o): fyq,
            ("gy", o): gyq,
            ("fz", o): jnp.where(last, 0.0, fzq),
            ("gz", o): jnp.where(first, 0.0, gzq),
        }
        for k, (key, value) in enumerate(new.items()):
            place[key] = edge_s.at[side, k]
            place[key][...] = value

    def masked(total, q):
        if q in (-1, nx):
            return jnp.where(get("d", q) > 0.0, total, 0.0)
        return mask_halo(total, place["d", q][ny:], ny)

    def in_plane(q):
        return [get(k, q) for k in ("fy", "gy", "fz", "gz")]

    def adjoint_at(w, q):
        v = get(w, q)
        total = get("dg", q) * v - get("fx", q) * get(w, q + 1)
        total = total - get("gx", q) * get(w, q - 1)
        return masked(total - in_plane_adjoint(v, *in_plane(q)), q)

    def forward_at(w, q):
        v = get(w, q)
        above = get("m", q) if q == nx else get("gx", q + 1) * get(w, q + 1)
        below = get("m", q) if q == -1 else get("fx", q - 1) * get(w, q - 1)
        total = get("dg", q) * v - above - below
        return masked(total - in_plane_forward(v, *in_plane(q)), q)

    sums = [part[k] for k in range(4)]

    def sweep(k, apply, w, name, out, ready):
        for q in range(-1, nx + 1):
            if ready <= q < nx - ready:
                out[q] = get(name, q)[0:ny]
                continue
            value = apply(w, q)
            keep(name, q, value)
            if 0 <= q < nx:
                out[q] = value[0:ny]
                sums[k] = sums[k] + square(value, ny)

    sweep(1, adjoint_at, "s", "p1", p1_out, 1)
    sweep(2, forward_at, "p1", "p2", p2_out, 2)
    for o, outward in ((-1, "gx"), (nx, "fx")):
        beyond = -2 if o == -1 else nx + 1
        keep("p2", beyond, get("q", o) - get(outward, o) * get("p1", o))
    for q in range(-1, nx + 1):
        if 3 <= q < nx - 3:
            p3_out[q + 1] = get("p3", q)
            continue
        value = adjoint_at("p2", q)
        p3_out[q + 1] = value
        if 0 <= q < nx:
            sums[3] = sums[3] + square(value, ny)

    slot = lax.broadcasted_iota(jnp.int32, (1, LANES), 1)
    row = jnp.zeros((1, LANES), F32)
    for k in range(4):
        row = jnp.where(slot == k, jnp.sum(sums[k]), row)
    moments[...] = jnp.broadcast_to(row, moments.shape)


def finish(copies, ny, *fields):
    nx, rows, nz = fields[0].shape
    steps = 4 + 6 + 2
    return pl.pallas_call(
        finish_kernel,
        out_shape=(
            f32(nx, ny, nz),
            f32(nx, ny, nz),
            f32(nx + 2, rows, nz),
            f32(2, 8, rows, nz),
            f32(copies, 1, LANES),
        ),
        in_specs=[VMEM] * len(fields),
        out_specs=(VMEM,) * 5,
        scratch_shapes=[
            pltpu.VMEM((2, FIELDS, rows, nz), F32),
            pltpu.VMEM((steps, rows, nz), F32),
        ],
        compiler_params=params(),
        name="finish",
    )(*fields)


def combine_kernel(
    moments, source, p1, p2, p3, edge, fx, gx, fy, gy, fz, gz, dg,
    adjoint_out, residual_out,
    adjoint, residual, sems,
):
    nx, ny, nz = source.shape
    m = jnp.sum(moments[...], axis=0)
    m0, m1, m2, m3 = (m[:, k : k + 1] for k in range(4))
    alpha = m0 / m1
    beta = alpha * (m2 / m1) - 1.0
    grow = 1.0 + beta
    image = grow * grow * m1 - 2.0 * grow * alpha * m2 + alpha * alpha * m3
    step = (beta * m0) / image
    near = alpha + step * grow
    far = step * alpha
    copies = []

    def send(src, dst, begin, end):
        planes = pl.ds(begin, end - begin)
        copies.append(
            pltpu.make_async_copy(src.at[planes], dst.at[planes], sems.at[len(copies)])
        )
        copies[-1].start()

    half = nx // 2
    for begin in (0, half):
        for x in range(begin, begin + half):
            adjoint[x] = near * p1[x] - far * p3[x + 1, 0:ny]
        send(adjoint, adjoint_out, begin, begin + half)
    for x in range(nx):
        v = p3[x + 1]
        above = edge[1, 0] if x == nx - 1 else gx[x + 1]
        below = edge[0, 0] if x == 0 else fx[x - 1]
        diagonal = edge[0, 3] if x == 0 else edge[1, 3] if x == nx - 1 else dg[x]
        p4 = diagonal * v - above * p3[x + 2] - below * p3[x]
        p4 = p4 - in_plane_forward(v, fy[x], gy[x], fz[x], gz[x])
        residual[x] = source[x] - near * p2[x] + far * p4[0:ny]
        if x % 2 == 1:
            send(residual, residual_out, x - 1, x + 1)
    for copy in copies:
        copy.wait()


def combine(moments, source, p1, p2, p3, edge, *couplings):
    nx, ny, nz = source.shape
    return pl.pallas_call(
        combine_kernel,
        out_shape=(f32(nx, ny, nz),) * 2,
        in_specs=[VMEM] * (6 + len(couplings)),
        out_specs=(pl.BlockSpec(memory_space=pltpu.HBM),) * 2,
        scratch_shapes=[
            pltpu.VMEM((nx, ny, nz), F32),
            pltpu.VMEM((nx, ny, nz), F32),
            pltpu.SemaphoreType.DMA((2 + nx // 2,)),
        ],
        compiler_params=params(),
        name="combine",
    )(moments, source, p1, p2, p3, edge, *couplings)


def swap(cells, axis, first):
    pairs = [(i, i + 1) for i in range(first, lax.axis_size(axis) - 1, 2)]
    return lax.ppermute(cells, axis, pairs + [(j, i) for i, j in pairs])


def local(conc, labels, kappa, source):
    ny = conc.shape[1]
    conc, source, diff = pack(conc, labels, kappa, source)
    xtwo = swap(pack_face(False, conc, diff, source), "gx", 0)
    xone = swap(pack_face(True, conc, diff, source), "gx", 1)
    yone, ytwo = pack_rows(conc, diff, source)
    yone = swap(yone, "gy", 1)
    ytwo = swap(ytwo, "gy", 0)
    cone, ctwo = pack_late(conc, diff, source, yone, ytwo)
    ctwo = swap(ctwo, "gx", 0)
    cone = swap(cone, "gx", 1)
    fields = own(conc, diff, source, yone, ytwo)
    inner = inside(*fields[1:])
    p1, p2, p3, edge, moments = finish(
        lax.axis_size(("gx", "gy")), ny, *fields, *inner, xtwo, xone, ctwo, cone
    )
    moments = lax.all_to_all(moments, ("gx", "gy"), 0, 0, tiled=True)
    return combine(moments, source, p1, p2, p3, edge, *fields[3:10])


def solution(mesh):
    return jax.shard_map(
        local,
        mesh=mesh,
        in_specs=(P("gx", "gy", None), P("gx", "gy", None), P(), P("gx", "gy", None)),
        out_specs=(P("gx", "gy", None), P("gx", "gy", None)),
        check_vma=False,
    )
```

```python
import functools

import jax
import jax.numpy as jnp
from jax import lax
from jax.experimental import pallas as pl
from jax.experimental.pallas import tpu as pltpu
from jax.sharding import PartitionSpec as P

ITERS = 2
DT = 0.5
W = 2 * ITERS
F32 = jnp.float32
LANES = 128
YROWS = (8, 8)
VMEM = pl.BlockSpec(memory_space=pltpu.VMEM)


def low_first(axis):
    return lax.axis_index(axis) % 2 == 0


def up(v, axis):
    return pltpu.roll(v, v.shape[axis] - 1, axis)


def down(v, axis):
    return pltpu.roll(v, 1, axis)


def z_ends(shape):
    index = lax.broadcasted_iota(jnp.int32, shape, 1)
    return index == 0, index == shape[1] - 1


def coupling(u, d, un, dn):
    return d + d * u - d * un + dn


def params(megabytes=16):
    return pltpu.CompilerParams(vmem_limit_bytes=megabytes << 20)


def f32(*shape):
    return jax.ShapeDtypeStruct(shape, F32)


FIELDS = 7


def late_rows(ny):
    rows = ny + 2 * W
    for field, n in ((0, 3), (1, 3), (2, 3), (3, 2), (4, 1), (5, 1)):
        yield field, ny, n
        yield field, rows - n, n
    for field, n in ((5, 1), (6, 2)):
        yield field, 0, n
        yield field, ny - n, n


def late_count(ny):
    return sum(n for _, _, n in late_rows(ny))


def pack_kernel(
    kappa_in, conc_in, labels_in, source_in,
    conc, source, diff,
    labels, kappa, sems,
):
    nx, ny, nz = conc.shape
    copies = [
        pltpu.make_async_copy(src, dst, sems.at[k])
        for k, (src, dst) in enumerate(
            (
                (labels_in, labels),
                (conc_in, conc),
                (kappa_in, kappa),
                (source_in, source),
            )
        )
    ]
    for copy in copies:
        copy.start()
    for copy in copies[:3]:
        copy.wait()
    k0, k1, k2 = ((0.5 * DT) * kappa[k] for k in range(3))

    def body(x, carry):
        lab = labels[x]
        base = jnp.where(lab == 0, k0, jnp.where(lab == 1, k1, k2))
        diff[x] = base * jnp.exp(conc[x])
        return carry

    lax.fori_loop(0, nx, body, 0, unroll=True)
    copies[3].wait()


def pack(conc, labels, kappa, source):
    nx, ny, nz = conc.shape
    outside = [
        pltpu.with_memory_space_constraint(v, pltpu.HBM)
        for v in (kappa, conc, labels, source)
    ]
    return pl.pallas_call(
        pack_kernel,
        out_shape=(f32(nx, ny, nz),) * 3,
        in_specs=[pl.BlockSpec(memory_space=pltpu.HBM)] * 4,
        out_specs=(VMEM,) * 3,
        scratch_shapes=[
            pltpu.VMEM((nx, ny, nz), jnp.int32),
            pltpu.SMEM((3,), F32),
            pltpu.SemaphoreType.DMA((4,)),
        ],
        compiler_params=params(),
        name="pack",
    )(*outside)


def pack_rows_kernel(conc, diff, source, yone, ytwo):
    nx, ny, nz = conc.shape
    flip = low_first("gy")
    for k, ref in enumerate((conc, diff, source)):
        for out, n, head in ((yone, YROWS[0], flip), (ytwo, YROWS[1], ~flip)):
            out[k, 0:nx] = jnp.where(head, ref[:, 0:n, :], ref[:, ny - n : ny, :])
        yone[k, nx] = jnp.zeros((YROWS[0], nz), F32)


def pack_rows(conc, diff, source):
    nx, ny, nz = conc.shape
    return pl.pallas_call(
        pack_rows_kernel,
        out_shape=(f32(3, nx + 1, YROWS[0], nz), f32(3, nx, YROWS[1], nz)),
        in_specs=[VMEM] * 3,
        out_specs=(VMEM,) * 2,
        compiler_params=params(),
        name="pack_rows",
    )(conc, diff, source)


def rows_beside(yone, ytwo, k, x):
    flip = low_first("gy")
    one, two = (slice(n - W, n) for n in YROWS)
    below = jnp.where(flip, yone[k, x, one], ytwo[k, x, two])
    return below, jnp.where(flip, ytwo[k, x, 0:W], yone[k, x, 0:W])


def in_plane_adjoint(v, fy, gy, fz, gz):
    total = fy * up(v, 0) + gy * down(v, 0)
    return total + (fz * up(v, 1) + gz * down(v, 1))


def in_plane_forward(v, fy, gy, fz, gz):
    total = up(gy * v, 0) + down(fy * v, 0)
    return total + (up(gz * v, 1) + down(fz * v, 1))


def in_plane_couplings(u, d):
    first, last = z_ends(u.shape)
    fy = coupling(u, d, up(u, 0), up(d, 0))
    gy = coupling(u, d, down(u, 0), down(d, 0))
    fz = coupling(u, d, jnp.where(last, 0.0, up(u, 1)), jnp.where(last, 0.0, up(d, 1)))
    gz = coupling(
        u, d, jnp.where(first, 0.0, down(u, 1)), jnp.where(first, 0.0, down(d, 1))
    )
    return fy, gy, fz, gz


def face_planes(first_swap, nx):
    at_head = low_first("gx") if first_swap else ~low_first("gx")
    return [jnp.where(at_head, k, nx - 1 - k) for k in range(4)]


def face_fields(u, d, s):
    first, last = z_ends(u[0].shape)

    def between(i, j):
        return coupling(u[i], d[i], u[j], d[j])

    def image(i, before, after):
        fy, gy, fz, gz = in_plane_couplings(u[i], d[i])
        diagonal = 1.0 + ((fy + gy) + (fz + gz)) + (before + after)
        beside = (fy, gy, jnp.where(last, 0.0, fz), jnp.where(first, 0.0, gz))
        total = diagonal * s[i] - before * s[i - 1] - after * s[i + 1]
        total = total - in_plane_adjoint(s[i], *beside)
        return jnp.where(d[i] > 0.0, total, 0.0), diagonal, beside

    back, inward = between(1, 0), between(2, 1)
    near, diagonal, beside = image(1, back, between(1, 2))
    far, _, _ = image(2, inward, between(2, 3))
    rest = diagonal * near - inward * far - in_plane_forward(near, *beside)
    return u[0], d[0], s[0], s[1], between(0, 1), back * near, rest


def face_rows(first_swap, ny):
    return FIELDS * ny + (-1 if first_swap else 1)


def pack_face_kernel(first_swap, conc, diff, source, slab):
    nx, ny, nz = conc.shape
    planes = face_planes(first_swap, nx)
    u, d, s = ([ref[x] for x in planes] for ref in (conc, diff, source))
    for k, v in enumerate(face_fields(u, d, s)):
        n = min(ny, slab.shape[0] - k * ny)
        slab[k * ny : k * ny + n] = v[0:n]
    if not first_swap:
        slab[FIELDS * ny :] = jnp.zeros((1, nz), F32)


def pack_face(first_swap, conc, diff, source):
    _, ny, nz = conc.shape
    return pl.pallas_call(
        functools.partial(pack_face_kernel, first_swap),
        out_shape=f32(face_rows(first_swap, ny), nz),
        in_specs=[VMEM] * 3,
        out_specs=VMEM,
        compiler_params=params(),
        name="pack_face",
    )(conc, diff, source)


def pack_late_kernel(
    conc, diff, source, yone, ytwo, cone, ctwo, near_s, out_s
):
    nx, ny, nz = conc.shape
    rows = ny + 2 * W

    def narrow(row):
        if row < ny:
            return row + W if row < W else row - ny + 3 * W
        return row - ny + 3 * W if row < ny + W else row - ny - W

    for first_swap, late in ((True, cone), (False, ctwo)):
        for j, x in enumerate(face_planes(first_swap, nx)):
            for k, ref in enumerate((conc, diff, source)):
                below, above = rows_beside(yone, ytwo, k, x)
                near_s[k, j, 0:W] = below
                near_s[k, j, W : 2 * W] = ref[x, 0:W]
                near_s[k, j, 2 * W : 3 * W] = ref[x, ny - W : ny]
                near_s[k, j, 3 * W :] = above
        fields = face_fields(*([near_s[k, j] for j in range(4)] for k in range(3)))
        for k, v in enumerate(fields):
            out_s[k] = v
        for at in (W - 2, 3 * W + 1):
            mine, following, k = (out_s[j, at : at + 1] for j in (2, 3, 4))
            out_s[3, at : at + 1] = mine - k * (mine - following)
        row = 0
        for k, begin, n in late_rows(ny):
            at = narrow(begin)
            late[row : row + n] = out_s[k, at : at + n]
            row += n


def pack_late(conc, diff, source, yone, ytwo):
    nx, ny, nz = conc.shape
    return pl.pallas_call(
        pack_late_kernel,
        out_shape=(f32(late_count(ny), nz),) * 2,
        in_specs=[VMEM] * 5,
        out_specs=(VMEM,) * 2,
        scratch_shapes=[
            pltpu.VMEM((3, 4, 4 * W, nz), F32),
            pltpu.VMEM((FIELDS, 4 * W, nz), F32),
        ],
        compiler_params=params(),
        name="pack_late",
    )(conc, diff, source, yone, ytwo)


def own_kernel(
    conc, diff, source, yone, ytwo,
    u_s, d_s, s_s, fx, gx, fy, gy, fz, gz, dg, p1,
):
    nx, ny, nz = conc.shape
    rows = ny + 2 * W
    for k, (own, ref) in enumerate(((conc, u_s), (diff, d_s), (source, s_s))):
        below, above = rows_beside(yone, ytwo, k, slice(0, nx))
        ref[:, 0:ny, :] = own[...]
        ref[:, ny : ny + W, :] = above
        ref[:, ny + W :, :] = below
    first, last = z_ends((rows, nz))

    for q in range(nx):
        u, d = u_s[q], d_s[q]
        fyq, gyq, fzq, gzq = in_plane_couplings(u, d)
        total = 1.0 + ((fyq + gyq) + (fzq + gzq))
        if q + 1 < nx:
            fxq = coupling(u, d, u_s[q + 1], d_s[q + 1])
            fx[q] = fxq
            total = total + fxq
        if q > 0:
            gxq = coupling(u, d, u_s[q - 1], d_s[q - 1])
            gx[q] = gxq
            total = total + gxq
        dg[q] = total
        fy[q] = fyq
        gy[q] = gyq
        fz[q] = jnp.where(last, 0.0, fzq)
        gz[q] = jnp.where(first, 0.0, gzq)

    for q in range(1, nx - 1):
        v = s_s[q]
        total = dg[q] * v - fx[q] * s_s[q + 1] - gx[q] * s_s[q - 1]
        total = total - in_plane_adjoint(v, fy[q], gy[q], fz[q], gz[q])
        p1[q] = jnp.where(d_s[q] > 0.0, total, 0.0)


def own(conc, diff, source, yone, ytwo):
    nx, ny, nz = conc.shape
    return pl.pallas_call(
        own_kernel,
        out_shape=(f32(nx, ny + 2 * W, nz),) * 11,
        in_specs=[VMEM] * 5,
        out_specs=(VMEM,) * 11,
        compiler_params=params(),
        name="own",
    )(conc, diff, source, yone, ytwo)


def mask_halo(total, d, ny):
    return jnp.concatenate([total[0:ny], jnp.where(d > 0.0, total[ny:], 0.0)], axis=0)


def product(v, w, ny):
    both = v[0:ny] * w[0:ny]
    return jnp.sum(both.reshape(ny // 8, 8, both.shape[1]), axis=0)


def ratio(over, under):
    over, under = (jnp.sum(v, axis=(0, 1), keepdims=True) for v in (over, under))
    return jnp.where(under > 0.0, over / jnp.where(under > 0.0, under, 1.0), 0.0)


SUMS = 6


def inside_kernel(d_s, s_s, fx, gx, fy, gy, fz, gz, dg, p1, p2, p3, part):
    nx, rows, nz = d_s.shape
    ny = rows - 2 * W
    sums = [jnp.zeros((8, nz), F32) for _ in range(SUMS)]
    over, under = jnp.zeros((8, nz), F32), jnp.zeros((8, nz), F32)
    for q in range(nx):
        sums[0] = sums[0] + product(s_s[q], s_s[q], ny)
    for q in range(1, nx - 1):
        sums[1] = sums[1] + product(p1[q], p1[q], ny)
    for q in range(2, nx - 2):
        v = p1[q]
        total = dg[q] * v - gx[q + 1] * p1[q + 1] - fx[q - 1] * p1[q - 1]
        total = total - in_plane_forward(v, fy[q], gy[q], fz[q], gz[q])
        p2[q] = jnp.where(d_s[q] > 0.0, total, 0.0)
        over = over + product(total, s_s[q], ny)
        under = under + product(s_s[q], s_s[q], ny)
    theta = ratio(over, under)
    for q in range(2, nx - 2):
        v = p2[q] - theta * s_s[q]
        sums[2] = sums[2] + product(s_s[q], v, ny)
        sums[3] = sums[3] + product(v, v, ny)
    over, under = jnp.zeros((8, nz), F32), jnp.zeros((8, nz), F32)
    for q in range(3, nx - 3):
        v = p2[q]
        total = dg[q] * v - fx[q] * p2[q + 1] - gx[q] * p2[q - 1]
        total = total - in_plane_adjoint(v, fy[q], gy[q], fz[q], gz[q])
        p3[q] = jnp.where(d_s[q] > 0.0, total, 0.0)
        over = over + product(total, p1[q], ny)
        under = under + product(p1[q], p1[q], ny)
    phi = ratio(over, under)
    for q in range(3, nx - 3):
        w = p3[q] - phi * p1[q]
        sums[4] = sums[4] + product(p1[q], w, ny)
        sums[5] = sums[5] + product(w, w, ny)
    for k, total in enumerate(sums):
        part[k] = total
    part[SUMS] = jnp.broadcast_to(theta, (8, nz))
    part[SUMS + 1] = jnp.broadcast_to(phi, (8, nz))


def inside(d_s, *fields):
    nx, rows, nz = d_s.shape
    return pl.pallas_call(
        inside_kernel,
        out_shape=(f32(nx, rows, nz),) * 2 + (f32(SUMS + 2, 8, nz),),
        in_specs=[VMEM] * 10,
        out_specs=(VMEM,) * 3,
        compiler_params=params(),
        cost_estimate=pl.CostEstimate(
            flops=1 << 22, bytes_accessed=1 << 23, transcendentals=0
        ),
        name="inside",
    )(d_s, *fields)


def finish_kernel(
    u_s, d_s, s_s, fx, gx, fy, gy, fz, gz, dg, p1_in, p2_in, p3_in, part,
    xtwo, xone, ctwo, cone,
    p1_out, p2_out, p3_out, edge_s, moments,
    side_s, w_s,
):
    nx, rows, nz = d_s.shape
    ny = rows - 2 * W
    flip = low_first("gx")
    first, last = z_ends((rows, nz))

    for side, one in ((0, flip), (1, ~flip)):
        for k in range(FIELDS):
            n = min(ny, xone.shape[0] - k * ny)
            held = slice(k * ny, k * ny + n)
            side_s[side, k, 0:n] = jnp.where(one, xone[held], xtwo[held])
        side_s[side, :, ny:] = jnp.zeros((FIELDS, 2 * W, nz), F32)
        for at in (ny + 1, rows - 2):
            side_s[side, 4, at : at + 1] = jnp.ones((1, nz), F32)
        late = jnp.where(one, cone[...], ctwo[...])
        row = 0
        for field, begin, n in late_rows(ny):
            side_s[side, field, begin : begin + n] = late[row : row + n]
            row += n

    names = dict(
        u=u_s, d=d_s, s=s_s, fx=fx, gx=gx, fy=fy, gy=gy, fz=fz, gz=gz, dg=dg,
        p1=p1_in, p2=p2_in, p3=p3_in,
    )
    place = {(k, q): names[k].at[q] for k in names for q in range(nx)}
    spare = iter(range(w_s.shape[0]))

    def keep(name, q, value):
        place[name, q] = w_s.at[next(spare)]
        place[name, q][...] = value

    def get(name, q):
        return place[name, q][...]

    for side, (o, e, outward, inward) in enumerate(
        ((-1, 0, "gx", "fx"), (nx, nx - 1, "fx", "gx"))
    ):
        beyond = 2 * o - e
        for k, name in enumerate(("u", "d", "s")):
            place[name, o] = side_s.at[side, k]
        place["s", beyond] = side_s.at[side, 3]
        place[outward, o] = side_s.at[side, 4]
        place["m", o] = side_s.at[side, 5]
        place["q", o] = side_s.at[side, 6]
        u, d, ue, de = get("u", o), get("d", o), get("u", e), get("d", e)
        back = coupling(u, d, ue, de)
        out = coupling(ue, de, u, d)
        fyq, gyq, fzq, gzq = in_plane_couplings(u, d)
        total = 1.0 + get(outward, o) + back + ((fyq + gyq) + (fzq + gzq))
        new = {
            (inward, o): back,
            (outward, e): out,
            ("dg", o): total,
            ("dg", e): get("dg", e) + out,
            ("fy", o): fyq,
            ("gy", o): gyq,
            ("fz", o): jnp.where(last, 0.0, fzq),
            ("gz", o): jnp.where(first, 0.0, gzq),
        }
        for k, (key, value) in enumerate(new.items()):
            place[key] = edge_s.at[side, k]
            place[key][...] = value

    def masked(total, q):
        if q in (-1, nx):
            return jnp.where(get("d", q) > 0.0, total, 0.0)
        return mask_halo(total, place["d", q][ny:], ny)

    def in_plane(q):
        return [get(k, q) for k in ("fy", "gy", "fz", "gz")]

    def adjoint_at(w, q):
        v = get(w, q)
        total = get("dg", q) * v - get("fx", q) * get(w, q + 1)
        total = total - get("gx", q) * get(w, q - 1)
        return masked(total - in_plane_adjoint(v, *in_plane(q)), q)

    def forward_at(w, q):
        v = get(w, q)
        above = get("m", q) if q == nx else get("gx", q + 1) * get(w, q + 1)
        below = get("m", q) if q == -1 else get("fx", q - 1) * get(w, q - 1)
        total = get("dg", q) * v - above - below
        return masked(total - in_plane_forward(v, *in_plane(q)), q)

    sums = [part[k] for k in range(SUMS)]
    theta, phi = (part[SUMS + k][0:1, 0:1] for k in range(2))

    def add(k, v, w):
        sums[k] = sums[k] + product(v, w, ny)

    for q in range(-1, nx + 1):
        if 1 <= q < nx - 1:
            p1_out[q] = get("p1", q)[0:ny]
            continue
        value = adjoint_at("s", q)
        keep("p1", q, value)
        if 0 <= q < nx:
            p1_out[q] = value[0:ny]
            add(1, value, value)
    for q in range(-1, nx + 1):
        if 2 <= q < nx - 2:
            p2_out[q] = get("p2", q)[0:ny]
            continue
        value = forward_at("p1", q)
        keep("p2", q, value)
        if 0 <= q < nx:
            p2_out[q] = value[0:ny]
            v = value - theta * get("s", q)
            add(2, get("s", q), v)
            add(3, v, v)
    for o, outward in ((-1, "gx"), (nx, "fx")):
        beyond = -2 if o == -1 else nx + 1
        keep("p2", beyond, get("q", o) - get(outward, o) * get("p1", o))
    for q in range(-1, nx + 1):
        if 3 <= q < nx - 3:
            p3_out[q + 1] = get("p3", q)
            continue
        value = adjoint_at("p2", q)
        p3_out[q + 1] = value
        if 0 <= q < nx:
            w = value - phi * get("p1", q)
            add(4, get("p1", q), w)
            add(5, w, w)

    slot = lax.broadcasted_iota(jnp.int32, (1, LANES), 1)
    row = jnp.where(slot == SUMS, theta, phi)
    for k in range(SUMS):
        row = jnp.where(slot == k, jnp.sum(sums[k]), row)
    moments[...] = jnp.broadcast_to(row, moments.shape)


def finish(copies, ny, *fields):
    nx, rows, nz = fields[0].shape
    steps = 4 + 6 + 2
    return pl.pallas_call(
        finish_kernel,
        out_shape=(
            f32(nx, ny, nz),
            f32(nx, ny, nz),
            f32(nx + 2, rows, nz),
            f32(2, 8, rows, nz),
            f32(copies, 1, LANES),
        ),
        in_specs=[VMEM] * len(fields),
        out_specs=(VMEM,) * 5,
        scratch_shapes=[
            pltpu.VMEM((2, FIELDS, rows, nz), F32),
            pltpu.VMEM((steps, rows, nz), F32),
        ],
        compiler_params=params(),
        name="finish",
    )(*fields)


def combine_kernel(
    moments, source, p1, p2, p3, edge, fx, gx, fy, gy, fz, gz, dg,
    adjoint_out, residual_out,
    adjoint, residual, sems,
):
    nx, ny, nz = source.shape
    sums = [moments[:, k : k + 1] for k in range(SUMS + 2)]
    ss, pp, sv, vv, pw, ww, theta, phi = sums

    def total(v):
        return jnp.sum(v, axis=0, keepdims=True)

    def norm(g, a, shift, first, mixed, second):
        rest = g - a * shift
        return total(rest * rest * first - 2.0 * a * rest * mixed + a * a * second)

    m0 = total(ss)
    alpha = m0 / total(pp)
    new = norm(1.0, alpha, theta, ss, sv, vv)
    grow = 1.0 + new / m0
    step = new / norm(grow, alpha, phi, pp, pw, ww)
    near = alpha + step * grow
    far = step * alpha
    copies = []

    def send(src, dst, begin, end):
        planes = pl.ds(begin, end - begin)
        copies.append(
            pltpu.make_async_copy(src.at[planes], dst.at[planes], sems.at[len(copies)])
        )
        copies[-1].start()

    half = nx // 2
    for begin in (0, half):
        for x in range(begin, begin + half):
            adjoint[x] = near * p1[x] - far * p3[x + 1, 0:ny]
        send(adjoint, adjoint_out, begin, begin + half)
    for x in range(nx):
        v = p3[x + 1]
        above = edge[1, 0] if x == nx - 1 else gx[x + 1]
        below = edge[0, 0] if x == 0 else fx[x - 1]
        diagonal = edge[0, 3] if x == 0 else edge[1, 3] if x == nx - 1 else dg[x]
        p4 = diagonal * v - above * p3[x + 2] - below * p3[x]
        p4 = p4 - in_plane_forward(v, fy[x], gy[x], fz[x], gz[x])
        residual[x] = source[x] - near * p2[x] + far * p4[0:ny]
        if x % 2 == 1:
            send(residual, residual_out, x - 1, x + 1)
    for copy in copies:
        copy.wait()


def combine(moments, source, p1, p2, p3, edge, *couplings):
    nx, ny, nz = source.shape
    return pl.pallas_call(
        combine_kernel,
        out_shape=(f32(nx, ny, nz),) * 2,
        in_specs=[VMEM] * (6 + len(couplings)),
        out_specs=(pl.BlockSpec(memory_space=pltpu.HBM),) * 2,
        scratch_shapes=[
            pltpu.VMEM((nx, ny, nz), F32),
            pltpu.VMEM((nx, ny, nz), F32),
            pltpu.SemaphoreType.DMA((2 + nx // 2,)),
        ],
        compiler_params=params(),
        name="combine",
    )(moments, source, p1, p2, p3, edge, *couplings)


def swap(cells, axis, first):
    pairs = [(i, i + 1) for i in range(first, lax.axis_size(axis) - 1, 2)]
    return lax.ppermute(cells, axis, pairs + [(j, i) for i, j in pairs])


def local(conc, labels, kappa, source):
    ny = conc.shape[1]
    conc, source, diff = pack(conc, labels, kappa, source)
    xtwo = swap(pack_face(False, conc, diff, source), "gx", 0)
    xone = swap(pack_face(True, conc, diff, source), "gx", 1)
    yone, ytwo = pack_rows(conc, diff, source)
    yone = swap(yone, "gy", 1)
    ytwo = swap(ytwo, "gy", 0)
    cone, ctwo = pack_late(conc, diff, source, yone, ytwo)
    ctwo = swap(ctwo, "gx", 0)
    cone = swap(cone, "gx", 1)
    fields = own(conc, diff, source, yone, ytwo)
    inner = inside(*fields[1:])
    p1, p2, p3, edge, moments = finish(
        lax.axis_size(("gx", "gy")), ny, *fields, *inner, xtwo, xone, ctwo, cone
    )
    moments = lax.all_to_all(moments, ("gx", "gy"), 0, 0, tiled=True)
    moments = moments.reshape(-1, LANES)
    return combine(moments, source, p1, p2, p3, edge, *fields[3:10])


def solution(mesh):
    return jax.shard_map(
        local,
        mesh=mesh,
        in_specs=(P("gx", "gy", None), P("gx", "gy", None), P(), P("gx", "gy", None)),
        out_specs=(P("gx", "gy", None), P("gx", "gy", None)),
        check_vma=False,
    )
```

```python
import functools

import jax
import jax.numpy as jnp
from jax import lax
from jax.experimental import pallas as pl
from jax.experimental.pallas import tpu as pltpu
from jax.sharding import PartitionSpec as P

ITERS = 2
DT = 0.5
W = 2 * ITERS
F32 = jnp.float32
LANES = 128
YROWS = (8, 8)
VMEM = pl.BlockSpec(memory_space=pltpu.VMEM)


def low_first(axis):
    return lax.axis_index(axis) % 2 == 0


def up(v, axis):
    return pltpu.roll(v, v.shape[axis] - 1, axis)


def down(v, axis):
    return pltpu.roll(v, 1, axis)


def z_ends(shape):
    index = lax.broadcasted_iota(jnp.int32, shape, 1)
    return index == 0, index == shape[1] - 1


def coupling(u, d, un, dn):
    return d + d * u - d * un + dn


def params(megabytes=16):
    return pltpu.CompilerParams(vmem_limit_bytes=megabytes << 20)


def f32(*shape):
    return jax.ShapeDtypeStruct(shape, F32)


FIELDS = 7


def late_rows(ny):
    rows = ny + 2 * W
    for field, n in ((0, 3), (1, 3), (2, 3), (3, 2), (4, 1), (5, 1)):
        yield field, ny, n
        yield field, rows - n, n
    for field, n in ((5, 1), (6, 2)):
        yield field, 0, n
        yield field, ny - n, n


def late_count(ny):
    return sum(n for _, _, n in late_rows(ny))


def pack_kernel(
    kappa_in, conc_in, labels_in, source_in,
    conc, source, diff,
    labels, kappa, sems,
):
    nx, ny, nz = conc.shape
    copies = [
        pltpu.make_async_copy(src, dst, sems.at[k])
        for k, (src, dst) in enumerate(
            (
                (labels_in, labels),
                (conc_in, conc),
                (kappa_in, kappa),
                (source_in, source),
            )
        )
    ]
    for copy in copies:
        copy.start()
    for copy in copies[:3]:
        copy.wait()
    k0, k1, k2 = ((0.5 * DT) * kappa[k] for k in range(3))

    def body(x, carry):
        lab = labels[x]
        base = jnp.where(lab == 0, k0, jnp.where(lab == 1, k1, k2))
        diff[x] = base * jnp.exp(conc[x])
        return carry

    lax.fori_loop(0, nx, body, 0, unroll=True)
    copies[3].wait()


def pack(conc, labels, kappa, source):
    nx, ny, nz = conc.shape
    outside = [
        pltpu.with_memory_space_constraint(v, pltpu.HBM)
        for v in (kappa, conc, labels, source)
    ]
    return pl.pallas_call(
        pack_kernel,
        out_shape=(f32(nx, ny, nz),) * 3,
        in_specs=[pl.BlockSpec(memory_space=pltpu.HBM)] * 4,
        out_specs=(VMEM,) * 3,
        scratch_shapes=[
            pltpu.VMEM((nx, ny, nz), jnp.int32),
            pltpu.SMEM((3,), F32),
            pltpu.SemaphoreType.DMA((4,)),
        ],
        compiler_params=params(),
        name="pack",
    )(*outside)


def pack_rows_kernel(conc, diff, source, yone, ytwo):
    nx, ny, nz = conc.shape
    flip = low_first("gy")
    for k, ref in enumerate((conc, diff, source)):
        for out, n, head in ((yone, YROWS[0], flip), (ytwo, YROWS[1], ~flip)):
            out[k, 0:nx] = jnp.where(head, ref[:, 0:n, :], ref[:, ny - n : ny, :])
        yone[k, nx] = jnp.zeros((YROWS[0], nz), F32)


def pack_rows(conc, diff, source):
    nx, ny, nz = conc.shape
    return pl.pallas_call(
        pack_rows_kernel,
        out_shape=(f32(3, nx + 1, YROWS[0], nz), f32(3, nx, YROWS[1], nz)),
        in_specs=[VMEM] * 3,
        out_specs=(VMEM,) * 2,
        compiler_params=params(),
        name="pack_rows",
    )(conc, diff, source)


def rows_beside(yone, ytwo, k, x):
    flip = low_first("gy")
    one, two = (slice(n - W, n) for n in YROWS)
    below = jnp.where(flip, yone[k, x, one], ytwo[k, x, two])
    return below, jnp.where(flip, ytwo[k, x, 0:W], yone[k, x, 0:W])


def in_plane_adjoint(v, fy, gy, fz, gz):
    total = fy * up(v, 0) + gy * down(v, 0)
    return total + (fz * up(v, 1) + gz * down(v, 1))


def in_plane_forward(v, fy, gy, fz, gz):
    total = up(gy * v, 0) + down(fy * v, 0)
    return total + (up(gz * v, 1) + down(fz * v, 1))


def in_plane_couplings(u, d):
    first, last = z_ends(u.shape)
    fy = coupling(u, d, up(u, 0), up(d, 0))
    gy = coupling(u, d, down(u, 0), down(d, 0))
    fz = coupling(u, d, jnp.where(last, 0.0, up(u, 1)), jnp.where(last, 0.0, up(d, 1)))
    gz = coupling(
        u, d, jnp.where(first, 0.0, down(u, 1)), jnp.where(first, 0.0, down(d, 1))
    )
    return fy, gy, fz, gz


def face_planes(first_swap, nx):
    at_head = low_first("gx") if first_swap else ~low_first("gx")
    return [jnp.where(at_head, k, nx - 1 - k) for k in range(4)]


def face_fields(u, d, s):
    first, last = z_ends(u[0].shape)

    def between(i, j):
        return coupling(u[i], d[i], u[j], d[j])

    def image(i, before, after):
        fy, gy, fz, gz = in_plane_couplings(u[i], d[i])
        diagonal = 1.0 + ((fy + gy) + (fz + gz)) + (before + after)
        beside = (fy, gy, jnp.where(last, 0.0, fz), jnp.where(first, 0.0, gz))
        total = diagonal * s[i] - before * s[i - 1] - after * s[i + 1]
        total = total - in_plane_adjoint(s[i], *beside)
        return jnp.where(d[i] > 0.0, total, 0.0), diagonal, beside

    back, inward = between(1, 0), between(2, 1)
    near, diagonal, beside = image(1, back, between(1, 2))
    far, _, _ = image(2, inward, between(2, 3))
    rest = diagonal * near - inward * far - in_plane_forward(near, *beside)
    return u[0], d[0], s[0], s[1], between(0, 1), back * near, rest


def face_rows(first_swap, ny):
    return FIELDS * ny + (-1 if first_swap else 1)


def pack_face_kernel(first_swap, conc, diff, source, slab):
    nx, ny, nz = conc.shape
    planes = face_planes(first_swap, nx)
    u, d, s = ([ref[x] for x in planes] for ref in (conc, diff, source))
    for k, v in enumerate(face_fields(u, d, s)):
        n = min(ny, slab.shape[0] - k * ny)
        slab[k * ny : k * ny + n] = v[0:n]
    if not first_swap:
        slab[FIELDS * ny :] = jnp.zeros((1, nz), F32)


def pack_face(first_swap, conc, diff, source):
    _, ny, nz = conc.shape
    return pl.pallas_call(
        functools.partial(pack_face_kernel, first_swap),
        out_shape=f32(face_rows(first_swap, ny), nz),
        in_specs=[VMEM] * 3,
        out_specs=VMEM,
        compiler_params=params(),
        name="pack_face",
    )(conc, diff, source)


def pack_late_kernel(
    conc, diff, source, yone, ytwo, cone, ctwo, near_s, out_s
):
    nx, ny, nz = conc.shape
    rows = ny + 2 * W

    def narrow(row):
        if row < ny:
            return row + W if row < W else row - ny + 3 * W
        return row - ny + 3 * W if row < ny + W else row - ny - W

    for first_swap, late in ((True, cone), (False, ctwo)):
        for j, x in enumerate(face_planes(first_swap, nx)):
            for k, ref in enumerate((conc, diff, source)):
                below, above = rows_beside(yone, ytwo, k, x)
                near_s[k, j, 0:W] = below
                near_s[k, j, W : 2 * W] = ref[x, 0:W]
                near_s[k, j, 2 * W : 3 * W] = ref[x, ny - W : ny]
                near_s[k, j, 3 * W :] = above
        fields = face_fields(*([near_s[k, j] for j in range(4)] for k in range(3)))
        for k, v in enumerate(fields):
            out_s[k] = v
        for at in (W - 2, 3 * W + 1):
            mine, following, k = (out_s[j, at : at + 1] for j in (2, 3, 4))
            out_s[3, at : at + 1] = mine - k * (mine - following)
        row = 0
        for k, begin, n in late_rows(ny):
            at = narrow(begin)
            late[row : row + n] = out_s[k, at : at + n]
            row += n


def pack_late(conc, diff, source, yone, ytwo):
    nx, ny, nz = conc.shape
    return pl.pallas_call(
        pack_late_kernel,
        out_shape=(f32(late_count(ny), nz),) * 2,
        in_specs=[VMEM] * 5,
        out_specs=(VMEM,) * 2,
        scratch_shapes=[
            pltpu.VMEM((3, 4, 4 * W, nz), F32),
            pltpu.VMEM((FIELDS, 4 * W, nz), F32),
        ],
        compiler_params=params(),
        name="pack_late",
    )(conc, diff, source, yone, ytwo)


def own_kernel(
    conc, diff, source, yone, ytwo,
    u_s, d_s, s_s, fx, gx, fy, gy, fz, gz, dg, p1,
):
    nx, ny, nz = conc.shape
    rows = ny + 2 * W
    for k, (own, ref) in enumerate(((conc, u_s), (diff, d_s), (source, s_s))):
        below, above = rows_beside(yone, ytwo, k, slice(0, nx))
        ref[:, 0:ny, :] = own[...]
        ref[:, ny : ny + W, :] = above
        ref[:, ny + W :, :] = below
    first, last = z_ends((rows, nz))

    for q in range(nx):
        u, d = u_s[q], d_s[q]
        fyq, gyq, fzq, gzq = in_plane_couplings(u, d)
        total = 1.0 + ((fyq + gyq) + (fzq + gzq))
        if q + 1 < nx:
            fxq = coupling(u, d, u_s[q + 1], d_s[q + 1])
            fx[q] = fxq
            total = total + fxq
        if q > 0:
            gxq = coupling(u, d, u_s[q - 1], d_s[q - 1])
            gx[q] = gxq
            total = total + gxq
        dg[q] = total
        fy[q] = fyq
        gy[q] = gyq
        fz[q] = jnp.where(last, 0.0, fzq)
        gz[q] = jnp.where(first, 0.0, gzq)

    for q in range(1, nx - 1):
        v = s_s[q]
        total = dg[q] * v - fx[q] * s_s[q + 1] - gx[q] * s_s[q - 1]
        total = total - in_plane_adjoint(v, fy[q], gy[q], fz[q], gz[q])
        p1[q] = jnp.where(d_s[q] > 0.0, total, 0.0)


def own(conc, diff, source, yone, ytwo):
    nx, ny, nz = conc.shape
    return pl.pallas_call(
        own_kernel,
        out_shape=(f32(nx, ny + 2 * W, nz),) * 11,
        in_specs=[VMEM] * 5,
        out_specs=(VMEM,) * 11,
        compiler_params=params(),
        name="own",
    )(conc, diff, source, yone, ytwo)


def mask_halo(total, d, ny):
    return jnp.concatenate([total[0:ny], jnp.where(d > 0.0, total[ny:], 0.0)], axis=0)


def product(v, w, ny):
    both = v[0:ny] * w[0:ny]
    return jnp.sum(both.reshape(ny // 8, 8, both.shape[1]), axis=0)


def ratio(over, under, whole):
    over, under, whole = (
        jnp.sum(v, axis=(0, 1), keepdims=True) for v in (over, under, whole)
    )
    under = jnp.where(whole <= 16.0 * under, under, whole)
    return jnp.where(under > 0.0, over / jnp.where(under > 0.0, under, 1.0), 0.0)


SUMS = 6


def inside_kernel(d_s, s_s, fx, gx, fy, gy, fz, gz, dg, p1, p2, p3, part):
    nx, rows, nz = d_s.shape
    ny = rows - 2 * W
    sums = [jnp.zeros((8, nz), F32) for _ in range(SUMS)]
    over, under = jnp.zeros((8, nz), F32), jnp.zeros((8, nz), F32)
    for q in range(nx):
        sums[0] = sums[0] + product(s_s[q], s_s[q], ny)
    for q in range(1, nx - 1):
        sums[1] = sums[1] + product(p1[q], p1[q], ny)
    for q in range(2, nx - 2):
        v = p1[q]
        total = dg[q] * v - gx[q + 1] * p1[q + 1] - fx[q - 1] * p1[q - 1]
        total = total - in_plane_forward(v, fy[q], gy[q], fz[q], gz[q])
        p2[q] = jnp.where(d_s[q] > 0.0, total, 0.0)
        over = over + product(total, s_s[q], ny)
        under = under + product(s_s[q], s_s[q], ny)
    theta = ratio(over, under, sums[0])
    for q in range(2, nx - 2):
        v = p2[q] - theta * s_s[q]
        sums[2] = sums[2] + product(s_s[q], v, ny)
        sums[3] = sums[3] + product(v, v, ny)
    over, under = jnp.zeros((8, nz), F32), jnp.zeros((8, nz), F32)
    for q in range(3, nx - 3):
        v = p2[q]
        total = dg[q] * v - fx[q] * p2[q + 1] - gx[q] * p2[q - 1]
        total = total - in_plane_adjoint(v, fy[q], gy[q], fz[q], gz[q])
        p3[q] = jnp.where(d_s[q] > 0.0, total, 0.0)
        over = over + product(total, p1[q], ny)
        under = under + product(p1[q], p1[q], ny)
    phi = ratio(over, under, sums[1])
    for q in range(3, nx - 3):
        w = p3[q] - phi * p1[q]
        sums[4] = sums[4] + product(p1[q], w, ny)
        sums[5] = sums[5] + product(w, w, ny)
    for k, total in enumerate(sums):
        part[k] = total
    part[SUMS] = jnp.broadcast_to(theta, (8, nz))
    part[SUMS + 1] = jnp.broadcast_to(phi, (8, nz))


def inside(d_s, *fields):
    nx, rows, nz = d_s.shape
    return pl.pallas_call(
        inside_kernel,
        out_shape=(f32(nx, rows, nz),) * 2 + (f32(SUMS + 2, 8, nz),),
        in_specs=[VMEM] * 10,
        out_specs=(VMEM,) * 3,
        compiler_params=params(),
        cost_estimate=pl.CostEstimate(
            flops=1 << 22, bytes_accessed=1 << 23, transcendentals=0
        ),
        name="inside",
    )(d_s, *fields)


def finish_kernel(
    u_s, d_s, s_s, fx, gx, fy, gy, fz, gz, dg, p1_in, p2_in, p3_in, part,
    xtwo, xone, ctwo, cone,
    p1_out, p2_out, p3_out, edge_s, moments,
    side_s, w_s,
):
    nx, rows, nz = d_s.shape
    ny = rows - 2 * W
    flip = low_first("gx")
    first, last = z_ends((rows, nz))

    for side, one in ((0, flip), (1, ~flip)):
        for k in range(FIELDS):
            n = min(ny, xone.shape[0] - k * ny)
            held = slice(k * ny, k * ny + n)
            side_s[side, k, 0:n] = jnp.where(one, xone[held], xtwo[held])
        side_s[side, :, ny:] = jnp.zeros((FIELDS, 2 * W, nz), F32)
        for at in (ny + 1, rows - 2):
            side_s[side, 4, at : at + 1] = jnp.ones((1, nz), F32)
        late = jnp.where(one, cone[...], ctwo[...])
        row = 0
        for field, begin, n in late_rows(ny):
            side_s[side, field, begin : begin + n] = late[row : row + n]
            row += n

    names = dict(
        u=u_s, d=d_s, s=s_s, fx=fx, gx=gx, fy=fy, gy=gy, fz=fz, gz=gz, dg=dg,
        p1=p1_in, p2=p2_in, p3=p3_in,
    )
    place = {(k, q): names[k].at[q] for k in names for q in range(nx)}
    spare = iter(range(w_s.shape[0]))

    def keep(name, q, value):
        place[name, q] = w_s.at[next(spare)]
        place[name, q][...] = value

    def get(name, q):
        return place[name, q][...]

    for side, (o, e, outward, inward) in enumerate(
        ((-1, 0, "gx", "fx"), (nx, nx - 1, "fx", "gx"))
    ):
        beyond = 2 * o - e
        for k, name in enumerate(("u", "d", "s")):
            place[name, o] = side_s.at[side, k]
        place["s", beyond] = side_s.at[side, 3]
        place[outward, o] = side_s.at[side, 4]
        place["m", o] = side_s.at[side, 5]
        place["q", o] = side_s.at[side, 6]
        u, d, ue, de = get("u", o), get("d", o), get("u", e), get("d", e)
        back = coupling(u, d, ue, de)
        out = coupling(ue, de, u, d)
        fyq, gyq, fzq, gzq = in_plane_couplings(u, d)
        total = 1.0 + get(outward, o) + back + ((fyq + gyq) + (fzq + gzq))
        new = {
            (inward, o): back,
            (outward, e): out,
            ("dg", o): total,
            ("dg", e): get("dg", e) + out,
            ("fy", o): fyq,
            ("gy", o): gyq,
            ("fz", o): jnp.where(last, 0.0, fzq),
            ("gz", o): jnp.where(first, 0.0, gzq),
        }
        for k, (key, value) in enumerate(new.items()):
            place[key] = edge_s.at[side, k]
            place[key][...] = value

    def masked(total, q):
        if q in (-1, nx):
            return jnp.where(get("d", q) > 0.0, total, 0.0)
        return mask_halo(total, place["d", q][ny:], ny)

    def in_plane(q):
        return [get(k, q) for k in ("fy", "gy", "fz", "gz")]

    def adjoint_at(w, q):
        v = get(w, q)
        total = get("dg", q) * v - get("fx", q) * get(w, q + 1)
        total = total - get("gx", q) * get(w, q - 1)
        return masked(total - in_plane_adjoint(v, *in_plane(q)), q)

    def forward_at(w, q):
        v = get(w, q)
        above = get("m", q) if q == nx else get("gx", q + 1) * get(w, q + 1)
        below = get("m", q) if q == -1 else get("fx", q - 1) * get(w, q - 1)
        total = get("dg", q) * v - above - below
        return masked(total - in_plane_forward(v, *in_plane(q)), q)

    sums = [part[k] for k in range(SUMS)]
    theta, phi = (part[SUMS + k][0:1, 0:1] for k in range(2))

    def add(k, v, w):
        sums[k] = sums[k] + product(v, w, ny)

    for q in range(-1, nx + 1):
        if 1 <= q < nx - 1:
            p1_out[q] = get("p1", q)[0:ny]
            continue
        value = adjoint_at("s", q)
        keep("p1", q, value)
        if 0 <= q < nx:
            p1_out[q] = value[0:ny]
            add(1, value, value)
    for q in range(-1, nx + 1):
        if 2 <= q < nx - 2:
            p2_out[q] = get("p2", q)[0:ny]
            continue
        value = forward_at("p1", q)
        keep("p2", q, value)
        if 0 <= q < nx:
            p2_out[q] = value[0:ny]
            v = value - theta * get("s", q)
            add(2, get("s", q), v)
            add(3, v, v)
    for o, outward in ((-1, "gx"), (nx, "fx")):
        beyond = -2 if o == -1 else nx + 1
        keep("p2", beyond, get("q", o) - get(outward, o) * get("p1", o))
    for q in range(-1, nx + 1):
        if 3 <= q < nx - 3:
            p3_out[q + 1] = get("p3", q)
            continue
        value = adjoint_at("p2", q)
        p3_out[q + 1] = value
        if 0 <= q < nx:
            w = value - phi * get("p1", q)
            add(4, get("p1", q), w)
            add(5, w, w)

    slot = lax.broadcasted_iota(jnp.int32, (1, LANES), 1)
    row = jnp.where(slot == SUMS, theta, phi)
    for k in range(SUMS):
        row = jnp.where(slot == k, jnp.sum(sums[k]), row)
    moments[...] = jnp.broadcast_to(row, moments.shape)


def finish(copies, ny, *fields):
    nx, rows, nz = fields[0].shape
    steps = 4 + 6 + 2
    return pl.pallas_call(
        finish_kernel,
        out_shape=(
            f32(nx, ny, nz),
            f32(nx, ny, nz),
            f32(nx + 2, rows, nz),
            f32(2, 8, rows, nz),
            f32(copies, 1, LANES),
        ),
        in_specs=[VMEM] * len(fields),
        out_specs=(VMEM,) * 5,
        scratch_shapes=[
            pltpu.VMEM((2, FIELDS, rows, nz), F32),
            pltpu.VMEM((steps, rows, nz), F32),
        ],
        compiler_params=params(),
        name="finish",
    )(*fields)


def combine_kernel(
    moments, source, p1, p2, p3, edge, fx, gx, fy, gy, fz, gz, dg,
    adjoint_out, residual_out,
    adjoint, residual, sems,
):
    nx, ny, nz = source.shape
    sums = [moments[:, k : k + 1] for k in range(SUMS + 2)]
    ss, pp, sv, vv, pw, ww, theta, phi = sums

    def total(v):
        return jnp.sum(v, axis=0, keepdims=True)

    def norm(g, a, shift, first, mixed, second):
        rest = g - a * shift
        return total(rest * rest * first - 2.0 * a * rest * mixed + a * a * second)

    m0 = total(ss)
    alpha = m0 / total(pp)
    new = norm(1.0, alpha, theta, ss, sv, vv)
    grow = 1.0 + new / m0
    step = new / norm(grow, alpha, phi, pp, pw, ww)
    near = alpha + step * grow
    far = step * alpha
    copies = []

    def send(src, dst, begin, end):
        planes = pl.ds(begin, end - begin)
        copies.append(
            pltpu.make_async_copy(src.at[planes], dst.at[planes], sems.at[len(copies)])
        )
        copies[-1].start()

    half = nx // 2
    for begin in (0, half):
        for x in range(begin, begin + half):
            adjoint[x] = near * p1[x] - far * p3[x + 1, 0:ny]
        send(adjoint, adjoint_out, begin, begin + half)
    for x in range(nx):
        v = p3[x + 1]
        above = edge[1, 0] if x == nx - 1 else gx[x + 1]
        below = edge[0, 0] if x == 0 else fx[x - 1]
        diagonal = edge[0, 3] if x == 0 else edge[1, 3] if x == nx - 1 else dg[x]
        p4 = diagonal * v - above * p3[x + 2] - below * p3[x]
        p4 = p4 - in_plane_forward(v, fy[x], gy[x], fz[x], gz[x])
        residual[x] = source[x] - near * p2[x] + far * p4[0:ny]
        if x % 2 == 1:
            send(residual, residual_out, x - 1, x + 1)
    for copy in copies:
        copy.wait()


def combine(moments, source, p1, p2, p3, edge, *couplings):
    nx, ny, nz = source.shape
    return pl.pallas_call(
        combine_kernel,
        out_shape=(f32(nx, ny, nz),) * 2,
        in_specs=[VMEM] * (6 + len(couplings)),
        out_specs=(pl.BlockSpec(memory_space=pltpu.HBM),) * 2,
        scratch_shapes=[
            pltpu.VMEM((nx, ny, nz), F32),
            pltpu.VMEM((nx, ny, nz), F32),
            pltpu.SemaphoreType.DMA((2 + nx // 2,)),
        ],
        compiler_params=params(),
        name="combine",
    )(moments, source, p1, p2, p3, edge, *couplings)


def swap(cells, axis, first):
    pairs = [(i, i + 1) for i in range(first, lax.axis_size(axis) - 1, 2)]
    return lax.ppermute(cells, axis, pairs + [(j, i) for i, j in pairs])


def local(conc, labels, kappa, source):
    ny = conc.shape[1]
    conc, source, diff = pack(conc, labels, kappa, source)
    xtwo = swap(pack_face(False, conc, diff, source), "gx", 0)
    xone = swap(pack_face(True, conc, diff, source), "gx", 1)
    yone, ytwo = pack_rows(conc, diff, source)
    yone = swap(yone, "gy", 1)
    ytwo = swap(ytwo, "gy", 0)
    cone, ctwo = pack_late(conc, diff, source, yone, ytwo)
    ctwo = swap(ctwo, "gx", 0)
    cone = swap(cone, "gx", 1)
    fields = own(conc, diff, source, yone, ytwo)
    inner = inside(*fields[1:])
    p1, p2, p3, edge, moments = finish(
        lax.axis_size(("gx", "gy")), ny, *fields, *inner, xtwo, xone, ctwo, cone
    )
    moments = lax.all_to_all(moments, ("gx", "gy"), 0, 0, tiled=True)
    moments = moments.reshape(-1, LANES)
    return combine(moments, source, p1, p2, p3, edge, *fields[3:10])


def solution(mesh):
    return jax.shard_map(
        local,
        mesh=mesh,
        in_specs=(P("gx", "gy", None), P("gx", "gy", None), P(), P("gx", "gy", None)),
        out_specs=(P("gx", "gy", None), P("gx", "gy", None)),
        check_vma=False,
    )
```

```python
import functools

import jax
import jax.numpy as jnp
from jax import lax
from jax.experimental import pallas as pl
from jax.experimental.pallas import tpu as pltpu
from jax.sharding import PartitionSpec as P

ITERS = 2
DT = 0.5
W = 2 * ITERS
F32 = jnp.float32
LANES = 128
YROWS = (8, 8)
VMEM = pl.BlockSpec(memory_space=pltpu.VMEM)


def low_first(axis):
    return lax.axis_index(axis) % 2 == 0


def up(v, axis):
    return pltpu.roll(v, v.shape[axis] - 1, axis)


def down(v, axis):
    return pltpu.roll(v, 1, axis)


def z_ends(shape):
    index = lax.broadcasted_iota(jnp.int32, shape, 1)
    return index == 0, index == shape[1] - 1


def coupling(u, d, un, dn):
    return d + d * u - d * un + dn


def params(megabytes=16):
    return pltpu.CompilerParams(vmem_limit_bytes=megabytes << 20)


def f32(*shape):
    return jax.ShapeDtypeStruct(shape, F32)


FIELDS = 7


def late_rows(ny):
    rows = ny + 2 * W
    for field, n in ((0, 3), (1, 3), (2, 3), (3, 2), (4, 1), (5, 1)):
        yield field, ny, n
        yield field, rows - n, n
    for field, n in ((5, 1), (6, 2)):
        yield field, 0, n
        yield field, ny - n, n


def late_count(ny):
    return sum(n for _, _, n in late_rows(ny))


def pack_kernel(
    kappa_in, conc_in, labels_in, source_in,
    conc, source, diff,
    labels, kappa, sems,
):
    nx, ny, nz = conc.shape
    copies = [
        pltpu.make_async_copy(src, dst, sems.at[k])
        for k, (src, dst) in enumerate(
            (
                (labels_in, labels),
                (conc_in, conc),
                (kappa_in, kappa),
                (source_in, source),
            )
        )
    ]
    for copy in copies:
        copy.start()
    for copy in copies[:3]:
        copy.wait()
    k0, k1, k2 = ((0.5 * DT) * kappa[k] for k in range(3))

    def body(x, carry):
        lab = labels[x]
        base = jnp.where(lab == 0, k0, jnp.where(lab == 1, k1, k2))
        diff[x] = base * jnp.exp(conc[x])
        return carry

    lax.fori_loop(0, nx, body, 0, unroll=True)
    copies[3].wait()


def pack(conc, labels, kappa, source):
    nx, ny, nz = conc.shape
    outside = [
        pltpu.with_memory_space_constraint(v, pltpu.HBM)
        for v in (kappa, conc, labels, source)
    ]
    return pl.pallas_call(
        pack_kernel,
        out_shape=(f32(nx, ny, nz),) * 3,
        in_specs=[pl.BlockSpec(memory_space=pltpu.HBM)] * 4,
        out_specs=(VMEM,) * 3,
        scratch_shapes=[
            pltpu.VMEM((nx, ny, nz), jnp.int32),
            pltpu.SMEM((3,), F32),
            pltpu.SemaphoreType.DMA((4,)),
        ],
        compiler_params=params(),
        name="pack",
    )(*outside)


def pack_rows_kernel(conc, diff, source, yone, ytwo):
    nx, ny, nz = conc.shape
    flip = low_first("gy")
    for k, ref in enumerate((conc, diff, source)):
        for out, n, head in ((yone, YROWS[0], flip), (ytwo, YROWS[1], ~flip)):
            out[k, 0:nx] = jnp.where(head, ref[:, 0:n, :], ref[:, ny - n : ny, :])
        yone[k, nx] = jnp.zeros((YROWS[0], nz), F32)


def pack_rows(conc, diff, source):
    nx, ny, nz = conc.shape
    return pl.pallas_call(
        pack_rows_kernel,
        out_shape=(f32(3, nx + 1, YROWS[0], nz), f32(3, nx, YROWS[1], nz)),
        in_specs=[VMEM] * 3,
        out_specs=(VMEM,) * 2,
        compiler_params=params(),
        name="pack_rows",
    )(conc, diff, source)


def rows_beside(yone, ytwo, k, x):
    flip = low_first("gy")
    one, two = (slice(n - W, n) for n in YROWS)
    below = jnp.where(flip, yone[k, x, one], ytwo[k, x, two])
    return below, jnp.where(flip, ytwo[k, x, 0:W], yone[k, x, 0:W])


def in_plane_adjoint(v, fy, gy, fz, gz):
    total = fy * up(v, 0) + gy * down(v, 0)
    return total + (fz * up(v, 1) + gz * down(v, 1))


def in_plane_forward(v, fy, gy, fz, gz):
    total = up(gy * v, 0) + down(fy * v, 0)
    return total + (up(gz * v, 1) + down(fz * v, 1))


def in_plane_couplings(u, d):
    first, last = z_ends(u.shape)
    fy = coupling(u, d, up(u, 0), up(d, 0))
    gy = coupling(u, d, down(u, 0), down(d, 0))
    fz = coupling(u, d, jnp.where(last, 0.0, up(u, 1)), jnp.where(last, 0.0, up(d, 1)))
    gz = coupling(
        u, d, jnp.where(first, 0.0, down(u, 1)), jnp.where(first, 0.0, down(d, 1))
    )
    return fy, gy, fz, gz


def face_planes(first_swap, nx):
    at_head = low_first("gx") if first_swap else ~low_first("gx")
    return [jnp.where(at_head, k, nx - 1 - k) for k in range(4)]


def face_fields(u, d, s):
    first, last = z_ends(u[0].shape)

    def between(i, j):
        return coupling(u[i], d[i], u[j], d[j])

    def image(i, before, after):
        fy, gy, fz, gz = in_plane_couplings(u[i], d[i])
        diagonal = 1.0 + ((fy + gy) + (fz + gz)) + (before + after)
        beside = (fy, gy, jnp.where(last, 0.0, fz), jnp.where(first, 0.0, gz))
        total = diagonal * s[i] - before * s[i - 1] - after * s[i + 1]
        total = total - in_plane_adjoint(s[i], *beside)
        return jnp.where(d[i] > 0.0, total, 0.0), diagonal, beside

    back, inward = between(1, 0), between(2, 1)
    near, diagonal, beside = image(1, back, between(1, 2))
    far, _, _ = image(2, inward, between(2, 3))
    rest = diagonal * near - inward * far - in_plane_forward(near, *beside)
    return u[0], d[0], s[0], s[1], between(0, 1), back * near, rest


def face_rows(first_swap, ny):
    return FIELDS * ny + (-1 if first_swap else 1)


def pack_face_kernel(first_swap, conc, diff, source, slab):
    nx, ny, nz = conc.shape
    planes = face_planes(first_swap, nx)
    u, d, s = ([ref[x] for x in planes] for ref in (conc, diff, source))
    for k, v in enumerate(face_fields(u, d, s)):
        n = min(ny, slab.shape[0] - k * ny)
        slab[k * ny : k * ny + n] = v[0:n]
    if not first_swap:
        slab[FIELDS * ny :] = jnp.zeros((1, nz), F32)


def pack_face(first_swap, conc, diff, source):
    _, ny, nz = conc.shape
    return pl.pallas_call(
        functools.partial(pack_face_kernel, first_swap),
        out_shape=f32(face_rows(first_swap, ny), nz),
        in_specs=[VMEM] * 3,
        out_specs=VMEM,
        compiler_params=params(),
        name="pack_face",
    )(conc, diff, source)


def pack_late_kernel(
    conc, diff, source, yone, ytwo, cone, ctwo, near_s, out_s
):
    nx, ny, nz = conc.shape
    rows = ny + 2 * W

    def narrow(row):
        if row < ny:
            return row + W if row < W else row - ny + 3 * W
        return row - ny + 3 * W if row < ny + W else row - ny - W

    for first_swap, late in ((True, cone), (False, ctwo)):
        for j, x in enumerate(face_planes(first_swap, nx)):
            for k, ref in enumerate((conc, diff, source)):
                below, above = rows_beside(yone, ytwo, k, x)
                near_s[k, j, 0:W] = below
                near_s[k, j, W : 2 * W] = ref[x, 0:W]
                near_s[k, j, 2 * W : 3 * W] = ref[x, ny - W : ny]
                near_s[k, j, 3 * W :] = above
        fields = face_fields(*([near_s[k, j] for j in range(4)] for k in range(3)))
        for k, v in enumerate(fields):
            out_s[k] = v
        for at in (W - 2, 3 * W + 1):
            mine, following, k = (out_s[j, at : at + 1] for j in (2, 3, 4))
            out_s[3, at : at + 1] = mine - k * (mine - following)
        row = 0
        for k, begin, n in late_rows(ny):
            at = narrow(begin)
            late[row : row + n] = out_s[k, at : at + n]
            row += n


def pack_late(conc, diff, source, yone, ytwo):
    nx, ny, nz = conc.shape
    return pl.pallas_call(
        pack_late_kernel,
        out_shape=(f32(late_count(ny), nz),) * 2,
        in_specs=[VMEM] * 5,
        out_specs=(VMEM,) * 2,
        scratch_shapes=[
            pltpu.VMEM((3, 4, 4 * W, nz), F32),
            pltpu.VMEM((FIELDS, 4 * W, nz), F32),
        ],
        compiler_params=params(),
        name="pack_late",
    )(conc, diff, source, yone, ytwo)


def own_kernel(
    conc, diff, source, yone, ytwo,
    u_s, d_s, s_s, fx, gx, fy, gy, fz, gz, dg, p1,
):
    nx, ny, nz = conc.shape
    rows = ny + 2 * W
    for k, (own, ref) in enumerate(((conc, u_s), (diff, d_s), (source, s_s))):
        below, above = rows_beside(yone, ytwo, k, slice(0, nx))
        ref[:, 0:ny, :] = own[...]
        ref[:, ny : ny + W, :] = above
        ref[:, ny + W :, :] = below
    first, last = z_ends((rows, nz))

    for q in range(nx):
        u, d = u_s[q], d_s[q]
        fyq, gyq, fzq, gzq = in_plane_couplings(u, d)
        total = 1.0 + ((fyq + gyq) + (fzq + gzq))
        if q + 1 < nx:
            fxq = coupling(u, d, u_s[q + 1], d_s[q + 1])
            fx[q] = fxq
            total = total + fxq
        if q > 0:
            gxq = coupling(u, d, u_s[q - 1], d_s[q - 1])
            gx[q] = gxq
            total = total + gxq
        dg[q] = total
        fy[q] = fyq
        gy[q] = gyq
        fz[q] = jnp.where(last, 0.0, fzq)
        gz[q] = jnp.where(first, 0.0, gzq)

    for q in range(1, nx - 1):
        v = s_s[q]
        total = dg[q] * v - fx[q] * s_s[q + 1] - gx[q] * s_s[q - 1]
        total = total - in_plane_adjoint(v, fy[q], gy[q], fz[q], gz[q])
        p1[q] = jnp.where(d_s[q] > 0.0, total, 0.0)


def own(conc, diff, source, yone, ytwo):
    nx, ny, nz = conc.shape
    return pl.pallas_call(
        own_kernel,
        out_shape=(f32(nx, ny + 2 * W, nz),) * 11,
        in_specs=[VMEM] * 5,
        out_specs=(VMEM,) * 11,
        compiler_params=params(),
        name="own",
    )(conc, diff, source, yone, ytwo)


def mask_halo(total, d, ny):
    return jnp.concatenate([total[0:ny], jnp.where(d > 0.0, total[ny:], 0.0)], axis=0)


def product(v, w, ny):
    both = v[0:ny] * w[0:ny]
    return jnp.sum(both.reshape(ny // 8, 8, both.shape[1]), axis=0)


def ratio(over, under, whole):
    over, under, whole = (
        jnp.sum(v, axis=(0, 1), keepdims=True) for v in (over, under, whole)
    )
    under = jnp.where(whole <= 16.0 * under, under, whole)
    return jnp.where(under > 0.0, over / jnp.where(under > 0.0, under, 1.0), 0.0)


SUMS = 6


def inside_kernel(d_s, s_s, fx, gx, fy, gy, fz, gz, dg, p1, p2, p3, part):
    nx, rows, nz = d_s.shape
    ny = rows - 2 * W
    sums = [jnp.zeros((8, nz), F32) for _ in range(SUMS)]
    over, under = jnp.zeros((8, nz), F32), jnp.zeros((8, nz), F32)
    for q in range(nx):
        sums[0] = sums[0] + product(s_s[q], s_s[q], ny)
    for q in range(1, nx - 1):
        sums[1] = sums[1] + product(p1[q], p1[q], ny)
    for q in range(2, nx - 2):
        v = p1[q]
        total = dg[q] * v - gx[q + 1] * p1[q + 1] - fx[q - 1] * p1[q - 1]
        total = total - in_plane_forward(v, fy[q], gy[q], fz[q], gz[q])
        p2[q] = jnp.where(d_s[q] > 0.0, total, 0.0)
        over = over + product(total, s_s[q], ny)
        under = under + product(s_s[q], s_s[q], ny)
    theta = ratio(over, under, sums[0])
    for q in range(2, nx - 2):
        v = p2[q] - theta * s_s[q]
        sums[2] = sums[2] + product(s_s[q], v, ny)
        sums[3] = sums[3] + product(v, v, ny)
    over, under = jnp.zeros((8, nz), F32), jnp.zeros((8, nz), F32)
    for q in range(3, nx - 3):
        v = p2[q]
        total = dg[q] * v - fx[q] * p2[q + 1] - gx[q] * p2[q - 1]
        total = total - in_plane_adjoint(v, fy[q], gy[q], fz[q], gz[q])
        p3[q] = jnp.where(d_s[q] > 0.0, total, 0.0)
        over = over + product(total, p1[q], ny)
        under = under + product(p1[q], p1[q], ny)
    phi = ratio(over, under, sums[1])
    for q in range(3, nx - 3):
        w = p3[q] - phi * p1[q]
        sums[4] = sums[4] + product(p1[q], w, ny)
        sums[5] = sums[5] + product(w, w, ny)
    for k, total in enumerate(sums):
        part[k] = total
    part[SUMS] = jnp.broadcast_to(theta, (8, nz))
    part[SUMS + 1] = jnp.broadcast_to(phi, (8, nz))


def inside(d_s, *fields):
    nx, rows, nz = d_s.shape
    return pl.pallas_call(
        inside_kernel,
        out_shape=(f32(nx, rows, nz),) * 2 + (f32(SUMS + 2, 8, nz),),
        in_specs=[VMEM] * 10,
        out_specs=(VMEM,) * 3,
        compiler_params=params(),
        cost_estimate=pl.CostEstimate(
            flops=1 << 22, bytes_accessed=1 << 23, transcendentals=0
        ),
        name="inside",
    )(d_s, *fields)


def finish_kernel(
    u_s, d_s, s_s, fx, gx, fy, gy, fz, gz, dg, p1_in, p2_in, p3_in, part,
    xtwo, xone, ctwo, cone,
    p1_out, p2_out, p3_out, edge_s, moments,
    side_s, w_s,
):
    nx, rows, nz = d_s.shape
    ny = rows - 2 * W
    flip = low_first("gx")
    first, last = z_ends((rows, nz))

    for side, one in ((0, flip), (1, ~flip)):
        for k in range(FIELDS):
            n = min(ny, xone.shape[0] - k * ny)
            held = slice(k * ny, k * ny + n)
            side_s[side, k, 0:n] = jnp.where(one, xone[held], xtwo[held])
        side_s[side, :, ny:] = jnp.zeros((FIELDS, 2 * W, nz), F32)
        for at in (ny + 1, rows - 2):
            side_s[side, 4, at : at + 1] = jnp.ones((1, nz), F32)
        late = jnp.where(one, cone[...], ctwo[...])
        row = 0
        for field, begin, n in late_rows(ny):
            side_s[side, field, begin : begin + n] = late[row : row + n]
            row += n

    names = dict(
        u=u_s, d=d_s, s=s_s, fx=fx, gx=gx, fy=fy, gy=gy, fz=fz, gz=gz, dg=dg,
        p1=p1_in, p2=p2_in, p3=p3_in,
    )
    place = {(k, q): names[k].at[q] for k in names for q in range(nx)}
    spare = iter(range(w_s.shape[0]))

    def keep(name, q, value):
        place[name, q] = w_s.at[next(spare)]
        place[name, q][...] = value

    def get(name, q):
        return place[name, q][...]

    for side, (o, e, outward, inward) in enumerate(
        ((-1, 0, "gx", "fx"), (nx, nx - 1, "fx", "gx"))
    ):
        beyond = 2 * o - e
        for k, name in enumerate(("u", "d", "s")):
            place[name, o] = side_s.at[side, k]
        place["s", beyond] = side_s.at[side, 3]
        place[outward, o] = side_s.at[side, 4]
        place["m", o] = side_s.at[side, 5]
        place["q", o] = side_s.at[side, 6]
        u, d, ue, de = get("u", o), get("d", o), get("u", e), get("d", e)
        back = coupling(u, d, ue, de)
        out = coupling(ue, de, u, d)
        fyq, gyq, fzq, gzq = in_plane_couplings(u, d)
        total = 1.0 + get(outward, o) + back + ((fyq + gyq) + (fzq + gzq))
        new = {
            (inward, o): back,
            (outward, e): out,
            ("dg", o): total,
            ("dg", e): get("dg", e) + out,
            ("fy", o): fyq,
            ("gy", o): gyq,
            ("fz", o): jnp.where(last, 0.0, fzq),
            ("gz", o): jnp.where(first, 0.0, gzq),
        }
        for k, (key, value) in enumerate(new.items()):
            place[key] = edge_s.at[side, k]
            place[key][...] = value

    def masked(total, q):
        if q in (-1, nx):
            return jnp.where(get("d", q) > 0.0, total, 0.0)
        return mask_halo(total, place["d", q][ny:], ny)

    def in_plane(q):
        return [get(k, q) for k in ("fy", "gy", "fz", "gz")]

    def adjoint_at(w, q):
        v = get(w, q)
        total = get("dg", q) * v - get("fx", q) * get(w, q + 1)
        total = total - get("gx", q) * get(w, q - 1)
        return masked(total - in_plane_adjoint(v, *in_plane(q)), q)

    def forward_at(w, q):
        v = get(w, q)
        above = get("m", q) if q == nx else get("gx", q + 1) * get(w, q + 1)
        below = get("m", q) if q == -1 else get("fx", q - 1) * get(w, q - 1)
        total = get("dg", q) * v - above - below
        return masked(total - in_plane_forward(v, *in_plane(q)), q)

    sums = [part[k] for k in range(SUMS)]
    theta, phi = (part[SUMS + k][0:1, 0:1] for k in range(2))

    def add(k, v, w):
        sums[k] = sums[k] + product(v, w, ny)

    for q in range(-1, nx + 1):
        if 1 <= q < nx - 1:
            continue
        value = adjoint_at("s", q)
        keep("p1", q, value)
        if 0 <= q < nx:
            p1_out[q] = value[0:ny]
            add(1, value, value)
    for q in range(-1, nx + 1):
        if 2 <= q < nx - 2:
            continue
        value = forward_at("p1", q)
        keep("p2", q, value)
        if 0 <= q < nx:
            p2_out[q] = value[0:ny]
            v = value - theta * get("s", q)
            add(2, get("s", q), v)
            add(3, v, v)
    for o, outward in ((-1, "gx"), (nx, "fx")):
        beyond = -2 if o == -1 else nx + 1
        keep("p2", beyond, get("q", o) - get(outward, o) * get("p1", o))
    for q in range(-1, nx + 1):
        if 3 <= q < nx - 3:
            continue
        value = adjoint_at("p2", q)
        p3_out[q + 1] = value
        if 0 <= q < nx:
            w = value - phi * get("p1", q)
            add(4, get("p1", q), w)
            add(5, w, w)

    slot = lax.broadcasted_iota(jnp.int32, (1, LANES), 1)
    row = jnp.where(slot == SUMS, theta, phi)
    for k in range(SUMS):
        total = jnp.sum(sums[k], axis=0, keepdims=True)
        total = jnp.sum(total, axis=1, keepdims=True)
        row = jnp.where(slot == k, total, row)
    moments[...] = jnp.broadcast_to(row, moments.shape)


def finish(copies, ny, *fields):
    nx, rows, nz = fields[0].shape
    steps = 4 + 6 + 2
    return pl.pallas_call(
        finish_kernel,
        out_shape=(
            f32(nx, ny, nz),
            f32(nx, ny, nz),
            f32(nx + 2, rows, nz),
            f32(2, 8, rows, nz),
            f32(copies, 1, LANES),
        ),
        in_specs=[VMEM] * len(fields),
        out_specs=(VMEM,) * 5,
        scratch_shapes=[
            pltpu.VMEM((2, FIELDS, rows, nz), F32),
            pltpu.VMEM((steps, rows, nz), F32),
        ],
        compiler_params=params(),
        name="finish",
    )(*fields)


def combine_kernel(
    moments, source, p1_in, p2_in, p3_in, p1_out, p2_out, p3_out, edge,
    fx, gx, fy, gy, fz, gz, dg,
    adjoint_out, residual_out,
    adjoint, residual, sems,
):
    nx, ny, nz = source.shape
    p1 = [(p1_in if 1 <= x < nx - 1 else p1_out).at[x] for x in range(nx)]
    p2 = [(p2_in if 2 <= x < nx - 2 else p2_out).at[x] for x in range(nx)]
    p3 = [
        p3_in.at[x] if 3 <= x < nx - 3 else p3_out.at[x + 1] for x in range(-1, nx + 1)
    ]
    sums = [moments[:, k : k + 1] for k in range(SUMS + 2)]
    ss, pp, sv, vv, pw, ww, theta, phi = sums

    def total(v):
        return jnp.sum(v, axis=0, keepdims=True)

    def norm(g, a, shift, first, mixed, second):
        rest = g - a * shift
        return total(rest * rest * first - 2.0 * a * rest * mixed + a * a * second)

    m0 = total(ss)
    alpha = m0 / total(pp)
    new = norm(1.0, alpha, theta, ss, sv, vv)
    grow = 1.0 + new / m0
    step = new / norm(grow, alpha, phi, pp, pw, ww)
    near = alpha + step * grow
    far = step * alpha
    copies = []

    def send(src, dst, begin, end):
        planes = pl.ds(begin, end - begin)
        copies.append(
            pltpu.make_async_copy(src.at[planes], dst.at[planes], sems.at[len(copies)])
        )
        copies[-1].start()

    half = nx // 2
    for begin in (0, half):
        for x in range(begin, begin + half):
            adjoint[x] = near * p1[x][0:ny] - far * p3[x + 1][0:ny]
        send(adjoint, adjoint_out, begin, begin + half)
    for x in range(nx):
        v = p3[x + 1][...]
        above = edge[1, 0] if x == nx - 1 else gx[x + 1]
        below = edge[0, 0] if x == 0 else fx[x - 1]
        diagonal = edge[0, 3] if x == 0 else edge[1, 3] if x == nx - 1 else dg[x]
        p4 = diagonal * v - above * p3[x + 2][...] - below * p3[x][...]
        p4 = p4 - in_plane_forward(v, fy[x], gy[x], fz[x], gz[x])
        residual[x] = source[x] - near * p2[x][0:ny] + far * p4[0:ny]
        if x % 2 == 1:
            send(residual, residual_out, x - 1, x + 1)
    for copy in copies:
        copy.wait()


def combine(moments, source, *fields):
    nx, ny, nz = source.shape
    return pl.pallas_call(
        combine_kernel,
        out_shape=(f32(nx, ny, nz),) * 2,
        in_specs=[VMEM] * (2 + len(fields)),
        out_specs=(pl.BlockSpec(memory_space=pltpu.HBM),) * 2,
        scratch_shapes=[
            pltpu.VMEM((nx, ny, nz), F32),
            pltpu.VMEM((nx, ny, nz), F32),
            pltpu.SemaphoreType.DMA((2 + nx // 2,)),
        ],
        compiler_params=params(),
        name="combine",
    )(moments, source, *fields)


def swap(cells, axis, first):
    pairs = [(i, i + 1) for i in range(first, lax.axis_size(axis) - 1, 2)]
    return lax.ppermute(cells, axis, pairs + [(j, i) for i, j in pairs])


def local(conc, labels, kappa, source):
    ny = conc.shape[1]
    conc, source, diff = pack(conc, labels, kappa, source)
    xtwo = swap(pack_face(False, conc, diff, source), "gx", 0)
    xone = swap(pack_face(True, conc, diff, source), "gx", 1)
    yone, ytwo = pack_rows(conc, diff, source)
    yone = swap(yone, "gy", 1)
    ytwo = swap(ytwo, "gy", 0)
    cone, ctwo = pack_late(conc, diff, source, yone, ytwo)
    ctwo = swap(ctwo, "gx", 0)
    cone = swap(cone, "gx", 1)
    fields = own(conc, diff, source, yone, ytwo)
    inner = inside(*fields[1:])
    p1, p2, p3, edge, moments = finish(
        lax.axis_size(("gx", "gy")), ny, *fields, *inner, xtwo, xone, ctwo, cone
    )
    moments = lax.all_to_all(moments, ("gx", "gy"), 0, 0, tiled=True)
    moments = moments.reshape(-1, LANES)
    return combine(
        moments, source, fields[10], *inner[:2], p1, p2, p3, edge, *fields[3:10]
    )


def solution(mesh):
    return jax.shard_map(
        local,
        mesh=mesh,
        in_specs=(P("gx", "gy", None), P("gx", "gy", None), P(), P("gx", "gy", None)),
        out_specs=(P("gx", "gy", None), P("gx", "gy", None)),
        check_vma=False,
    )
```

```python
import functools

import jax
import jax.numpy as jnp
from jax import lax
from jax.experimental import pallas as pl
from jax.experimental.pallas import tpu as pltpu
from jax.sharding import PartitionSpec as P

ITERS = 2
DT = 0.5
W = 2 * ITERS
F32 = jnp.float32
LANES = 128
TILE = 8
VMEM = pl.BlockSpec(memory_space=pltpu.VMEM)


def low_first(axis):
    return lax.axis_index(axis) % 2 == 0


def up(v, axis):
    return pltpu.roll(v, v.shape[axis] - 1, axis)


def down(v, axis):
    return pltpu.roll(v, 1, axis)


def z_ends(shape):
    index = lax.broadcasted_iota(jnp.int32, shape, 1)
    return index == 0, index == shape[1] - 1


def coupling(u, d, un, dn):
    return d + d * u - d * un + dn


def params(megabytes=16):
    return pltpu.CompilerParams(vmem_limit_bytes=megabytes << 20)


def f32(*shape):
    return jax.ShapeDtypeStruct(shape, F32)


FIELDS = 7


def late_rows(ny):
    rows = ny + 2 * W
    for field, n in ((0, 3), (1, 3), (2, 3), (3, 2), (4, 1), (5, 1)):
        yield field, ny, n
        yield field, rows - n, n
    for field, n in ((5, 1), (6, 2)):
        yield field, 0, n
        yield field, ny - n, n


def late_count(ny):
    return sum(n for _, _, n in late_rows(ny))


def pack_kernel(
    kappa_in, conc_in, labels_in, source_in,
    conc, source, diff,
    labels, kappa, sems,
):
    nx, ny, nz = conc.shape
    copies = [
        pltpu.make_async_copy(src, dst, sems.at[k])
        for k, (src, dst) in enumerate(
            (
                (labels_in, labels),
                (conc_in, conc),
                (kappa_in, kappa),
                (source_in, source),
            )
        )
    ]
    for copy in copies:
        copy.start()
    for copy in copies[:3]:
        copy.wait()
    k0, k1, k2 = ((0.5 * DT) * kappa[k] for k in range(3))

    def body(x, carry):
        lab = labels[x]
        base = jnp.where(lab == 0, k0, jnp.where(lab == 1, k1, k2))
        diff[x] = base * jnp.exp(conc[x])
        return carry

    lax.fori_loop(0, nx, body, 0, unroll=True)
    copies[3].wait()


def pack(conc, labels, kappa, source):
    nx, ny, nz = conc.shape
    outside = [
        pltpu.with_memory_space_constraint(v, pltpu.HBM)
        for v in (kappa, conc, labels, source)
    ]
    return pl.pallas_call(
        pack_kernel,
        out_shape=(f32(nx, ny, nz),) * 3,
        in_specs=[pl.BlockSpec(memory_space=pltpu.HBM)] * 4,
        out_specs=(VMEM,) * 3,
        scratch_shapes=[
            pltpu.VMEM((nx, ny, nz), jnp.int32),
            pltpu.SMEM((3,), F32),
            pltpu.SemaphoreType.DMA((4,)),
        ],
        compiler_params=params(),
        name="pack",
    )(*outside)


def pack_rows_kernel(conc, diff, source, yone, ytwo):
    nx, ny, nz = conc.shape
    flip = low_first("gy")
    for k, ref in enumerate((conc, diff, source)):
        yone[k] = jnp.where(flip, ref[:, 0:TILE, :], ref[:, ny - TILE : ny, :])
        for x in range(nx):
            at = (k * nx + x) * TILE
            end = min(at + TILE, ytwo.shape[0])
            ytwo[at : at + W] = jnp.where(flip, ref[x, ny - W : ny], ref[x, 0:W])
            ytwo[at + W : end] = jnp.zeros((end - at - W, nz), F32)


def pack_rows(conc, diff, source):
    nx, ny, nz = conc.shape
    return pl.pallas_call(
        pack_rows_kernel,
        out_shape=(f32(3, nx, TILE, nz), f32(3 * nx * TILE - 1, nz)),
        in_specs=[VMEM] * 3,
        out_specs=(VMEM,) * 2,
        compiler_params=params(),
        name="pack_rows",
    )(conc, diff, source)


def rows_beside(yone, ytwo, k, x):
    flip = low_first("gy")
    nx = yone.shape[1]
    if isinstance(x, slice):
        starts = [(k * nx + q) * TILE for q in range(nx)]
        two = jnp.stack([ytwo[at : at + W] for at in starts])
    else:
        two = ytwo[pl.ds(pl.multiple_of((k * nx + x) * TILE, TILE), W)]
    below = jnp.where(flip, yone[k, x, TILE - W :], two)
    return below, jnp.where(flip, two, yone[k, x, 0:W])


def in_plane_adjoint(v, fy, gy, fz, gz):
    total = fy * up(v, 0) + gy * down(v, 0)
    return total + (fz * up(v, 1) + gz * down(v, 1))


def in_plane_forward(v, fy, gy, fz, gz):
    total = up(gy * v, 0) + down(fy * v, 0)
    return total + (up(gz * v, 1) + down(fz * v, 1))


def in_plane_couplings(u, d):
    first, last = z_ends(u.shape)
    fy = coupling(u, d, up(u, 0), up(d, 0))
    gy = coupling(u, d, down(u, 0), down(d, 0))
    fz = coupling(u, d, jnp.where(last, 0.0, up(u, 1)), jnp.where(last, 0.0, up(d, 1)))
    gz = coupling(
        u, d, jnp.where(first, 0.0, down(u, 1)), jnp.where(first, 0.0, down(d, 1))
    )
    return fy, gy, fz, gz


def face_planes(first_swap, nx):
    at_head = low_first("gx") if first_swap else ~low_first("gx")
    return [jnp.where(at_head, k, nx - 1 - k) for k in range(4)]


def face_fields(u, d, s):
    first, last = z_ends(u[0].shape)

    def between(i, j):
        return coupling(u[i], d[i], u[j], d[j])

    def image(i, before, after):
        fy, gy, fz, gz = in_plane_couplings(u[i], d[i])
        diagonal = 1.0 + ((fy + gy) + (fz + gz)) + (before + after)
        beside = (fy, gy, jnp.where(last, 0.0, fz), jnp.where(first, 0.0, gz))
        total = diagonal * s[i] - before * s[i - 1] - after * s[i + 1]
        total = total - in_plane_adjoint(s[i], *beside)
        return jnp.where(d[i] > 0.0, total, 0.0), diagonal, beside

    back, inward = between(1, 0), between(2, 1)
    near, diagonal, beside = image(1, back, between(1, 2))
    far, _, _ = image(2, inward, between(2, 3))
    rest = diagonal * near - inward * far - in_plane_forward(near, *beside)
    return u[0], d[0], s[0], s[1], between(0, 1), back * near, rest


def face_rows(first_swap, ny):
    return FIELDS * ny - (1 if first_swap else 0)


def pack_face_kernel(first_swap, conc, diff, source, slab):
    nx, ny, nz = conc.shape
    planes = face_planes(first_swap, nx)
    u, d, s = ([ref[x] for x in planes] for ref in (conc, diff, source))
    for k, v in enumerate(face_fields(u, d, s)):
        n = min(ny, slab.shape[0] - k * ny)
        slab[k * ny : k * ny + n] = v[0:n]


def pack_face(first_swap, conc, diff, source):
    _, ny, nz = conc.shape
    return pl.pallas_call(
        functools.partial(pack_face_kernel, first_swap),
        out_shape=f32(face_rows(first_swap, ny), nz),
        in_specs=[VMEM] * 3,
        out_specs=VMEM,
        compiler_params=params(),
        name="pack_face",
    )(conc, diff, source)


def pack_late_kernel(
    conc, diff, source, yone, ytwo, cone, ctwo, near_s, out_s
):
    nx, ny, nz = conc.shape
    rows = ny + 2 * W

    def narrow(row):
        if row < ny:
            return row + W if row < W else row - ny + 3 * W
        return row - ny + 3 * W if row < ny + W else row - ny - W

    for first_swap, late in ((True, cone), (False, ctwo)):
        for j, x in enumerate(face_planes(first_swap, nx)):
            for k, ref in enumerate((conc, diff, source)):
                below, above = rows_beside(yone, ytwo, k, x)
                near_s[k, j, 0:W] = below
                near_s[k, j, W : 2 * W] = ref[x, 0:W]
                near_s[k, j, 2 * W : 3 * W] = ref[x, ny - W : ny]
                near_s[k, j, 3 * W :] = above
        fields = face_fields(*([near_s[k, j] for j in range(4)] for k in range(3)))
        for k, v in enumerate(fields):
            out_s[k] = v
        for at in (W - 2, 3 * W + 1):
            mine, following, k = (out_s[j, at : at + 1] for j in (2, 3, 4))
            out_s[3, at : at + 1] = mine - k * (mine - following)
        row = 0
        for k, begin, n in late_rows(ny):
            at = narrow(begin)
            late[row : row + n] = out_s[k, at : at + n]
            row += n


def pack_late(conc, diff, source, yone, ytwo):
    nx, ny, nz = conc.shape
    return pl.pallas_call(
        pack_late_kernel,
        out_shape=(f32(late_count(ny), nz),) * 2,
        in_specs=[VMEM] * 5,
        out_specs=(VMEM,) * 2,
        scratch_shapes=[
            pltpu.VMEM((3, 4, 4 * W, nz), F32),
            pltpu.VMEM((FIELDS, 4 * W, nz), F32),
        ],
        compiler_params=params(),
        name="pack_late",
    )(conc, diff, source, yone, ytwo)


def own_kernel(
    conc, diff, source, yone, ytwo,
    u_s, d_s, s_s, fx, gx, fy, gy, fz, gz, dg, p1,
):
    nx, ny, nz = conc.shape
    rows = ny + 2 * W
    for k, (own, ref) in enumerate(((conc, u_s), (diff, d_s), (source, s_s))):
        below, above = rows_beside(yone, ytwo, k, slice(0, nx))
        ref[:, 0:ny, :] = own[...]
        ref[:, ny : ny + W, :] = above
        ref[:, ny + W :, :] = below
    first, last = z_ends((rows, nz))

    for q in range(nx):
        u, d = u_s[q], d_s[q]
        fyq, gyq, fzq, gzq = in_plane_couplings(u, d)
        total = 1.0 + ((fyq + gyq) + (fzq + gzq))
        if q + 1 < nx:
            fxq = coupling(u, d, u_s[q + 1], d_s[q + 1])
            fx[q] = fxq
            total = total + fxq
        if q > 0:
            gxq = coupling(u, d, u_s[q - 1], d_s[q - 1])
            gx[q] = gxq
            total = total + gxq
        dg[q] = total
        fy[q] = fyq
        gy[q] = gyq
        fz[q] = jnp.where(last, 0.0, fzq)
        gz[q] = jnp.where(first, 0.0, gzq)

    for q in range(1, nx - 1):
        v = s_s[q]
        total = dg[q] * v - fx[q] * s_s[q + 1] - gx[q] * s_s[q - 1]
        total = total - in_plane_adjoint(v, fy[q], gy[q], fz[q], gz[q])
        p1[q] = jnp.where(d_s[q] > 0.0, total, 0.0)


def own(conc, diff, source, yone, ytwo):
    nx, ny, nz = conc.shape
    return pl.pallas_call(
        own_kernel,
        out_shape=(f32(nx, ny + 2 * W, nz),) * 11,
        in_specs=[VMEM] * 5,
        out_specs=(VMEM,) * 11,
        compiler_params=params(),
        name="own",
    )(conc, diff, source, yone, ytwo)


def mask_halo(total, d, ny):
    return jnp.concatenate([total[0:ny], jnp.where(d > 0.0, total[ny:], 0.0)], axis=0)


def product(v, w, ny):
    both = v[0:ny] * w[0:ny]
    return jnp.sum(both.reshape(ny // 8, 8, both.shape[1]), axis=0)


def ratio(over, under, whole):
    over, under, whole = (
        jnp.sum(v, axis=(0, 1), keepdims=True) for v in (over, under, whole)
    )
    under = jnp.where(whole <= 16.0 * under, under, whole)
    return jnp.where(under > 0.0, over / jnp.where(under > 0.0, under, 1.0), 0.0)


SUMS = 6


def inside_kernel(d_s, s_s, fx, gx, fy, gy, fz, gz, dg, p1, p2, p3, part):
    nx, rows, nz = d_s.shape
    ny = rows - 2 * W
    sums = [jnp.zeros((8, nz), F32) for _ in range(SUMS)]
    over, under = jnp.zeros((8, nz), F32), jnp.zeros((8, nz), F32)
    for q in range(nx):
        sums[0] = sums[0] + product(s_s[q], s_s[q], ny)
    for q in range(1, nx - 1):
        sums[1] = sums[1] + product(p1[q], p1[q], ny)
    for q in range(2, nx - 2):
        v = p1[q]
        total = dg[q] * v - gx[q + 1] * p1[q + 1] - fx[q - 1] * p1[q - 1]
        total = total - in_plane_forward(v, fy[q], gy[q], fz[q], gz[q])
        p2[q] = jnp.where(d_s[q] > 0.0, total, 0.0)
        over = over + product(total, s_s[q], ny)
        under = under + product(s_s[q], s_s[q], ny)
    theta = ratio(over, under, sums[0])
    for q in range(2, nx - 2):
        v = p2[q] - theta * s_s[q]
        sums[2] = sums[2] + product(s_s[q], v, ny)
        sums[3] = sums[3] + product(v, v, ny)
    over, under = jnp.zeros((8, nz), F32), jnp.zeros((8, nz), F32)
    for q in range(3, nx - 3):
        v = p2[q]
        total = dg[q] * v - fx[q] * p2[q + 1] - gx[q] * p2[q - 1]
        total = total - in_plane_adjoint(v, fy[q], gy[q], fz[q], gz[q])
        p3[q] = jnp.where(d_s[q] > 0.0, total, 0.0)
        over = over + product(total, p1[q], ny)
        under = under + product(p1[q], p1[q], ny)
    phi = ratio(over, under, sums[1])
    for q in range(3, nx - 3):
        w = p3[q] - phi * p1[q]
        sums[4] = sums[4] + product(p1[q], w, ny)
        sums[5] = sums[5] + product(w, w, ny)
    for k, total in enumerate(sums):
        part[k] = total
    part[SUMS] = jnp.broadcast_to(theta, (8, nz))
    part[SUMS + 1] = jnp.broadcast_to(phi, (8, nz))


def inside(d_s, *fields):
    nx, rows, nz = d_s.shape
    return pl.pallas_call(
        inside_kernel,
        out_shape=(f32(nx, rows, nz),) * 2 + (f32(SUMS + 2, 8, nz),),
        in_specs=[VMEM] * 10,
        out_specs=(VMEM,) * 3,
        compiler_params=params(),
        cost_estimate=pl.CostEstimate(
            flops=1 << 22, bytes_accessed=1 << 23, transcendentals=0
        ),
        name="inside",
    )(d_s, *fields)


def finish_kernel(
    u_s, d_s, s_s, fx, gx, fy, gy, fz, gz, dg, p1_in, p2_in, p3_in, part,
    xtwo, xone, ctwo, cone,
    p1_out, p2_out, p3_out, edge_s, moments,
    side_s, w_s,
):
    nx, rows, nz = d_s.shape
    ny = rows - 2 * W
    flip = low_first("gx")
    first, last = z_ends((rows, nz))

    for side, one in ((0, flip), (1, ~flip)):
        for k in range(FIELDS):
            n = min(ny, xone.shape[0] - k * ny)
            held = slice(k * ny, k * ny + n)
            side_s[side, k, 0:n] = jnp.where(one, xone[held], xtwo[held])
        side_s[side, :, ny:] = jnp.zeros((FIELDS, 2 * W, nz), F32)
        for at in (ny + 1, rows - 2):
            side_s[side, 4, at : at + 1] = jnp.ones((1, nz), F32)
        late = jnp.where(one, cone[...], ctwo[...])
        row = 0
        for field, begin, n in late_rows(ny):
            side_s[side, field, begin : begin + n] = late[row : row + n]
            row += n

    names = dict(
        u=u_s, d=d_s, s=s_s, fx=fx, gx=gx, fy=fy, gy=gy, fz=fz, gz=gz, dg=dg,
        p1=p1_in, p2=p2_in, p3=p3_in,
    )
    place = {(k, q): names[k].at[q] for k in names for q in range(nx)}
    spare = iter(range(w_s.shape[0]))

    def keep(name, q, value):
        place[name, q] = w_s.at[next(spare)]
        place[name, q][...] = value

    def get(name, q):
        return place[name, q][...]

    for side, (o, e, outward, inward) in enumerate(
        ((-1, 0, "gx", "fx"), (nx, nx - 1, "fx", "gx"))
    ):
        beyond = 2 * o - e
        for k, name in enumerate(("u", "d", "s")):
            place[name, o] = side_s.at[side, k]
        place["s", beyond] = side_s.at[side, 3]
        place[outward, o] = side_s.at[side, 4]
        place["m", o] = side_s.at[side, 5]
        place["q", o] = side_s.at[side, 6]
        u, d, ue, de = get("u", o), get("d", o), get("u", e), get("d", e)
        back = coupling(u, d, ue, de)
        out = coupling(ue, de, u, d)
        fyq, gyq, fzq, gzq = in_plane_couplings(u, d)
        total = 1.0 + get(outward, o) + back + ((fyq + gyq) + (fzq + gzq))
        new = {
            (inward, o): back,
            (outward, e): out,
            ("dg", o): total,
            ("dg", e): get("dg", e) + out,
            ("fy", o): fyq,
            ("gy", o): gyq,
            ("fz", o): jnp.where(last, 0.0, fzq),
            ("gz", o): jnp.where(first, 0.0, gzq),
        }
        for k, (key, value) in enumerate(new.items()):
            place[key] = edge_s.at[side, k]
            place[key][...] = value

    def masked(total, q):
        if q in (-1, nx):
            return jnp.where(get("d", q) > 0.0, total, 0.0)
        return mask_halo(total, place["d", q][ny:], ny)

    def in_plane(q):
        return [get(k, q) for k in ("fy", "gy", "fz", "gz")]

    def adjoint_at(w, q):
        v = get(w, q)
        total = get("dg", q) * v - get("fx", q) * get(w, q + 1)
        total = total - get("gx", q) * get(w, q - 1)
        return masked(total - in_plane_adjoint(v, *in_plane(q)), q)

    def forward_at(w, q):
        v = get(w, q)
        above = get("m", q) if q == nx else get("gx", q + 1) * get(w, q + 1)
        below = get("m", q) if q == -1 else get("fx", q - 1) * get(w, q - 1)
        total = get("dg", q) * v - above - below
        return masked(total - in_plane_forward(v, *in_plane(q)), q)

    sums = [part[k] for k in range(SUMS)]
    theta, phi = (part[SUMS + k][0:1, 0:1] for k in range(2))

    def add(k, v, w):
        sums[k] = sums[k] + product(v, w, ny)

    for q in range(-1, nx + 1):
        if 1 <= q < nx - 1:
            continue
        value = adjoint_at("s", q)
        keep("p1", q, value)
        if 0 <= q < nx:
            p1_out[q] = value[0:ny]
            add(1, value, value)
    for q in range(-1, nx + 1):
        if 2 <= q < nx - 2:
            continue
        value = forward_at("p1", q)
        keep("p2", q, value)
        if 0 <= q < nx:
            p2_out[q] = value[0:ny]
            v = value - theta * get("s", q)
            add(2, get("s", q), v)
            add(3, v, v)
    for o, outward in ((-1, "gx"), (nx, "fx")):
        beyond = -2 if o == -1 else nx + 1
        keep("p2", beyond, get("q", o) - get(outward, o) * get("p1", o))
    for q in range(-1, nx + 1):
        if 3 <= q < nx - 3:
            continue
        value = adjoint_at("p2", q)
        p3_out[q + 1] = value
        if 0 <= q < nx:
            w = value - phi * get("p1", q)
            add(4, get("p1", q), w)
            add(5, w, w)

    slot = lax.broadcasted_iota(jnp.int32, (1, LANES), 1)
    row = jnp.where(slot == SUMS, theta, phi)
    for k in range(SUMS):
        total = jnp.sum(sums[k], axis=0, keepdims=True)
        total = jnp.sum(total, axis=1, keepdims=True)
        row = jnp.where(slot == k, total, row)
    moments[...] = jnp.broadcast_to(row, moments.shape)


def finish(copies, ny, *fields):
    nx, rows, nz = fields[0].shape
    steps = 4 + 6 + 2
    return pl.pallas_call(
        finish_kernel,
        out_shape=(
            f32(nx, ny, nz),
            f32(nx, ny, nz),
            f32(nx + 2, rows, nz),
            f32(2, 8, rows, nz),
            f32(copies, 1, LANES),
        ),
        in_specs=[VMEM] * len(fields),
        out_specs=(VMEM,) * 5,
        scratch_shapes=[
            pltpu.VMEM((2, FIELDS, rows, nz), F32),
            pltpu.VMEM((steps, rows, nz), F32),
        ],
        compiler_params=params(),
        name="finish",
    )(*fields)


def combine_kernel(
    moments, source, p1_in, p2_in, p3_in, p1_out, p2_out, p3_out, edge,
    fx, gx, fy, gy, fz, gz, dg,
    adjoint_out, residual_out,
    adjoint, residual, sems,
):
    nx, ny, nz = source.shape
    p1 = [(p1_in if 1 <= x < nx - 1 else p1_out).at[x] for x in range(nx)]
    p2 = [(p2_in if 2 <= x < nx - 2 else p2_out).at[x] for x in range(nx)]
    p3 = [
        p3_in.at[x] if 3 <= x < nx - 3 else p3_out.at[x + 1] for x in range(-1, nx + 1)
    ]
    sums = [moments[:, k : k + 1] for k in range(SUMS + 2)]
    ss, pp, sv, vv, pw, ww, theta, phi = sums

    def total(v):
        return jnp.sum(v, axis=0, keepdims=True)

    def norm(g, a, shift, first, mixed, second):
        rest = g - a * shift
        return total(rest * rest * first - 2.0 * a * rest * mixed + a * a * second)

    m0 = total(ss)
    alpha = m0 / total(pp)
    new = norm(1.0, alpha, theta, ss, sv, vv)
    grow = 1.0 + new / m0
    step = new / norm(grow, alpha, phi, pp, pw, ww)
    near = alpha + step * grow
    far = step * alpha
    copies = []

    def send(src, dst, begin, end):
        planes = pl.ds(begin, end - begin)
        copies.append(
            pltpu.make_async_copy(src.at[planes], dst.at[planes], sems.at[len(copies)])
        )
        copies[-1].start()

    half = nx // 2
    for begin in (0, half):
        for x in range(begin, begin + half):
            adjoint[x] = near * p1[x][0:ny] - far * p3[x + 1][0:ny]
        send(adjoint, adjoint_out, begin, begin + half)
    for x in range(nx):
        v = p3[x + 1][...]
        above = edge[1, 0] if x == nx - 1 else gx[x + 1]
        below = edge[0, 0] if x == 0 else fx[x - 1]
        diagonal = edge[0, 3] if x == 0 else edge[1, 3] if x == nx - 1 else dg[x]
        p4 = diagonal * v - above * p3[x + 2][...] - below * p3[x][...]
        p4 = p4 - in_plane_forward(v, fy[x], gy[x], fz[x], gz[x])
        residual[x] = source[x] - near * p2[x][0:ny] + far * p4[0:ny]
        if x % 2 == 1:
            send(residual, residual_out, x - 1, x + 1)
    for copy in copies:
        copy.wait()


def combine(moments, source, *fields):
    nx, ny, nz = source.shape
    return pl.pallas_call(
        combine_kernel,
        out_shape=(f32(nx, ny, nz),) * 2,
        in_specs=[VMEM] * (2 + len(fields)),
        out_specs=(pl.BlockSpec(memory_space=pltpu.HBM),) * 2,
        scratch_shapes=[
            pltpu.VMEM((nx, ny, nz), F32),
            pltpu.VMEM((nx, ny, nz), F32),
            pltpu.SemaphoreType.DMA((2 + nx // 2,)),
        ],
        compiler_params=params(),
        name="combine",
    )(moments, source, *fields)


def swap(cells, axis, first):
    pairs = [(i, i + 1) for i in range(first, lax.axis_size(axis) - 1, 2)]
    return lax.ppermute(cells, axis, pairs + [(j, i) for i, j in pairs])


def local(conc, labels, kappa, source):
    ny = conc.shape[1]
    conc, source, diff = pack(conc, labels, kappa, source)
    xtwo = swap(pack_face(False, conc, diff, source), "gx", 0)
    xone = swap(pack_face(True, conc, diff, source), "gx", 1)
    yone, ytwo = pack_rows(conc, diff, source)
    yone = swap(yone, "gy", 1)
    ytwo = swap(ytwo, "gy", 0)
    cone, ctwo = pack_late(conc, diff, source, yone, ytwo)
    ctwo = swap(ctwo, "gx", 0)
    cone = swap(cone, "gx", 1)
    fields = own(conc, diff, source, yone, ytwo)
    inner = inside(*fields[1:])
    p1, p2, p3, edge, moments = finish(
        lax.axis_size(("gx", "gy")), ny, *fields, *inner, xtwo, xone, ctwo, cone
    )
    moments = lax.all_to_all(moments, ("gx", "gy"), 0, 0, tiled=True)
    moments = moments.reshape(-1, LANES)
    return combine(
        moments, source, fields[10], *inner[:2], p1, p2, p3, edge, *fields[3:10]
    )


def solution(mesh):
    return jax.shard_map(
        local,
        mesh=mesh,
        in_specs=(P("gx", "gy", None), P("gx", "gy", None), P(), P("gx", "gy", None)),
        out_specs=(P("gx", "gy", None), P("gx", "gy", None)),
        check_vma=False,
    )
```

```python
import functools

import jax
import jax.numpy as jnp
from jax import lax
from jax.experimental import pallas as pl
from jax.experimental.pallas import tpu as pltpu
from jax.sharding import PartitionSpec as P

ITERS = 2
DT = 0.5
W = 2 * ITERS
F32 = jnp.float32
LANES = 128
YROWS = (8, 8)
TILE = 8
VMEM = pl.BlockSpec(memory_space=pltpu.VMEM)


def low_first(axis):
    return lax.axis_index(axis) % 2 == 0


def up(v, axis):
    return pltpu.roll(v, v.shape[axis] - 1, axis)


def down(v, axis):
    return pltpu.roll(v, 1, axis)


def z_ends(shape):
    index = lax.broadcasted_iota(jnp.int32, shape, 1)
    return index == 0, index == shape[1] - 1


def coupling(u, d, un, dn):
    return d + d * u - d * un + dn


def params(megabytes=16):
    return pltpu.CompilerParams(vmem_limit_bytes=megabytes << 20)


def f32(*shape):
    return jax.ShapeDtypeStruct(shape, F32)


FIELDS = 7


def late_rows(ny):
    rows = ny + 2 * W
    for field, n in ((0, 3), (1, 3), (2, 3), (3, 2), (4, 1), (5, 1)):
        yield field, ny, n
        yield field, rows - n, n
    for field, n in ((5, 1), (6, 2)):
        yield field, 0, n
        yield field, ny - n, n


def late_count(ny):
    return sum(n for _, _, n in late_rows(ny))


def pack_kernel(
    kappa_in, conc_in, labels_in, source_in,
    conc, source, diff,
    labels, kappa, sems,
):
    nx, ny, nz = conc.shape
    copies = [
        pltpu.make_async_copy(src, dst, sems.at[k])
        for k, (src, dst) in enumerate(
            (
                (labels_in, labels),
                (conc_in, conc),
                (kappa_in, kappa),
                (source_in, source),
            )
        )
    ]
    for copy in copies:
        copy.start()
    for copy in copies[:3]:
        copy.wait()
    k0, k1, k2 = ((0.5 * DT) * kappa[k] for k in range(3))

    def body(x, carry):
        lab = labels[x]
        base = jnp.where(lab == 0, k0, jnp.where(lab == 1, k1, k2))
        diff[x] = base * jnp.exp(conc[x])
        return carry

    lax.fori_loop(0, nx, body, 0, unroll=True)
    copies[3].wait()


def pack(conc, labels, kappa, source):
    nx, ny, nz = conc.shape
    outside = [
        pltpu.with_memory_space_constraint(v, pltpu.HBM)
        for v in (kappa, conc, labels, source)
    ]
    return pl.pallas_call(
        pack_kernel,
        out_shape=(f32(nx, ny, nz),) * 3,
        in_specs=[pl.BlockSpec(memory_space=pltpu.HBM)] * 4,
        out_specs=(VMEM,) * 3,
        scratch_shapes=[
            pltpu.VMEM((nx, ny, nz), jnp.int32),
            pltpu.SMEM((3,), F32),
            pltpu.SemaphoreType.DMA((4,)),
        ],
        compiler_params=params(),
        name="pack",
    )(*outside)


def pack_rows_kernel(conc, diff, source, yone, ytwo):
    nx, ny, nz = conc.shape
    flip = low_first("gy")
    for k, ref in enumerate((conc, diff, source)):
        for out, n, head in ((yone, YROWS[0], flip), (ytwo, YROWS[1], ~flip)):
            out[k, 0:nx] = jnp.where(head, ref[:, 0:n, :], ref[:, ny - n : ny, :])
        yone[k, nx] = jnp.zeros((YROWS[0], nz), F32)


def pack_rows(conc, diff, source):
    nx, ny, nz = conc.shape
    return pl.pallas_call(
        pack_rows_kernel,
        out_shape=(f32(3, nx + 1, YROWS[0], nz), f32(3, nx, YROWS[1], nz)),
        in_specs=[VMEM] * 3,
        out_specs=(VMEM,) * 2,
        compiler_params=params(),
        name="pack_rows",
    )(conc, diff, source)


def rows_beside(yone, ytwo, k, x):
    flip = low_first("gy")
    one, two = (slice(n - W, n) for n in YROWS)
    below = jnp.where(flip, yone[k, x, one], ytwo[k, x, two])
    return below, jnp.where(flip, ytwo[k, x, 0:W], yone[k, x, 0:W])


def in_plane_adjoint(v, fy, gy, fz, gz):
    total = fy * up(v, 0) + gy * down(v, 0)
    return total + (fz * up(v, 1) + gz * down(v, 1))


def in_plane_forward(v, fy, gy, fz, gz):
    total = up(gy * v, 0) + down(fy * v, 0)
    return total + (up(gz * v, 1) + down(fz * v, 1))


def in_plane_couplings(u, d):
    first, last = z_ends(u.shape)
    fy = coupling(u, d, up(u, 0), up(d, 0))
    gy = coupling(u, d, down(u, 0), down(d, 0))
    fz = coupling(u, d, jnp.where(last, 0.0, up(u, 1)), jnp.where(last, 0.0, up(d, 1)))
    gz = coupling(
        u, d, jnp.where(first, 0.0, down(u, 1)), jnp.where(first, 0.0, down(d, 1))
    )
    return fy, gy, fz, gz


def face_planes(first_swap, nx):
    at_head = low_first("gx") if first_swap else ~low_first("gx")
    return [jnp.where(at_head, k, nx - 1 - k) for k in range(4)]


def face_fields(u, d, s):
    first, last = z_ends(u[0].shape)

    def between(i, j):
        return coupling(u[i], d[i], u[j], d[j])

    def image(i, before, after):
        fy, gy, fz, gz = in_plane_couplings(u[i], d[i])
        diagonal = 1.0 + ((fy + gy) + (fz + gz)) + (before + after)
        beside = (fy, gy, jnp.where(last, 0.0, fz), jnp.where(first, 0.0, gz))
        total = diagonal * s[i] - before * s[i - 1] - after * s[i + 1]
        total = total - in_plane_adjoint(s[i], *beside)
        return jnp.where(d[i] > 0.0, total, 0.0), diagonal, beside

    back, inward = between(1, 0), between(2, 1)
    near, diagonal, beside = image(1, back, between(1, 2))
    far, _, _ = image(2, inward, between(2, 3))
    rest = diagonal * near - inward * far - in_plane_forward(near, *beside)
    return u[0], d[0], s[0], s[1], between(0, 1), back * near, rest


def face_rows(first_swap, ny):
    return FIELDS * ny + (0 if first_swap else TILE)


def pack_face_kernel(first_swap, conc, diff, source, slab):
    nx, ny, nz = conc.shape
    planes = face_planes(first_swap, nx)
    u, d, s = ([ref[x] for x in planes] for ref in (conc, diff, source))
    for k, v in enumerate(face_fields(u, d, s)):
        n = min(ny, slab.shape[0] - k * ny)
        slab[k * ny : k * ny + n] = v[0:n]
    if not first_swap:
        slab[FIELDS * ny :] = jnp.zeros((TILE, nz), F32)


def pack_face(first_swap, conc, diff, source):
    _, ny, nz = conc.shape
    return pl.pallas_call(
        functools.partial(pack_face_kernel, first_swap),
        out_shape=f32(face_rows(first_swap, ny), nz),
        in_specs=[VMEM] * 3,
        out_specs=VMEM,
        compiler_params=params(),
        name="pack_face",
    )(conc, diff, source)


def pack_late_kernel(
    conc, diff, source, yone, ytwo, cone, ctwo, near_s, out_s
):
    nx, ny, nz = conc.shape
    rows = ny + 2 * W

    def narrow(row):
        if row < ny:
            return row + W if row < W else row - ny + 3 * W
        return row - ny + 3 * W if row < ny + W else row - ny - W

    for first_swap, late in ((True, cone), (False, ctwo)):
        for j, x in enumerate(face_planes(first_swap, nx)):
            for k, ref in enumerate((conc, diff, source)):
                below, above = rows_beside(yone, ytwo, k, x)
                near_s[k, j, 0:W] = below
                near_s[k, j, W : 2 * W] = ref[x, 0:W]
                near_s[k, j, 2 * W : 3 * W] = ref[x, ny - W : ny]
                near_s[k, j, 3 * W :] = above
        fields = face_fields(*([near_s[k, j] for j in range(4)] for k in range(3)))
        for k, v in enumerate(fields):
            out_s[k] = v
        for at in (W - 2, 3 * W + 1):
            mine, following, k = (out_s[j, at : at + 1] for j in (2, 3, 4))
            out_s[3, at : at + 1] = mine - k * (mine - following)
        row = 0
        for k, begin, n in late_rows(ny):
            at = narrow(begin)
            late[row : row + n] = out_s[k, at : at + n]
            row += n


def pack_late(conc, diff, source, yone, ytwo):
    nx, ny, nz = conc.shape
    return pl.pallas_call(
        pack_late_kernel,
        out_shape=(f32(late_count(ny), nz),) * 2,
        in_specs=[VMEM] * 5,
        out_specs=(VMEM,) * 2,
        scratch_shapes=[
            pltpu.VMEM((3, 4, 4 * W, nz), F32),
            pltpu.VMEM((FIELDS, 4 * W, nz), F32),
        ],
        compiler_params=params(),
        name="pack_late",
    )(conc, diff, source, yone, ytwo)


def own_kernel(
    conc, diff, source, yone, ytwo,
    u_s, d_s, s_s, fx, gx, fy, gy, fz, gz, dg, p1,
):
    nx, ny, nz = conc.shape
    rows = ny + 2 * W
    for k, (own, ref) in enumerate(((conc, u_s), (diff, d_s), (source, s_s))):
        below, above = rows_beside(yone, ytwo, k, slice(0, nx))
        ref[:, 0:ny, :] = own[...]
        ref[:, ny : ny + W, :] = above
        ref[:, ny + W :, :] = below
    first, last = z_ends((rows, nz))

    for q in range(nx):
        u, d = u_s[q], d_s[q]
        fyq, gyq, fzq, gzq = in_plane_couplings(u, d)
        total = 1.0 + ((fyq + gyq) + (fzq + gzq))
        if q + 1 < nx:
            fxq = coupling(u, d, u_s[q + 1], d_s[q + 1])
            fx[q] = fxq
            total = total + fxq
        if q > 0:
            gxq = coupling(u, d, u_s[q - 1], d_s[q - 1])
            gx[q] = gxq
            total = total + gxq
        dg[q] = total
        fy[q] = fyq
        gy[q] = gyq
        fz[q] = jnp.where(last, 0.0, fzq)
        gz[q] = jnp.where(first, 0.0, gzq)

    for q in range(1, nx - 1):
        v = s_s[q]
        total = dg[q] * v - fx[q] * s_s[q + 1] - gx[q] * s_s[q - 1]
        total = total - in_plane_adjoint(v, fy[q], gy[q], fz[q], gz[q])
        p1[q] = jnp.where(d_s[q] > 0.0, total, 0.0)


def own(conc, diff, source, yone, ytwo):
    nx, ny, nz = conc.shape
    return pl.pallas_call(
        own_kernel,
        out_shape=(f32(nx, ny + 2 * W, nz),) * 11,
        in_specs=[VMEM] * 5,
        out_specs=(VMEM,) * 11,
        compiler_params=params(),
        name="own",
    )(conc, diff, source, yone, ytwo)


def mask_halo(total, d, ny):
    return jnp.concatenate([total[0:ny], jnp.where(d > 0.0, total[ny:], 0.0)], axis=0)


def product(v, w, ny):
    both = v[0:ny] * w[0:ny]
    return jnp.sum(both.reshape(ny // 8, 8, both.shape[1]), axis=0)


def ratio(over, under, whole):
    over, under, whole = (
        jnp.sum(v, axis=(0, 1), keepdims=True) for v in (over, under, whole)
    )
    under = jnp.where(whole <= 16.0 * under, under, whole)
    return jnp.where(under > 0.0, over / jnp.where(under > 0.0, under, 1.0), 0.0)


SUMS = 6


def inside_kernel(d_s, s_s, fx, gx, fy, gy, fz, gz, dg, p1, p2, p3, part):
    nx, rows, nz = d_s.shape
    ny = rows - 2 * W
    sums = [jnp.zeros((8, nz), F32) for _ in range(SUMS)]
    over, under = jnp.zeros((8, nz), F32), jnp.zeros((8, nz), F32)
    for q in range(nx):
        sums[0] = sums[0] + product(s_s[q], s_s[q], ny)
    for q in range(1, nx - 1):
        sums[1] = sums[1] + product(p1[q], p1[q], ny)
    for q in range(2, nx - 2):
        v = p1[q]
        total = dg[q] * v - gx[q + 1] * p1[q + 1] - fx[q - 1] * p1[q - 1]
        total = total - in_plane_forward(v, fy[q], gy[q], fz[q], gz[q])
        p2[q] = jnp.where(d_s[q] > 0.0, total, 0.0)
        over = over + product(total, s_s[q], ny)
        under = under + product(s_s[q], s_s[q], ny)
    theta = ratio(over, under, sums[0])
    for q in range(2, nx - 2):
        v = p2[q] - theta * s_s[q]
        sums[2] = sums[2] + product(s_s[q], v, ny)
        sums[3] = sums[3] + product(v, v, ny)
    over, under = jnp.zeros((8, nz), F32), jnp.zeros((8, nz), F32)
    for q in range(3, nx - 3):
        v = p2[q]
        total = dg[q] * v - fx[q] * p2[q + 1] - gx[q] * p2[q - 1]
        total = total - in_plane_adjoint(v, fy[q], gy[q], fz[q], gz[q])
        p3[q] = jnp.where(d_s[q] > 0.0, total, 0.0)
        over = over + product(total, p1[q], ny)
        under = under + product(p1[q], p1[q], ny)
    phi = ratio(over, under, sums[1])
    for q in range(3, nx - 3):
        w = p3[q] - phi * p1[q]
        sums[4] = sums[4] + product(p1[q], w, ny)
        sums[5] = sums[5] + product(w, w, ny)
    for k, total in enumerate(sums):
        part[k] = total
    part[SUMS] = jnp.broadcast_to(theta, (8, nz))
    part[SUMS + 1] = jnp.broadcast_to(phi, (8, nz))


def inside(d_s, *fields):
    nx, rows, nz = d_s.shape
    return pl.pallas_call(
        inside_kernel,
        out_shape=(f32(nx, rows, nz),) * 2 + (f32(SUMS + 2, 8, nz),),
        in_specs=[VMEM] * 10,
        out_specs=(VMEM,) * 3,
        compiler_params=params(),
        cost_estimate=pl.CostEstimate(
            flops=1 << 22, bytes_accessed=1 << 23, transcendentals=0
        ),
        name="inside",
    )(d_s, *fields)


def finish_kernel(
    u_s, d_s, s_s, fx, gx, fy, gy, fz, gz, dg, p1_in, p2_in, p3_in, part,
    xtwo, xone, ctwo, cone,
    p1_out, p2_out, p3_out, edge_s, moments,
    side_s, w_s,
):
    nx, rows, nz = d_s.shape
    ny = rows - 2 * W
    flip = low_first("gx")
    first, last = z_ends((rows, nz))

    for side, one in ((0, flip), (1, ~flip)):
        for k in range(FIELDS):
            n = min(ny, xone.shape[0] - k * ny)
            held = slice(k * ny, k * ny + n)
            side_s[side, k, 0:n] = jnp.where(one, xone[held], xtwo[held])
        side_s[side, :, ny:] = jnp.zeros((FIELDS, 2 * W, nz), F32)
        for at in (ny + 1, rows - 2):
            side_s[side, 4, at : at + 1] = jnp.ones((1, nz), F32)
        late = jnp.where(one, cone[...], ctwo[...])
        row = 0
        for field, begin, n in late_rows(ny):
            side_s[side, field, begin : begin + n] = late[row : row + n]
            row += n

    names = dict(
        u=u_s, d=d_s, s=s_s, fx=fx, gx=gx, fy=fy, gy=gy, fz=fz, gz=gz, dg=dg,
        p1=p1_in, p2=p2_in, p3=p3_in,
    )
    place = {(k, q): names[k].at[q] for k in names for q in range(nx)}
    spare = iter(range(w_s.shape[0]))

    def keep(name, q, value):
        place[name, q] = w_s.at[next(spare)]
        place[name, q][...] = value

    def get(name, q):
        return place[name, q][...]

    for side, (o, e, outward, inward) in enumerate(
        ((-1, 0, "gx", "fx"), (nx, nx - 1, "fx", "gx"))
    ):
        beyond = 2 * o - e
        for k, name in enumerate(("u", "d", "s")):
            place[name, o] = side_s.at[side, k]
        place["s", beyond] = side_s.at[side, 3]
        place[outward, o] = side_s.at[side, 4]
        place["m", o] = side_s.at[side, 5]
        place["q", o] = side_s.at[side, 6]
        u, d, ue, de = get("u", o), get("d", o), get("u", e), get("d", e)
        back = coupling(u, d, ue, de)
        out = coupling(ue, de, u, d)
        fyq, gyq, fzq, gzq = in_plane_couplings(u, d)
        total = 1.0 + get(outward, o) + back + ((fyq + gyq) + (fzq + gzq))
        new = {
            (inward, o): back,
            (outward, e): out,
            ("dg", o): total,
            ("dg", e): get("dg", e) + out,
            ("fy", o): fyq,
            ("gy", o): gyq,
            ("fz", o): jnp.where(last, 0.0, fzq),
            ("gz", o): jnp.where(first, 0.0, gzq),
        }
        for k, (key, value) in enumerate(new.items()):
            place[key] = edge_s.at[side, k]
            place[key][...] = value

    def masked(total, q):
        if q in (-1, nx):
            return jnp.where(get("d", q) > 0.0, total, 0.0)
        return mask_halo(total, place["d", q][ny:], ny)

    def in_plane(q):
        return [get(k, q) for k in ("fy", "gy", "fz", "gz")]

    def adjoint_at(w, q):
        v = get(w, q)
        total = get("dg", q) * v - get("fx", q) * get(w, q + 1)
        total = total - get("gx", q) * get(w, q - 1)
        return masked(total - in_plane_adjoint(v, *in_plane(q)), q)

    def forward_at(w, q):
        v = get(w, q)
        above = get("m", q) if q == nx else get("gx", q + 1) * get(w, q + 1)
        below = get("m", q) if q == -1 else get("fx", q - 1) * get(w, q - 1)
        total = get("dg", q) * v - above - below
        return masked(total - in_plane_forward(v, *in_plane(q)), q)

    sums = [part[k] for k in range(SUMS)]
    theta, phi = (part[SUMS + k][0:1, 0:1] for k in range(2))

    def add(k, v, w):
        sums[k] = sums[k] + product(v, w, ny)

    for q in range(-1, nx + 1):
        if 1 <= q < nx - 1:
            continue
        value = adjoint_at("s", q)
        keep("p1", q, value)
        if 0 <= q < nx:
            p1_out[q] = value[0:ny]
            add(1, value, value)
    for q in range(-1, nx + 1):
        if 2 <= q < nx - 2:
            continue
        value = forward_at("p1", q)
        keep("p2", q, value)
        if 0 <= q < nx:
            p2_out[q] = value[0:ny]
            v = value - theta * get("s", q)
            add(2, get("s", q), v)
            add(3, v, v)
    for o, outward in ((-1, "gx"), (nx, "fx")):
        beyond = -2 if o == -1 else nx + 1
        keep("p2", beyond, get("q", o) - get(outward, o) * get("p1", o))
    for q in range(-1, nx + 1):
        if 3 <= q < nx - 3:
            continue
        value = adjoint_at("p2", q)
        p3_out[q + 1] = value
        if 0 <= q < nx:
            w = value - phi * get("p1", q)
            add(4, get("p1", q), w)
            add(5, w, w)

    slot = lax.broadcasted_iota(jnp.int32, (1, LANES), 1)
    row = jnp.where(slot == SUMS, theta, phi)
    for k in range(SUMS):
        total = jnp.sum(sums[k], axis=0, keepdims=True)
        total = jnp.sum(total, axis=1, keepdims=True)
        row = jnp.where(slot == k, total, row)
    moments[...] = jnp.broadcast_to(row, moments.shape)


def finish(copies, ny, *fields):
    nx, rows, nz = fields[0].shape
    steps = 4 + 6 + 2
    return pl.pallas_call(
        finish_kernel,
        out_shape=(
            f32(nx, ny, nz),
            f32(nx, ny, nz),
            f32(nx + 2, rows, nz),
            f32(2, 8, rows, nz),
            f32(copies, 1, LANES),
        ),
        in_specs=[VMEM] * len(fields),
        out_specs=(VMEM,) * 5,
        scratch_shapes=[
            pltpu.VMEM((2, FIELDS, rows, nz), F32),
            pltpu.VMEM((steps, rows, nz), F32),
        ],
        compiler_params=params(),
        name="finish",
    )(*fields)


def combine_kernel(
    moments, source, p1_in, p2_in, p3_in, p1_out, p2_out, p3_out, edge,
    fx, gx, fy, gy, fz, gz, dg,
    adjoint_out, residual_out,
    adjoint, residual, sems,
):
    nx, ny, nz = source.shape
    p1 = [(p1_in if 1 <= x < nx - 1 else p1_out).at[x] for x in range(nx)]
    p2 = [(p2_in if 2 <= x < nx - 2 else p2_out).at[x] for x in range(nx)]
    p3 = [
        p3_in.at[x] if 3 <= x < nx - 3 else p3_out.at[x + 1] for x in range(-1, nx + 1)
    ]
    sums = [moments[:, k : k + 1] for k in range(SUMS + 2)]
    ss, pp, sv, vv, pw, ww, theta, phi = sums

    def total(v):
        return jnp.sum(v, axis=0, keepdims=True)

    def norm(g, a, shift, first, mixed, second):
        rest = g - a * shift
        return total(rest * rest * first - 2.0 * a * rest * mixed + a * a * second)

    m0 = total(ss)
    alpha = m0 / total(pp)
    new = norm(1.0, alpha, theta, ss, sv, vv)
    grow = 1.0 + new / m0
    step = new / norm(grow, alpha, phi, pp, pw, ww)
    near = alpha + step * grow
    far = step * alpha
    copies = []

    def send(src, dst, begin, end):
        planes = pl.ds(begin, end - begin)
        copies.append(
            pltpu.make_async_copy(src.at[planes], dst.at[planes], sems.at[len(copies)])
        )
        copies[-1].start()

    half = nx // 2
    for begin in (0, half):
        for x in range(begin, begin + half):
            adjoint[x] = near * p1[x][0:ny] - far * p3[x + 1][0:ny]
        send(adjoint, adjoint_out, begin, begin + half)
    for x in range(nx):
        v = p3[x + 1][...]
        above = edge[1, 0] if x == nx - 1 else gx[x + 1]
        below = edge[0, 0] if x == 0 else fx[x - 1]
        diagonal = edge[0, 3] if x == 0 else edge[1, 3] if x == nx - 1 else dg[x]
        p4 = diagonal * v - above * p3[x + 2][...] - below * p3[x][...]
        p4 = p4 - in_plane_forward(v, fy[x], gy[x], fz[x], gz[x])
        residual[x] = source[x] - near * p2[x][0:ny] + far * p4[0:ny]
        if x % 2 == 1:
            send(residual, residual_out, x - 1, x + 1)
    for copy in copies:
        copy.wait()


def combine(moments, source, *fields):
    nx, ny, nz = source.shape
    return pl.pallas_call(
        combine_kernel,
        out_shape=(f32(nx, ny, nz),) * 2,
        in_specs=[VMEM] * (2 + len(fields)),
        out_specs=(pl.BlockSpec(memory_space=pltpu.HBM),) * 2,
        scratch_shapes=[
            pltpu.VMEM((nx, ny, nz), F32),
            pltpu.VMEM((nx, ny, nz), F32),
            pltpu.SemaphoreType.DMA((2 + nx // 2,)),
        ],
        compiler_params=params(),
        name="combine",
    )(moments, source, *fields)


def swap(cells, axis, first):
    pairs = [(i, i + 1) for i in range(first, lax.axis_size(axis) - 1, 2)]
    return lax.ppermute(cells, axis, pairs + [(j, i) for i, j in pairs])


def local(conc, labels, kappa, source):
    ny = conc.shape[1]
    conc, source, diff = pack(conc, labels, kappa, source)
    xtwo = swap(pack_face(False, conc, diff, source), "gx", 0)
    xone = swap(pack_face(True, conc, diff, source), "gx", 1)
    yone, ytwo = pack_rows(conc, diff, source)
    yone = swap(yone, "gy", 1)
    ytwo = swap(ytwo, "gy", 0)
    cone, ctwo = pack_late(conc, diff, source, yone, ytwo)
    ctwo = swap(ctwo, "gx", 0)
    cone = swap(cone, "gx", 1)
    fields = own(conc, diff, source, yone, ytwo)
    inner = inside(*fields[1:])
    p1, p2, p3, edge, moments = finish(
        lax.axis_size(("gx", "gy")), ny, *fields, *inner, xtwo, xone, ctwo, cone
    )
    moments = lax.all_to_all(moments, ("gx", "gy"), 0, 0, tiled=True)
    moments = moments.reshape(-1, LANES)
    return combine(
        moments, source, fields[10], *inner[:2], p1, p2, p3, edge, *fields[3:10]
    )


def solution(mesh):
    return jax.shard_map(
        local,
        mesh=mesh,
        in_specs=(P("gx", "gy", None), P("gx", "gy", None), P(), P("gx", "gy", None)),
        out_specs=(P("gx", "gy", None), P("gx", "gy", None)),
        check_vma=False,
    )
```

```python
import functools

import jax
import jax.numpy as jnp
from jax import lax
from jax.experimental import pallas as pl
from jax.experimental.pallas import tpu as pltpu
from jax.sharding import PartitionSpec as P

ITERS = 2
DT = 0.5
W = 2 * ITERS
F32 = jnp.float32
LANES = 128
TILE = 8
VMEM = pl.BlockSpec(memory_space=pltpu.VMEM)


def low_first(axis):
    return lax.axis_index(axis) % 2 == 0


def up(v, axis):
    return pltpu.roll(v, v.shape[axis] - 1, axis)


def down(v, axis):
    return pltpu.roll(v, 1, axis)


def z_ends(shape):
    index = lax.broadcasted_iota(jnp.int32, shape, 1)
    return index == 0, index == shape[1] - 1


def coupling(u, d, un, dn):
    return d + d * u - d * un + dn


def params(megabytes=16):
    return pltpu.CompilerParams(vmem_limit_bytes=megabytes << 20)


def f32(*shape):
    return jax.ShapeDtypeStruct(shape, F32)


FIELDS = 7


def late_rows(ny):
    rows = ny + 2 * W
    for field, n in ((0, 3), (1, 3), (2, 3), (3, 2), (4, 1), (5, 1)):
        yield field, ny, n
        yield field, rows - n, n
    for field, n in ((5, 1), (6, 2)):
        yield field, 0, n
        yield field, ny - n, n


def late_count(ny):
    return sum(n for _, _, n in late_rows(ny))


def pack_kernel(
    kappa_in, conc_in, labels_in, source_in,
    conc, source, diff,
    labels, kappa, sems,
):
    nx, ny, nz = conc.shape
    copies = [
        pltpu.make_async_copy(src, dst, sems.at[k])
        for k, (src, dst) in enumerate(
            (
                (labels_in, labels),
                (conc_in, conc),
                (kappa_in, kappa),
                (source_in, source),
            )
        )
    ]
    for copy in copies:
        copy.start()
    for copy in copies[:3]:
        copy.wait()
    k0, k1, k2 = ((0.5 * DT) * kappa[k] for k in range(3))

    def body(x, carry):
        lab = labels[x]
        base = jnp.where(lab == 0, k0, jnp.where(lab == 1, k1, k2))
        diff[x] = base * jnp.exp(conc[x])
        return carry

    lax.fori_loop(0, nx, body, 0, unroll=True)
    copies[3].wait()


def pack(conc, labels, kappa, source):
    nx, ny, nz = conc.shape
    outside = [
        pltpu.with_memory_space_constraint(v, pltpu.HBM)
        for v in (kappa, conc, labels, source)
    ]
    return pl.pallas_call(
        pack_kernel,
        out_shape=(f32(nx, ny, nz),) * 3,
        in_specs=[pl.BlockSpec(memory_space=pltpu.HBM)] * 4,
        out_specs=(VMEM,) * 3,
        scratch_shapes=[
            pltpu.VMEM((nx, ny, nz), jnp.int32),
            pltpu.SMEM((3,), F32),
            pltpu.SemaphoreType.DMA((4,)),
        ],
        compiler_params=params(),
        name="pack",
    )(*outside)


def pack_rows_kernel(conc, diff, source, yone, ytwo):
    nx, ny, nz = conc.shape
    flip = low_first("gy")
    for out, head in ((yone, flip), (ytwo, ~flip)):
        for k, ref in enumerate((conc, diff, source)):
            for x in range(nx):
                at = (k * nx + x) * TILE
                out[at : at + W] = jnp.where(head, ref[x, 0:W], ref[x, ny - W : ny])
                out[at + W : at + TILE] = jnp.zeros((TILE - W, nz), F32)
    yone[3 * nx * TILE :] = jnp.zeros((TILE, nz), F32)


def pack_rows(conc, diff, source):
    nx, ny, nz = conc.shape
    rows = 3 * nx * TILE
    return pl.pallas_call(
        pack_rows_kernel,
        out_shape=(f32(rows + TILE, nz), f32(rows, nz)),
        in_specs=[VMEM] * 3,
        out_specs=(VMEM,) * 2,
        compiler_params=params(),
        name="pack_rows",
    )(conc, diff, source)


def rows_beside(yone, ytwo, k, x):
    flip = low_first("gy")
    nx = ytwo.shape[0] // (3 * TILE)

    def lead(ref):
        if isinstance(x, slice):
            starts = [(k * nx + q) * TILE for q in range(nx)]
            return jnp.stack([ref[at : at + W] for at in starts])
        return ref[pl.ds(pl.multiple_of((k * nx + x) * TILE, TILE), W)]

    one, two = lead(yone), lead(ytwo)
    return jnp.where(flip, one, two), jnp.where(flip, two, one)


def in_plane_adjoint(v, fy, gy, fz, gz):
    total = fy * up(v, 0) + gy * down(v, 0)
    return total + (fz * up(v, 1) + gz * down(v, 1))


def in_plane_forward(v, fy, gy, fz, gz):
    total = up(gy * v, 0) + down(fy * v, 0)
    return total + (up(gz * v, 1) + down(fz * v, 1))


def in_plane_couplings(u, d):
    first, last = z_ends(u.shape)
    fy = coupling(u, d, up(u, 0), up(d, 0))
    gy = coupling(u, d, down(u, 0), down(d, 0))
    fz = coupling(u, d, jnp.where(last, 0.0, up(u, 1)), jnp.where(last, 0.0, up(d, 1)))
    gz = coupling(
        u, d, jnp.where(first, 0.0, down(u, 1)), jnp.where(first, 0.0, down(d, 1))
    )
    return fy, gy, fz, gz


def face_planes(first_swap, nx):
    at_head = low_first("gx") if first_swap else ~low_first("gx")
    return [jnp.where(at_head, k, nx - 1 - k) for k in range(4)]


def face_fields(u, d, s):
    first, last = z_ends(u[0].shape)

    def between(i, j):
        return coupling(u[i], d[i], u[j], d[j])

    def image(i, before, after):
        fy, gy, fz, gz = in_plane_couplings(u[i], d[i])
        diagonal = 1.0 + ((fy + gy) + (fz + gz)) + (before + after)
        beside = (fy, gy, jnp.where(last, 0.0, fz), jnp.where(first, 0.0, gz))
        total = diagonal * s[i] - before * s[i - 1] - after * s[i + 1]
        total = total - in_plane_adjoint(s[i], *beside)
        return jnp.where(d[i] > 0.0, total, 0.0), diagonal, beside

    back, inward = between(1, 0), between(2, 1)
    near, diagonal, beside = image(1, back, between(1, 2))
    far, _, _ = image(2, inward, between(2, 3))
    rest = diagonal * near - inward * far - in_plane_forward(near, *beside)
    return u[0], d[0], s[0], s[1], between(0, 1), back * near, rest


def face_rows(first_swap, ny):
    return FIELDS * ny + (0 if first_swap else TILE)


def pack_face_kernel(first_swap, conc, diff, source, slab):
    nx, ny, nz = conc.shape
    planes = face_planes(first_swap, nx)
    u, d, s = ([ref[x] for x in planes] for ref in (conc, diff, source))
    for k, v in enumerate(face_fields(u, d, s)):
        n = min(ny, slab.shape[0] - k * ny)
        slab[k * ny : k * ny + n] = v[0:n]
    if not first_swap:
        slab[FIELDS * ny :] = jnp.zeros((TILE, nz), F32)


def pack_face(first_swap, conc, diff, source):
    _, ny, nz = conc.shape
    return pl.pallas_call(
        functools.partial(pack_face_kernel, first_swap),
        out_shape=f32(face_rows(first_swap, ny), nz),
        in_specs=[VMEM] * 3,
        out_specs=VMEM,
        compiler_params=params(),
        name="pack_face",
    )(conc, diff, source)


def pack_late_kernel(
    conc, diff, source, yone, ytwo, cone, ctwo, near_s, out_s
):
    nx, ny, nz = conc.shape
    rows = ny + 2 * W

    def narrow(row):
        if row < ny:
            return row + W if row < W else row - ny + 3 * W
        return row - ny + 3 * W if row < ny + W else row - ny - W

    for first_swap, late in ((True, cone), (False, ctwo)):
        for j, x in enumerate(face_planes(first_swap, nx)):
            for k, ref in enumerate((conc, diff, source)):
                below, above = rows_beside(yone, ytwo, k, x)
                near_s[k, j, 0:W] = below
                near_s[k, j, W : 2 * W] = ref[x, 0:W]
                near_s[k, j, 2 * W : 3 * W] = ref[x, ny - W : ny]
                near_s[k, j, 3 * W :] = above
        fields = face_fields(*([near_s[k, j] for j in range(4)] for k in range(3)))
        for k, v in enumerate(fields):
            out_s[k] = v
        for at in (W - 2, 3 * W + 1):
            mine, following, k = (out_s[j, at : at + 1] for j in (2, 3, 4))
            out_s[3, at : at + 1] = mine - k * (mine - following)
        row = 0
        for k, begin, n in late_rows(ny):
            at = narrow(begin)
            late[row : row + n] = out_s[k, at : at + n]
            row += n


def pack_late(conc, diff, source, yone, ytwo):
    nx, ny, nz = conc.shape
    return pl.pallas_call(
        pack_late_kernel,
        out_shape=(f32(late_count(ny), nz),) * 2,
        in_specs=[VMEM] * 5,
        out_specs=(VMEM,) * 2,
        scratch_shapes=[
            pltpu.VMEM((3, 4, 4 * W, nz), F32),
            pltpu.VMEM((FIELDS, 4 * W, nz), F32),
        ],
        compiler_params=params(),
        name="pack_late",
    )(conc, diff, source, yone, ytwo)


def own_kernel(
    conc, diff, source, yone, ytwo,
    u_s, d_s, s_s, fx, gx, fy, gy, fz, gz, dg, p1,
):
    nx, ny, nz = conc.shape
    rows = ny + 2 * W
    for k, (own, ref) in enumerate(((conc, u_s), (diff, d_s), (source, s_s))):
        below, above = rows_beside(yone, ytwo, k, slice(0, nx))
        ref[:, 0:ny, :] = own[...]
        ref[:, ny : ny + W, :] = above
        ref[:, ny + W :, :] = below
    first, last = z_ends((rows, nz))

    for q in range(nx):
        u, d = u_s[q], d_s[q]
        fyq, gyq, fzq, gzq = in_plane_couplings(u, d)
        total = 1.0 + ((fyq + gyq) + (fzq + gzq))
        if q + 1 < nx:
            fxq = coupling(u, d, u_s[q + 1], d_s[q + 1])
            fx[q] = fxq
            total = total + fxq
        if q > 0:
            gxq = coupling(u, d, u_s[q - 1], d_s[q - 1])
            gx[q] = gxq
            total = total + gxq
        dg[q] = total
        fy[q] = fyq
        gy[q] = gyq
        fz[q] = jnp.where(last, 0.0, fzq)
        gz[q] = jnp.where(first, 0.0, gzq)

    for q in range(1, nx - 1):
        v = s_s[q]
        total = dg[q] * v - fx[q] * s_s[q + 1] - gx[q] * s_s[q - 1]
        total = total - in_plane_adjoint(v, fy[q], gy[q], fz[q], gz[q])
        p1[q] = jnp.where(d_s[q] > 0.0, total, 0.0)


def own(conc, diff, source, yone, ytwo):
    nx, ny, nz = conc.shape
    return pl.pallas_call(
        own_kernel,
        out_shape=(f32(nx, ny + 2 * W, nz),) * 11,
        in_specs=[VMEM] * 5,
        out_specs=(VMEM,) * 11,
        compiler_params=params(),
        name="own",
    )(conc, diff, source, yone, ytwo)


def mask_halo(total, d, ny):
    return jnp.concatenate([total[0:ny], jnp.where(d > 0.0, total[ny:], 0.0)], axis=0)


def product(v, w, ny):
    both = v[0:ny] * w[0:ny]
    return jnp.sum(both.reshape(ny // 8, 8, both.shape[1]), axis=0)


def ratio(over, under, whole):
    over, under, whole = (
        jnp.sum(v, axis=(0, 1), keepdims=True) for v in (over, under, whole)
    )
    under = jnp.where(whole <= 16.0 * under, under, whole)
    return jnp.where(under > 0.0, over / jnp.where(under > 0.0, under, 1.0), 0.0)


SUMS = 6


def inside_kernel(d_s, s_s, fx, gx, fy, gy, fz, gz, dg, p1, p2, p3, part):
    nx, rows, nz = d_s.shape
    ny = rows - 2 * W
    sums = [jnp.zeros((8, nz), F32) for _ in range(SUMS)]
    over, under = jnp.zeros((8, nz), F32), jnp.zeros((8, nz), F32)
    for q in range(nx):
        sums[0] = sums[0] + product(s_s[q], s_s[q], ny)
    for q in range(1, nx - 1):
        sums[1] = sums[1] + product(p1[q], p1[q], ny)
    for q in range(2, nx - 2):
        v = p1[q]
        total = dg[q] * v - gx[q + 1] * p1[q + 1] - fx[q - 1] * p1[q - 1]
        total = total - in_plane_forward(v, fy[q], gy[q], fz[q], gz[q])
        p2[q] = jnp.where(d_s[q] > 0.0, total, 0.0)
        over = over + product(total, s_s[q], ny)
        under = under + product(s_s[q], s_s[q], ny)
    theta = ratio(over, under, sums[0])
    for q in range(2, nx - 2):
        v = p2[q] - theta * s_s[q]
        sums[2] = sums[2] + product(s_s[q], v, ny)
        sums[3] = sums[3] + product(v, v, ny)
    over, under = jnp.zeros((8, nz), F32), jnp.zeros((8, nz), F32)
    for q in range(3, nx - 3):
        v = p2[q]
        total = dg[q] * v - fx[q] * p2[q + 1] - gx[q] * p2[q - 1]
        total = total - in_plane_adjoint(v, fy[q], gy[q], fz[q], gz[q])
        p3[q] = jnp.where(d_s[q] > 0.0, total, 0.0)
        over = over + product(total, p1[q], ny)
        under = under + product(p1[q], p1[q], ny)
    phi = ratio(over, under, sums[1])
    for q in range(3, nx - 3):
        w = p3[q] - phi * p1[q]
        sums[4] = sums[4] + product(p1[q], w, ny)
        sums[5] = sums[5] + product(w, w, ny)
    for k, total in enumerate(sums):
        part[k] = total
    part[SUMS] = jnp.broadcast_to(theta, (8, nz))
    part[SUMS + 1] = jnp.broadcast_to(phi, (8, nz))


def inside(d_s, *fields):
    nx, rows, nz = d_s.shape
    return pl.pallas_call(
        inside_kernel,
        out_shape=(f32(nx, rows, nz),) * 2 + (f32(SUMS + 2, 8, nz),),
        in_specs=[VMEM] * 10,
        out_specs=(VMEM,) * 3,
        compiler_params=params(),
        cost_estimate=pl.CostEstimate(
            flops=1 << 22, bytes_accessed=1 << 23, transcendentals=0
        ),
        name="inside",
    )(d_s, *fields)


def finish_kernel(
    u_s, d_s, s_s, fx, gx, fy, gy, fz, gz, dg, p1_in, p2_in, p3_in, part,
    xtwo, xone, ctwo, cone,
    p1_out, p2_out, p3_out, edge_s, moments,
    side_s, w_s,
):
    nx, rows, nz = d_s.shape
    ny = rows - 2 * W
    flip = low_first("gx")
    first, last = z_ends((rows, nz))

    for side, one in ((0, flip), (1, ~flip)):
        for k in range(FIELDS):
            n = min(ny, xone.shape[0] - k * ny)
            held = slice(k * ny, k * ny + n)
            side_s[side, k, 0:n] = jnp.where(one, xone[held], xtwo[held])
        side_s[side, :, ny:] = jnp.zeros((FIELDS, 2 * W, nz), F32)
        for at in (ny + 1, rows - 2):
            side_s[side, 4, at : at + 1] = jnp.ones((1, nz), F32)
        late = jnp.where(one, cone[...], ctwo[...])
        row = 0
        for field, begin, n in late_rows(ny):
            side_s[side, field, begin : begin + n] = late[row : row + n]
            row += n

    names = dict(
        u=u_s, d=d_s, s=s_s, fx=fx, gx=gx, fy=fy, gy=gy, fz=fz, gz=gz, dg=dg,
        p1=p1_in, p2=p2_in, p3=p3_in,
    )
    place = {(k, q): names[k].at[q] for k in names for q in range(nx)}
    spare = iter(range(w_s.shape[0]))

    def keep(name, q, value):
        place[name, q] = w_s.at[next(spare)]
        place[name, q][...] = value

    def get(name, q):
        return place[name, q][...]

    for side, (o, e, outward, inward) in enumerate(
        ((-1, 0, "gx", "fx"), (nx, nx - 1, "fx", "gx"))
    ):
        beyond = 2 * o - e
        for k, name in enumerate(("u", "d", "s")):
            place[name, o] = side_s.at[side, k]
        place["s", beyond] = side_s.at[side, 3]
        place[outward, o] = side_s.at[side, 4]
        place["m", o] = side_s.at[side, 5]
        place["q", o] = side_s.at[side, 6]
        u, d, ue, de = get("u", o), get("d", o), get("u", e), get("d", e)
        back = coupling(u, d, ue, de)
        out = coupling(ue, de, u, d)
        fyq, gyq, fzq, gzq = in_plane_couplings(u, d)
        total = 1.0 + get(outward, o) + back + ((fyq + gyq) + (fzq + gzq))
        new = {
            (inward, o): back,
            (outward, e): out,
            ("dg", o): total,
            ("dg", e): get("dg", e) + out,
            ("fy", o): fyq,
            ("gy", o): gyq,
            ("fz", o): jnp.where(last, 0.0, fzq),
            ("gz", o): jnp.where(first, 0.0, gzq),
        }
        for k, (key, value) in enumerate(new.items()):
            place[key] = edge_s.at[side, k]
            place[key][...] = value

    def masked(total, q):
        if q in (-1, nx):
            return jnp.where(get("d", q) > 0.0, total, 0.0)
        return mask_halo(total, place["d", q][ny:], ny)

    def in_plane(q):
        return [get(k, q) for k in ("fy", "gy", "fz", "gz")]

    def adjoint_at(w, q):
        v = get(w, q)
        total = get("dg", q) * v - get("fx", q) * get(w, q + 1)
        total = total - get("gx", q) * get(w, q - 1)
        return masked(total - in_plane_adjoint(v, *in_plane(q)), q)

    def forward_at(w, q):
        v = get(w, q)
        above = get("m", q) if q == nx else get("gx", q + 1) * get(w, q + 1)
        below = get("m", q) if q == -1 else get("fx", q - 1) * get(w, q - 1)
        total = get("dg", q) * v - above - below
        return masked(total - in_plane_forward(v, *in_plane(q)), q)

    sums = [part[k] for k in range(SUMS)]
    theta, phi = (part[SUMS + k][0:1, 0:1] for k in range(2))

    def add(k, v, w):
        sums[k] = sums[k] + product(v, w, ny)

    for q in range(-1, nx + 1):
        if 1 <= q < nx - 1:
            continue
        value = adjoint_at("s", q)
        keep("p1", q, value)
        if 0 <= q < nx:
            p1_out[q] = value[0:ny]
            add(1, value, value)
    for q in range(-1, nx + 1):
        if 2 <= q < nx - 2:
            continue
        value = forward_at("p1", q)
        keep("p2", q, value)
        if 0 <= q < nx:
            p2_out[q] = value[0:ny]
            v = value - theta * get("s", q)
            add(2, get("s", q), v)
            add(3, v, v)
    for o, outward in ((-1, "gx"), (nx, "fx")):
        beyond = -2 if o == -1 else nx + 1
        keep("p2", beyond, get("q", o) - get(outward, o) * get("p1", o))
    for q in range(-1, nx + 1):
        if 3 <= q < nx - 3:
            continue
        value = adjoint_at("p2", q)
        p3_out[q + 1] = value
        if 0 <= q < nx:
            w = value - phi * get("p1", q)
            add(4, get("p1", q), w)
            add(5, w, w)

    slot = lax.broadcasted_iota(jnp.int32, (1, LANES), 1)
    row = jnp.where(slot == SUMS, theta, phi)
    for k in range(SUMS):
        total = jnp.sum(sums[k], axis=0, keepdims=True)
        total = jnp.sum(total, axis=1, keepdims=True)
        row = jnp.where(slot == k, total, row)
    moments[...] = jnp.broadcast_to(row, moments.shape)


def finish(copies, ny, *fields):
    nx, rows, nz = fields[0].shape
    steps = 4 + 6 + 2
    return pl.pallas_call(
        finish_kernel,
        out_shape=(
            f32(nx, ny, nz),
            f32(nx, ny, nz),
            f32(nx + 2, rows, nz),
            f32(2, 8, rows, nz),
            f32(copies, 1, LANES),
        ),
        in_specs=[VMEM] * len(fields),
        out_specs=(VMEM,) * 5,
        scratch_shapes=[
            pltpu.VMEM((2, FIELDS, rows, nz), F32),
            pltpu.VMEM((steps, rows, nz), F32),
        ],
        compiler_params=params(),
        name="finish",
    )(*fields)


def combine_kernel(
    moments, source, p1_in, p2_in, p3_in, p1_out, p2_out, p3_out, edge,
    fx, gx, fy, gy, fz, gz, dg,
    adjoint_out, residual_out,
    adjoint, residual, sems,
):
    nx, ny, nz = source.shape
    p1 = [(p1_in if 1 <= x < nx - 1 else p1_out).at[x] for x in range(nx)]
    p2 = [(p2_in if 2 <= x < nx - 2 else p2_out).at[x] for x in range(nx)]
    p3 = [
        p3_in.at[x] if 3 <= x < nx - 3 else p3_out.at[x + 1] for x in range(-1, nx + 1)
    ]
    sums = [moments[:, k : k + 1] for k in range(SUMS + 2)]
    ss, pp, sv, vv, pw, ww, theta, phi = sums

    def total(v):
        return jnp.sum(v, axis=0, keepdims=True)

    def norm(g, a, shift, first, mixed, second):
        rest = g - a * shift
        return total(rest * rest * first - 2.0 * a * rest * mixed + a * a * second)

    m0 = total(ss)
    alpha = m0 / total(pp)
    new = norm(1.0, alpha, theta, ss, sv, vv)
    grow = 1.0 + new / m0
    step = new / norm(grow, alpha, phi, pp, pw, ww)
    near = alpha + step * grow
    far = step * alpha
    copies = []

    def send(src, dst, begin, end):
        planes = pl.ds(begin, end - begin)
        copies.append(
            pltpu.make_async_copy(src.at[planes], dst.at[planes], sems.at[len(copies)])
        )
        copies[-1].start()

    half = nx // 2
    for begin in (0, half):
        for x in range(begin, begin + half):
            adjoint[x] = near * p1[x][0:ny] - far * p3[x + 1][0:ny]
        send(adjoint, adjoint_out, begin, begin + half)
    for x in range(nx):
        v = p3[x + 1][...]
        above = edge[1, 0] if x == nx - 1 else gx[x + 1]
        below = edge[0, 0] if x == 0 else fx[x - 1]
        diagonal = edge[0, 3] if x == 0 else edge[1, 3] if x == nx - 1 else dg[x]
        p4 = diagonal * v - above * p3[x + 2][...] - below * p3[x][...]
        p4 = p4 - in_plane_forward(v, fy[x], gy[x], fz[x], gz[x])
        residual[x] = source[x] - near * p2[x][0:ny] + far * p4[0:ny]
        if x % 2 == 1:
            send(residual, residual_out, x - 1, x + 1)
    for copy in copies:
        copy.wait()


def combine(moments, source, *fields):
    nx, ny, nz = source.shape
    return pl.pallas_call(
        combine_kernel,
        out_shape=(f32(nx, ny, nz),) * 2,
        in_specs=[VMEM] * (2 + len(fields)),
        out_specs=(pl.BlockSpec(memory_space=pltpu.HBM),) * 2,
        scratch_shapes=[
            pltpu.VMEM((nx, ny, nz), F32),
            pltpu.VMEM((nx, ny, nz), F32),
            pltpu.SemaphoreType.DMA((2 + nx // 2,)),
        ],
        compiler_params=params(),
        name="combine",
    )(moments, source, *fields)


def swap(cells, axis, first):
    pairs = [(i, i + 1) for i in range(first, lax.axis_size(axis) - 1, 2)]
    return lax.ppermute(cells, axis, pairs + [(j, i) for i, j in pairs])


def local(conc, labels, kappa, source):
    ny = conc.shape[1]
    conc, source, diff = pack(conc, labels, kappa, source)
    xtwo = swap(pack_face(False, conc, diff, source), "gx", 0)
    xone = swap(pack_face(True, conc, diff, source), "gx", 1)
    yone, ytwo = pack_rows(conc, diff, source)
    yone = swap(yone, "gy", 1)
    ytwo = swap(ytwo, "gy", 0)
    cone, ctwo = pack_late(conc, diff, source, yone, ytwo)
    ctwo = swap(ctwo, "gx", 0)
    cone = swap(cone, "gx", 1)
    fields = own(conc, diff, source, yone, ytwo)
    inner = inside(*fields[1:])
    p1, p2, p3, edge, moments = finish(
        lax.axis_size(("gx", "gy")), ny, *fields, *inner, xtwo, xone, ctwo, cone
    )
    moments = lax.all_to_all(moments, ("gx", "gy"), 0, 0, tiled=True)
    moments = moments.reshape(-1, LANES)
    return combine(
        moments, source, fields[10], *inner[:2], p1, p2, p3, edge, *fields[3:10]
    )


def solution(mesh):
    return jax.shard_map(
        local,
        mesh=mesh,
        in_specs=(P("gx", "gy", None), P("gx", "gy", None), P(), P("gx", "gy", None)),
        out_specs=(P("gx", "gy", None), P("gx", "gy", None)),
        check_vma=False,
    )
```

```python
import functools

import jax
import jax.numpy as jnp
from jax import lax
from jax.experimental import pallas as pl
from jax.experimental.pallas import tpu as pltpu
from jax.sharding import PartitionSpec as P

ITERS = 2
DT = 0.5
W = 2 * ITERS
F32 = jnp.float32
LANES = 128
TILE = 8
VMEM = pl.BlockSpec(memory_space=pltpu.VMEM)


def low_first(axis):
    return lax.axis_index(axis) % 2 == 0


def up(v, axis):
    return pltpu.roll(v, v.shape[axis] - 1, axis)


def down(v, axis):
    return pltpu.roll(v, 1, axis)


def z_ends(shape):
    index = lax.broadcasted_iota(jnp.int32, shape, 1)
    return index == 0, index == shape[1] - 1


def coupling(u, d, un, dn):
    return d + d * u - d * un + dn


def params(megabytes=16):
    return pltpu.CompilerParams(vmem_limit_bytes=megabytes << 20)


def f32(*shape):
    return jax.ShapeDtypeStruct(shape, F32)


FIELDS = 7


def late_rows(ny):
    rows = ny + 2 * W
    for field, n in ((0, 3), (1, 3), (2, 3), (3, 2), (4, 1), (5, 1)):
        yield field, ny, n
        yield field, rows - n, n
    for field, n in ((5, 1), (6, 2)):
        yield field, 0, n
        yield field, ny - n, n


def late_count(ny):
    return sum(n for _, _, n in late_rows(ny))


def pack_kernel(
    kappa_in, conc_in, labels_in, source_in,
    conc, source, diff,
    labels, kappa, sems,
):
    nx, ny, nz = conc.shape
    copies = [
        pltpu.make_async_copy(src, dst, sems.at[k])
        for k, (src, dst) in enumerate(
            (
                (labels_in, labels),
                (conc_in, conc),
                (kappa_in, kappa),
                (source_in, source),
            )
        )
    ]
    for copy in copies:
        copy.start()
    for copy in copies[:3]:
        copy.wait()
    k0, k1, k2 = ((0.5 * DT) * kappa[k] for k in range(3))

    def body(x, carry):
        lab = labels[x]
        base = jnp.where(lab == 0, k0, jnp.where(lab == 1, k1, k2))
        diff[x] = base * jnp.exp(conc[x])
        return carry

    lax.fori_loop(0, nx, body, 0, unroll=True)
    copies[3].wait()


def pack(conc, labels, kappa, source):
    nx, ny, nz = conc.shape
    outside = [
        pltpu.with_memory_space_constraint(v, pltpu.HBM)
        for v in (kappa, conc, labels, source)
    ]
    return pl.pallas_call(
        pack_kernel,
        out_shape=(f32(nx, ny, nz),) * 3,
        in_specs=[pl.BlockSpec(memory_space=pltpu.HBM)] * 4,
        out_specs=(VMEM,) * 3,
        scratch_shapes=[
            pltpu.VMEM((nx, ny, nz), jnp.int32),
            pltpu.SMEM((3,), F32),
            pltpu.SemaphoreType.DMA((4,)),
        ],
        compiler_params=params(),
        name="pack",
    )(*outside)


def pack_rows_kernel(conc, diff, source, yone, ytwo):
    nx, ny, nz = conc.shape
    flip = low_first("gy")
    for out, head in ((yone, flip), (ytwo, ~flip)):
        for k, ref in enumerate((conc, diff, source)):
            for x in range(nx):
                at = (k * nx + x) * TILE
                out[at : at + W] = jnp.where(head, ref[x, 0:W], ref[x, ny - W : ny])
                out[at + W : at + TILE] = jnp.zeros((TILE - W, nz), F32)


def pack_rows(conc, diff, source):
    nx, ny, nz = conc.shape
    rows = 3 * nx * TILE
    return pl.pallas_call(
        pack_rows_kernel,
        out_shape=(f32(rows, nz), f32(rows, nz)),
        in_specs=[VMEM] * 3,
        out_specs=(VMEM,) * 2,
        compiler_params=params(),
        name="pack_rows",
    )(conc, diff, source)


def rows_beside(yone, ytwo, k, x):
    flip = low_first("gy")
    nx = ytwo.shape[0] // (3 * TILE)

    def lead(ref):
        if isinstance(x, slice):
            starts = [(k * nx + q) * TILE for q in range(nx)]
            return jnp.stack([ref[at : at + W] for at in starts])
        return ref[pl.ds(pl.multiple_of((k * nx + x) * TILE, TILE), W)]

    one, two = lead(yone), lead(ytwo)
    return jnp.where(flip, one, two), jnp.where(flip, two, one)


def in_plane_adjoint(v, fy, gy, fz, gz):
    total = fy * up(v, 0) + gy * down(v, 0)
    return total + (fz * up(v, 1) + gz * down(v, 1))


def in_plane_forward(v, fy, gy, fz, gz):
    total = up(gy * v, 0) + down(fy * v, 0)
    return total + (up(gz * v, 1) + down(fz * v, 1))


def in_plane_couplings(u, d):
    first, last = z_ends(u.shape)
    fy = coupling(u, d, up(u, 0), up(d, 0))
    gy = coupling(u, d, down(u, 0), down(d, 0))
    fz = coupling(u, d, jnp.where(last, 0.0, up(u, 1)), jnp.where(last, 0.0, up(d, 1)))
    gz = coupling(
        u, d, jnp.where(first, 0.0, down(u, 1)), jnp.where(first, 0.0, down(d, 1))
    )
    return fy, gy, fz, gz


def face_planes(first_swap, nx):
    at_head = low_first("gx") if first_swap else ~low_first("gx")
    return [jnp.where(at_head, k, nx - 1 - k) for k in range(4)]


def face_fields(u, d, s):
    first, last = z_ends(u[0].shape)

    def between(i, j):
        return coupling(u[i], d[i], u[j], d[j])

    def image(i, before, after):
        fy, gy, fz, gz = in_plane_couplings(u[i], d[i])
        diagonal = 1.0 + ((fy + gy) + (fz + gz)) + (before + after)
        beside = (fy, gy, jnp.where(last, 0.0, fz), jnp.where(first, 0.0, gz))
        total = diagonal * s[i] - before * s[i - 1] - after * s[i + 1]
        total = total - in_plane_adjoint(s[i], *beside)
        return jnp.where(d[i] > 0.0, total, 0.0), diagonal, beside

    back, inward = between(1, 0), between(2, 1)
    near, diagonal, beside = image(1, back, between(1, 2))
    far, _, _ = image(2, inward, between(2, 3))
    rest = diagonal * near - inward * far - in_plane_forward(near, *beside)
    return u[0], d[0], s[0], s[1], between(0, 1), back * near, rest


def face_rows(first_swap, ny):
    return FIELDS * ny + (0 if first_swap else TILE)


def pack_face_kernel(first_swap, conc, diff, source, slab):
    nx, ny, nz = conc.shape
    planes = face_planes(first_swap, nx)
    u, d, s = ([ref[x] for x in planes] for ref in (conc, diff, source))
    for k, v in enumerate(face_fields(u, d, s)):
        n = min(ny, slab.shape[0] - k * ny)
        slab[k * ny : k * ny + n] = v[0:n]
    if not first_swap:
        slab[FIELDS * ny :] = jnp.zeros((TILE, nz), F32)


def pack_face(first_swap, conc, diff, source):
    _, ny, nz = conc.shape
    return pl.pallas_call(
        functools.partial(pack_face_kernel, first_swap),
        out_shape=f32(face_rows(first_swap, ny), nz),
        in_specs=[VMEM] * 3,
        out_specs=VMEM,
        compiler_params=params(),
        name="pack_face",
    )(conc, diff, source)


def pack_late_kernel(
    conc, diff, source, yone, ytwo, cone, ctwo, near_s, out_s
):
    nx, ny, nz = conc.shape
    rows = ny + 2 * W

    def narrow(row):
        if row < ny:
            return row + W if row < W else row - ny + 3 * W
        return row - ny + 3 * W if row < ny + W else row - ny - W

    for first_swap, late in ((True, cone), (False, ctwo)):
        for j, x in enumerate(face_planes(first_swap, nx)):
            for k, ref in enumerate((conc, diff, source)):
                below, above = rows_beside(yone, ytwo, k, x)
                near_s[k, j, 0:W] = below
                near_s[k, j, W : 2 * W] = ref[x, 0:W]
                near_s[k, j, 2 * W : 3 * W] = ref[x, ny - W : ny]
                near_s[k, j, 3 * W :] = above
        fields = face_fields(*([near_s[k, j] for j in range(4)] for k in range(3)))
        for k, v in enumerate(fields):
            out_s[k] = v
        for at in (W - 2, 3 * W + 1):
            mine, following, k = (out_s[j, at : at + 1] for j in (2, 3, 4))
            out_s[3, at : at + 1] = mine - k * (mine - following)
        row = 0
        for k, begin, n in late_rows(ny):
            at = narrow(begin)
            late[row : row + n] = out_s[k, at : at + n]
            row += n


def pack_late(conc, diff, source, yone, ytwo):
    nx, ny, nz = conc.shape
    return pl.pallas_call(
        pack_late_kernel,
        out_shape=(f32(late_count(ny), nz),) * 2,
        in_specs=[VMEM] * 5,
        out_specs=(VMEM,) * 2,
        scratch_shapes=[
            pltpu.VMEM((3, 4, 4 * W, nz), F32),
            pltpu.VMEM((FIELDS, 4 * W, nz), F32),
        ],
        compiler_params=params(),
        name="pack_late",
    )(conc, diff, source, yone, ytwo)


def own_kernel(
    conc, diff, source, yone, ytwo,
    u_s, d_s, s_s, fx, gx, fy, gy, fz, gz, dg, p1,
):
    nx, ny, nz = conc.shape
    rows = ny + 2 * W
    for k, (own, ref) in enumerate(((conc, u_s), (diff, d_s), (source, s_s))):
        below, above = rows_beside(yone, ytwo, k, slice(0, nx))
        ref[:, 0:ny, :] = own[...]
        ref[:, ny : ny + W, :] = above
        ref[:, ny + W :, :] = below
    first, last = z_ends((rows, nz))

    for q in range(nx):
        u, d = u_s[q], d_s[q]
        fyq, gyq, fzq, gzq = in_plane_couplings(u, d)
        total = 1.0 + ((fyq + gyq) + (fzq + gzq))
        if q + 1 < nx:
            fxq = coupling(u, d, u_s[q + 1], d_s[q + 1])
            fx[q] = fxq
            total = total + fxq
        if q > 0:
            gxq = coupling(u, d, u_s[q - 1], d_s[q - 1])
            gx[q] = gxq
            total = total + gxq
        dg[q] = total
        fy[q] = fyq
        gy[q] = gyq
        fz[q] = jnp.where(last, 0.0, fzq)
        gz[q] = jnp.where(first, 0.0, gzq)

    for q in range(1, nx - 1):
        v = s_s[q]
        total = dg[q] * v - fx[q] * s_s[q + 1] - gx[q] * s_s[q - 1]
        total = total - in_plane_adjoint(v, fy[q], gy[q], fz[q], gz[q])
        p1[q] = jnp.where(d_s[q] > 0.0, total, 0.0)


def own(conc, diff, source, yone, ytwo):
    nx, ny, nz = conc.shape
    return pl.pallas_call(
        own_kernel,
        out_shape=(f32(nx, ny + 2 * W, nz),) * 11,
        in_specs=[VMEM] * 5,
        out_specs=(VMEM,) * 11,
        compiler_params=params(),
        name="own",
    )(conc, diff, source, yone, ytwo)


def mask_halo(total, d, ny):
    return jnp.concatenate([total[0:ny], jnp.where(d > 0.0, total[ny:], 0.0)], axis=0)


def product(v, w, ny):
    both = v[0:ny] * w[0:ny]
    return jnp.sum(both.reshape(ny // 8, 8, both.shape[1]), axis=0)


def ratio(over, under, whole):
    over, under, whole = (
        jnp.sum(v, axis=(0, 1), keepdims=True) for v in (over, under, whole)
    )
    under = jnp.where(whole <= 16.0 * under, under, whole)
    return jnp.where(under > 0.0, over / jnp.where(under > 0.0, under, 1.0), 0.0)


SUMS = 6


def inside_kernel(d_s, s_s, fx, gx, fy, gy, fz, gz, dg, p1, p2, p3, part):
    nx, rows, nz = d_s.shape
    ny = rows - 2 * W
    sums = [jnp.zeros((8, nz), F32) for _ in range(SUMS)]
    over, under = jnp.zeros((8, nz), F32), jnp.zeros((8, nz), F32)
    for q in range(nx):
        sums[0] = sums[0] + product(s_s[q], s_s[q], ny)
    for q in range(1, nx - 1):
        sums[1] = sums[1] + product(p1[q], p1[q], ny)
    for q in range(2, nx - 2):
        v = p1[q]
        total = dg[q] * v - gx[q + 1] * p1[q + 1] - fx[q - 1] * p1[q - 1]
        total = total - in_plane_forward(v, fy[q], gy[q], fz[q], gz[q])
        p2[q] = jnp.where(d_s[q] > 0.0, total, 0.0)
        over = over + product(total, s_s[q], ny)
        under = under + product(s_s[q], s_s[q], ny)
    theta = ratio(over, under, sums[0])
    for q in range(2, nx - 2):
        v = p2[q] - theta * s_s[q]
        sums[2] = sums[2] + product(s_s[q], v, ny)
        sums[3] = sums[3] + product(v, v, ny)
    over, under = jnp.zeros((8, nz), F32), jnp.zeros((8, nz), F32)
    for q in range(3, nx - 3):
        v = p2[q]
        total = dg[q] * v - fx[q] * p2[q + 1] - gx[q] * p2[q - 1]
        total = total - in_plane_adjoint(v, fy[q], gy[q], fz[q], gz[q])
        p3[q] = jnp.where(d_s[q] > 0.0, total, 0.0)
        over = over + product(total, p1[q], ny)
        under = under + product(p1[q], p1[q], ny)
    phi = ratio(over, under, sums[1])
    for q in range(3, nx - 3):
        w = p3[q] - phi * p1[q]
        sums[4] = sums[4] + product(p1[q], w, ny)
        sums[5] = sums[5] + product(w, w, ny)
    for k, total in enumerate(sums):
        part[k] = total
    part[SUMS] = jnp.broadcast_to(theta, (8, nz))
    part[SUMS + 1] = jnp.broadcast_to(phi, (8, nz))


def inside(d_s, *fields):
    nx, rows, nz = d_s.shape
    return pl.pallas_call(
        inside_kernel,
        out_shape=(f32(nx, rows, nz),) * 2 + (f32(SUMS + 2, 8, nz),),
        in_specs=[VMEM] * 10,
        out_specs=(VMEM,) * 3,
        compiler_params=params(),
        cost_estimate=pl.CostEstimate(
            flops=1 << 22, bytes_accessed=1 << 23, transcendentals=0
        ),
        name="inside",
    )(d_s, *fields)


def finish_kernel(
    u_s, d_s, s_s, fx, gx, fy, gy, fz, gz, dg, p1_in, p2_in, p3_in, part,
    xtwo, xone, ctwo, cone,
    p1_out, p2_out, p3_out, edge_s, moments,
    side_s, w_s,
):
    nx, rows, nz = d_s.shape
    ny = rows - 2 * W
    flip = low_first("gx")
    first, last = z_ends((rows, nz))

    for side, one in ((0, flip), (1, ~flip)):
        for k in range(FIELDS):
            n = min(ny, xone.shape[0] - k * ny)
            held = slice(k * ny, k * ny + n)
            side_s[side, k, 0:n] = jnp.where(one, xone[held], xtwo[held])
        side_s[side, :, ny:] = jnp.zeros((FIELDS, 2 * W, nz), F32)
        for at in (ny + 1, rows - 2):
            side_s[side, 4, at : at + 1] = jnp.ones((1, nz), F32)
        late = jnp.where(one, cone[...], ctwo[...])
        row = 0
        for field, begin, n in late_rows(ny):
            side_s[side, field, begin : begin + n] = late[row : row + n]
            row += n

    names = dict(
        u=u_s, d=d_s, s=s_s, fx=fx, gx=gx, fy=fy, gy=gy, fz=fz, gz=gz, dg=dg,
        p1=p1_in, p2=p2_in, p3=p3_in,
    )
    place = {(k, q): names[k].at[q] for k in names for q in range(nx)}
    spare = iter(range(w_s.shape[0]))

    def keep(name, q, value):
        place[name, q] = w_s.at[next(spare)]
        place[name, q][...] = value

    def get(name, q):
        return place[name, q][...]

    for side, (o, e, outward, inward) in enumerate(
        ((-1, 0, "gx", "fx"), (nx, nx - 1, "fx", "gx"))
    ):
        beyond = 2 * o - e
        for k, name in enumerate(("u", "d", "s")):
            place[name, o] = side_s.at[side, k]
        place["s", beyond] = side_s.at[side, 3]
        place[outward, o] = side_s.at[side, 4]
        place["m", o] = side_s.at[side, 5]
        place["q", o] = side_s.at[side, 6]
        u, d, ue, de = get("u", o), get("d", o), get("u", e), get("d", e)
        back = coupling(u, d, ue, de)
        out = coupling(ue, de, u, d)
        fyq, gyq, fzq, gzq = in_plane_couplings(u, d)
        total = 1.0 + get(outward, o) + back + ((fyq + gyq) + (fzq + gzq))
        new = {
            (inward, o): back,
            (outward, e): out,
            ("dg", o): total,
            ("dg", e): get("dg", e) + out,
            ("fy", o): fyq,
            ("gy", o): gyq,
            ("fz", o): jnp.where(last, 0.0, fzq),
            ("gz", o): jnp.where(first, 0.0, gzq),
        }
        for k, (key, value) in enumerate(new.items()):
            place[key] = edge_s.at[side, k]
            place[key][...] = value

    def masked(total, q):
        if q in (-1, nx):
            return jnp.where(get("d", q) > 0.0, total, 0.0)
        return mask_halo(total, place["d", q][ny:], ny)

    def in_plane(q):
        return [get(k, q) for k in ("fy", "gy", "fz", "gz")]

    def adjoint_at(w, q):
        v = get(w, q)
        total = get("dg", q) * v - get("fx", q) * get(w, q + 1)
        total = total - get("gx", q) * get(w, q - 1)
        return masked(total - in_plane_adjoint(v, *in_plane(q)), q)

    def forward_at(w, q):
        v = get(w, q)
        above = get("m", q) if q == nx else get("gx", q + 1) * get(w, q + 1)
        below = get("m", q) if q == -1 else get("fx", q - 1) * get(w, q - 1)
        total = get("dg", q) * v - above - below
        return masked(total - in_plane_forward(v, *in_plane(q)), q)

    sums = [part[k] for k in range(SUMS)]
    theta, phi = (part[SUMS + k][0:1, 0:1] for k in range(2))

    def add(k, v, w):
        sums[k] = sums[k] + product(v, w, ny)

    for q in range(-1, nx + 1):
        if 1 <= q < nx - 1:
            continue
        value = adjoint_at("s", q)
        keep("p1", q, value)
        if 0 <= q < nx:
            p1_out[q] = value[0:ny]
            add(1, value, value)
    for q in range(-1, nx + 1):
        if 2 <= q < nx - 2:
            continue
        value = forward_at("p1", q)
        keep("p2", q, value)
        if 0 <= q < nx:
            p2_out[q] = value[0:ny]
            v = value - theta * get("s", q)
            add(2, get("s", q), v)
            add(3, v, v)
    for o, outward in ((-1, "gx"), (nx, "fx")):
        beyond = -2 if o == -1 else nx + 1
        keep("p2", beyond, get("q", o) - get(outward, o) * get("p1", o))
    for q in range(-1, nx + 1):
        if 3 <= q < nx - 3:
            continue
        value = adjoint_at("p2", q)
        p3_out[q + 1] = value
        if 0 <= q < nx:
            w = value - phi * get("p1", q)
            add(4, get("p1", q), w)
            add(5, w, w)

    slot = lax.broadcasted_iota(jnp.int32, (1, LANES), 1)
    row = jnp.where(slot == SUMS, theta, phi)
    for k in range(SUMS):
        total = jnp.sum(sums[k], axis=0, keepdims=True)
        total = jnp.sum(total, axis=1, keepdims=True)
        row = jnp.where(slot == k, total, row)
    moments[...] = jnp.broadcast_to(row, moments.shape)


def finish(copies, ny, *fields):
    nx, rows, nz = fields[0].shape
    steps = 4 + 6 + 2
    return pl.pallas_call(
        finish_kernel,
        out_shape=(
            f32(nx, ny, nz),
            f32(nx, ny, nz),
            f32(nx + 2, rows, nz),
            f32(2, 8, rows, nz),
            f32(copies, 1, LANES),
        ),
        in_specs=[VMEM] * len(fields),
        out_specs=(VMEM,) * 5,
        scratch_shapes=[
            pltpu.VMEM((2, FIELDS, rows, nz), F32),
            pltpu.VMEM((steps, rows, nz), F32),
        ],
        compiler_params=params(),
        name="finish",
    )(*fields)


def combine_kernel(
    moments, source, p1_in, p2_in, p3_in, p1_out, p2_out, p3_out, edge,
    fx, gx, fy, gy, fz, gz, dg,
    adjoint_out, residual_out,
    adjoint, residual, sems,
):
    nx, ny, nz = source.shape
    p1 = [(p1_in if 1 <= x < nx - 1 else p1_out).at[x] for x in range(nx)]
    p2 = [(p2_in if 2 <= x < nx - 2 else p2_out).at[x] for x in range(nx)]
    p3 = [
        p3_in.at[x] if 3 <= x < nx - 3 else p3_out.at[x + 1] for x in range(-1, nx + 1)
    ]
    sums = [moments[:, k : k + 1] for k in range(SUMS + 2)]
    ss, pp, sv, vv, pw, ww, theta, phi = sums

    def total(v):
        return jnp.sum(v, axis=0, keepdims=True)

    def norm(g, a, shift, first, mixed, second):
        rest = g - a * shift
        return total(rest * rest * first - 2.0 * a * rest * mixed + a * a * second)

    m0 = total(ss)
    alpha = m0 / total(pp)
    new = norm(1.0, alpha, theta, ss, sv, vv)
    grow = 1.0 + new / m0
    step = new / norm(grow, alpha, phi, pp, pw, ww)
    near = alpha + step * grow
    far = step * alpha
    copies = []

    def send(src, dst, begin, end):
        planes = pl.ds(begin, end - begin)
        copies.append(
            pltpu.make_async_copy(src.at[planes], dst.at[planes], sems.at[len(copies)])
        )
        copies[-1].start()

    half = nx // 2
    for begin in (0, half):
        for x in range(begin, begin + half):
            adjoint[x] = near * p1[x][0:ny] - far * p3[x + 1][0:ny]
        send(adjoint, adjoint_out, begin, begin + half)
    for x in range(nx):
        v = p3[x + 1][...]
        above = edge[1, 0] if x == nx - 1 else gx[x + 1]
        below = edge[0, 0] if x == 0 else fx[x - 1]
        diagonal = edge[0, 3] if x == 0 else edge[1, 3] if x == nx - 1 else dg[x]
        p4 = diagonal * v - above * p3[x + 2][...] - below * p3[x][...]
        p4 = p4 - in_plane_forward(v, fy[x], gy[x], fz[x], gz[x])
        residual[x] = source[x] - near * p2[x][0:ny] + far * p4[0:ny]
        if x % 2 == 1:
            send(residual, residual_out, x - 1, x + 1)
    for copy in copies:
        copy.wait()


def combine(moments, source, *fields):
    nx, ny, nz = source.shape
    return pl.pallas_call(
        combine_kernel,
        out_shape=(f32(nx, ny, nz),) * 2,
        in_specs=[VMEM] * (2 + len(fields)),
        out_specs=(pl.BlockSpec(memory_space=pltpu.HBM),) * 2,
        scratch_shapes=[
            pltpu.VMEM((nx, ny, nz), F32),
            pltpu.VMEM((nx, ny, nz), F32),
            pltpu.SemaphoreType.DMA((2 + nx // 2,)),
        ],
        compiler_params=params(),
        name="combine",
    )(moments, source, *fields)


def swap(cells, axis, first):
    pairs = [(i, i + 1) for i in range(first, lax.axis_size(axis) - 1, 2)]
    return lax.ppermute(cells, axis, pairs + [(j, i) for i, j in pairs])


def local(conc, labels, kappa, source):
    ny = conc.shape[1]
    conc, source, diff = pack(conc, labels, kappa, source)
    xtwo = swap(pack_face(False, conc, diff, source), "gx", 0)
    xone = swap(pack_face(True, conc, diff, source), "gx", 1)
    yone, ytwo = pack_rows(conc, diff, source)
    yone = swap(yone, "gy", 1)
    ytwo = swap(ytwo, "gy", 0)
    cone, ctwo = pack_late(conc, diff, source, yone, ytwo)
    ctwo = swap(ctwo, "gx", 0)
    cone = swap(cone, "gx", 1)
    fields = own(conc, diff, source, yone, ytwo)
    inner = inside(*fields[1:])
    p1, p2, p3, edge, moments = finish(
        lax.axis_size(("gx", "gy")), ny, *fields, *inner, xtwo, xone, ctwo, cone
    )
    moments = lax.all_to_all(moments, ("gx", "gy"), 0, 0, tiled=True)
    moments = moments.reshape(-1, LANES)
    return combine(
        moments, source, fields[10], *inner[:2], p1, p2, p3, edge, *fields[3:10]
    )


def solution(mesh):
    return jax.shard_map(
        local,
        mesh=mesh,
        in_specs=(P("gx", "gy", None), P("gx", "gy", None), P(), P("gx", "gy", None)),
        out_specs=(P("gx", "gy", None), P("gx", "gy", None)),
        check_vma=False,
    )
```

```python
import functools

import jax
import jax.numpy as jnp
from jax import lax
from jax.experimental import pallas as pl
from jax.experimental.pallas import tpu as pltpu
from jax.sharding import PartitionSpec as P

ITERS = 2
DT = 0.5
W = 2 * ITERS
F32 = jnp.float32
LANES = 128
YROWS = (8, 8)
TILE = 8
VMEM = pl.BlockSpec(memory_space=pltpu.VMEM)


def low_first(axis):
    return lax.axis_index(axis) % 2 == 0


def up(v, axis):
    return pltpu.roll(v, v.shape[axis] - 1, axis)


def down(v, axis):
    return pltpu.roll(v, 1, axis)


def z_ends(shape):
    index = lax.broadcasted_iota(jnp.int32, shape, 1)
    return index == 0, index == shape[1] - 1


def coupling(u, d, un, dn):
    return d + d * u - d * un + dn


def params(megabytes=16):
    return pltpu.CompilerParams(vmem_limit_bytes=megabytes << 20)


def f32(*shape):
    return jax.ShapeDtypeStruct(shape, F32)


FIELDS = 7


def late_rows(ny):
    rows = ny + 2 * W
    for field, n in ((0, 3), (1, 3), (2, 3), (3, 2), (4, 1), (5, 1)):
        yield field, ny, n
        yield field, rows - n, n
    for field, n in ((5, 1), (6, 2)):
        yield field, 0, n
        yield field, ny - n, n


def late_count(ny):
    return sum(n for _, _, n in late_rows(ny))


def pack_rows_kernel(conc, diff, source, yone, ytwo):
    nx, ny, nz = conc.shape
    flip = low_first("gy")
    for k, ref in enumerate((conc, diff, source)):
        for out, n, head in ((yone, YROWS[0], flip), (ytwo, YROWS[1], ~flip)):
            out[k, 0:nx] = jnp.where(head, ref[:, 0:n, :], ref[:, ny - n : ny, :])
        yone[k, nx] = jnp.zeros((YROWS[0], nz), F32)


def pack_kernel(
    kappa_in, conc_in, labels_in, source_in,
    conc, source, diff, yone, ytwo,
    labels, kappa, sems,
):
    nx, ny, nz = conc.shape
    copies = [
        pltpu.make_async_copy(src, dst, sems.at[k])
        for k, (src, dst) in enumerate(
            (
                (labels_in, labels),
                (conc_in, conc),
                (kappa_in, kappa),
                (source_in, source),
            )
        )
    ]
    for copy in copies:
        copy.start()
    for copy in copies[:3]:
        copy.wait()
    k0, k1, k2 = ((0.5 * DT) * kappa[k] for k in range(3))

    def body(x, carry):
        lab = labels[x]
        base = jnp.where(lab == 0, k0, jnp.where(lab == 1, k1, k2))
        diff[x] = base * jnp.exp(conc[x])
        return carry

    lax.fori_loop(0, nx, body, 0, unroll=True)
    copies[3].wait()
    pack_rows_kernel(conc, diff, source, yone, ytwo)


def pack(conc, labels, kappa, source):
    nx, ny, nz = conc.shape
    outside = [
        pltpu.with_memory_space_constraint(v, pltpu.HBM)
        for v in (kappa, conc, labels, source)
    ]
    return pl.pallas_call(
        pack_kernel,
        out_shape=(f32(nx, ny, nz),) * 3
        + (f32(3, nx + 1, YROWS[0], nz), f32(3, nx, YROWS[1], nz)),
        in_specs=[pl.BlockSpec(memory_space=pltpu.HBM)] * 4,
        out_specs=(VMEM,) * 5,
        scratch_shapes=[
            pltpu.VMEM((nx, ny, nz), jnp.int32),
            pltpu.SMEM((3,), F32),
            pltpu.SemaphoreType.DMA((4,)),
        ],
        compiler_params=params(),
        name="pack",
    )(*outside)


def rows_beside(yone, ytwo, k, x):
    flip = low_first("gy")
    one, two = (slice(n - W, n) for n in YROWS)
    below = jnp.where(flip, yone[k, x, one], ytwo[k, x, two])
    return below, jnp.where(flip, ytwo[k, x, 0:W], yone[k, x, 0:W])


def in_plane_adjoint(v, fy, gy, fz, gz):
    total = fy * up(v, 0) + gy * down(v, 0)
    return total + (fz * up(v, 1) + gz * down(v, 1))


def in_plane_forward(v, fy, gy, fz, gz):
    total = up(gy * v, 0) + down(fy * v, 0)
    return total + (up(gz * v, 1) + down(fz * v, 1))


def in_plane_couplings(u, d):
    first, last = z_ends(u.shape)
    fy = coupling(u, d, up(u, 0), up(d, 0))
    gy = coupling(u, d, down(u, 0), down(d, 0))
    fz = coupling(u, d, jnp.where(last, 0.0, up(u, 1)), jnp.where(last, 0.0, up(d, 1)))
    gz = coupling(
        u, d, jnp.where(first, 0.0, down(u, 1)), jnp.where(first, 0.0, down(d, 1))
    )
    return fy, gy, fz, gz


def face_planes(first_swap, nx):
    at_head = low_first("gx") if first_swap else ~low_first("gx")
    return [jnp.where(at_head, k, nx - 1 - k) for k in range(4)]


def face_fields(u, d, s):
    first, last = z_ends(u[0].shape)

    def between(i, j):
        return coupling(u[i], d[i], u[j], d[j])

    def image(i, before, after):
        fy, gy, fz, gz = in_plane_couplings(u[i], d[i])
        diagonal = 1.0 + ((fy + gy) + (fz + gz)) + (before + after)
        beside = (fy, gy, jnp.where(last, 0.0, fz), jnp.where(first, 0.0, gz))
        total = diagonal * s[i] - before * s[i - 1] - after * s[i + 1]
        total = total - in_plane_adjoint(s[i], *beside)
        return jnp.where(d[i] > 0.0, total, 0.0), diagonal, beside

    back, inward = between(1, 0), between(2, 1)
    near, diagonal, beside = image(1, back, between(1, 2))
    far, _, _ = image(2, inward, between(2, 3))
    rest = diagonal * near - inward * far - in_plane_forward(near, *beside)
    return u[0], d[0], s[0], s[1], between(0, 1), back * near, rest


def face_rows(first_swap, ny):
    return FIELDS * ny + (0 if first_swap else TILE)


def pack_face_kernel(first_swap, conc, diff, source, slab):
    nx, ny, nz = conc.shape
    planes = face_planes(first_swap, nx)
    u, d, s = ([ref[x] for x in planes] for ref in (conc, diff, source))
    for k, v in enumerate(face_fields(u, d, s)):
        n = min(ny, slab.shape[0] - k * ny)
        slab[k * ny : k * ny + n] = v[0:n]
    if not first_swap:
        slab[FIELDS * ny :] = jnp.zeros((TILE, nz), F32)


def pack_face(first_swap, conc, diff, source):
    _, ny, nz = conc.shape
    return pl.pallas_call(
        functools.partial(pack_face_kernel, first_swap),
        out_shape=f32(face_rows(first_swap, ny), nz),
        in_specs=[VMEM] * 3,
        out_specs=VMEM,
        compiler_params=params(),
        name="pack_face",
    )(conc, diff, source)


def pack_late_kernel(
    conc, diff, source, yone, ytwo, cone, ctwo, near_s, out_s
):
    nx, ny, nz = conc.shape
    rows = ny + 2 * W

    def narrow(row):
        if row < ny:
            return row + W if row < W else row - ny + 3 * W
        return row - ny + 3 * W if row < ny + W else row - ny - W

    for first_swap, late in ((True, cone), (False, ctwo)):
        for j, x in enumerate(face_planes(first_swap, nx)):
            for k, ref in enumerate((conc, diff, source)):
                below, above = rows_beside(yone, ytwo, k, x)
                near_s[k, j, 0:W] = below
                near_s[k, j, W : 2 * W] = ref[x, 0:W]
                near_s[k, j, 2 * W : 3 * W] = ref[x, ny - W : ny]
                near_s[k, j, 3 * W :] = above
        fields = face_fields(*([near_s[k, j] for j in range(4)] for k in range(3)))
        for k, v in enumerate(fields):
            out_s[k] = v
        for at in (W - 2, 3 * W + 1):
            mine, following, k = (out_s[j, at : at + 1] for j in (2, 3, 4))
            out_s[3, at : at + 1] = mine - k * (mine - following)
        row = 0
        for k, begin, n in late_rows(ny):
            at = narrow(begin)
            late[row : row + n] = out_s[k, at : at + n]
            row += n


def pack_late(conc, diff, source, yone, ytwo):
    nx, ny, nz = conc.shape
    return pl.pallas_call(
        pack_late_kernel,
        out_shape=(f32(late_count(ny), nz),) * 2,
        in_specs=[VMEM] * 5,
        out_specs=(VMEM,) * 2,
        scratch_shapes=[
            pltpu.VMEM((3, 4, 4 * W, nz), F32),
            pltpu.VMEM((FIELDS, 4 * W, nz), F32),
        ],
        compiler_params=params(),
        name="pack_late",
    )(conc, diff, source, yone, ytwo)


def own_kernel(
    conc, diff, source, yone, ytwo,
    u_s, d_s, s_s, fx, gx, fy, gy, fz, gz, dg, p1,
):
    nx, ny, nz = conc.shape
    rows = ny + 2 * W
    for k, (own, ref) in enumerate(((conc, u_s), (diff, d_s), (source, s_s))):
        below, above = rows_beside(yone, ytwo, k, slice(0, nx))
        ref[:, 0:ny, :] = own[...]
        ref[:, ny : ny + W, :] = above
        ref[:, ny + W :, :] = below
    first, last = z_ends((rows, nz))

    for q in range(nx):
        u, d = u_s[q], d_s[q]
        fyq, gyq, fzq, gzq = in_plane_couplings(u, d)
        total = 1.0 + ((fyq + gyq) + (fzq + gzq))
        if q + 1 < nx:
            fxq = coupling(u, d, u_s[q + 1], d_s[q + 1])
            fx[q] = fxq
            total = total + fxq
        if q > 0:
            gxq = coupling(u, d, u_s[q - 1], d_s[q - 1])
            gx[q] = gxq
            total = total + gxq
        dg[q] = total
        fy[q] = fyq
        gy[q] = gyq
        fz[q] = jnp.where(last, 0.0, fzq)
        gz[q] = jnp.where(first, 0.0, gzq)

    for q in range(1, nx - 1):
        v = s_s[q]
        total = dg[q] * v - fx[q] * s_s[q + 1] - gx[q] * s_s[q - 1]
        total = total - in_plane_adjoint(v, fy[q], gy[q], fz[q], gz[q])
        p1[q] = jnp.where(d_s[q] > 0.0, total, 0.0)


def own(conc, diff, source, yone, ytwo):
    nx, ny, nz = conc.shape
    return pl.pallas_call(
        own_kernel,
        out_shape=(f32(nx, ny + 2 * W, nz),) * 11,
        in_specs=[VMEM] * 5,
        out_specs=(VMEM,) * 11,
        compiler_params=params(),
        name="own",
    )(conc, diff, source, yone, ytwo)


def mask_halo(total, d, ny):
    return jnp.concatenate([total[0:ny], jnp.where(d > 0.0, total[ny:], 0.0)], axis=0)


def product(v, w, ny):
    both = v[0:ny] * w[0:ny]
    return jnp.sum(both.reshape(ny // 8, 8, both.shape[1]), axis=0)


def ratio(over, under, whole):
    over, under, whole = (
        jnp.sum(v, axis=(0, 1), keepdims=True) for v in (over, under, whole)
    )
    under = jnp.where(whole <= 16.0 * under, under, whole)
    return jnp.where(under > 0.0, over / jnp.where(under > 0.0, under, 1.0), 0.0)


SUMS = 6


def inside_kernel(d_s, s_s, fx, gx, fy, gy, fz, gz, dg, p1, p2, p3, part):
    nx, rows, nz = d_s.shape
    ny = rows - 2 * W
    sums = [jnp.zeros((8, nz), F32) for _ in range(SUMS)]
    over, under = jnp.zeros((8, nz), F32), jnp.zeros((8, nz), F32)
    for q in range(nx):
        sums[0] = sums[0] + product(s_s[q], s_s[q], ny)
    for q in range(1, nx - 1):
        sums[1] = sums[1] + product(p1[q], p1[q], ny)
    for q in range(2, nx - 2):
        v = p1[q]
        total = dg[q] * v - gx[q + 1] * p1[q + 1] - fx[q - 1] * p1[q - 1]
        total = total - in_plane_forward(v, fy[q], gy[q], fz[q], gz[q])
        p2[q] = jnp.where(d_s[q] > 0.0, total, 0.0)
        over = over + product(total, s_s[q], ny)
        under = under + product(s_s[q], s_s[q], ny)
    theta = ratio(over, under, sums[0])
    for q in range(2, nx - 2):
        v = p2[q] - theta * s_s[q]
        sums[2] = sums[2] + product(s_s[q], v, ny)
        sums[3] = sums[3] + product(v, v, ny)
    over, under = jnp.zeros((8, nz), F32), jnp.zeros((8, nz), F32)
    for q in range(3, nx - 3):
        v = p2[q]
        total = dg[q] * v - fx[q] * p2[q + 1] - gx[q] * p2[q - 1]
        total = total - in_plane_adjoint(v, fy[q], gy[q], fz[q], gz[q])
        p3[q] = jnp.where(d_s[q] > 0.0, total, 0.0)
        over = over + product(total, p1[q], ny)
        under = under + product(p1[q], p1[q], ny)
    phi = ratio(over, under, sums[1])
    for q in range(3, nx - 3):
        w = p3[q] - phi * p1[q]
        sums[4] = sums[4] + product(p1[q], w, ny)
        sums[5] = sums[5] + product(w, w, ny)
    for k, total in enumerate(sums):
        part[k] = total
    whole = jnp.sum(sums[0], axis=(0, 1), keepdims=True)
    part[0] = jnp.broadcast_to(whole, (8, nz))
    part[SUMS] = jnp.broadcast_to(theta, (8, nz))
    part[SUMS + 1] = jnp.broadcast_to(phi, (8, nz))


def inside(d_s, *fields):
    nx, rows, nz = d_s.shape
    return pl.pallas_call(
        inside_kernel,
        out_shape=(f32(nx, rows, nz),) * 2 + (f32(SUMS + 2, 8, nz),),
        in_specs=[VMEM] * 10,
        out_specs=(VMEM,) * 3,
        compiler_params=params(),
        cost_estimate=pl.CostEstimate(
            flops=1 << 22, bytes_accessed=1 << 23, transcendentals=0
        ),
        name="inside",
    )(d_s, *fields)


def finish_kernel(
    u_s, d_s, s_s, fx, gx, fy, gy, fz, gz, dg, p1_in, p2_in, p3_in, part,
    xtwo, xone, ctwo, cone,
    p1_out, p2_out, p3_out, edge_s, moments,
    side_s, w_s,
):
    nx, rows, nz = d_s.shape
    ny = rows - 2 * W
    flip = low_first("gx")
    first, last = z_ends((rows, nz))

    for side, one in ((0, flip), (1, ~flip)):
        for k in range(FIELDS):
            n = min(ny, xone.shape[0] - k * ny)
            held = slice(k * ny, k * ny + n)
            side_s[side, k, 0:n] = jnp.where(one, xone[held], xtwo[held])
        side_s[side, :, ny:] = jnp.zeros((FIELDS, 2 * W, nz), F32)
        for at in (ny + 1, rows - 2):
            side_s[side, 4, at : at + 1] = jnp.ones((1, nz), F32)
        late = jnp.where(one, cone[...], ctwo[...])
        row = 0
        for field, begin, n in late_rows(ny):
            side_s[side, field, begin : begin + n] = late[row : row + n]
            row += n

    names = dict(
        u=u_s, d=d_s, s=s_s, fx=fx, gx=gx, fy=fy, gy=gy, fz=fz, gz=gz, dg=dg,
        p1=p1_in, p2=p2_in, p3=p3_in,
    )
    place = {(k, q): names[k].at[q] for k in names for q in range(nx)}
    spare = iter(range(w_s.shape[0]))

    def keep(name, q, value):
        place[name, q] = w_s.at[next(spare)]
        place[name, q][...] = value

    def get(name, q):
        return place[name, q][...]

    for side, (o, e, outward, inward) in enumerate(
        ((-1, 0, "gx", "fx"), (nx, nx - 1, "fx", "gx"))
    ):
        beyond = 2 * o - e
        for k, name in enumerate(("u", "d", "s")):
            place[name, o] = side_s.at[side, k]
        place["s", beyond] = side_s.at[side, 3]
        place[outward, o] = side_s.at[side, 4]
        place["m", o] = side_s.at[side, 5]
        place["q", o] = side_s.at[side, 6]
        u, d, ue, de = get("u", o), get("d", o), get("u", e), get("d", e)
        back = coupling(u, d, ue, de)
        out = coupling(ue, de, u, d)
        fyq, gyq, fzq, gzq = in_plane_couplings(u, d)
        total = 1.0 + get(outward, o) + back + ((fyq + gyq) + (fzq + gzq))
        new = {
            (inward, o): back,
            (outward, e): out,
            ("dg", o): total,
            ("dg", e): get("dg", e) + out,
            ("fy", o): fyq,
            ("gy", o): gyq,
            ("fz", o): jnp.where(last, 0.0, fzq),
            ("gz", o): jnp.where(first, 0.0, gzq),
        }
        for k, (key, value) in enumerate(new.items()):
            place[key] = edge_s.at[side, k]
            place[key][...] = value

    def masked(total, q):
        if q in (-1, nx):
            return jnp.where(get("d", q) > 0.0, total, 0.0)
        return mask_halo(total, place["d", q][ny:], ny)

    def in_plane(q):
        return [get(k, q) for k in ("fy", "gy", "fz", "gz")]

    def adjoint_at(w, q):
        v = get(w, q)
        total = get("dg", q) * v - get("fx", q) * get(w, q + 1)
        total = total - get("gx", q) * get(w, q - 1)
        return masked(total - in_plane_adjoint(v, *in_plane(q)), q)

    def forward_at(w, q):
        v = get(w, q)
        above = get("m", q) if q == nx else get("gx", q + 1) * get(w, q + 1)
        below = get("m", q) if q == -1 else get("fx", q - 1) * get(w, q - 1)
        total = get("dg", q) * v - above - below
        return masked(total - in_plane_forward(v, *in_plane(q)), q)

    sums = [part[k] for k in range(SUMS)]
    theta, phi = (part[SUMS + k][0:1, 0:1] for k in range(2))

    def add(k, v, w):
        sums[k] = sums[k] + product(v, w, ny)

    for q in range(-1, nx + 1):
        if 1 <= q < nx - 1:
            continue
        value = adjoint_at("s", q)
        keep("p1", q, value)
        if 0 <= q < nx:
            p1_out[q] = value[0:ny]
            add(1, value, value)
    for q in range(-1, nx + 1):
        if 2 <= q < nx - 2:
            continue
        value = forward_at("p1", q)
        keep("p2", q, value)
        if 0 <= q < nx:
            p2_out[q] = value[0:ny]
            v = value - theta * get("s", q)
            add(2, get("s", q), v)
            add(3, v, v)
    for o, outward in ((-1, "gx"), (nx, "fx")):
        beyond = -2 if o == -1 else nx + 1
        keep("p2", beyond, get("q", o) - get(outward, o) * get("p1", o))
    for q in range(-1, nx + 1):
        if 3 <= q < nx - 3:
            continue
        value = adjoint_at("p2", q)
        p3_out[q + 1] = value
        if 0 <= q < nx:
            w = value - phi * get("p1", q)
            add(4, get("p1", q), w)
            add(5, w, w)

    slot = lax.broadcasted_iota(jnp.int32, (1, LANES), 1)
    row = jnp.where(slot == SUMS, theta, phi)
    row = jnp.where(slot == 0, part[0][0:1, 0:1], row)
    for k in range(1, SUMS):
        total = jnp.sum(sums[k], axis=0, keepdims=True)
        total = jnp.sum(total, axis=1, keepdims=True)
        row = jnp.where(slot == k, total, row)
    moments[...] = jnp.broadcast_to(row, moments.shape)


def finish(copies, ny, *fields):
    nx, rows, nz = fields[0].shape
    steps = 4 + 6 + 2
    return pl.pallas_call(
        finish_kernel,
        out_shape=(
            f32(nx, ny, nz),
            f32(nx, ny, nz),
            f32(nx + 2, rows, nz),
            f32(2, 8, rows, nz),
            f32(copies, 1, LANES),
        ),
        in_specs=[VMEM] * len(fields),
        out_specs=(VMEM,) * 5,
        scratch_shapes=[
            pltpu.VMEM((2, FIELDS, rows, nz), F32),
            pltpu.VMEM((steps, rows, nz), F32),
        ],
        compiler_params=params(),
        name="finish",
    )(*fields)


def combine_kernel(
    moments, source, p1_in, p2_in, p3_in, p1_out, p2_out, p3_out, edge,
    fx, gx, fy, gy, fz, gz, dg,
    adjoint_out, residual_out,
    adjoint, residual, sems,
):
    nx, ny, nz = source.shape
    p1 = [(p1_in if 1 <= x < nx - 1 else p1_out).at[x] for x in range(nx)]
    p2 = [(p2_in if 2 <= x < nx - 2 else p2_out).at[x] for x in range(nx)]
    p3 = [
        p3_in.at[x] if 3 <= x < nx - 3 else p3_out.at[x + 1] for x in range(-1, nx + 1)
    ]
    sums = [moments[:, k : k + 1] for k in range(SUMS + 2)]
    ss, pp, sv, vv, pw, ww, theta, phi = sums

    def total(v):
        return jnp.sum(v, axis=0, keepdims=True)

    def norm(g, a, shift, first, mixed, second):
        rest = g - a * shift
        return total(rest * rest * first - 2.0 * a * rest * mixed + a * a * second)

    m0 = total(ss)
    alpha = m0 / total(pp)
    new = norm(1.0, alpha, theta, ss, sv, vv)
    grow = 1.0 + new / m0
    step = new / norm(grow, alpha, phi, pp, pw, ww)
    near = alpha + step * grow
    far = step * alpha
    copies = []

    def send(src, dst, begin, end):
        planes = pl.ds(begin, end - begin)
        copies.append(
            pltpu.make_async_copy(src.at[planes], dst.at[planes], sems.at[len(copies)])
        )
        copies[-1].start()

    half = nx // 2
    for begin in (0, half):
        for x in range(begin, begin + half):
            adjoint[x] = near * p1[x][0:ny] - far * p3[x + 1][0:ny]
        send(adjoint, adjoint_out, begin, begin + half)
    for x in range(nx):
        v = p3[x + 1][...]
        above = edge[1, 0] if x == nx - 1 else gx[x + 1]
        below = edge[0, 0] if x == 0 else fx[x - 1]
        diagonal = edge[0, 3] if x == 0 else edge[1, 3] if x == nx - 1 else dg[x]
        p4 = diagonal * v - above * p3[x + 2][...] - below * p3[x][...]
        p4 = p4 - in_plane_forward(v, fy[x], gy[x], fz[x], gz[x])
        residual[x] = source[x] - near * p2[x][0:ny] + far * p4[0:ny]
        if x % 2 == 1:
            send(residual, residual_out, x - 1, x + 1)
    for copy in copies:
        copy.wait()


def combine(moments, source, *fields):
    nx, ny, nz = source.shape
    return pl.pallas_call(
        combine_kernel,
        out_shape=(f32(nx, ny, nz),) * 2,
        in_specs=[VMEM] * (2 + len(fields)),
        out_specs=(pl.BlockSpec(memory_space=pltpu.HBM),) * 2,
        scratch_shapes=[
            pltpu.VMEM((nx, ny, nz), F32),
            pltpu.VMEM((nx, ny, nz), F32),
            pltpu.SemaphoreType.DMA((2 + nx // 2,)),
        ],
        compiler_params=params(),
        name="combine",
    )(moments, source, *fields)


def swap(cells, axis, first):
    pairs = [(i, i + 1) for i in range(first, lax.axis_size(axis) - 1, 2)]
    return lax.ppermute(cells, axis, pairs + [(j, i) for i, j in pairs])


def local(conc, labels, kappa, source):
    ny = conc.shape[1]
    conc, source, diff, yone, ytwo = pack(conc, labels, kappa, source)
    xtwo = swap(pack_face(False, conc, diff, source), "gx", 0)
    xone = swap(pack_face(True, conc, diff, source), "gx", 1)
    yone = swap(yone, "gy", 1)
    ytwo = swap(ytwo, "gy", 0)
    cone, ctwo = pack_late(conc, diff, source, yone, ytwo)
    ctwo = swap(ctwo, "gx", 0)
    cone = swap(cone, "gx", 1)
    fields = own(conc, diff, source, yone, ytwo)
    inner = inside(*fields[1:])
    p1, p2, p3, edge, moments = finish(
        lax.axis_size(("gx", "gy")), ny, *fields, *inner, xtwo, xone, ctwo, cone
    )
    moments = lax.all_to_all(moments, ("gx", "gy"), 0, 0, tiled=True)
    moments = moments.reshape(-1, LANES)
    return combine(
        moments, source, fields[10], *inner[:2], p1, p2, p3, edge, *fields[3:10]
    )


def solution(mesh):
    return jax.shard_map(
        local,
        mesh=mesh,
        in_specs=(P("gx", "gy", None), P("gx", "gy", None), P(), P("gx", "gy", None)),
        out_specs=(P("gx", "gy", None), P("gx", "gy", None)),
        check_vma=False,
    )
```

```python
import functools

import jax
import jax.numpy as jnp
from jax import lax
from jax.experimental import pallas as pl
from jax.experimental.pallas import tpu as pltpu
from jax.sharding import PartitionSpec as P

ITERS = 2
DT = 0.5
W = 2 * ITERS
F32 = jnp.float32
LANES = 128
YROWS = (8, 8)
TILE = 8
VMEM = pl.BlockSpec(memory_space=pltpu.VMEM)


def low_first(axis):
    return lax.axis_index(axis) % 2 == 0


def up(v, axis):
    return pltpu.roll(v, v.shape[axis] - 1, axis)


def down(v, axis):
    return pltpu.roll(v, 1, axis)


def z_ends(shape):
    index = lax.broadcasted_iota(jnp.int32, shape, 1)
    return index == 0, index == shape[1] - 1


def coupling(u, d, un, dn):
    return d + d * u - d * un + dn


def params(megabytes=16):
    return pltpu.CompilerParams(vmem_limit_bytes=megabytes << 20)


def f32(*shape):
    return jax.ShapeDtypeStruct(shape, F32)


FIELDS = 7


def late_rows(ny):
    rows = ny + 2 * W
    for field, n in ((0, 3), (1, 3), (2, 3), (3, 2), (4, 1), (5, 1)):
        yield field, ny, n
        yield field, rows - n, n
    for field, n in ((5, 1), (6, 2)):
        yield field, 0, n
        yield field, ny - n, n


def late_count(ny):
    return sum(n for _, _, n in late_rows(ny))


def pack_kernel(
    kappa_in, conc_in, labels_in, source_in,
    conc, source, diff,
    labels, kappa, sems,
):
    nx, ny, nz = conc.shape
    copies = [
        pltpu.make_async_copy(src, dst, sems.at[k])
        for k, (src, dst) in enumerate(
            (
                (labels_in, labels),
                (conc_in, conc),
                (kappa_in, kappa),
                (source_in, source),
            )
        )
    ]
    for copy in copies:
        copy.start()
    for copy in copies[:3]:
        copy.wait()
    k0, k1, k2 = ((0.5 * DT) * kappa[k] for k in range(3))

    def body(x, carry):
        lab = labels[x]
        base = jnp.where(lab == 0, k0, jnp.where(lab == 1, k1, k2))
        diff[x] = base * jnp.exp(conc[x])
        return carry

    lax.fori_loop(0, nx, body, 0, unroll=True)
    copies[3].wait()


def pack(conc, labels, kappa, source):
    nx, ny, nz = conc.shape
    outside = [
        pltpu.with_memory_space_constraint(v, pltpu.HBM)
        for v in (kappa, conc, labels, source)
    ]
    return pl.pallas_call(
        pack_kernel,
        out_shape=(f32(nx, ny, nz),) * 3,
        in_specs=[pl.BlockSpec(memory_space=pltpu.HBM)] * 4,
        out_specs=(VMEM,) * 3,
        scratch_shapes=[
            pltpu.VMEM((nx, ny, nz), jnp.int32),
            pltpu.SMEM((3,), F32),
            pltpu.SemaphoreType.DMA((4,)),
        ],
        compiler_params=params(),
        name="pack",
    )(*outside)


def pack_rows_kernel(conc, diff, source, yone, ytwo):
    nx, ny, nz = conc.shape
    flip = low_first("gy")
    for k, ref in enumerate((conc, diff, source)):
        for out, n, head in ((yone, YROWS[0], flip), (ytwo, YROWS[1], ~flip)):
            out[k, 0:nx] = jnp.where(head, ref[:, 0:n, :], ref[:, ny - n : ny, :])
        yone[k, nx] = jnp.zeros((YROWS[0], nz), F32)


def pack_rows(conc, diff, source):
    nx, ny, nz = conc.shape
    return pl.pallas_call(
        pack_rows_kernel,
        out_shape=(f32(3, nx + 1, YROWS[0], nz), f32(3, nx, YROWS[1], nz)),
        in_specs=[VMEM] * 3,
        out_specs=(VMEM,) * 2,
        compiler_params=params(),
        name="pack_rows",
    )(conc, diff, source)


def rows_beside(yone, ytwo, k, x):
    flip = low_first("gy")
    one, two = (slice(n - W, n) for n in YROWS)
    below = jnp.where(flip, yone[k, x, one], ytwo[k, x, two])
    return below, jnp.where(flip, ytwo[k, x, 0:W], yone[k, x, 0:W])


def in_plane_adjoint(v, fy, gy, fz, gz):
    total = fy * up(v, 0) + gy * down(v, 0)
    return total + (fz * up(v, 1) + gz * down(v, 1))


def in_plane_forward(v, fy, gy, fz, gz):
    total = up(gy * v, 0) + down(fy * v, 0)
    return total + (up(gz * v, 1) + down(fz * v, 1))


def in_plane_couplings(u, d):
    first, last = z_ends(u.shape)
    fy = coupling(u, d, up(u, 0), up(d, 0))
    gy = coupling(u, d, down(u, 0), down(d, 0))
    fz = coupling(u, d, jnp.where(last, 0.0, up(u, 1)), jnp.where(last, 0.0, up(d, 1)))
    gz = coupling(
        u, d, jnp.where(first, 0.0, down(u, 1)), jnp.where(first, 0.0, down(d, 1))
    )
    return fy, gy, fz, gz


def face_planes(first_swap, nx):
    at_head = low_first("gx") if first_swap else ~low_first("gx")
    return [jnp.where(at_head, k, nx - 1 - k) for k in range(4)]


def face_fields(u, d, s, own_rows=False):
    first, last = z_ends(u[0].shape)

    def between(i, j):
        return coupling(u[i], d[i], u[j], d[j])

    def image(i, before, after):
        fy, gy, fz, gz = in_plane_couplings(u[i], d[i])
        diagonal = 1.0 + ((fy + gy) + (fz + gz)) + (before + after)
        beside = (fy, gy, jnp.where(last, 0.0, fz), jnp.where(first, 0.0, gz))
        total = diagonal * s[i] - before * s[i - 1] - after * s[i + 1]
        total = total - in_plane_adjoint(s[i], *beside)
        if not own_rows:
            total = jnp.where(d[i] > 0.0, total, 0.0)
        return total, diagonal, beside

    back, inward = between(1, 0), between(2, 1)
    near, diagonal, beside = image(1, back, between(1, 2))
    far, _, _ = image(2, inward, between(2, 3))
    rest = diagonal * near - inward * far - in_plane_forward(near, *beside)
    return u[0], d[0], s[0], s[1], between(0, 1), back * near, rest


def face_rows(first_swap, ny):
    return FIELDS * ny + (0 if first_swap else TILE)


def pack_face_kernel(first_swap, conc, diff, source, slab):
    nx, ny, nz = conc.shape
    planes = face_planes(first_swap, nx)
    u, d, s = ([ref[x] for x in planes] for ref in (conc, diff, source))
    for k, v in enumerate(face_fields(u, d, s, own_rows=True)):
        n = min(ny, slab.shape[0] - k * ny)
        slab[k * ny : k * ny + n] = v[0:n]
    if not first_swap:
        slab[FIELDS * ny :] = jnp.zeros((TILE, nz), F32)


def pack_face(first_swap, conc, diff, source):
    _, ny, nz = conc.shape
    return pl.pallas_call(
        functools.partial(pack_face_kernel, first_swap),
        out_shape=f32(face_rows(first_swap, ny), nz),
        in_specs=[VMEM] * 3,
        out_specs=VMEM,
        compiler_params=params(),
        name="pack_face",
    )(conc, diff, source)


def pack_late_kernel(
    conc, diff, source, yone, ytwo, cone, ctwo, near_s, out_s
):
    nx, ny, nz = conc.shape
    rows = ny + 2 * W

    def narrow(row):
        if row < ny:
            return row + W if row < W else row - ny + 3 * W
        return row - ny + 3 * W if row < ny + W else row - ny - W

    for first_swap, late in ((True, cone), (False, ctwo)):
        for j, x in enumerate(face_planes(first_swap, nx)):
            for k, ref in enumerate((conc, diff, source)):
                below, above = rows_beside(yone, ytwo, k, x)
                near_s[k, j, 0:W] = below
                near_s[k, j, W : 2 * W] = ref[x, 0:W]
                near_s[k, j, 2 * W : 3 * W] = ref[x, ny - W : ny]
                near_s[k, j, 3 * W :] = above
        fields = face_fields(*([near_s[k, j] for j in range(4)] for k in range(3)))
        for k, v in enumerate(fields):
            out_s[k] = v
        for at in (W - 2, 3 * W + 1):
            mine, following, k = (out_s[j, at : at + 1] for j in (2, 3, 4))
            out_s[3, at : at + 1] = mine - k * (mine - following)
        row = 0
        for k, begin, n in late_rows(ny):
            at = narrow(begin)
            late[row : row + n] = out_s[k, at : at + n]
            row += n


def pack_late(conc, diff, source, yone, ytwo):
    nx, ny, nz = conc.shape
    return pl.pallas_call(
        pack_late_kernel,
        out_shape=(f32(late_count(ny), nz),) * 2,
        in_specs=[VMEM] * 5,
        out_specs=(VMEM,) * 2,
        scratch_shapes=[
            pltpu.VMEM((3, 4, 4 * W, nz), F32),
            pltpu.VMEM((FIELDS, 4 * W, nz), F32),
        ],
        compiler_params=params(),
        name="pack_late",
    )(conc, diff, source, yone, ytwo)


def own_kernel(
    conc, diff, source, yone, ytwo,
    u_s, d_s, s_s, fx, gx, fy, gy, fz, gz, dg, p1,
):
    nx, ny, nz = conc.shape
    rows = ny + 2 * W
    for k, (own, ref) in enumerate(((conc, u_s), (diff, d_s), (source, s_s))):
        below, above = rows_beside(yone, ytwo, k, slice(0, nx))
        ref[:, 0:ny, :] = own[...]
        ref[:, ny : ny + W, :] = above
        ref[:, ny + W :, :] = below
    first, last = z_ends((rows, nz))

    for q in range(nx):
        u, d = u_s[q], d_s[q]
        fyq, gyq, fzq, gzq = in_plane_couplings(u, d)
        total = 1.0 + ((fyq + gyq) + (fzq + gzq))
        if q + 1 < nx:
            fxq = coupling(u, d, u_s[q + 1], d_s[q + 1])
            fx[q] = fxq
            total = total + fxq
        if q > 0:
            gxq = coupling(u, d, u_s[q - 1], d_s[q - 1])
            gx[q] = gxq
            total = total + gxq
        dg[q] = total
        fy[q] = fyq
        gy[q] = gyq
        fz[q] = jnp.where(last, 0.0, fzq)
        gz[q] = jnp.where(first, 0.0, gzq)

    for q in range(1, nx - 1):
        v = s_s[q]
        total = dg[q] * v - fx[q] * s_s[q + 1] - gx[q] * s_s[q - 1]
        total = total - in_plane_adjoint(v, fy[q], gy[q], fz[q], gz[q])
        p1[q] = jnp.where(d_s[q] > 0.0, total, 0.0)


def own(conc, diff, source, yone, ytwo):
    nx, ny, nz = conc.shape
    return pl.pallas_call(
        own_kernel,
        out_shape=(f32(nx, ny + 2 * W, nz),) * 11,
        in_specs=[VMEM] * 5,
        out_specs=(VMEM,) * 11,
        compiler_params=params(),
        name="own",
    )(conc, diff, source, yone, ytwo)


def mask_halo(total, d, ny):
    return jnp.concatenate([total[0:ny], jnp.where(d > 0.0, total[ny:], 0.0)], axis=0)


def product(v, w, ny):
    both = v[0:ny] * w[0:ny]
    return jnp.sum(both.reshape(ny // 8, 8, both.shape[1]), axis=0)


def ratio(over, under, whole):
    over, under, whole = (
        jnp.sum(v, axis=(0, 1), keepdims=True) for v in (over, under, whole)
    )
    under = jnp.where(whole <= 16.0 * under, under, whole)
    return jnp.where(under > 0.0, over / jnp.where(under > 0.0, under, 1.0), 0.0)


SUMS = 6


def inside_kernel(d_s, s_s, fx, gx, fy, gy, fz, gz, dg, p1, p2, p3, part):
    nx, rows, nz = d_s.shape
    ny = rows - 2 * W
    sums = [jnp.zeros((8, nz), F32) for _ in range(SUMS)]
    over, under = jnp.zeros((8, nz), F32), jnp.zeros((8, nz), F32)
    for q in range(nx):
        sums[0] = sums[0] + product(s_s[q], s_s[q], ny)
    for q in range(1, nx - 1):
        sums[1] = sums[1] + product(p1[q], p1[q], ny)
    for q in range(2, nx - 2):
        v = p1[q]
        total = dg[q] * v - gx[q + 1] * p1[q + 1] - fx[q - 1] * p1[q - 1]
        total = total - in_plane_forward(v, fy[q], gy[q], fz[q], gz[q])
        p2[q] = jnp.where(d_s[q] > 0.0, total, 0.0)
        over = over + product(total, s_s[q], ny)
        under = under + product(s_s[q], s_s[q], ny)
    theta = ratio(over, under, sums[0])
    for q in range(2, nx - 2):
        v = p2[q] - theta * s_s[q]
        sums[2] = sums[2] + product(s_s[q], v, ny)
        sums[3] = sums[3] + product(v, v, ny)
    over, under = jnp.zeros((8, nz), F32), jnp.zeros((8, nz), F32)
    for q in range(3, nx - 3):
        v = p2[q]
        total = dg[q] * v - fx[q] * p2[q + 1] - gx[q] * p2[q - 1]
        total = total - in_plane_adjoint(v, fy[q], gy[q], fz[q], gz[q])
        p3[q] = jnp.where(d_s[q] > 0.0, total, 0.0)
        over = over + product(total, p1[q], ny)
        under = under + product(p1[q], p1[q], ny)
    phi = ratio(over, under, sums[1])
    for q in range(3, nx - 3):
        w = p3[q] - phi * p1[q]
        sums[4] = sums[4] + product(p1[q], w, ny)
        sums[5] = sums[5] + product(w, w, ny)
    for k, total in enumerate(sums):
        part[k] = total
    part[SUMS] = jnp.broadcast_to(theta, (8, nz))
    part[SUMS + 1] = jnp.broadcast_to(phi, (8, nz))


def inside(d_s, *fields):
    nx, rows, nz = d_s.shape
    return pl.pallas_call(
        inside_kernel,
        out_shape=(f32(nx, rows, nz),) * 2 + (f32(SUMS + 2, 8, nz),),
        in_specs=[VMEM] * 10,
        out_specs=(VMEM,) * 3,
        compiler_params=params(),
        cost_estimate=pl.CostEstimate(
            flops=1 << 22, bytes_accessed=1 << 23, transcendentals=0
        ),
        name="inside",
    )(d_s, *fields)


def finish_kernel(
    u_s, d_s, s_s, fx, gx, fy, gy, fz, gz, dg, p1_in, p2_in, p3_in, part,
    xtwo, xone, ctwo, cone,
    p1_out, p2_out, p3_out, edge_s, moments,
    side_s, w_s,
):
    nx, rows, nz = d_s.shape
    ny = rows - 2 * W
    flip = low_first("gx")
    first, last = z_ends((rows, nz))

    for side, one in ((0, flip), (1, ~flip)):
        for k in range(FIELDS):
            n = min(ny, xone.shape[0] - k * ny)
            held = slice(k * ny, k * ny + n)
            side_s[side, k, 0:n] = jnp.where(one, xone[held], xtwo[held])
        side_s[side, :, ny:] = jnp.zeros((FIELDS, 2 * W, nz), F32)
        for at in (ny + 1, rows - 2):
            side_s[side, 4, at : at + 1] = jnp.ones((1, nz), F32)
        late = jnp.where(one, cone[...], ctwo[...])
        row = 0
        for field, begin, n in late_rows(ny):
            side_s[side, field, begin : begin + n] = late[row : row + n]
            row += n

    names = dict(
        u=u_s, d=d_s, s=s_s, fx=fx, gx=gx, fy=fy, gy=gy, fz=fz, gz=gz, dg=dg,
        p1=p1_in, p2=p2_in, p3=p3_in,
    )
    place = {(k, q): names[k].at[q] for k in names for q in range(nx)}
    spare = iter(range(w_s.shape[0]))

    def keep(name, q, value):
        place[name, q] = w_s.at[next(spare)]
        place[name, q][...] = value

    def get(name, q):
        return place[name, q][...]

    for side, (o, e, outward, inward) in enumerate(
        ((-1, 0, "gx", "fx"), (nx, nx - 1, "fx", "gx"))
    ):
        beyond = 2 * o - e
        for k, name in enumerate(("u", "d", "s")):
            place[name, o] = side_s.at[side, k]
        place["s", beyond] = side_s.at[side, 3]
        place[outward, o] = side_s.at[side, 4]
        place["m", o] = side_s.at[side, 5]
        place["q", o] = side_s.at[side, 6]
        u, d, ue, de = get("u", o), get("d", o), get("u", e), get("d", e)
        back = coupling(u, d, ue, de)
        out = coupling(ue, de, u, d)
        fyq, gyq, fzq, gzq = in_plane_couplings(u, d)
        total = 1.0 + get(outward, o) + back + ((fyq + gyq) + (fzq + gzq))
        new = {
            (inward, o): back,
            (outward, e): out,
            ("dg", o): total,
            ("dg", e): get("dg", e) + out,
            ("fy", o): fyq,
            ("gy", o): gyq,
            ("fz", o): jnp.where(last, 0.0, fzq),
            ("gz", o): jnp.where(first, 0.0, gzq),
        }
        for k, (key, value) in enumerate(new.items()):
            place[key] = edge_s.at[side, k]
            place[key][...] = value

    def masked(total, q):
        if q in (-1, nx):
            return jnp.where(get("d", q) > 0.0, total, 0.0)
        return mask_halo(total, place["d", q][ny:], ny)

    def in_plane(q):
        return [get(k, q) for k in ("fy", "gy", "fz", "gz")]

    def adjoint_at(w, q):
        v = get(w, q)
        total = get("dg", q) * v - get("fx", q) * get(w, q + 1)
        total = total - get("gx", q) * get(w, q - 1)
        return masked(total - in_plane_adjoint(v, *in_plane(q)), q)

    def forward_at(w, q):
        v = get(w, q)
        above = get("m", q) if q == nx else get("gx", q + 1) * get(w, q + 1)
        below = get("m", q) if q == -1 else get("fx", q - 1) * get(w, q - 1)
        total = get("dg", q) * v - above - below
        return masked(total - in_plane_forward(v, *in_plane(q)), q)

    sums = [part[k] for k in range(SUMS)]
    theta, phi = (part[SUMS + k][0:1, 0:1] for k in range(2))

    def add(k, v, w):
        sums[k] = sums[k] + product(v, w, ny)

    for q in range(-1, nx + 1):
        if 1 <= q < nx - 1:
            continue
        value = adjoint_at("s", q)
        keep("p1", q, value)
        if 0 <= q < nx:
            p1_out[q] = value[0:ny]
            add(1, value, value)
    for q in range(-1, nx + 1):
        if 2 <= q < nx - 2:
            continue
        value = forward_at("p1", q)
        keep("p2", q, value)
        if 0 <= q < nx:
            p2_out[q] = value[0:ny]
            v = value - theta * get("s", q)
            add(2, get("s", q), v)
            add(3, v, v)
    for o, outward in ((-1, "gx"), (nx, "fx")):
        beyond = -2 if o == -1 else nx + 1
        keep("p2", beyond, get("q", o) - get(outward, o) * get("p1", o))
    for q in range(-1, nx + 1):
        if 3 <= q < nx - 3:
            continue
        value = adjoint_at("p2", q)
        p3_out[q + 1] = value
        if 0 <= q < nx:
            w = value - phi * get("p1", q)
            add(4, get("p1", q), w)
            add(5, w, w)

    slot = lax.broadcasted_iota(jnp.int32, (1, LANES), 1)
    row = jnp.where(slot == SUMS, theta, phi)
    for k in range(SUMS):
        total = jnp.sum(sums[k], axis=0, keepdims=True)
        total = jnp.sum(total, axis=1, keepdims=True)
        row = jnp.where(slot == k, total, row)
    moments[...] = jnp.broadcast_to(row, moments.shape)


def finish(copies, ny, *fields):
    nx, rows, nz = fields[0].shape
    steps = 4 + 6 + 2
    return pl.pallas_call(
        finish_kernel,
        out_shape=(
            f32(nx, ny, nz),
            f32(nx, ny, nz),
            f32(nx + 2, rows, nz),
            f32(2, 8, rows, nz),
            f32(copies, 1, LANES),
        ),
        in_specs=[VMEM] * len(fields),
        out_specs=(VMEM,) * 5,
        scratch_shapes=[
            pltpu.VMEM((2, FIELDS, rows, nz), F32),
            pltpu.VMEM((steps, rows, nz), F32),
        ],
        compiler_params=params(),
        name="finish",
    )(*fields)


def combine_kernel(
    moments, source, p1_in, p2_in, p3_in, p1_out, p2_out, p3_out, edge,
    fx, gx, fy, gy, fz, gz, dg,
    adjoint_out, residual_out,
    adjoint, residual, sems,
):
    nx, ny, nz = source.shape
    p1 = [(p1_in if 1 <= x < nx - 1 else p1_out).at[x] for x in range(nx)]
    p2 = [(p2_in if 2 <= x < nx - 2 else p2_out).at[x] for x in range(nx)]
    p3 = [
        p3_in.at[x] if 3 <= x < nx - 3 else p3_out.at[x + 1] for x in range(-1, nx + 1)
    ]
    sums = [moments[:, k : k + 1] for k in range(SUMS + 2)]
    ss, pp, sv, vv, pw, ww, theta, phi = sums

    def total(v):
        return jnp.sum(v, axis=0, keepdims=True)

    def norm(g, a, shift, first, mixed, second):
        rest = g - a * shift
        return total(rest * rest * first - 2.0 * a * rest * mixed + a * a * second)

    m0 = total(ss)
    alpha = m0 / total(pp)
    new = norm(1.0, alpha, theta, ss, sv, vv)
    grow = 1.0 + new / m0
    step = new / norm(grow, alpha, phi, pp, pw, ww)
    near = alpha + step * grow
    far = step * alpha
    copies = []

    def send(src, dst, begin, end):
        planes = pl.ds(begin, end - begin)
        copies.append(
            pltpu.make_async_copy(src.at[planes], dst.at[planes], sems.at[len(copies)])
        )
        copies[-1].start()

    half = nx // 2
    for begin in (0, half):
        for x in range(begin, begin + half):
            adjoint[x] = near * p1[x][0:ny] - far * p3[x + 1][0:ny]
        send(adjoint, adjoint_out, begin, begin + half)
    for x in range(nx):
        v = p3[x + 1][...]
        above = edge[1, 0] if x == nx - 1 else gx[x + 1]
        below = edge[0, 0] if x == 0 else fx[x - 1]
        diagonal = edge[0, 3] if x == 0 else edge[1, 3] if x == nx - 1 else dg[x]
        p4 = diagonal * v - above * p3[x + 2][...] - below * p3[x][...]
        p4 = p4 - in_plane_forward(v, fy[x], gy[x], fz[x], gz[x])
        residual[x] = source[x] - near * p2[x][0:ny] + far * p4[0:ny]
        if x % 2 == 1:
            send(residual, residual_out, x - 1, x + 1)
    for copy in copies:
        copy.wait()


def combine(moments, source, *fields):
    nx, ny, nz = source.shape
    return pl.pallas_call(
        combine_kernel,
        out_shape=(f32(nx, ny, nz),) * 2,
        in_specs=[VMEM] * (2 + len(fields)),
        out_specs=(pl.BlockSpec(memory_space=pltpu.HBM),) * 2,
        scratch_shapes=[
            pltpu.VMEM((nx, ny, nz), F32),
            pltpu.VMEM((nx, ny, nz), F32),
            pltpu.SemaphoreType.DMA((2 + nx // 2,)),
        ],
        compiler_params=params(),
        name="combine",
    )(moments, source, *fields)


def swap(cells, axis, first):
    pairs = [(i, i + 1) for i in range(first, lax.axis_size(axis) - 1, 2)]
    return lax.ppermute(cells, axis, pairs + [(j, i) for i, j in pairs])


def local(conc, labels, kappa, source):
    ny = conc.shape[1]
    conc, source, diff = pack(conc, labels, kappa, source)
    xtwo = swap(pack_face(False, conc, diff, source), "gx", 0)
    xone = swap(pack_face(True, conc, diff, source), "gx", 1)
    yone, ytwo = pack_rows(conc, diff, source)
    yone = swap(yone, "gy", 1)
    ytwo = swap(ytwo, "gy", 0)
    cone, ctwo = pack_late(conc, diff, source, yone, ytwo)
    ctwo = swap(ctwo, "gx", 0)
    cone = swap(cone, "gx", 1)
    fields = own(conc, diff, source, yone, ytwo)
    inner = inside(*fields[1:])
    p1, p2, p3, edge, moments = finish(
        lax.axis_size(("gx", "gy")), ny, *fields, *inner, xtwo, xone, ctwo, cone
    )
    moments = lax.all_to_all(moments, ("gx", "gy"), 0, 0, tiled=True)
    moments = moments.reshape(-1, LANES)
    return combine(
        moments, source, fields[10], *inner[:2], p1, p2, p3, edge, *fields[3:10]
    )


def solution(mesh):
    return jax.shard_map(
        local,
        mesh=mesh,
        in_specs=(P("gx", "gy", None), P("gx", "gy", None), P(), P("gx", "gy", None)),
        out_specs=(P("gx", "gy", None), P("gx", "gy", None)),
        check_vma=False,
    )
```
